128 devices in a mesh: section: 2 (over core), dp: 64 (over y, z, x).
Axes of the slice: x: 4, y: 4, z: 4, core: 2. Of those that a mesh axis runs over, the one named last changes fastest.
Arguments:
- layer_input: bfloat16 [2, 8192, 1024], P(None, 'dp'), may hold values from -6 to 6
- out_grad: bfloat16 [2, 8192, 1024], P(None, 'dp'), may hold values from -6 to 6
- in_weight: bfloat16 [2, 1024, 3352], P('section', 'dp'), may hold values from -0.1875 to 0.1875
- query_weight: bfloat16 [2, 1024, 512], P('section', 'dp'), may hold values from -0.1875 to 0.1875
- key_weight: bfloat16 [2, 1024, 128], P('section', 'dp'), may hold values from -0.1875 to 0.1875
- value_weight: bfloat16 [2, 1024, 128], P('section', 'dp'), may hold values from -0.1875 to 0.1875
- out_weight: bfloat16 [2, 1536, 1024], P('section', 'dp'), may hold values from -0.15625 to 0.15625
- heads_weight: bfloat16 [2, 512, 1024], P('section', 'dp'), may hold values from -1 to 1
- gate_weight: bfloat16 [2, 1024, 2048], P('section', 'dp'), may hold values from -0.1875 to 0.1875
- up_weight: bfloat16 [2, 1024, 2048], P('section', 'dp'), may hold values from -0.1875 to 0.1875
- down_weight: bfloat16 [2, 2048, 1024], P('section', 'dp'), may hold values from -0.1875 to 0.1875
- input_gain: float32 [2, 1024], P('section'), may hold values from 0.25 to 1.75
- conv_kernel: float32 [2, 4, 1792], P('section'), may hold values from -3 to 3
- conv_bias: float32 [2, 1792], P('section'), may hold values from -0.5 to 0.5
- step_bias: float32 [2, 24], P('section'), may hold values from -4 to -0.5
- decay_log: float32 [2, 24], P('section'), may hold values from -2 to 1
- skip_gain: float32 [2, 24], P('section'), may hold values from 0.5 to 2
- mixer_gain: float32 [2, 1536], P('section'), may hold values from 0.25 to 1.75
- feed_gain: float32 [2, 1024], P('section'), may hold values from 0.25 to 1.75
Outputs:
- layer_outputs: bfloat16 [2, 2, 8192, 1024], P('section', None, 'dp')
- input_grads: float32 [2, 2, 8192, 1024], P('section', None, 'dp')
- in_weight_grad: float32 [2, 1024, 3352], P('section', 'dp')
- query_weight_grad: float32 [2, 1024, 512], P('section', 'dp')
- key_weight_grad: float32 [2, 1024, 128], P('section', 'dp')
- value_weight_grad: float32 [2, 1024, 128], P('section', 'dp')
- out_weight_grad: float32 [2, 1536, 1024], P('section', 'dp')
- heads_weight_grad: float32 [2, 512, 1024], P('section', 'dp')
- gate_weight_grad: float32 [2, 1024, 2048], P('section', 'dp')
- up_weight_grad: float32 [2, 1024, 2048], P('section', 'dp')
- down_weight_grad: float32 [2, 2048, 1024], P('section', 'dp')
- input_gain_grad: float32 [2, 1024], P('section')
- conv_kernel_grad: float32 [2, 4, 1792], P('section')
- conv_bias_grad: float32 [2, 1792], P('section')
- step_bias_grad: float32 [2, 24], P('section')
- decay_log_grad: float32 [2, 24], P('section')
- skip_gain_grad: float32 [2, 24], P('section')
- mixer_gain_grad: float32 [2, 1536], P('section')
- feed_gain_grad: float32 [2, 1024], P('section')
The draws below stay inside these ranges and needn't reach their ends.
All inputs are finite; a program needn't handle non-finite values.
Results may differ from the reference program's by a relative error of at most 0.025.
Values may be sent and summed in bfloat16 or wider, within the bound.
No kernel may reach another device: no remote copies, remote signals or barrier semaphores. Data moves between devices by JAX's collectives and lax.ppermute only.
A program may use at most 256 MiB of HBM per device.

```python
import math
import jax
import jax.numpy as jnp
from jax import lax

D = 1024
FF = 2048
QH = 8
KVH = 2
HD = 64
MH = 24
KCONV = 4
LEN = 128
MICRO = 2
DS = 1536
CONVW = 1792
PROJ = 3352
BATCH = 8192


def levels(stream_key, dims, shards, low, top_value):
    factor_of, own = 1.0, jax.random.fold_in(stream_key, 6)
    for dim, shards_of in shards:
        heights = jnp.exp(jax.random.uniform(jax.random.fold_in(own, dim), (shards_of,), jnp.float32, low / len(shards), top_value / len(shards)))
        factor_of = factor_of * jnp.repeat(heights, dims[dim] // shards_of).reshape([-1 if axis == dim else 1 for axis in range(len(dims))])
    return factor_of


def noise(rng, dims, deviation, limit, cuts=(), dtype=jnp.bfloat16):
    result = deviation * jax.random.normal(rng, dims, jnp.float32)
    if cuts:
        result = result * levels(rng, dims, cuts, -0.22, 0.18)
    return jnp.clip(result, -limit, limit).astype(dtype)


def setup_inputs(seed: int = 0) -> dict:
    streams_of = jax.random.split(jax.random.key(seed), 20)
    return {
        "layer_input": noise(streams_of[0], (MICRO, BATCH, D), 1.0, 6.0, ((1, 64),)),
        "out_grad": noise(streams_of[1], (MICRO, BATCH, D), 1.0, 6.0, ((1, 64),)),
        "in_weight": noise(streams_of[2], (2, D, PROJ), D ** -0.5, 0.1875, ((0, 2), (1, 64))),
        "query_weight": noise(streams_of[3], (2, D, QH * HD), D ** -0.5, 0.1875, ((0, 2), (1, 64))),
        "key_weight": noise(streams_of[4], (2, D, KVH * HD), D ** -0.5, 0.1875, ((0, 2), (1, 64))),
        "value_weight": noise(streams_of[5], (2, D, KVH * HD), D ** -0.5, 0.1875, ((0, 2), (1, 64))),
        "out_weight": noise(streams_of[6], (2, DS, D), DS ** -0.5, 0.15625, ((0, 2), (1, 64))),
        "heads_weight": noise(streams_of[7], (2, QH * HD, D), (QH * HD // 16) ** -0.5, 1.0, ((0, 2), (1, 64))),
        "gate_weight": noise(streams_of[8], (2, D, FF), D ** -0.5, 0.1875, ((0, 2), (1, 64))),
        "up_weight": noise(streams_of[9], (2, D, FF), D ** -0.5, 0.1875, ((0, 2), (1, 64))),
        "down_weight": noise(streams_of[10], (2, FF, D), (FF // 2) ** -0.5, 0.1875, ((0, 2), (1, 64))),
        "input_gain": jnp.clip(1.0 + 0.15 * jax.random.normal(streams_of[11], (2, D), jnp.float32), 0.25, 1.75),
        "conv_kernel": noise(streams_of[12], (2, KCONV, CONVW), KCONV ** -0.5, 3.0, ((0, 2),), jnp.float32),
        "conv_bias": jnp.clip(jax.random.uniform(streams_of[13], (2, CONVW), jnp.float32, -0.5, 0.5) * levels(streams_of[13], (2, CONVW), ((0, 2),), -0.4, 0.0), -0.5, 0.5),
        "step_bias": jnp.clip(-4.0 + 3.5 * jax.random.uniform(streams_of[14], (2, MH), jnp.float32) ** levels(streams_of[14], (2, MH), ((0, 2),), -0.2, 0.2), -4.0, -0.5),
        "decay_log": jnp.clip(-2.0 + 3.0 * jax.random.uniform(streams_of[15], (2, MH), jnp.float32) ** levels(streams_of[15], (2, MH), ((0, 2),), -0.2, 0.2), -2.0, 1.0),
        "skip_gain": jnp.clip(0.5 + 1.5 * jax.random.uniform(streams_of[16], (2, MH), jnp.float32) ** levels(streams_of[16], (2, MH), ((0, 2),), -0.2, 0.2), 0.5, 2.0),
        "mixer_gain": jnp.clip(1.0 + 0.15 * jax.random.normal(streams_of[17], (2, DS), jnp.float32), 0.25, 1.75),
        "feed_gain": jnp.clip(1.0 + 0.15 * jax.random.normal(streams_of[18], (2, D), jnp.float32), 0.25, 1.75),
    }


@jax.custom_vjp
def low(v):
    return lax.optimization_barrier(v.astype(jnp.bfloat16)).astype(jnp.float32)

@jax.custom_vjp
def low_back(v):
    return v

def low_keep(v):
    return (low(v), None)

def low_pass(kept, grad):
    return (grad,)

def back_keep(v):
    return (v, None)

def back_low(kept, grad):
    return (low(grad),)
low.defvjp(low_keep, low_pass)
low_back.defvjp(back_keep, back_low)

def matmul(left, right):
    return jnp.dot(left, right, precision=lax.Precision.HIGHEST, preferred_element_type=jnp.float32)

def rms_scale(value, gain):
    return value * lax.rsqrt(lax.optimization_barrier(jnp.mean(value * value, axis=-1, keepdims=True)) + 1e-05) * gain

def rotate(value, cosine, sine, sign):
    half = value.shape[-1] // 2
    turned = jnp.concatenate([-value[..., half:], value[..., :half]], axis=-1)
    return value * cosine + sign * turned * sine

def tables(length, width):
    position = jnp.arange(length).astype(jnp.float32)
    inverse = 10000.0 ** (-(jnp.arange(width // 2).astype(jnp.float32) * 2.0) / width)
    angle = position[:, None] * inverse[None, :]
    angle = jnp.concatenate([angle, angle], axis=-1)
    return (jnp.cos(angle)[:, None, :], jnp.sin(angle)[:, None, :])

def mamba_core(proj, conv_kernel, conv_bias, step_bias, decay_log, skip_gain, mixer_gain):
    seqs, length = (proj.shape[0], proj.shape[1])
    heads = step_bias.shape[0]
    inner = mixer_gain.shape[0]
    channels = conv_bias.shape[0]
    state = (channels - inner) // 2
    taps = conv_kernel.shape[0]
    gate_z = proj[..., :inner]
    mixed = proj[..., inner:inner + channels]
    step_raw = proj[..., inner + channels:]
    padded = jnp.pad(mixed, ((0, 0), (taps - 1, 0), (0, 0)))
    total = conv_bias + padded[:, 0:length] * conv_kernel[0]
    for tap in range(1, taps):
        total = total + padded[:, tap:tap + length] * conv_kernel[tap]
    active = jax.nn.silu(total)
    inputs = active[..., :inner].reshape(seqs, length, heads, inner // heads)
    state_in = active[..., inner:inner + state]
    state_out = active[..., inner + state:]
    step = jax.nn.softplus(step_raw + step_bias)
    rate = -step * jnp.exp(decay_log)
    cumul = jnp.cumsum(rate, axis=1)
    spread = cumul[:, :, None, :] - cumul[:, None, :, :]
    causal = (jnp.arange(length)[:, None] >= jnp.arange(length)[None, :])[None, :, :, None]
    decay = jnp.where(causal, jnp.exp(jnp.where(causal, spread, 0.0)), 0.0)
    intersection = jnp.einsum('sin,sjn->sij', state_out, state_in, precision=lax.Precision.HIGHEST)
    mixing = intersection[..., None] * decay * step[:, None, :, :]
    output = jnp.einsum('sijh,sjhp->sihp', mixing, inputs, precision=lax.Precision.HIGHEST)
    output = output + skip_gain[:, None] * inputs
    output = output.reshape(seqs, length, inner)
    return rms_scale(output * jax.nn.silu(gate_z), mixer_gain)

def attend_core(q_raw, k_raw, values, cosine, sine):
    groups = k_raw.shape[2]
    queries = low(rotate(q_raw, cosine, sine, 1.0))
    keys = low(rotate(k_raw, cosine, sine, 1.0))
    seqs, length, heads, size = queries.shape
    grouped = queries.reshape(seqs, length, groups, heads // groups, size)
    scores = jnp.einsum('sigrd,sjgd->sgrij', grouped, keys, precision=lax.Precision.HIGHEST)
    scores = low_back(scores * size ** (-0.5))
    causal = jnp.arange(length)[:, None] >= jnp.arange(length)[None, :]
    scores = jnp.where(causal, scores, -1e+30)
    top = lax.optimization_barrier(jnp.max(scores, axis=-1, keepdims=True))
    expo = jnp.exp(scores - top)
    probs = low(expo / lax.optimization_barrier(jnp.sum(expo, axis=-1, keepdims=True)))
    mixed = jnp.einsum('sgrij,sjgd->sigrd', probs, values, precision=lax.Precision.HIGHEST)
    return low(low_back(mixed.reshape(seqs, length, heads * size)))

def layer(state, params, cosine, sine):
    in_weight, query_weight, key_weight, value_weight, out_weight, heads_weight, gate_weight, up_weight, down_weight, input_gain, conv_kernel, conv_bias, step_bias, decay_log, skip_gain, mixer_gain, feed_gain = params
    rows = state.shape[0]
    seqs = rows // LEN
    group = math.gcd(seqs, 32)
    blocks = seqs // group
    normed = low(rms_scale(state, input_gain))
    proj = low_back(matmul(normed, in_weight))
    q_raw = low_back(matmul(normed, query_weight))
    k_raw = low_back(matmul(normed, key_weight))
    values = low(low_back(matmul(normed, value_weight)))

    def block(pieces):
        part_proj, part_q, part_k, part_v = pieces
        mamba = mamba_core(part_proj, conv_kernel, conv_bias, step_bias, decay_log, skip_gain, mixer_gain)
        attended = attend_core(part_q, part_k, part_v, cosine, sine)
        return (mamba, attended)
    pieces = (proj.reshape(blocks, group, LEN, -1), q_raw.reshape(blocks, group, LEN, QH, HD), k_raw.reshape(blocks, group, LEN, KVH, HD), values.reshape(blocks, group, LEN, KVH, HD))
    mamba, attended = lax.map(jax.checkpoint(block), pieces)
    mamba = low(mamba.reshape(rows, -1))
    attended = attended.reshape(rows, -1)
    middle = state + low_back(matmul(mamba, out_weight)) + low_back(matmul(attended, heads_weight))
    ffin = low(rms_scale(middle, feed_gain))
    gate = low_back(matmul(ffin, gate_weight))
    upper = low_back(matmul(ffin, up_weight))
    hidden = low(jax.nn.silu(gate) * upper)
    return middle + low_back(matmul(hidden, down_weight))

def reference(layer_input, out_grad, in_weight, query_weight, key_weight, value_weight, out_weight, heads_weight, gate_weight, up_weight, down_weight, input_gain, conv_kernel, conv_bias, step_bias, decay_log, skip_gain, mixer_gain, feed_gain):
    weights = tuple((item.astype(jnp.float32) for item in (in_weight, query_weight, key_weight, value_weight, out_weight, heads_weight, gate_weight, up_weight, down_weight, input_gain, conv_kernel, conv_bias, step_bias, decay_log, skip_gain, mixer_gain, feed_gain)))
    micro, batch, width = layer_input.shape
    inputs = layer_input.astype(jnp.float32).reshape(micro * batch, width)
    cosine, sine = tables(LEN, HD)

    def forward(start, offset, params):
        first = layer(start, tuple((item[0] for item in params)), cosine, sine)
        second_in = low_back(low(first)) + offset
        return (layer(second_in, tuple((item[1] for item in params)), cosine, sine), first)
    offset = jnp.zeros_like(inputs)
    final, pull, first = jax.vjp(forward, inputs, offset, weights, has_aux=True)
    grad_start, grad_offset, grads = pull(out_grad.astype(jnp.float32).reshape(micro * batch, width))
    outputs = jnp.stack([first, final]).astype(jnp.bfloat16).reshape(2, micro, batch, width)
    input_grads = jnp.stack([grad_start, grad_offset]).reshape(2, micro, batch, width)
    return (outputs, input_grads, grads[0], grads[1], grads[2], grads[3], grads[4], grads[5], grads[6], grads[7], grads[8], grads[9], grads[10], grads[11], grads[12], grads[13], grads[14], grads[15], grads[16])
```

```python
import jax
import jax.numpy as jnp
from jax import lax
from jax.sharding import Mesh
from jax.sharding import PartitionSpec as P

QH = 8
KVH = 2
HD = 64
LEN = 128
DP = ("dp_0", "dp_1", "dp_2")


def matmul(left, right):
    return jnp.dot(left, right, preferred_element_type=jnp.float32)


def transposed(left, right):
    return lax.dot_general(
        left, right, (((0,), (0,)), ((), ())), preferred_element_type=jnp.float32
    )


def backward_product(grad, weight):
    return lax.dot_general(
        grad, weight, (((1,), (1,)), ((), ())), preferred_element_type=jnp.float32
    )


def rms_scale(value, gain):
    return value * lax.rsqrt(jnp.mean(value * value, axis=-1, keepdims=True) + 1e-05) * gain


def rotate(value, cosine, sine, sign):
    half = value.shape[-1] // 2
    turned = jnp.concatenate([-value[..., half:], value[..., :half]], axis=-1)
    return value * cosine + sign * turned * sine


def tables(length, width):
    position = jnp.arange(length).astype(jnp.float32)
    inverse = 10000.0 ** (-(jnp.arange(width // 2).astype(jnp.float32) * 2.0) / width)
    angle = position[:, None] * inverse[None, :]
    angle = jnp.concatenate([angle, angle], axis=-1)
    return (jnp.cos(angle)[:, None, :], jnp.sin(angle)[:, None, :])


def mamba_core(proj, conv_kernel, conv_bias, step_bias, decay_log, skip_gain, mixer_gain):
    seqs, length = (proj.shape[0], proj.shape[1])
    heads = step_bias.shape[0]
    inner = mixer_gain.shape[0]
    channels = conv_bias.shape[0]
    state = (channels - inner) // 2
    taps = conv_kernel.shape[0]
    gate_z = proj[..., :inner]
    mixed = proj[..., inner : inner + channels]
    step_raw = proj[..., inner + channels :]
    padded = jnp.pad(mixed, ((0, 0), (taps - 1, 0), (0, 0)))
    total = conv_bias + padded[:, 0:length] * conv_kernel[0]
    for tap in range(1, taps):
        total = total + padded[:, tap : tap + length] * conv_kernel[tap]
    active = jax.nn.silu(total)
    inputs = active[..., :inner].reshape(seqs, length, heads, inner // heads)
    state_in = active[..., inner : inner + state]
    state_out = active[..., inner + state :]
    step = jax.nn.softplus(step_raw + step_bias)
    rate = -step * jnp.exp(decay_log)
    cumul = jnp.cumsum(rate, axis=1)
    spread = cumul[:, :, None, :] - cumul[:, None, :, :]
    causal = (jnp.arange(length)[:, None] >= jnp.arange(length)[None, :])[None, :, :, None]
    decay = jnp.where(causal, jnp.exp(jnp.where(causal, spread, 0.0)), 0.0)
    intersection = jnp.einsum("sin,sjn->sij", state_out, state_in)
    mixing = intersection[..., None] * decay * step[:, None, :, :]
    output = jnp.einsum("sijh,sjhp->sihp", mixing, inputs)
    output = output + skip_gain[:, None] * inputs
    output = output.reshape(seqs, length, inner)
    return rms_scale(output * jax.nn.silu(gate_z), mixer_gain)


def masked_scores(queries, keys):
    seqs, length, heads, size = queries.shape
    groups = keys.shape[2]
    grouped = queries.reshape(seqs, length, groups, heads // groups, size)
    scores = jnp.einsum(
        "sigrd,sjgd->sgrij", grouped, keys, preferred_element_type=jnp.float32
    ) * size ** (-0.5)
    causal = jnp.arange(length)[:, None] >= jnp.arange(length)[None, :]
    return (grouped, jnp.where(causal, scores, -1e30))


def attend_forward(queries, keys, values):
    seqs, length, heads, size = queries.shape
    grouped, scores = masked_scores(queries, keys)
    top = jnp.max(scores, axis=-1, keepdims=True)
    expo = jnp.exp(scores - top)
    total = jnp.sum(expo, axis=-1, keepdims=True)
    probs = (expo / total).astype(jnp.bfloat16)
    mixed = jnp.einsum("sgrij,sjgd->sigrd", probs, values, preferred_element_type=jnp.float32)
    return (mixed.reshape(seqs, length, heads * size).astype(jnp.bfloat16), top + jnp.log(total))


def attend_backward(queries, keys, values, logsum, grad_out):
    seqs, length, heads, size = queries.shape
    groups = keys.shape[2]
    grouped, scores = masked_scores(queries, keys)
    probs = jnp.exp(scores - logsum)
    rounded = probs.astype(jnp.bfloat16)
    grad_grouped = grad_out.reshape(seqs, length, groups, heads // groups, size)
    grad_values = jnp.einsum(
        "sgrij,sigrd->sjgd", rounded, grad_grouped, preferred_element_type=jnp.float32
    )
    grad_probs = jnp.einsum(
        "sigrd,sjgd->sgrij", grad_grouped, values, preferred_element_type=jnp.float32
    )
    grad_scores = probs * (grad_probs - jnp.sum(probs * grad_probs, axis=-1, keepdims=True))
    grad_scores = grad_scores.astype(jnp.bfloat16)
    scale = size ** (-0.5)
    grad_queries = (
        jnp.einsum("sgrij,sjgd->sigrd", grad_scores, keys, preferred_element_type=jnp.float32)
        * scale
    )
    grad_keys = (
        jnp.einsum("sgrij,sigrd->sjgd", grad_scores, grouped, preferred_element_type=jnp.float32)
        * scale
    )
    return (grad_queries.reshape(seqs, length, heads, size), grad_keys, grad_values)


def silu_product(gate, upper):
    return jax.nn.silu(gate) * upper


CAT = 4224


def run_forward(start, mats, small):
    cat_weight, out_weight, heads_weight, gate_weight, up_weight, down_weight = mats
    input_gain, conv_kernel, conv_bias, step_bias, decay_log, skip_gain, mixer_gain, feed_gain = (
        small
    )
    rows = start.shape[0]
    seqs = rows // LEN
    cosine, sine = tables(LEN, HD)
    state = start.astype(jnp.float32)
    normed = rms_scale(state, input_gain).astype(jnp.bfloat16)
    proj = matmul(normed, cat_weight)
    values = proj[:, 640:768].astype(jnp.bfloat16)
    mamba = (
        mamba_core(
            proj[:, 768:4120].reshape(seqs, LEN, -1),
            conv_kernel,
            conv_bias,
            step_bias,
            decay_log,
            skip_gain,
            mixer_gain,
        )
        .reshape(rows, -1)
        .astype(jnp.bfloat16)
    )
    queries = rotate(proj[:, :512].reshape(seqs, LEN, QH, HD), cosine, sine, 1.0)
    keys = rotate(proj[:, 512:640].reshape(seqs, LEN, KVH, HD), cosine, sine, 1.0)
    queries = queries.astype(jnp.bfloat16)
    keys = keys.astype(jnp.bfloat16)
    attended, logsum = attend_forward(queries, keys, values.reshape(seqs, LEN, KVH, HD))
    attended = attended.reshape(rows, QH * HD)
    middle = state + matmul(mamba, out_weight) + matmul(attended, heads_weight)
    ffin = rms_scale(middle, feed_gain).astype(jnp.bfloat16)
    gate = matmul(ffin, gate_weight)
    upper = matmul(ffin, up_weight)
    hidden = silu_product(gate, upper).astype(jnp.bfloat16)
    result = middle + matmul(hidden, down_weight)
    kept = (state, normed, proj, queries, keys, values, mamba, attended, logsum, middle, ffin)
    return (result.astype(jnp.bfloat16), (*kept, gate, upper, hidden))


def backward_feed(kept, mats, small, grad_top):
    gate_weight, up_weight, down_weight = mats[3:]
    middle, ffin, gate, upper, hidden = kept[9:]
    feed_gain = small[7]
    grad_low = grad_top.astype(jnp.bfloat16)
    grad_hidden = backward_product(grad_low, down_weight)
    unused, swiglu_pull = jax.vjp(silu_product, gate, upper)
    grad_gate, grad_upper = swiglu_pull(grad_hidden)
    grad_gate = grad_gate.astype(jnp.bfloat16)
    grad_upper = grad_upper.astype(jnp.bfloat16)
    grad_ffin = backward_product(grad_gate, gate_weight) + backward_product(grad_upper, up_weight)
    unused, feed_pull = jax.vjp(rms_scale, middle, feed_gain)
    grad_part, feed_grad = feed_pull(grad_ffin)
    return (grad_top + grad_part, feed_grad, (hidden, ffin, grad_low, grad_gate, grad_upper))


def backward_mix(kept, mats, small, grad_middle):
    cat_weight, out_weight, heads_weight = mats[:3]
    input_gain, conv_kernel, conv_bias, step_bias, decay_log, skip_gain, mixer_gain, feed_gain = (
        small
    )
    state, normed, proj, queries, keys, values, mamba, attended, logsum = kept[:9]
    rows = state.shape[0]
    seqs = rows // LEN
    cosine, sine = tables(LEN, HD)
    grad_branch = grad_middle.astype(jnp.bfloat16)
    grad_mamba = backward_product(grad_branch, out_weight)
    grad_attended = backward_product(grad_branch, heads_weight).astype(jnp.bfloat16)
    grad_queries, grad_keys, grad_values = attend_backward(
        queries,
        keys,
        values.reshape(seqs, LEN, KVH, HD),
        logsum,
        grad_attended.reshape(seqs, LEN, QH, HD),
    )
    grad_query = rotate(grad_queries, cosine, sine, -1.0).reshape(rows, -1).astype(jnp.bfloat16)
    grad_key = rotate(grad_keys, cosine, sine, -1.0).reshape(rows, -1).astype(jnp.bfloat16)
    grad_value = grad_values.reshape(rows, -1).astype(jnp.bfloat16)
    unused, mamba_pull = jax.vjp(
        mamba_core,
        proj[:, 768:4120].reshape(seqs, LEN, -1),
        conv_kernel,
        conv_bias,
        step_bias,
        decay_log,
        skip_gain,
        mixer_gain,
    )
    grad_proj, kernel_grad, bias_grad, step_grad, decay_grad, skip_grad, mixer_grad = mamba_pull(
        grad_mamba.reshape(seqs, LEN, -1)
    )
    grad_proj = grad_proj.reshape(rows, -1).astype(jnp.bfloat16)
    pad = jnp.zeros((rows, CAT - 4120), jnp.bfloat16)
    grad_cat = jnp.concatenate([grad_query, grad_key, grad_value, grad_proj, pad], axis=1)
    grad_normed = backward_product(grad_cat, cat_weight)
    unused, input_pull = jax.vjp(rms_scale, state, input_gain)
    grad_state, input_grad = input_pull(grad_normed)
    small_grads = (
        input_grad,
        kernel_grad,
        bias_grad,
        step_grad,
        decay_grad,
        skip_grad,
        mixer_grad,
    )
    factors = (normed, mamba, attended, grad_branch, grad_cat)
    return (grad_middle + grad_state, small_grads, factors)


def around(axis, by):
    length = lax.axis_size(axis)
    return [(i, (i + by) % length) for i in range(length)]


def send(shard, axis, by):
    return lax.ppermute(shard, axis, around(axis, by))


def columns(left, place, piece):
    shape = left.shape
    parts = left.reshape(shape[0], 4, 4, 4, shape[1] // 64)
    return lax.dynamic_index_in_dim(parts, piece, 1 + place, keepdims=False)


def scatter_first(left, right, place):
    axis = DP[place]
    me = lax.axis_index(axis)
    pieces = [columns(left, place, lax.rem(me + by, 4)) for by in range(4)]
    low = [p[:, :2] for p in pieces]
    high = [p[:, 2:] for p in pieces]

    def product(part):
        flat = part.reshape(part.shape[0], -1)
        return transposed(flat, right)

    up_one = product(jnp.concatenate([low[2], high[1]], axis=1)).astype(jnp.bfloat16)
    down_one = product(jnp.concatenate([high[2], low[3]], axis=1)).astype(jnp.bfloat16)
    from_below = send(up_one, axis, 1)
    from_above = send(down_one, axis, -1)
    half = up_one.shape[0] // 2
    up_two = (product(low[1]) + from_below[:half].astype(jnp.float32)).astype(jnp.bfloat16)
    down_two = (product(high[3]) + from_above[:half].astype(jnp.float32)).astype(jnp.bfloat16)
    below_two = send(up_two, axis, 1)
    above_two = send(down_two, axis, -1)
    own_low = product(low[0]) + below_two.astype(jnp.float32) + from_above[half:].astype(jnp.float32)
    own_high = product(high[0]) + above_two.astype(jnp.float32) + from_below[half:].astype(jnp.float32)
    own = jnp.concatenate([own_low, own_high], axis=0).astype(jnp.bfloat16)
    return own.reshape(4, 4, left.shape[1] // 64, right.shape[1])


def scatter_next(array, axis, dim):
    me = lax.axis_index(axis)

    def piece(by):
        return lax.dynamic_index_in_dim(array, lax.rem(me + by, 4), dim, keepdims=False)

    one = send(piece(1), axis, 1)
    three = send(piece(3), axis, -1)
    two = send(piece(2), axis, 2)
    total = piece(0).astype(jnp.float32) + one.astype(jnp.float32)
    return total + three.astype(jnp.float32) + two.astype(jnp.float32)


def scattered(left, right, order):
    array = scatter_first(left, right, order[0])
    rest = [0, 1, 2]
    rest.remove(order[0])
    array = scatter_next(array, DP[order[1]], rest.index(order[1])).astype(jnp.bfloat16)
    return scatter_next(array, DP[order[2]], 0)


def summed_over(vector):
    for axis in DP:
        one = send(vector, axis, 1)
        two = send(vector, axis, 2)
        three = send(vector, axis, 3)
        me = lax.axis_index(axis)
        terms = jnp.stack([vector, one, two, three])
        total = lax.dynamic_index_in_dim(terms, me, 0, keepdims=False)
        for place in range(1, 4):
            total = total + lax.dynamic_index_in_dim(
                terms, lax.rem(me + 4 - place, 4), 0, keepdims=False
            )
        vector = total
    return vector


def on_device(
    layer_input,
    out_grad,
    in_weight,
    query_weight,
    key_weight,
    value_weight,
    out_weight,
    heads_weight,
    gate_weight,
    up_weight,
    down_weight,
    input_gain,
    conv_kernel,
    conv_bias,
    step_bias,
    decay_log,
    skip_gain,
    mixer_gain,
    feed_gain,
):
    micro, part, width = layer_input.shape
    rows = micro * part
    own = jnp.concatenate(
        [
            query_weight[0],
            key_weight[0],
            value_weight[0],
            in_weight[0],
            jnp.zeros((16, CAT - 4120), jnp.bfloat16),
            gate_weight[0],
            up_weight[0],
            down_weight[0].reshape(16, 2048),
            out_weight[0].reshape(16, 1536),
            heads_weight[0].reshape(16, 512),
        ],
        axis=1,
    )
    whole = lax.all_gather(own, DP, axis=0, tiled=True)
    mats = (
        whole[:, :CAT],
        whole[:, CAT + 6144 : CAT + 7680].reshape(1536, 1024),
        whole[:, CAT + 7680 :].reshape(512, 1024),
        whole[:, CAT : CAT + 2048],
        whole[:, CAT + 2048 : CAT + 4096],
        whole[:, CAT + 4096 : CAT + 6144].reshape(2048, 1024),
    )
    small = tuple(
        (
            piece[0]
            for piece in (
                input_gain,
                conv_kernel,
                conv_bias,
                step_bias,
                decay_log,
                skip_gain,
                mixer_gain,
                feed_gain,
            )
        )
    )
    first = lax.axis_index("section") == 0
    start = layer_input.reshape(rows, width)
    result_low, kept_low = run_forward(start, mats, small)
    handed = lax.ppermute(result_low, "section", [(0, 1)])
    result_high, kept_high = run_forward(handed, mats, small)
    layer_outputs = jnp.where(first, result_low, result_high).reshape(1, micro, part, width)

    def backward(kept, grad_top):
        grad_middle, feed_grad, feed_factors = backward_feed(kept, mats, small, grad_top)
        grad_start, small_grads, mix_factors = backward_mix(kept, mats, small, grad_middle)
        return (grad_start, (*small_grads, feed_grad), feed_factors, mix_factors)

    high = backward(kept_high, out_grad.reshape(rows, width).astype(jnp.float32))
    handed = lax.ppermute(high[0].astype(jnp.bfloat16), "section", [(1, 0)])
    input_grads, small_grads, feed_factors, mix_factors = lax.cond(
        first,
        lambda kept, grad, other: backward(kept, grad.astype(jnp.float32)),
        lambda kept, grad, other: other,
        kept_low,
        handed,
        high,
    )
    hidden, ffin, grad_low, grad_gate, grad_upper = feed_factors
    normed, mamba, attended, grad_branch, grad_cat = mix_factors
    down_grad = scattered(hidden, grad_low, (2, 0, 1))
    gate_grad = scattered(ffin, grad_gate, (0, 1, 2))
    up_grad = scattered(ffin, grad_upper, (1, 2, 0))
    cat_left = scattered(normed, grad_cat[:, :2048], (0, 1, 2))
    cat_right = scattered(normed, grad_cat[:, 2048:], (1, 2, 0))
    out_grad_own = scattered(mamba, grad_branch, (2, 0, 1))
    heads_grad = scattered(attended, grad_branch, (2, 0, 1))
    cat_grad = jnp.concatenate([cat_left, cat_right], axis=1)
    packed = jnp.concatenate([piece.reshape(-1) for piece in small_grads])
    packed = jnp.pad(packed, (0, -packed.shape[0] % 1024)).reshape(-1, 128)
    total = summed_over(packed).reshape(-1)
    summed, at = ([], 0)
    for piece in small_grads:
        summed.append(total[at : at + piece.size].reshape(1, *piece.shape))
        at += piece.size
    return (
        layer_outputs,
        input_grads.reshape(1, micro, part, width),
        cat_grad[None, :, 768:4120],
        cat_grad[None, :, :512],
        cat_grad[None, :, 512:640],
        cat_grad[None, :, 640:768],
        out_grad_own[None],
        heads_grad[None],
        gate_grad[None],
        up_grad[None],
        down_grad[None],
        *summed,
    )


def solution(mesh):
    torus = Mesh(
        mesh.devices.reshape(mesh.shape["section"], 4, 4, 4), ("section", "dp_0", "dp_1", "dp_2")
    )
    in_specs = (
        P(None, DP, None),
        P(None, DP, None),
        P("section", DP, None),
        P("section", DP, None),
        P("section", DP, None),
        P("section", DP, None),
        P("section", DP, None),
        P("section", DP, None),
        P("section", DP, None),
        P("section", DP, None),
        P("section", DP, None),
        P("section", None),
        P("section", None, None),
        P("section", None),
        P("section", None),
        P("section", None),
        P("section", None),
        P("section", None),
        P("section", None),
    )
    out_specs = (
        P("section", None, DP, None),
        P("section", None, DP, None),
        P("section", DP, None),
        P("section", DP, None),
        P("section", DP, None),
        P("section", DP, None),
        P("section", DP, None),
        P("section", DP, None),
        P("section", DP, None),
        P("section", DP, None),
        P("section", DP, None),
        P("section", None),
        P("section", None, None),
        P("section", None),
        P("section", None),
        P("section", None),
        P("section", None),
        P("section", None),
        P("section", None),
    )
    return jax.shard_map(
        on_device, mesh=torus, in_specs=in_specs, out_specs=out_specs, check_vma=False
    )
```

```python
import jax
import jax.numpy as jnp
from jax import lax
from jax.experimental import pallas as pl
from jax.experimental.pallas import tpu as pltpu
from jax.sharding import Mesh
from jax.sharding import PartitionSpec as P

LEN = 128
ROWS = 256
WIDTH = 1024
FEED = 2048
INNER = 1536
MIXED = 1792
CAT = 4224
HEADS = 24
DP = ("dp_0", "dp_1", "dp_2")
F32 = jnp.float32
BF16 = jnp.bfloat16
HIDE = -1e30
Q0, K0, V0, Z0, X0, T0 = 0, 512, 640, 768, 2304, 4096
GATE0, UP0, DOWN0, OUT0, HEADS0, DT0, PACKED = 64, 96, 128, 160, 184, 192, 200


def dot(left, right):
    return jnp.dot(left, right, preferred_element_type=F32)


def dot_nt(left, right):
    return lax.dot_general(left, right, (((1,), (1,)), ((), ())), preferred_element_type=F32)


def dot_tn(left, right):
    return lax.dot_general(left, right, (((0,), (0,)), ((), ())), preferred_element_type=F32)


def dot_full(left, right):
    return jnp.dot(left, right, precision=lax.Precision.HIGHEST, preferred_element_type=F32)


def iota(shape, dim):
    return lax.broadcasted_iota(jnp.int32, shape, dim)


def sigmoid(v):
    return 1.0 / (1.0 + jnp.exp(-v))


def softplus(v):
    return jnp.maximum(v, 0.0) + jnp.log(1.0 + jnp.exp(-jnp.abs(v)))


def swap_halves(v):
    width = v.shape[1]
    near = lax.rem(iota(v.shape, 1), 64) < 32
    return jnp.where(near, pltpu.roll(v, width - 32, 1), pltpu.roll(v, 32, 1))


def shifted_down(v, by):
    if by == 0:
        return v
    return jnp.where(iota(v.shape, 0) >= by, pltpu.roll(v, by, 0), 0.0)


def shifted_up(v, by):
    if by == 0:
        return v
    rows = v.shape[0]
    return jnp.where(iota(v.shape, 0) < rows - by, pltpu.roll(v, rows - by, 0), 0.0)


def rms(v):
    return lax.rsqrt(jnp.mean(v * v, axis=-1, keepdims=True) + 1e-05)


def rms_backward(v, gain, grad):
    scale = rms(v)
    gained = grad * gain
    inner = jnp.mean(gained * v, axis=-1, keepdims=True)
    grad_v = scale * gained - v * (scale * scale * scale * inner)
    return grad_v, jnp.sum(grad * v * scale, axis=0, keepdims=True)


def left_half():
    return iota((LEN, 128), 1) < 64


def both_halves(v, group, left):
    turned = pltpu.roll(v, 64, 1)
    return jnp.where(left, v, turned) if group == 0 else jnp.where(left, turned, v)


def stacked(pairs, left):
    parts = []
    for pair in pairs:
        parts.append(jnp.where(left, pair, 0.0))
        parts.append(jnp.where(left, 0.0, pair))
    return jnp.concatenate(parts, axis=0).astype(BF16)


def unstacked(rows, index, left):
    low = rows[2 * index * LEN : (2 * index + 1) * LEN]
    high = rows[(2 * index + 1) * LEN : (2 * index + 2) * LEN]
    return jnp.where(left, low, high)


def attention_parts(proj, rows, cosine, sine):
    left = left_half()
    query = proj[rows, Q0:K0]
    query = query * cosine[...] + swap_halves(query) * sine[...]
    key = proj[rows, K0:V0]
    key = key * cosine[:, :128] + swap_halves(key) * sine[:, :128]
    value = proj[rows, V0:Z0]
    groups = []
    for group in range(2):
        pairs = [query[:, 128 * p : 128 * p + 128] for p in (2 * group, 2 * group + 1)]
        queries = stacked(pairs, left)
        keys = both_halves(key, group, left).astype(BF16)
        values = both_halves(value, group, left).astype(BF16)
        scores = dot_nt(queries, keys) * 0.125
        time = lax.rem(iota(scores.shape, 0), LEN)
        scores = jnp.where(iota(scores.shape, 1) <= time, scores, HIDE)
        top = jnp.max(scores, axis=-1, keepdims=True)
        expo = jnp.exp(scores - top)
        probs = expo / jnp.sum(expo, axis=-1, keepdims=True)
        groups.append((queries, keys, values, probs))
    return left, groups


def attention_forward(proj, rows, cosine, sine, attended):
    left, groups = attention_parts(proj, rows, cosine, sine)
    for group, (queries, keys, values, probs) in enumerate(groups):
        mixed = dot(probs.astype(BF16), values)
        for index in range(2):
            at = 256 * group + 128 * index
            attended[rows, at : at + 128] = unstacked(mixed, index, left).astype(BF16)


def attention_backward(proj, rows, cosine, sine, grad_attended, grad_cat):
    left, groups = attention_parts(proj, rows, cosine, sine)
    key_parts, value_parts = [], []
    for group, (queries, keys, values, probs) in enumerate(groups):
        pairs = [grad_attended[:, 128 * p : 128 * p + 128] for p in (2 * group, 2 * group + 1)]
        grads = stacked(pairs, left)
        grad_values = dot_tn(probs.astype(BF16), grads)
        grad_probs = dot_nt(grads, values)
        inner = jnp.sum(probs * grad_probs, axis=-1, keepdims=True)
        grad_scores = (probs * (grad_probs - inner)).astype(BF16)
        grad_queries = dot(grad_scores, keys) * 0.125
        grad_keys = dot_tn(grad_scores, queries) * 0.125
        for index in range(2):
            at = 256 * group + 128 * index
            grad = unstacked(grad_queries, index, left)
            grad = grad * cosine[:, :128] - swap_halves(grad) * sine[:, :128]
            grad_cat[rows, at : at + 128] = grad.astype(BF16)
        key_parts.append(grad_keys + pltpu.roll(grad_keys, 64, 1))
        value_parts.append(grad_values + pltpu.roll(grad_values, 64, 1))
    grad = jnp.where(left, key_parts[0], key_parts[1])
    grad = grad * cosine[:, :128] - swap_halves(grad) * sine[:, :128]
    grad_cat[rows, K0:V0] = grad.astype(BF16)
    grad_cat[rows, V0:Z0] = jnp.where(left, value_parts[0], value_parts[1]).astype(BF16)


def mamba_parts(proj, rows, kernel, bias, step_bias, decay_log):
    mixed = proj[rows, X0:T0]
    total = bias[...] + mixed * kernel[3:4, :]
    for tap in range(3):
        total = total + shifted_down(mixed, 3 - tap) * kernel[tap : tap + 1, :]
    active = total * sigmoid(total)
    step = softplus(proj[rows, T0:CAT] + step_bias[...])
    rate = -step * jnp.exp(decay_log[...])
    earlier = (iota((LEN, LEN), 0) >= iota((LEN, LEN), 1)).astype(F32)
    cumul = dot_full(earlier, rate)
    state_in = active[:, INNER : INNER + 128].astype(BF16)
    state_out = active[:, INNER + 128 :].astype(BF16)
    return mixed, total, active, step, rate, cumul, state_in, state_out


def stepped(step, pair, left):
    return jnp.where(left, step[:, 2 * pair : 2 * pair + 1], step[:, 2 * pair + 1 : 2 * pair + 2])


def mamba_forward(proj, rows, kernel, bias, step_bias, decay_log, skip, gain, ssm, mamba):
    left = left_half()
    parts = mamba_parts(proj, rows, kernel, bias, step_bias, decay_log)
    mixed, total, active, step, rate, cumul, state_in, state_out = parts
    across = cumul.T
    hidden = jnp.where(iota((LEN, LEN), 0) >= iota((LEN, LEN), 1), 0.0, HIDE)
    meeting = dot_nt(state_out, state_in)
    for pair in range(HEADS // 2):
        at = 128 * pair
        inputs = active[:, at : at + 128]
        scaled = (inputs * stepped(step, pair, left)).astype(BF16)
        mixing = []
        for head in (2 * pair, 2 * pair + 1):
            spread = cumul[:, head : head + 1] - across[head : head + 1, :] + hidden
            mixing.append((meeting * jnp.exp(spread)).astype(BF16))
        both = dot(jnp.concatenate(mixing, axis=0), scaled)
        out = unstacked(both, 0, left) + skip[:, at : at + 128] * inputs
        ssm[rows, at : at + 128] = out
    z = proj[rows, Z0:X0]
    gated = ssm[rows, :] * (z * sigmoid(z))
    mamba[rows, :] = (gated * rms(gated) * gain[...]).astype(BF16)


def head_sums(v, pick):
    high = v.astype(BF16)
    low = (v - high.astype(F32)).astype(BF16)
    return dot(high, pick) + dot(low, pick)


def mamba_backward(
    proj, rows, kernel, bias, step_bias, decay_log, skip, gain, pick, ssm, grad_mamba, grad_cat,
    across_scratch, balance_scratch, touch_scratch, grad_active, add_small,
):
    left = left_half()
    parts = mamba_parts(proj, rows, kernel, bias, step_bias, decay_log)
    mixed, total, active, step, rate, cumul, state_in, state_out = parts
    across = cumul.T
    hidden = jnp.where(iota((LEN, LEN), 1) >= iota((LEN, LEN), 0), 0.0, HIDE)
    meeting = dot_nt(state_out, state_in).T
    z = proj[rows, Z0:X0]
    out = ssm[rows, :]
    gate = sigmoid(z)
    gated = out * (z * gate)
    grad_gated, grad_gain = rms_backward(gated, gain[...], grad_mamba)
    add_small(6, grad_gain)
    grad_cat[rows, Z0:X0] = (grad_gated * out * (gate * (1.0 + z * (1.0 - gate)))).astype(BF16)
    grad_out = grad_gated * (z * gate)
    add_small(5, jnp.sum(grad_out * active[:, :INNER], axis=0, keepdims=True))
    grad_meeting = jnp.zeros((LEN, LEN), F32)
    for pair in range(HEADS // 2):
        at = 128 * pair
        inputs = active[:, at : at + 128]
        steps = stepped(step, pair, left)
        scaled = (inputs * steps).astype(BF16)
        grad_pair = grad_out[:, at : at + 128]
        grad_low = grad_pair.astype(BF16)
        halves = jnp.concatenate(
            [jnp.where(left, scaled, jnp.zeros_like(scaled)), jnp.where(left, jnp.zeros_like(scaled), scaled)],
            axis=0,
        )
        grad_mixing = dot_nt(halves, grad_low)
        mixing = []
        for place, head in enumerate((2 * pair, 2 * pair + 1)):
            spread = across[head : head + 1, :] - cumul[:, head : head + 1] + hidden
            decay = jnp.exp(spread)
            mixing.append((meeting * decay).astype(BF16))
            grad_meeting = grad_meeting + grad_mixing[LEN * place : LEN * place + LEN] * decay
        both = dot(jnp.concatenate(mixing, axis=0), grad_low)
        grad_scaled = unstacked(both, 0, left)
        skips = skip[:, at : at + 128]
        grad_active[:, at : at + 128] = grad_scaled * steps + skips * grad_pair
        touch_scratch[:, at : at + 128] = grad_scaled * inputs
        balance_scratch[:, at : at + 128] = grad_low.astype(F32) * (
            out[:, at : at + 128] - skips * inputs
        ) - scaled.astype(F32) * grad_scaled
    grad_low = grad_meeting.astype(BF16)
    grad_active[:, INNER : INNER + 128] = dot(grad_low, state_out)
    grad_active[:, INNER + 128 :] = dot_tn(grad_low, state_in)
    later = (iota((LEN, LEN), 1) >= iota((LEN, LEN), 0)).astype(F32)
    grad_rate = dot_full(later, head_sums(balance_scratch[...], pick[...]))
    add_small(4, jnp.sum(grad_rate * rate, axis=0, keepdims=True))
    grad_step = head_sums(touch_scratch[...], pick[...]) - grad_rate * jnp.exp(decay_log[...])
    grad_dt = grad_step * sigmoid(proj[rows, T0:CAT] + step_bias[...])
    add_small(3, jnp.sum(grad_dt, axis=0, keepdims=True))
    grad_cat[rows, T0:CAT] = grad_dt.astype(BF16)
    slope = sigmoid(total)
    grad_total = grad_active[...] * (slope * (1.0 + total * (1.0 - slope)))
    add_small(2, jnp.sum(grad_total, axis=0, keepdims=True))
    grad_mixed = grad_total * kernel[3:4, :]
    taps = []
    for tap in range(4):
        taps.append(jnp.sum(grad_total * shifted_down(mixed, 3 - tap), axis=0, keepdims=True))
        if tap < 3:
            grad_mixed = grad_mixed + shifted_up(grad_total, 3 - tap) * kernel[tap : tap + 1, :]
    add_small(1, jnp.concatenate(taps, axis=0))
    grad_cat[rows, X0:T0] = grad_mixed.astype(BF16)


def flat(block):
    return block.reshape(block.shape[0] * block.shape[1], block.shape[2])


def start_all(copies):
    for copy in copies:
        copy.start()


def forward_kernel(
    x, packed, dt_weight, out_weight, heads_weight, input_gain, kernel, bias, step_bias, decay_log, skip,
    mixer_gain, feed_gain, cosine, sine,
    result, normed, proj, ssm, mamba, attended, middle, ffin, gate, upper, hidden,
    cat, gate_up, down, out_mat, heads_mat, sems,
):
    copies = [
        pltpu.make_async_copy(packed.at[:, pl.ds(16 * j, 16), :], cat.at[j], sems.at[j])
        for j in range(4)
    ]
    copies.append(pltpu.make_async_copy(out_weight, out_mat, sems.at[4]))
    copies.append(pltpu.make_async_copy(heads_weight, heads_mat, sems.at[5]))
    for j in range(4):
        copies.append(
            pltpu.make_async_copy(
                packed.at[:, pl.ds(GATE0 + 16 * j, 16), :], gate_up.at[j], sems.at[6 + j]
            )
        )
    copies.append(pltpu.make_async_copy(packed.at[:, pl.ds(DOWN0, 32), :], down, sems.at[10]))
    start_all(copies)
    state = x[...].astype(F32)
    normed[...] = (state * rms(state) * input_gain[...]).astype(BF16)
    proj[:, T0:CAT] = dot(normed[...], dt_weight[...])
    for j in range(4):
        copies[j].wait()

        def columns(tile, carry, j=j):
            at = pl.multiple_of(tile * 256, 256)
            block = flat(cat[j, :, :, pl.ds(at, 256)])
            proj[:, pl.ds(pl.multiple_of(j * 1024 + at, 256), 256)] = dot(normed[...], block)
            return carry

        lax.fori_loop(0, 4, columns, 0)

    def sequence(index, carry):
        rows = pl.ds(pl.multiple_of(index * LEN, LEN), LEN)
        attention_forward(proj, rows, cosine, sine, attended)
        mamba_forward(proj, rows, kernel, bias, step_bias, decay_log, skip, mixer_gain, ssm, mamba)
        return carry

    lax.fori_loop(0, 2, sequence, 0)
    copies[4].wait()
    copies[5].wait()

    def joined(tile, carry):
        at = pl.ds(pl.multiple_of(tile * 256, 256), 256)
        part = dot(mamba[...], out_mat[:, at]) + dot(attended[...], heads_mat[:, at])
        middle[:, at] = x[:, at].astype(F32) + part
        return carry

    lax.fori_loop(0, 4, joined, 0)
    value = middle[...]
    ffin[...] = (value * rms(value) * feed_gain[...]).astype(BF16)
    for j in range(2):
        copies[6 + j].wait()
        copies[8 + j].wait()

        def feed(tile, carry, j=j):
            at = pl.multiple_of(tile * 256, 256)
            to = pl.ds(pl.multiple_of(j * 1024 + at, 256), 256)
            low = dot(ffin[...], flat(gate_up[j, :, :, pl.ds(at, 256)]))
            high = dot(ffin[...], flat(gate_up[2 + j, :, :, pl.ds(at, 256)]))
            gate[:, to] = low
            upper[:, to] = high
            hidden[:, to] = (low * sigmoid(low) * high).astype(BF16)
            return carry

        lax.fori_loop(0, 4, feed, 0)
    copies[10].wait()

    def last(tile, carry):
        at = pl.ds(pl.multiple_of(tile * 256, 256), 256)
        result[:, at] = (middle[:, at] + dot(hidden[...], flat(down[:, :, at]))).astype(BF16)
        return carry

    lax.fori_loop(0, 4, last, 0)


def feed_backward_kernel(
    grad_top, packed, gate, upper, middle, feed_gain,
    grad_gate, grad_upper, grad_middle, feed_grad,
    gate_up, down, grad_ffin, sems,
):
    copies = [pltpu.make_async_copy(packed.at[:, pl.ds(DOWN0, 32), :], down, sems.at[4])]
    for j in range(4):
        copies.append(
            pltpu.make_async_copy(
                packed.at[:, pl.ds(GATE0 + 16 * j, 16), :], gate_up.at[j], sems.at[j]
            )
        )
    start_all(copies)
    copies[0].wait()

    def through(tile, carry):
        at = pl.ds(pl.multiple_of(tile * 256, 256), 256)
        block = flat(down[pl.ds(tile * 8, 8)])
        grad_hidden = dot_nt(grad_top[...], block)
        low, high = gate[:, at], upper[:, at]
        slope = sigmoid(low)
        grad_upper[:, at] = (grad_hidden * (low * slope)).astype(BF16)
        part = grad_hidden * high * (slope * (1.0 + low * (1.0 - slope)))
        grad_gate[:, at] = part.astype(BF16)
        return carry

    lax.fori_loop(0, 8, through, 0)
    for copy in copies[1:]:
        copy.wait()

    def back(tile, carry):
        at = pl.ds(pl.multiple_of(tile * 256, 256), 256)
        total = jnp.zeros((ROWS, 256), F32)
        for j in range(2):
            block = flat(gate_up[j, pl.ds(tile * 16, 16)])
            total = total + dot_nt(grad_gate[:, 1024 * j : 1024 * j + 1024], block)
            block = flat(gate_up[2 + j, pl.ds(tile * 16, 16)])
            total = total + dot_nt(grad_upper[:, 1024 * j : 1024 * j + 1024], block)
        grad_ffin[:, at] = total
        return carry

    lax.fori_loop(0, 4, back, 0)
    grad_part, grad_gain = rms_backward(middle[...], feed_gain[...], grad_ffin[...])
    feed_grad[...] = grad_gain
    grad_middle[...] = grad_top[...].astype(F32) + grad_part


def mix_backward_kernel(
    grad_middle, x, packed, dt_weight, out_weight, heads_weight, proj, ssm, input_gain, kernel, bias,
    step_bias, decay_log, skip, mixer_gain, cosine, sine, pick,
    grad_branch, grad_cat, grad_start, input_grad, kernel_grad, bias_grad, step_grad, decay_grad,
    skip_grad, mixer_grad,
    cat, out_mat, heads_mat, grad_mamba, grad_attended, balance, touch, grad_active, grad_normed, sems,
):
    copies = [
        pltpu.make_async_copy(out_weight, out_mat, sems.at[4]),
        pltpu.make_async_copy(heads_weight, heads_mat, sems.at[5]),
    ]
    for j in range(4):
        copies.append(
            pltpu.make_async_copy(packed.at[:, pl.ds(16 * j, 16), :], cat.at[j], sems.at[j])
        )
    start_all(copies)
    grad_branch[...] = grad_middle[...].astype(BF16)
    copies[0].wait()
    copies[1].wait()

    def through(tile, carry):
        at = pl.ds(pl.multiple_of(tile * 256, 256), 256)
        grad_mamba[:, at] = dot_nt(grad_branch[...], out_mat[at, :])
        return carry

    lax.fori_loop(0, 6, through, 0)

    def through_heads(tile, carry):
        at = pl.ds(pl.multiple_of(tile * 256, 256), 256)
        grad_attended[:, at] = dot_nt(grad_branch[...], heads_mat[at, :])
        return carry

    lax.fori_loop(0, 2, through_heads, 0)
    small = {
        1: kernel_grad,
        2: bias_grad,
        3: step_grad,
        4: decay_grad,
        5: skip_grad,
        6: mixer_grad,
    }
    for ref in small.values():
        ref[...] = jnp.zeros_like(ref)

    def add_small(slot, value):
        small[slot][...] += value

    def sequence(index, carry):
        rows = pl.ds(pl.multiple_of(index * LEN, LEN), LEN)
        grads = grad_attended[rows, :]
        attention_backward(proj, rows, cosine, sine, grads, grad_cat)
        mamba_backward(
            proj, rows, kernel, bias, step_bias, decay_log, skip, mixer_gain, pick, ssm,
            grad_mamba[rows, :], grad_cat, None, balance, touch, grad_active, add_small,
        )
        return carry

    lax.fori_loop(0, 2, sequence, 0)
    for copy in copies[2:]:
        copy.wait()

    def back(tile, carry):
        at = pl.ds(pl.multiple_of(tile * 256, 256), 256)
        total = dot_nt(grad_cat[:, T0:CAT], dt_weight[at, :])
        for j in range(4):
            block = flat(cat[j, pl.ds(tile * 16, 16)])
            total = total + dot_nt(grad_cat[:, 1024 * j : 1024 * j + 1024], block)
        grad_normed[:, at] = total
        return carry

    lax.fori_loop(0, 4, back, 0)
    state = x[...].astype(F32)
    grad_state, grad_gain = rms_backward(state, input_gain[...], grad_normed[...])
    input_grad[...] = grad_gain
    grad_start[...] = grad_middle[...] + grad_state


VMEM = pl.BlockSpec(memory_space=pltpu.VMEM)
ANY = pl.BlockSpec(memory_space=pl.ANY)
LIMIT = 60 * 1024 * 1024


def shape(rows, columns, dtype):
    return jax.ShapeDtypeStruct((rows, columns), dtype)


def scratch(*dims, dtype=BF16):
    return pltpu.VMEM(dims, dtype)


def run_forward(start, mats, small, rope):
    packed, dt_weight, out_weight, heads_weight = mats
    input_gain, kernel, bias, step_bias, decay_log, skip, mixer_gain, feed_gain = small
    return pl.pallas_call(
        forward_kernel,
        out_shape=(
            shape(ROWS, WIDTH, BF16),
            shape(ROWS, WIDTH, BF16),
            shape(ROWS, CAT, F32),
            shape(ROWS, INNER, F32),
            shape(ROWS, INNER, BF16),
            shape(ROWS, 512, BF16),
            shape(ROWS, WIDTH, F32),
            shape(ROWS, WIDTH, BF16),
            shape(ROWS, FEED, F32),
            shape(ROWS, FEED, F32),
            shape(ROWS, FEED, BF16),
        ),
        in_specs=[VMEM, ANY, VMEM, ANY, ANY] + [VMEM] * 10,
        out_specs=(VMEM,) * 11,
        scratch_shapes=[
            scratch(4, 64, 16, 1024),
            scratch(4, 64, 16, 1024),
            scratch(64, 32, 1024),
            scratch(INNER, WIDTH),
            scratch(512, WIDTH),
            pltpu.SemaphoreType.DMA((11,)),
        ],
        compiler_params=pltpu.CompilerParams(vmem_limit_bytes=LIMIT),
        cost_estimate=pl.CostEstimate(
            flops=2 * ROWS * 12_600_000, bytes_accessed=40_000_000, transcendentals=2_000_000
        ),
        name="forward",
    )(start, packed, dt_weight, out_weight, heads_weight, *small, *rope)


def run_feed_backward(grad_top, mats, gate, upper, middle, feed_gain):
    return pl.pallas_call(
        feed_backward_kernel,
        out_shape=(
            shape(ROWS, FEED, BF16),
            shape(ROWS, FEED, BF16),
            shape(ROWS, WIDTH, F32),
            shape(1, WIDTH, F32),
        ),
        in_specs=[VMEM, ANY] + [VMEM] * 4,
        out_specs=(VMEM,) * 4,
        scratch_shapes=[
            scratch(4, 64, 16, 1024),
            scratch(64, 32, 1024),
            scratch(ROWS, WIDTH, dtype=F32),
            pltpu.SemaphoreType.DMA((5,)),
        ],
        compiler_params=pltpu.CompilerParams(vmem_limit_bytes=LIMIT),
        cost_estimate=pl.CostEstimate(
            flops=2 * ROWS * 6_300_000, bytes_accessed=22_000_000, transcendentals=1_000_000
        ),
        name="feed_backward",
    )(grad_top, mats[0], gate, upper, middle, feed_gain)


def run_mix_backward(grad_middle, start, mats, proj, ssm, small, rope, pick):
    packed, dt_weight, out_weight, heads_weight = mats
    return pl.pallas_call(
        mix_backward_kernel,
        out_shape=(
            shape(ROWS, WIDTH, BF16),
            shape(ROWS, CAT, BF16),
            shape(ROWS, WIDTH, F32),
            shape(1, WIDTH, F32),
            shape(4, MIXED, F32),
            shape(1, MIXED, F32),
            shape(1, 128, F32),
            shape(1, 128, F32),
            shape(1, INNER, F32),
            shape(1, INNER, F32),
        ),
        in_specs=[VMEM, VMEM, ANY, VMEM, ANY, ANY] + [VMEM] * 12,
        out_specs=(VMEM,) * 10,
        scratch_shapes=[
            scratch(4, 64, 16, 1024),
            scratch(INNER, WIDTH),
            scratch(512, WIDTH),
            scratch(ROWS, INNER, dtype=F32),
            scratch(ROWS, 512, dtype=F32),
            scratch(LEN, INNER, dtype=F32),
            scratch(LEN, INNER, dtype=F32),
            scratch(LEN, MIXED, dtype=F32),
            scratch(ROWS, WIDTH, dtype=F32),
            pltpu.SemaphoreType.DMA((6,)),
        ],
        compiler_params=pltpu.CompilerParams(vmem_limit_bytes=LIMIT),
        cost_estimate=pl.CostEstimate(
            flops=2 * ROWS * 6_300_000, bytes_accessed=25_000_000, transcendentals=4_000_000
        ),
        name="mix_backward",
    )(
        grad_middle, start, packed, dt_weight, out_weight, heads_weight, proj, ssm, *small[:7], *rope, pick
    )


def rope_tables():
    position = jnp.arange(LEN).astype(F32)
    inverse = 10000.0 ** (-(jnp.arange(32).astype(F32) * 2.0) / 64)
    angle = position[:, None] * inverse[None, :]
    cosine = jnp.tile(jnp.cos(angle), (1, 16))
    sine = jnp.sin(angle)
    return cosine, jnp.tile(jnp.concatenate([-sine, sine], axis=1), (1, 8))


def head_pick():
    lanes = lax.broadcasted_iota(jnp.int32, (INNER, 128), 0) // 64
    return (lanes == lax.broadcasted_iota(jnp.int32, (INNER, 128), 1)).astype(BF16)


def prepared_small(pieces):
    input_gain, kernel, bias, step_bias, decay_log, skip, mixer_gain, feed_gain = pieces

    def padded(v):
        return jnp.pad(v, (0, 128 - HEADS))[None]

    return (
        input_gain[None],
        kernel,
        bias[None],
        padded(step_bias),
        padded(decay_log),
        jnp.repeat(skip, 64)[None],
        mixer_gain[None],
        feed_gain[None],
    )


FIRST = (1, 0, 3, 2)
SECOND = (3, 2, 1, 0)


def partners(axis, turn):
    order = (FIRST, SECOND) if turn == 0 else (SECOND, FIRST)
    me = lax.axis_index(axis)
    near = me + 1 - 2 * lax.rem(me, 2)
    found = (near, 3 - me) if turn == 0 else (3 - me, near)
    return me, found, [[(i, table[i]) for i in range(4)] for table in order]


def halved(part, axis, turn):
    me, (one, two), (swap_one, swap_two) = partners(axis, turn)
    sent = part([one, lax.rem(me + 2, 4)])
    got = lax.ppermute(sent.astype(BF16), axis, swap_one)
    half = got.shape[0] // 2
    handed = part([two]) + got[half:].astype(F32)
    last = lax.ppermute(handed.astype(BF16), axis, swap_two)
    return part([me]) + got[:half].astype(F32) + last.astype(F32)


def scattered(left, right, order, turn):
    depth = left.shape[0] // 64
    blocks = left.reshape(4, 4, 4, depth, left.shape[1])

    def product(places):
        picked = [lax.dynamic_index_in_dim(blocks, p, order[0], keepdims=False) for p in places]
        return dot(jnp.concatenate(picked, axis=0).reshape(-1, left.shape[1]), right)

    array = halved(product, DP[order[0]], turn).astype(BF16)
    array = array.reshape(4, 4, depth, right.shape[1])
    rest = [0, 1, 2]
    rest.remove(order[0])

    def quarters(array, dim):
        def part(places):
            picked = [lax.dynamic_index_in_dim(array, p, dim, keepdims=False) for p in places]
            return jnp.concatenate(picked, axis=0).reshape(-1, array.shape[-1]).astype(F32)

        return part

    array = halved(quarters(array, rest.index(order[1])), DP[order[1]], turn).astype(BF16)
    array = array.reshape(4, depth, right.shape[1])
    return halved(quarters(array, 0), DP[order[2]], turn)


def summed_over(vector):
    for axis in DP:
        for table in (FIRST, SECOND):
            vector = vector + lax.ppermute(vector, axis, [(i, table[i]) for i in range(4)])
    return vector


def column_blocks(matrix):
    return [matrix[:, at : at + 1024] for at in range(0, matrix.shape[1], 1024)]


def on_device(
    layer_input,
    out_grad,
    in_weight,
    query_weight,
    key_weight,
    value_weight,
    out_weight,
    heads_weight,
    gate_weight,
    up_weight,
    down_weight,
    *pieces,
):
    micro, part, width = layer_input.shape
    rows = micro * part
    cat = jnp.concatenate(
        [query_weight[0], key_weight[0], value_weight[0], in_weight[0, :, :3328]], axis=1
    )
    steps = jnp.pad(in_weight[0, :, 3328:].reshape(1, -1), ((0, 7), (0, 1024 - 16 * HEADS)))
    own = jnp.concatenate(
        [
            *column_blocks(cat),
            *column_blocks(gate_weight[0]),
            *column_blocks(up_weight[0]),
            down_weight[0],
            out_weight[0],
            heads_weight[0],
            steps,
        ],
        axis=0,
    )
    packed = lax.all_gather(own, DP, axis=0, tiled=False)
    dt_weight = packed[:, DT0, : 16 * HEADS].reshape(WIDTH, HEADS)
    mats = (
        packed,
        jnp.pad(dt_weight, ((0, 0), (0, 128 - HEADS))),
        packed[:, OUT0:HEADS0].reshape(INNER, WIDTH),
        packed[:, HEADS0:DT0].reshape(512, WIDTH),
    )
    small = prepared_small([piece[0] for piece in pieces])
    rope = rope_tables()
    pick = head_pick()
    first = lax.axis_index("section") == 0

    start_low = layer_input.reshape(rows, width)
    kept_low = run_forward(start_low, mats, small, rope)
    start_high = lax.ppermute(kept_low[0], "section", [(0, 1)])
    kept_high = run_forward(start_high, mats, small, rope)
    layer_outputs = jnp.where(first, kept_low[0], kept_high[0]).reshape(1, micro, part, width)

    def feed_backward(kept, grad_top):
        result, normed, proj, ssm, mamba, attended, middle, ffin, gate, upper, hidden = kept
        out = run_feed_backward(grad_top, mats, gate, upper, middle, small[7])
        return (*out, grad_top, hidden.T, ffin.T)

    def mix_backward(kept, start, grad_middle):
        result, normed, proj, ssm, mamba, attended, middle, ffin, gate, upper, hidden = kept
        out = run_mix_backward(grad_middle, start, mats, proj, ssm, small, rope, pick)
        joined = jnp.concatenate(
            [mamba.T.reshape(64, 24, rows), attended.T.reshape(64, 8, rows)], axis=1
        )
        return (*out, normed.T, joined.reshape(2048, rows))

    top = out_grad.reshape(rows, width)
    feed_high = feed_backward(kept_high, top)
    mix_high = mix_backward(kept_high, start_high, feed_high[2])
    top = lax.ppermute(mix_high[2].astype(BF16), "section", [(1, 0)])
    feed = lax.cond(
        first,
        lambda kept, grad, other: feed_backward(kept, grad),
        lambda kept, grad, other: other,
        kept_low,
        top,
        feed_high,
    )
    grad_gate, grad_upper, grad_middle, feed_grad, grad_low, hidden_t, ffin_t = feed
    down_grad = scattered(hidden_t, grad_low, (2, 0, 1), 0)
    gate_grad = scattered(ffin_t, grad_gate, (0, 1, 2), 0)
    up_grad = scattered(ffin_t, grad_upper, (1, 2, 0), 0)
    mix = lax.cond(
        first,
        lambda kept, start, grad, other: mix_backward(kept, start, grad),
        lambda kept, start, grad, other: other,
        kept_low,
        start_low,
        grad_middle,
        mix_high,
    )
    grad_branch, grad_cat, grad_start, *small_grads, normed_t, joined_t = mix
    joined_grad = scattered(joined_t, grad_branch, (2, 0, 1), 1)
    cat_left = scattered(normed_t, grad_cat[:, :2048], (0, 1, 2), 1)
    cat_right = scattered(normed_t, grad_cat[:, 2048:], (1, 2, 0), 1)
    cat_grad = jnp.concatenate([cat_left, cat_right], axis=1)

    input_g, kernel_g, bias_g, step_g, decay_g, skip_g, mixer_g = small_grads
    small_grads = (
        input_g[0],
        kernel_g,
        bias_g[0],
        step_g[0, :HEADS],
        decay_g[0, :HEADS],
        skip_g.reshape(HEADS, 64).sum(axis=1),
        mixer_g[0],
        feed_grad[0],
    )
    vector = jnp.concatenate([piece.reshape(-1) for piece in small_grads])
    vector = jnp.pad(vector, (0, -vector.shape[0] % 1024)).reshape(-1, 128)
    total = summed_over(vector).reshape(-1)
    summed, at = ([], 0)
    for piece in small_grads:
        summed.append(total[at : at + piece.size].reshape(1, *piece.shape))
        at += piece.size
    return (
        layer_outputs,
        grad_start.reshape(1, micro, part, width),
        cat_grad[None, :, Z0 : T0 + HEADS],
        cat_grad[None, :, :K0],
        cat_grad[None, :, K0:V0],
        cat_grad[None, :, V0:Z0],
        joined_grad[None, :24],
        joined_grad[None, 24:],
        gate_grad[None],
        up_grad[None],
        down_grad[None],
        *summed,
    )


def solution(mesh):
    torus = Mesh(
        mesh.devices.reshape(mesh.shape["section"], 4, 4, 4), ("section", "dp_0", "dp_1", "dp_2")
    )
    in_specs = (
        P(None, DP, None),
        P(None, DP, None),
        P("section", DP, None),
        P("section", DP, None),
        P("section", DP, None),
        P("section", DP, None),
        P("section", DP, None),
        P("section", DP, None),
        P("section", DP, None),
        P("section", DP, None),
        P("section", DP, None),
        P("section", None),
        P("section", None, None),
        P("section", None),
        P("section", None),
        P("section", None),
        P("section", None),
        P("section", None),
        P("section", None),
    )
    out_specs = (
        P("section", None, DP, None),
        P("section", None, DP, None),
        P("section", DP, None),
        P("section", DP, None),
        P("section", DP, None),
        P("section", DP, None),
        P("section", DP, None),
        P("section", DP, None),
        P("section", DP, None),
        P("section", DP, None),
        P("section", DP, None),
        P("section", None),
        P("section", None, None),
        P("section", None),
        P("section", None),
        P("section", None),
        P("section", None),
        P("section", None),
        P("section", None),
    )
    return jax.shard_map(
        on_device, mesh=torus, in_specs=in_specs, out_specs=out_specs, check_vma=False
    )
```

```python
import functools

import jax
import jax.numpy as jnp
from jax import lax
from jax.experimental import pallas as pl
from jax.experimental.pallas import tpu as pltpu
from jax.sharding import Mesh
from jax.sharding import PartitionSpec as P

LEN = 128
ROWS = 256
WIDTH = 1024
FEED = 2048
INNER = 1536
MIXED = 1792
CAT = 4224
HEADS = 24
DP = ("dp_0", "dp_1", "dp_2")
F32 = jnp.float32
BF16 = jnp.bfloat16
HIDE = -1e30
Q0, K0, V0, Z0, X0, T0 = 0, 512, 640, 768, 2304, 4096
GATE0, UP0, DOWN0, OUT0, HEADS0, DT0, PACKED = 64, 96, 128, 160, 184, 192, 200


def dot(left, right):
    return jnp.dot(left, right, preferred_element_type=F32)


def dot_nt(left, right):
    return lax.dot_general(left, right, (((1,), (1,)), ((), ())), preferred_element_type=F32)


def dot_tn(left, right):
    return lax.dot_general(left, right, (((0,), (0,)), ((), ())), preferred_element_type=F32)


def dot_full(left, right):
    return jnp.dot(left, right, precision=lax.Precision.HIGHEST, preferred_element_type=F32)


def iota(shape, dim):
    return lax.broadcasted_iota(jnp.int32, shape, dim)


def sigmoid(v):
    return 1.0 / (1.0 + jnp.exp(-v))


def softplus(v):
    return jnp.maximum(v, 0.0) + jnp.log(1.0 + jnp.exp(-jnp.abs(v)))


def swap_halves(v):
    width = v.shape[1]
    near = lax.rem(iota(v.shape, 1), 64) < 32
    return jnp.where(near, pltpu.roll(v, width - 32, 1), pltpu.roll(v, 32, 1))


def shifted_down(v, by):
    if by == 0:
        return v
    return jnp.where(iota(v.shape, 0) >= by, pltpu.roll(v, by, 0), 0.0)


def shifted_up(v, by):
    if by == 0:
        return v
    rows = v.shape[0]
    return jnp.where(iota(v.shape, 0) < rows - by, pltpu.roll(v, rows - by, 0), 0.0)


def rms(v):
    return lax.rsqrt(jnp.mean(v * v, axis=-1, keepdims=True) + 1e-05)


def rms_backward(v, gain, grad):
    scale = rms(v)
    gained = grad * gain
    inner = jnp.mean(gained * v, axis=-1, keepdims=True)
    grad_v = scale * gained - v * (scale * scale * scale * inner)
    return grad_v, jnp.sum(grad * v * scale, axis=0, keepdims=True)


def left_half():
    return iota((LEN, 128), 1) < 64


def both_halves(v, group, left):
    turned = pltpu.roll(v, 64, 1)
    return jnp.where(left, v, turned) if group == 0 else jnp.where(left, turned, v)


def stacked(pairs, left):
    parts = []
    for pair in pairs:
        parts.append(jnp.where(left, pair, 0.0))
        parts.append(jnp.where(left, 0.0, pair))
    return jnp.concatenate(parts, axis=0).astype(BF16)


def unstacked(rows, index, left):
    low = rows[2 * index * LEN : (2 * index + 1) * LEN]
    high = rows[(2 * index + 1) * LEN : (2 * index + 2) * LEN]
    return jnp.where(left, low, high)


def attention_parts(proj, rows, cosine, sine):
    left = left_half()
    query = proj[rows, Q0:K0]
    query = query * cosine[...] + swap_halves(query) * sine[...]
    key = proj[rows, K0:V0]
    key = key * cosine[:, :128] + swap_halves(key) * sine[:, :128]
    value = proj[rows, V0:Z0]
    groups = []
    for group in range(2):
        pairs = [query[:, 128 * p : 128 * p + 128] for p in (2 * group, 2 * group + 1)]
        queries = stacked(pairs, left)
        keys = both_halves(key, group, left).astype(BF16)
        values = both_halves(value, group, left).astype(BF16)
        scores = dot_nt(queries, keys) * 0.125
        time = lax.rem(iota(scores.shape, 0), LEN)
        scores = jnp.where(iota(scores.shape, 1) <= time, scores, HIDE)
        top = jnp.max(scores, axis=-1, keepdims=True)
        expo = jnp.exp(scores - top)
        probs = expo / jnp.sum(expo, axis=-1, keepdims=True)
        groups.append((queries, keys, values, probs))
    return left, groups


def attention_forward(proj, rows, cosine, sine, attended):
    left, groups = attention_parts(proj, rows, cosine, sine)
    for group, (queries, keys, values, probs) in enumerate(groups):
        mixed = dot(probs.astype(BF16), values)
        for index in range(2):
            at = 256 * group + 128 * index
            attended[rows, at : at + 128] = unstacked(mixed, index, left).astype(BF16)


def attention_backward(proj, rows, cosine, sine, grad_attended, grad_cat):
    left, groups = attention_parts(proj, rows, cosine, sine)
    key_parts, value_parts = [], []
    for group, (queries, keys, values, probs) in enumerate(groups):
        pairs = [grad_attended[:, 128 * p : 128 * p + 128] for p in (2 * group, 2 * group + 1)]
        grads = stacked(pairs, left)
        grad_values = dot_tn(probs.astype(BF16), grads)
        grad_probs = dot_nt(grads, values)
        inner = jnp.sum(probs * grad_probs, axis=-1, keepdims=True)
        grad_scores = (probs * (grad_probs - inner)).astype(BF16)
        grad_queries = dot(grad_scores, keys) * 0.125
        grad_keys = dot_tn(grad_scores, queries) * 0.125
        for index in range(2):
            at = 256 * group + 128 * index
            grad = unstacked(grad_queries, index, left)
            grad = grad * cosine[:, :128] - swap_halves(grad) * sine[:, :128]
            grad_cat[rows, at : at + 128] = grad.astype(BF16)
        key_parts.append(grad_keys + pltpu.roll(grad_keys, 64, 1))
        value_parts.append(grad_values + pltpu.roll(grad_values, 64, 1))
    grad = jnp.where(left, key_parts[0], key_parts[1])
    grad = grad * cosine[:, :128] - swap_halves(grad) * sine[:, :128]
    grad_cat[rows, K0:V0] = grad.astype(BF16)
    grad_cat[rows, V0:Z0] = jnp.where(left, value_parts[0], value_parts[1]).astype(BF16)


def mamba_parts(proj, rows, kernel, bias, step_bias, decay_log):
    mixed = proj[rows, X0:T0]
    total = bias[...] + mixed * kernel[3:4, :]
    for tap in range(3):
        total = total + shifted_down(mixed, 3 - tap) * kernel[tap : tap + 1, :]
    active = total * sigmoid(total)
    step = softplus(proj[rows, T0:CAT] + step_bias[...])
    rate = -step * jnp.exp(decay_log[...])
    earlier = (iota((LEN, LEN), 0) >= iota((LEN, LEN), 1)).astype(F32)
    cumul = dot_full(earlier, rate)
    state_in = active[:, INNER : INNER + 128].astype(BF16)
    state_out = active[:, INNER + 128 :].astype(BF16)
    return mixed, total, active, step, rate, cumul, state_in, state_out


def stepped(step, pair, left):
    return jnp.where(left, step[:, 2 * pair : 2 * pair + 1], step[:, 2 * pair + 1 : 2 * pair + 2])


def mamba_forward(proj, rows, kernel, bias, step_bias, decay_log, skip, gain, ssm, mamba):
    left = left_half()
    parts = mamba_parts(proj, rows, kernel, bias, step_bias, decay_log)
    mixed, total, active, step, rate, cumul, state_in, state_out = parts
    across = cumul.T
    hidden = jnp.where(iota((LEN, LEN), 0) >= iota((LEN, LEN), 1), 0.0, HIDE)
    meeting = dot_nt(state_out, state_in)
    for pair in range(HEADS // 2):
        at = 128 * pair
        inputs = active[:, at : at + 128]
        scaled = (inputs * stepped(step, pair, left)).astype(BF16)
        mixing = []
        for head in (2 * pair, 2 * pair + 1):
            spread = cumul[:, head : head + 1] - across[head : head + 1, :] + hidden
            mixing.append((meeting * jnp.exp(spread)).astype(BF16))
        both = dot(jnp.concatenate(mixing, axis=0), scaled)
        out = unstacked(both, 0, left) + skip[:, at : at + 128] * inputs
        ssm[rows, at : at + 128] = out
    z = proj[rows, Z0:X0]
    gated = ssm[rows, :] * (z * sigmoid(z))
    mamba[rows, :] = (gated * rms(gated) * gain[...]).astype(BF16)


def head_sums(v, pick):
    high = v.astype(BF16)
    low = (v - high.astype(F32)).astype(BF16)
    return dot(high, pick) + dot(low, pick)


def mamba_backward(
    proj, rows, kernel, bias, step_bias, decay_log, skip, gain, pick, ssm, grad_mamba, grad_cat,
    across_scratch, balance_scratch, touch_scratch, grad_active, add_small,
):
    left = left_half()
    parts = mamba_parts(proj, rows, kernel, bias, step_bias, decay_log)
    mixed, total, active, step, rate, cumul, state_in, state_out = parts
    across = cumul.T
    hidden = jnp.where(iota((LEN, LEN), 1) >= iota((LEN, LEN), 0), 0.0, HIDE)
    meeting = dot_nt(state_out, state_in).T
    z = proj[rows, Z0:X0]
    out = ssm[rows, :]
    gate = sigmoid(z)
    gated = out * (z * gate)
    grad_gated, grad_gain = rms_backward(gated, gain[...], grad_mamba)
    add_small(6, grad_gain)
    grad_cat[rows, Z0:X0] = (grad_gated * out * (gate * (1.0 + z * (1.0 - gate)))).astype(BF16)
    grad_out = grad_gated * (z * gate)
    add_small(5, jnp.sum(grad_out * active[:, :INNER], axis=0, keepdims=True))
    grad_meeting = jnp.zeros((LEN, LEN), F32)
    for pair in range(HEADS // 2):
        at = 128 * pair
        inputs = active[:, at : at + 128]
        steps = stepped(step, pair, left)
        scaled = (inputs * steps).astype(BF16)
        grad_pair = grad_out[:, at : at + 128]
        grad_low = grad_pair.astype(BF16)
        halves = jnp.concatenate(
            [jnp.where(left, scaled, jnp.zeros_like(scaled)), jnp.where(left, jnp.zeros_like(scaled), scaled)],
            axis=0,
        )
        grad_mixing = dot_nt(halves, grad_low)
        mixing = []
        for place, head in enumerate((2 * pair, 2 * pair + 1)):
            spread = across[head : head + 1, :] - cumul[:, head : head + 1] + hidden
            decay = jnp.exp(spread)
            mixing.append((meeting * decay).astype(BF16))
            grad_meeting = grad_meeting + grad_mixing[LEN * place : LEN * place + LEN] * decay
        both = dot(jnp.concatenate(mixing, axis=0), grad_low)
        grad_scaled = unstacked(both, 0, left)
        skips = skip[:, at : at + 128]
        grad_active[:, at : at + 128] = grad_scaled * steps + skips * grad_pair
        touch_scratch[:, at : at + 128] = grad_scaled * inputs
        balance_scratch[:, at : at + 128] = grad_low.astype(F32) * (
            out[:, at : at + 128] - skips * inputs
        ) - scaled.astype(F32) * grad_scaled
    grad_low = grad_meeting.astype(BF16)
    grad_active[:, INNER : INNER + 128] = dot(grad_low, state_out)
    grad_active[:, INNER + 128 :] = dot_tn(grad_low, state_in)
    later = (iota((LEN, LEN), 1) >= iota((LEN, LEN), 0)).astype(F32)
    grad_rate = dot_full(later, head_sums(balance_scratch[...], pick[...]))
    add_small(4, jnp.sum(grad_rate * rate, axis=0, keepdims=True))
    grad_step = head_sums(touch_scratch[...], pick[...]) - grad_rate * jnp.exp(decay_log[...])
    grad_dt = grad_step * sigmoid(proj[rows, T0:CAT] + step_bias[...])
    add_small(3, jnp.sum(grad_dt, axis=0, keepdims=True))
    grad_cat[rows, T0:CAT] = grad_dt.astype(BF16)
    slope = sigmoid(total)
    grad_total = grad_active[...] * (slope * (1.0 + total * (1.0 - slope)))
    add_small(2, jnp.sum(grad_total, axis=0, keepdims=True))
    grad_mixed = grad_total * kernel[3:4, :]
    taps = []
    for tap in range(4):
        taps.append(jnp.sum(grad_total * shifted_down(mixed, 3 - tap), axis=0, keepdims=True))
        if tap < 3:
            grad_mixed = grad_mixed + shifted_up(grad_total, 3 - tap) * kernel[tap : tap + 1, :]
    add_small(1, jnp.concatenate(taps, axis=0))
    grad_cat[rows, X0:T0] = grad_mixed.astype(BF16)


def flat(block):
    return block.reshape(block.shape[0] * block.shape[1], block.shape[2])


def start_all(copies):
    for copy in copies:
        copy.start()


def forward_kernel(
    x, packed, dt_weight, out_weight, heads_weight, input_gain, kernel, bias, step_bias, decay_log, skip,
    mixer_gain, feed_gain, cosine, sine,
    result_out, normed_out, proj_out, ssm_out, mamba_out, attended_out, middle_out, ffin_out, gate_out,
    upper_out, hidden_out,
    result, normed, proj, ssm, mamba, attended, middle, ffin, gate, upper, hidden,
    cat, gate_up, down, out_mat, heads_mat, sems, out_sems,
):
    leaving = []

    def leave(*pairs):
        for source, target in pairs:
            copy = pltpu.make_async_copy(source, target, out_sems.at[len(leaving)])
            copy.start()
            leaving.append(copy)

    copies = [
        pltpu.make_async_copy(packed.at[:, pl.ds(16 * j, 16), :], cat.at[j], sems.at[j])
        for j in range(4)
    ]
    copies.append(pltpu.make_async_copy(out_weight, out_mat, sems.at[4]))
    copies.append(pltpu.make_async_copy(heads_weight, heads_mat, sems.at[5]))
    for j in range(4):
        copies.append(
            pltpu.make_async_copy(
                packed.at[:, pl.ds(GATE0 + 16 * j, 16), :], gate_up.at[j], sems.at[6 + j]
            )
        )
    copies.append(pltpu.make_async_copy(packed.at[:, pl.ds(DOWN0, 32), :], down, sems.at[10]))
    start_all(copies)
    state = x[...].astype(F32)
    normed[...] = (state * rms(state) * input_gain[...]).astype(BF16)
    proj[:, T0:CAT] = dot(normed[...], dt_weight[...])
    for j in range(4):
        copies[j].wait()

        def columns(tile, carry, j=j):
            at = pl.multiple_of(tile * 256, 256)
            block = flat(cat[j, :, :, pl.ds(at, 256)])
            proj[:, pl.ds(pl.multiple_of(j * 1024 + at, 256), 256)] = dot(normed[...], block)
            return carry

        lax.fori_loop(0, 4, columns, 0)
    leave((normed, normed_out), (proj, proj_out))

    def sequence(index, carry):
        rows = pl.ds(pl.multiple_of(index * LEN, LEN), LEN)
        attention_forward(proj, rows, cosine, sine, attended)
        mamba_forward(proj, rows, kernel, bias, step_bias, decay_log, skip, mixer_gain, ssm, mamba)
        return carry

    lax.fori_loop(0, 2, sequence, 0)
    leave((ssm, ssm_out), (mamba, mamba_out), (attended, attended_out))
    copies[4].wait()
    copies[5].wait()

    def joined(tile, carry):
        at = pl.ds(pl.multiple_of(tile * 256, 256), 256)
        part = dot(mamba[...], out_mat[:, at]) + dot(attended[...], heads_mat[:, at])
        middle[:, at] = x[:, at].astype(F32) + part
        return carry

    lax.fori_loop(0, 4, joined, 0)
    value = middle[...]
    ffin[...] = (value * rms(value) * feed_gain[...]).astype(BF16)
    leave((middle, middle_out), (ffin, ffin_out))
    for j in range(2):
        copies[6 + j].wait()
        copies[8 + j].wait()

        def feed(tile, carry, j=j):
            at = pl.multiple_of(tile * 256, 256)
            to = pl.ds(pl.multiple_of(j * 1024 + at, 256), 256)
            low = dot(ffin[...], flat(gate_up[j, :, :, pl.ds(at, 256)]))
            high = dot(ffin[...], flat(gate_up[2 + j, :, :, pl.ds(at, 256)]))
            gate[:, to] = low
            upper[:, to] = high
            hidden[:, to] = (low * sigmoid(low) * high).astype(BF16)
            return carry

        lax.fori_loop(0, 4, feed, 0)
    leave((gate, gate_out), (upper, upper_out), (hidden, hidden_out))
    copies[10].wait()

    def last(tile, carry):
        at = pl.ds(pl.multiple_of(tile * 256, 256), 256)
        result[:, at] = (middle[:, at] + dot(hidden[...], flat(down[:, :, at]))).astype(BF16)
        return carry

    lax.fori_loop(0, 4, last, 0)
    leave((result, result_out))
    for copy in leaving:
        copy.wait()


def leave_all(pairs, sems):
    copies = [
        pltpu.make_async_copy(source, target, sems.at[k]) for k, (source, target) in enumerate(pairs)
    ]
    start_all(copies)
    return copies


def feed_backward_kernel(earlier, active, *refs):
    @pl.when(active[0] == 1)
    def run():
        feed_backward_body(*refs[:6], *refs[6 + earlier :])


def feed_backward_body(
    grad_top, packed, gate_in, upper_in, middle_in, feed_gain,
    grad_gate_out, grad_upper_out, grad_middle_out, feed_grad_out,
    grad_gate, grad_upper, grad_middle, feed_grad,
    gate, upper, middle, gate_up, down, grad_ffin, sems, out_sems,
):
    inputs = [
        pltpu.make_async_copy(gate_in, gate, sems.at[5]),
        pltpu.make_async_copy(upper_in, upper, sems.at[6]),
        pltpu.make_async_copy(middle_in, middle, sems.at[7]),
    ]
    copies = [
        pltpu.make_async_copy(packed.at[:, pl.ds(DOWN0, 32), :], down, sems.at[4]),
    ]
    for j in range(4):
        copies.append(
            pltpu.make_async_copy(
                packed.at[:, pl.ds(GATE0 + 16 * j, 16), :], gate_up.at[j], sems.at[j]
            )
        )
    start_all(copies[:1] + inputs + copies[1:])
    copies[0].wait()
    for copy in inputs:
        copy.wait()

    def through(tile, carry):
        at = pl.ds(pl.multiple_of(tile * 256, 256), 256)
        block = flat(down[pl.ds(tile * 8, 8)])
        grad_hidden = dot_nt(grad_top[...], block)
        low, high = gate[:, at], upper[:, at]
        slope = sigmoid(low)
        grad_upper[:, at] = (grad_hidden * (low * slope)).astype(BF16)
        part = grad_hidden * high * (slope * (1.0 + low * (1.0 - slope)))
        grad_gate[:, at] = part.astype(BF16)
        return carry

    lax.fori_loop(0, 8, through, 0)
    leaving = leave_all(((grad_gate, grad_gate_out), (grad_upper, grad_upper_out)), out_sems)
    for copy in copies[1:]:
        copy.wait()

    def back(tile, carry):
        at = pl.ds(pl.multiple_of(tile * 256, 256), 256)
        total = jnp.zeros((ROWS, 256), F32)
        for j in range(2):
            block = flat(gate_up[j, pl.ds(tile * 16, 16)])
            total = total + dot_nt(grad_gate[:, 1024 * j : 1024 * j + 1024], block)
            block = flat(gate_up[2 + j, pl.ds(tile * 16, 16)])
            total = total + dot_nt(grad_upper[:, 1024 * j : 1024 * j + 1024], block)
        grad_ffin[:, at] = total
        return carry

    lax.fori_loop(0, 4, back, 0)
    grad_part, grad_gain = rms_backward(middle[...], feed_gain[...], grad_ffin[...])
    feed_grad[...] = grad_gain
    grad_middle[...] = grad_top[...].astype(F32) + grad_part
    leaving += leave_all(
        ((grad_middle, grad_middle_out), (feed_grad, feed_grad_out)), out_sems.at[pl.ds(2, 2)]
    )
    for copy in leaving:
        copy.wait()


def mix_backward_kernel(earlier, active, *refs):
    @pl.when(active[0] == 1)
    def run():
        mix_backward_body(*refs[:14], *refs[14 + earlier :])


def mix_backward_body(
    grad_middle, out_weight, heads_weight, proj_in, ssm_in, kernel, bias,
    step_bias, decay_log, skip, mixer_gain, cosine, sine, pick,
    grad_branch_out, grad_cat_out, kernel_grad_out, bias_grad_out,
    step_grad_out, decay_grad_out, skip_grad_out, mixer_grad_out,
    grad_branch, grad_cat, kernel_grad, bias_grad, step_grad, decay_grad,
    skip_grad, mixer_grad,
    proj, ssm,
    out_mat, heads_mat, grad_mamba, grad_attended, balance, touch, grad_active, sems,
    out_sems,
):
    copies = [
        pltpu.make_async_copy(out_weight, out_mat, sems.at[0]),
        pltpu.make_async_copy(heads_weight, heads_mat, sems.at[1]),
        pltpu.make_async_copy(proj_in, proj, sems.at[2]),
        pltpu.make_async_copy(ssm_in, ssm, sems.at[3]),
    ]
    start_all(copies)
    grad_branch[...] = grad_middle[...].astype(BF16)
    copies[0].wait()
    copies[1].wait()

    def through(tile, carry):
        at = pl.ds(pl.multiple_of(tile * 256, 256), 256)
        grad_mamba[:, at] = dot_nt(grad_branch[...], out_mat[at, :])
        return carry

    lax.fori_loop(0, 6, through, 0)

    def through_heads(tile, carry):
        at = pl.ds(pl.multiple_of(tile * 256, 256), 256)
        grad_attended[:, at] = dot_nt(grad_branch[...], heads_mat[at, :])
        return carry

    lax.fori_loop(0, 2, through_heads, 0)
    small = {
        1: kernel_grad,
        2: bias_grad,
        3: step_grad,
        4: decay_grad,
        5: skip_grad,
        6: mixer_grad,
    }
    for ref in small.values():
        ref[...] = jnp.zeros_like(ref)

    def add_small(slot, value):
        small[slot][...] += value

    copies[2].wait()
    copies[3].wait()

    def sequence(index, carry):
        rows = pl.ds(pl.multiple_of(index * LEN, LEN), LEN)
        grads = grad_attended[rows, :]
        attention_backward(proj, rows, cosine, sine, grads, grad_cat)
        mamba_backward(
            proj, rows, kernel, bias, step_bias, decay_log, skip, mixer_gain, pick, ssm,
            grad_mamba[rows, :], grad_cat, None, balance, touch, grad_active, add_small,
        )
        return carry

    lax.fori_loop(0, 2, sequence, 0)
    leaving = leave_all(
        (
            (grad_branch, grad_branch_out),
            (grad_cat, grad_cat_out),
            (kernel_grad, kernel_grad_out),
            (bias_grad, bias_grad_out),
            (step_grad, step_grad_out),
            (decay_grad, decay_grad_out),
            (skip_grad, skip_grad_out),
            (mixer_grad, mixer_grad_out),
        ),
        out_sems,
    )
    for copy in leaving:
        copy.wait()


def input_backward_kernel(earlier, active, *refs):
    @pl.when(active[0] == 1)
    def run():
        input_backward_body(*refs[:6], *refs[6 + earlier :])


def input_backward_body(
    grad_cat, grad_middle, x, packed, dt_weight, input_gain,
    grad_start_out, input_grad_out,
    grad_start, input_grad,
    cat, grad_normed, sems, out_sems,
):
    copies = [
        pltpu.make_async_copy(packed.at[:, pl.ds(16 * j, 16), :], cat.at[j], sems.at[j])
        for j in range(4)
    ]
    start_all(copies)
    for copy in copies:
        copy.wait()

    def back(tile, carry):
        at = pl.ds(pl.multiple_of(tile * 256, 256), 256)
        total = dot_nt(grad_cat[:, T0:CAT], dt_weight[at, :])
        for j in range(4):
            block = flat(cat[j, pl.ds(tile * 16, 16)])
            total = total + dot_nt(grad_cat[:, 1024 * j : 1024 * j + 1024], block)
        grad_normed[:, at] = total
        return carry

    lax.fori_loop(0, 4, back, 0)
    state = x[...].astype(F32)
    grad_state, grad_gain = rms_backward(state, input_gain[...], grad_normed[...])
    input_grad[...] = grad_gain
    grad_start[...] = grad_middle[...] + grad_state
    leaving = leave_all(((grad_start, grad_start_out), (input_grad, input_grad_out)), out_sems)
    for copy in leaving:
        copy.wait()


VMEM = pl.BlockSpec(memory_space=pltpu.VMEM)
SMEM = pl.BlockSpec(memory_space=pltpu.SMEM)
ANY = pl.BlockSpec(memory_space=pl.ANY)
LIMIT = 60 * 1024 * 1024


def shape(rows, columns, dtype):
    return jax.ShapeDtypeStruct((rows, columns), dtype)


def scratch(*dims, dtype=BF16):
    return pltpu.VMEM(dims, dtype)


def mirrored(shapes):
    return [pltpu.VMEM(s.shape, s.dtype) for s in shapes]


def run_forward(start, mats, small, rope):
    packed, dt_weight, out_weight, heads_weight = mats
    shapes = (
        shape(ROWS, WIDTH, BF16),
        shape(ROWS, WIDTH, BF16),
        shape(ROWS, CAT, F32),
        shape(ROWS, INNER, F32),
        shape(ROWS, INNER, BF16),
        shape(ROWS, 512, BF16),
        shape(ROWS, WIDTH, F32),
        shape(ROWS, WIDTH, BF16),
        shape(ROWS, FEED, F32),
        shape(ROWS, FEED, F32),
        shape(ROWS, FEED, BF16),
    )
    return pl.pallas_call(
        forward_kernel,
        out_shape=shapes,
        in_specs=[VMEM, ANY, VMEM, ANY, ANY] + [VMEM] * 10,
        out_specs=(ANY,) * len(shapes),
        scratch_shapes=[
            *mirrored(shapes),
            scratch(4, 64, 16, 1024),
            scratch(4, 64, 16, 1024),
            scratch(64, 32, 1024),
            scratch(INNER, WIDTH),
            scratch(512, WIDTH),
            pltpu.SemaphoreType.DMA((11,)),
            pltpu.SemaphoreType.DMA((len(shapes),)),
        ],
        compiler_params=pltpu.CompilerParams(vmem_limit_bytes=LIMIT),
        cost_estimate=pl.CostEstimate(
            flops=2 * ROWS * 12_600_000, bytes_accessed=40_000_000, transcendentals=2_000_000
        ),
        name="forward",
    )(start, packed, dt_weight, out_weight, heads_weight, *small, *rope)


def run_feed_backward(active, grad_top, mats, gate, upper, middle, feed_gain, earlier=()):
    shapes = (
        shape(ROWS, FEED, BF16),
        shape(ROWS, FEED, BF16),
        shape(ROWS, WIDTH, F32),
        shape(1, WIDTH, F32),
    )
    return pl.pallas_call(
        functools.partial(feed_backward_kernel, len(earlier)),
        out_shape=shapes,
        in_specs=[SMEM, VMEM, ANY, ANY, ANY, ANY, VMEM] + [ANY] * len(earlier),
        out_specs=(ANY,) * len(shapes),
        scratch_shapes=[
            *mirrored(shapes),
            scratch(ROWS, FEED, dtype=F32),
            scratch(ROWS, FEED, dtype=F32),
            scratch(ROWS, WIDTH, dtype=F32),
            scratch(4, 64, 16, 1024),
            scratch(64, 32, 1024),
            scratch(ROWS, WIDTH, dtype=F32),
            pltpu.SemaphoreType.DMA((8,)),
            pltpu.SemaphoreType.DMA((4,)),
        ],
        input_output_aliases={7 + k: k for k in range(len(earlier))},
        compiler_params=pltpu.CompilerParams(vmem_limit_bytes=LIMIT),
        cost_estimate=pl.CostEstimate(
            flops=2 * ROWS * 6_300_000, bytes_accessed=22_000_000, transcendentals=1_000_000
        ),
        name="feed_backward",
    )(active, grad_top, mats[0], gate, upper, middle, feed_gain, *earlier)


def run_mix_backward(active, grad_middle, mats, proj, ssm, small, rope, pick, earlier=()):
    packed, dt_weight, out_weight, heads_weight = mats
    shapes = (
        shape(ROWS, WIDTH, BF16),
        shape(ROWS, CAT, BF16),
        shape(4, MIXED, F32),
        shape(1, MIXED, F32),
        shape(1, 128, F32),
        shape(1, 128, F32),
        shape(1, INNER, F32),
        shape(1, INNER, F32),
    )
    return pl.pallas_call(
        functools.partial(mix_backward_kernel, len(earlier)),
        out_shape=shapes,
        in_specs=[SMEM, VMEM] + [ANY] * 4 + [VMEM] * 9 + [ANY] * len(earlier),
        out_specs=(ANY,) * len(shapes),
        scratch_shapes=[
            *mirrored(shapes),
            scratch(ROWS, CAT, dtype=F32),
            scratch(ROWS, INNER, dtype=F32),
            scratch(INNER, WIDTH),
            scratch(512, WIDTH),
            scratch(ROWS, INNER, dtype=F32),
            scratch(ROWS, 512, dtype=F32),
            scratch(LEN, INNER, dtype=F32),
            scratch(LEN, INNER, dtype=F32),
            scratch(LEN, MIXED, dtype=F32),
            pltpu.SemaphoreType.DMA((4,)),
            pltpu.SemaphoreType.DMA((8,)),
        ],
        input_output_aliases={15 + k: k for k in range(len(earlier))},
        compiler_params=pltpu.CompilerParams(vmem_limit_bytes=LIMIT),
        cost_estimate=pl.CostEstimate(
            flops=2 * ROWS * 2_100_000, bytes_accessed=14_000_000, transcendentals=4_000_000
        ),
        name="mix_backward",
    )(
        active, grad_middle, out_weight, heads_weight, proj, ssm, *small[1:7], *rope, pick, *earlier
    )


def run_input_backward(active, grad_cat, grad_middle, start, mats, input_gain, earlier=()):
    shapes = (shape(ROWS, WIDTH, F32), shape(1, WIDTH, F32))
    return pl.pallas_call(
        functools.partial(input_backward_kernel, len(earlier)),
        out_shape=shapes,
        in_specs=[SMEM, VMEM, VMEM, VMEM, ANY, VMEM, VMEM] + [ANY] * len(earlier),
        out_specs=(ANY,) * len(shapes),
        scratch_shapes=[
            *mirrored(shapes),
            scratch(4, 64, 16, 1024),
            scratch(ROWS, WIDTH, dtype=F32),
            pltpu.SemaphoreType.DMA((4,)),
            pltpu.SemaphoreType.DMA((2,)),
        ],
        input_output_aliases={7 + k: k for k in range(len(earlier))},
        compiler_params=pltpu.CompilerParams(vmem_limit_bytes=LIMIT),
        cost_estimate=pl.CostEstimate(
            flops=2 * ROWS * 4_200_000, bytes_accessed=13_000_000, transcendentals=1000
        ),
        name="input_backward",
    )(active, grad_cat, grad_middle, start, *mats[:2], input_gain, *earlier)


def rope_tables():
    position = jnp.arange(LEN).astype(F32)
    inverse = 10000.0 ** (-(jnp.arange(32).astype(F32) * 2.0) / 64)
    angle = position[:, None] * inverse[None, :]
    cosine = jnp.tile(jnp.cos(angle), (1, 16))
    sine = jnp.sin(angle)
    return cosine, jnp.tile(jnp.concatenate([-sine, sine], axis=1), (1, 8))


def head_pick():
    lanes = lax.broadcasted_iota(jnp.int32, (INNER, 128), 0) // 64
    return (lanes == lax.broadcasted_iota(jnp.int32, (INNER, 128), 1)).astype(BF16)


def prepared_small(pieces):
    input_gain, kernel, bias, step_bias, decay_log, skip, mixer_gain, feed_gain = pieces

    def padded(v):
        return jnp.pad(v, (0, 128 - HEADS))[None]

    return (
        input_gain[None],
        kernel,
        bias[None],
        padded(step_bias),
        padded(decay_log),
        jnp.repeat(skip, 64)[None],
        mixer_gain[None],
        feed_gain[None],
    )


FIRST = (1, 0, 3, 2)
SECOND = (3, 2, 1, 0)


def partners(axis, turn):
    order = (FIRST, SECOND) if turn == 0 else (SECOND, FIRST)
    me = lax.axis_index(axis)
    near = me + 1 - 2 * lax.rem(me, 2)
    found = (near, 3 - me) if turn == 0 else (3 - me, near)
    return me, found, [[(i, table[i]) for i in range(4)] for table in order]


def first_sent(part, axis, turn):
    me, (one, two), swaps = partners(axis, turn)
    return part([one, lax.rem(me + 2, 4)]).astype(BF16)


def first_got(sent, axis, turn):
    return lax.ppermute(sent, axis, partners(axis, turn)[2][0])


def exchanged(part, got, axis, turn):
    me, (one, two), (swap_one, swap_two) = partners(axis, turn)
    half = got.shape[0] // 2
    handed = part([two]) + got[half:].astype(F32)
    last = lax.ppermute(handed.astype(BF16), axis, swap_two)
    return part([me]) + got[:half].astype(F32) + last.astype(F32)


def product_of(left, right, place):
    blocks = left.reshape(4, 4, 4, left.shape[0] // 64, left.shape[1])

    def part(places):
        picked = [lax.dynamic_index_in_dim(blocks, p, place, keepdims=False) for p in places]
        return dot(jnp.concatenate(picked, axis=0).reshape(-1, left.shape[1]), right)

    return part


def quarters_of(array, dim):
    def part(places):
        picked = [lax.dynamic_index_in_dim(array, p, dim, keepdims=False) for p in places]
        return jnp.concatenate(picked, axis=0).reshape(-1, array.shape[-1]).astype(F32)

    return part


def summed_on(array, axis, dim, turn):
    part = quarters_of(array, dim)
    got = first_got(first_sent(part, axis, turn), axis, turn)
    return exchanged(part, got, axis, turn)


def finished(parts, order, depth):
    array = jnp.concatenate([p.astype(BF16) for p in parts], axis=1)
    width = array.shape[1]
    rest = [0, 1, 2]
    rest.remove(order[0])
    array = array.reshape(4, 4, depth, width)
    array = summed_on(array, DP[order[1]], rest.index(order[1]), 0).astype(BF16)
    return summed_on(array.reshape(4, depth, width), DP[order[2]], 0, 0)


def column_blocks(matrix):
    return [matrix[:, at : at + 1024] for at in range(0, matrix.shape[1], 1024)]


def on_device(
    layer_input,
    out_grad,
    in_weight,
    query_weight,
    key_weight,
    value_weight,
    out_weight,
    heads_weight,
    gate_weight,
    up_weight,
    down_weight,
    *pieces,
):
    micro, part, width = layer_input.shape
    rows = micro * part
    cat = jnp.concatenate(
        [query_weight[0], key_weight[0], value_weight[0], in_weight[0, :, :3328]], axis=1
    )
    steps = jnp.pad(in_weight[0, :, 3328:].reshape(1, -1), ((0, 7), (0, 1024 - 16 * HEADS)))
    own = jnp.concatenate(
        [
            *column_blocks(cat),
            *column_blocks(gate_weight[0]),
            *column_blocks(up_weight[0]),
            down_weight[0],
            out_weight[0],
            heads_weight[0],
            steps,
        ],
        axis=0,
    )
    packed = lax.all_gather(own, DP, axis=0, tiled=False)
    dt_weight = packed[:, DT0, : 16 * HEADS].reshape(WIDTH, HEADS)
    mats = (
        packed,
        jnp.pad(dt_weight, ((0, 0), (0, 128 - HEADS))),
        packed[:, OUT0:HEADS0].reshape(INNER, WIDTH),
        packed[:, HEADS0:DT0].reshape(512, WIDTH),
    )
    small = prepared_small([piece[0] for piece in pieces])
    rope = rope_tables()
    pick = head_pick()
    first = lax.axis_index("section") == 0

    start_low = layer_input.reshape(rows, width)
    kept_low = run_forward(start_low, mats, small, rope)
    start_high = lax.ppermute(kept_low[0], "section", [(0, 1)])
    kept_high = run_forward(start_high, mats, small, rope)
    layer_outputs = jnp.where(first, kept_low[0], kept_high[0]).reshape(1, micro, part, width)

    on_high = jnp.where(first, 0, 1).astype(jnp.int32).reshape(1)
    on_low = 1 - on_high
    top_high = out_grad.reshape(rows, width)
    feed_high = run_feed_backward(
        on_high, top_high, mats, kept_high[8], kept_high[9], kept_high[6], small[7]
    )
    mix_high = run_mix_backward(
        on_high, feed_high[2], mats, kept_high[2], kept_high[3], small, rope, pick
    )
    input_high = run_input_backward(
        on_high, mix_high[1], feed_high[2], start_high, mats, small[0]
    )
    top_low = lax.ppermute(input_high[0].astype(BF16), "section", [(1, 0)])

    def chosen(slot):
        return jnp.where(first, kept_low[slot], kept_high[slot])

    normed_t, ffin_t, hidden_t = (chosen(slot).T for slot in (1, 7, 10))
    joined_t = jnp.concatenate(
        [chosen(4).T.reshape(64, 24, rows), chosen(5).T.reshape(64, 8, rows)], axis=1
    ).reshape(2048, rows)

    feed = run_feed_backward(
        on_low, top_low, mats, kept_low[8], kept_low[9], kept_low[6], small[7], feed_high
    )
    grad_gate, grad_upper, grad_middle, feed_grad = feed
    grad_low = jnp.where(first, top_low, top_high)
    orders = ((2, 0, 1), (0, 1, 2), (1, 2, 0))
    products = [
        product_of(left, right, order[0])
        for left, right, order in zip(
            (hidden_t, ffin_t, ffin_t), (grad_low, grad_gate, grad_upper), orders
        )
    ]
    sents = [first_sent(p, DP[order[0]], 0) for p, order in zip(products, orders)]
    grad_middle, *sents = lax.optimization_barrier((grad_middle, *sents))
    gots = [first_got(sent, DP[order[0]], 0) for sent, order in zip(sents, orders)]
    mix = run_mix_backward(
        on_low, grad_middle, mats, kept_low[2], kept_low[3], small, rope, pick, mix_high
    )
    grad_branch, grad_cat, *small_grads = mix
    grad_branch, grad_cat, *gots = lax.optimization_barrier((grad_branch, grad_cat, *gots))
    feed_parts = [
        exchanged(p, got, DP[order[0]], 0) for p, got, order in zip(products, gots, orders)
    ]
    products = [
        product_of(left, right, order[0])
        for left, right, order in zip(
            (joined_t, normed_t, normed_t),
            (grad_branch, grad_cat[:, :2048], grad_cat[:, 2048:]),
            orders,
        )
    ]
    sents = [first_sent(p, DP[order[0]], 1) for p, order in zip(products, orders)]
    grad_middle, *sents = lax.optimization_barrier((grad_middle, *sents))
    mix_parts = []
    for p, sent, order in zip(products, sents, orders):
        got = first_got(sent, DP[order[0]], 1)
        mix_parts.append(exchanged(p, got, DP[order[0]], 1))
    grad_start, input_grad = run_input_backward(
        on_low, grad_cat, grad_middle, start_low, mats, small[0], input_high
    )
    small_grads = [input_grad, *small_grads]
    rows_grad, gate_cat, up_cat = (
        finished(pair, order, depth)
        for pair, order, depth in zip(zip(feed_parts, mix_parts), orders, (32, 16, 16))
    )
    down_grad, joined_grad = rows_grad[:, :WIDTH], rows_grad[:, WIDTH:]
    gate_grad, up_grad = gate_cat[:, :FEED], up_cat[:, :FEED]
    cat_grad = jnp.concatenate([gate_cat[:, FEED:], up_cat[:, FEED:]], axis=1)

    input_g, kernel_g, bias_g, step_g, decay_g, skip_g, mixer_g = small_grads
    small_grads = (
        input_g[0],
        kernel_g,
        bias_g[0],
        step_g[0, :HEADS],
        decay_g[0, :HEADS],
        skip_g.reshape(HEADS, 64).sum(axis=1),
        mixer_g[0],
        feed_grad[0],
    )
    vector = jnp.concatenate([piece.reshape(-1) for piece in small_grads])
    vector = jnp.pad(vector, (0, -vector.shape[0] % 1024)).reshape(-1, 128)
    total = jnp.sum(lax.all_gather(vector, DP, axis=0, tiled=False), axis=0).reshape(-1)
    summed, at = ([], 0)
    for piece in small_grads:
        summed.append(total[at : at + piece.size].reshape(1, *piece.shape))
        at += piece.size
    return (
        layer_outputs,
        grad_start.reshape(1, micro, part, width),
        cat_grad[None, :, Z0 : T0 + HEADS],
        cat_grad[None, :, :K0],
        cat_grad[None, :, K0:V0],
        cat_grad[None, :, V0:Z0],
        joined_grad[None, :24],
        joined_grad[None, 24:],
        gate_grad[None],
        up_grad[None],
        down_grad[None],
        *summed,
    )


def solution(mesh):
    torus = Mesh(
        mesh.devices.reshape(mesh.shape["section"], 4, 4, 4), ("section", "dp_0", "dp_1", "dp_2")
    )
    in_specs = (
        P(None, DP, None),
        P(None, DP, None),
        P("section", DP, None),
        P("section", DP, None),
        P("section", DP, None),
        P("section", DP, None),
        P("section", DP, None),
        P("section", DP, None),
        P("section", DP, None),
        P("section", DP, None),
        P("section", DP, None),
        P("section", None),
        P("section", None, None),
        P("section", None),
        P("section", None),
        P("section", None),
        P("section", None),
        P("section", None),
        P("section", None),
    )
    out_specs = (
        P("section", None, DP, None),
        P("section", None, DP, None),
        P("section", DP, None),
        P("section", DP, None),
        P("section", DP, None),
        P("section", DP, None),
        P("section", DP, None),
        P("section", DP, None),
        P("section", DP, None),
        P("section", DP, None),
        P("section", DP, None),
        P("section", None),
        P("section", None, None),
        P("section", None),
        P("section", None),
        P("section", None),
        P("section", None),
        P("section", None),
        P("section", None),
    )
    return jax.shard_map(
        on_device, mesh=torus, in_specs=in_specs, out_specs=out_specs, check_vma=False
    )
```

```python
import functools

import jax
import jax.numpy as jnp
from jax import lax
from jax.experimental import pallas as pl
from jax.experimental.pallas import tpu as pltpu
from jax.sharding import Mesh
from jax.sharding import PartitionSpec as P

LEN = 128
ROWS = 256
WIDTH = 1024
FEED = 2048
INNER = 1536
MIXED = 1792
CAT = 4224
HEADS = 24
DP = ("dp_0", "dp_1", "dp_2")
F32 = jnp.float32
BF16 = jnp.bfloat16
HIDE = -1e30
Q0, K0, V0, Z0, X0, T0 = 0, 512, 640, 768, 2304, 4096
GATE0, UP0, DOWN0, OUT0, HEADS0, DT0, PACKED = 64, 96, 128, 160, 184, 192, 200


def dot(left, right):
    return jnp.dot(left, right, preferred_element_type=F32)


def dot_nt(left, right):
    return lax.dot_general(left, right, (((1,), (1,)), ((), ())), preferred_element_type=F32)


def dot_tn(left, right):
    return lax.dot_general(left, right, (((0,), (0,)), ((), ())), preferred_element_type=F32)


def dot_full(left, right):
    return jnp.dot(left, right, precision=lax.Precision.HIGHEST, preferred_element_type=F32)


def iota(shape, dim):
    return lax.broadcasted_iota(jnp.int32, shape, dim)


def sigmoid(v):
    return 1.0 / (1.0 + jnp.exp(-v))


def softplus(v):
    return jnp.maximum(v, 0.0) + jnp.log(1.0 + jnp.exp(-jnp.abs(v)))


def swap_halves(v):
    width = v.shape[1]
    near = lax.rem(iota(v.shape, 1), 64) < 32
    return jnp.where(near, pltpu.roll(v, width - 32, 1), pltpu.roll(v, 32, 1))


def shifted_down(v, by):
    if by == 0:
        return v
    return jnp.where(iota(v.shape, 0) >= by, pltpu.roll(v, by, 0), 0.0)


def shifted_up(v, by):
    if by == 0:
        return v
    rows = v.shape[0]
    return jnp.where(iota(v.shape, 0) < rows - by, pltpu.roll(v, rows - by, 0), 0.0)


def rms(v):
    return lax.rsqrt(jnp.mean(v * v, axis=-1, keepdims=True) + 1e-05)


def rms_backward(v, gain, grad):
    scale = rms(v)
    gained = grad * gain
    inner = jnp.mean(gained * v, axis=-1, keepdims=True)
    grad_v = scale * gained - v * (scale * scale * scale * inner)
    return grad_v, jnp.sum(grad * v * scale, axis=0, keepdims=True)


def left_half():
    return iota((LEN, 128), 1) < 64


def both_halves(v, group, left):
    turned = pltpu.roll(v, 64, 1)
    return jnp.where(left, v, turned) if group == 0 else jnp.where(left, turned, v)


def stacked(pairs, left):
    parts = []
    for pair in pairs:
        parts.append(jnp.where(left, pair, 0.0))
        parts.append(jnp.where(left, 0.0, pair))
    return jnp.concatenate(parts, axis=0).astype(BF16)


def unstacked(rows, index, left):
    low = rows[2 * index * LEN : (2 * index + 1) * LEN]
    high = rows[(2 * index + 1) * LEN : (2 * index + 2) * LEN]
    return jnp.where(left, low, high)


def attention_parts(proj, rows, cosine, sine):
    left = left_half()
    query = proj[rows, Q0:K0]
    query = query * cosine[...] + swap_halves(query) * sine[...]
    key = proj[rows, K0:V0]
    key = key * cosine[:, :128] + swap_halves(key) * sine[:, :128]
    value = proj[rows, V0:Z0]
    groups = []
    for group in range(2):
        pairs = [query[:, 128 * p : 128 * p + 128] for p in (2 * group, 2 * group + 1)]
        queries = stacked(pairs, left)
        keys = both_halves(key, group, left).astype(BF16)
        values = both_halves(value, group, left).astype(BF16)
        scores = dot_nt(queries, keys) * 0.125
        time = lax.rem(iota(scores.shape, 0), LEN)
        scores = jnp.where(iota(scores.shape, 1) <= time, scores, HIDE)
        top = jnp.max(scores, axis=-1, keepdims=True)
        expo = jnp.exp(scores - top)
        probs = expo / jnp.sum(expo, axis=-1, keepdims=True)
        groups.append((queries, keys, values, probs))
    return left, groups


def attention_forward(proj, rows, cosine, sine, attended):
    left, groups = attention_parts(proj, rows, cosine, sine)
    for group, (queries, keys, values, probs) in enumerate(groups):
        mixed = dot(probs.astype(BF16), values)
        for index in range(2):
            at = 256 * group + 128 * index
            attended[rows, at : at + 128] = unstacked(mixed, index, left).astype(BF16)


def attention_backward(proj, rows, cosine, sine, grad_attended, grad_cat):
    left, groups = attention_parts(proj, rows, cosine, sine)
    key_parts, value_parts = [], []
    for group, (queries, keys, values, probs) in enumerate(groups):
        pairs = [grad_attended[:, 128 * p : 128 * p + 128] for p in (2 * group, 2 * group + 1)]
        grads = stacked(pairs, left)
        grad_values = dot_tn(probs.astype(BF16), grads)
        grad_probs = dot_nt(grads, values)
        inner = jnp.sum(probs * grad_probs, axis=-1, keepdims=True)
        grad_scores = (probs * (grad_probs - inner)).astype(BF16)
        grad_queries = dot(grad_scores, keys) * 0.125
        grad_keys = dot_tn(grad_scores, queries) * 0.125
        for index in range(2):
            at = 256 * group + 128 * index
            grad = unstacked(grad_queries, index, left)
            grad = grad * cosine[:, :128] - swap_halves(grad) * sine[:, :128]
            grad_cat[rows, at : at + 128] = grad.astype(BF16)
        key_parts.append(grad_keys + pltpu.roll(grad_keys, 64, 1))
        value_parts.append(grad_values + pltpu.roll(grad_values, 64, 1))
    grad = jnp.where(left, key_parts[0], key_parts[1])
    grad = grad * cosine[:, :128] - swap_halves(grad) * sine[:, :128]
    grad_cat[rows, K0:V0] = grad.astype(BF16)
    grad_cat[rows, V0:Z0] = jnp.where(left, value_parts[0], value_parts[1]).astype(BF16)


def mamba_parts(proj, rows, kernel, bias, step_bias, decay_log):
    mixed = proj[rows, X0:T0]
    total = bias[...] + mixed * kernel[3:4, :]
    for tap in range(3):
        total = total + shifted_down(mixed, 3 - tap) * kernel[tap : tap + 1, :]
    active = total * sigmoid(total)
    step = softplus(proj[rows, T0:CAT] + step_bias[...])
    rate = -step * jnp.exp(decay_log[...])
    earlier = (iota((LEN, LEN), 0) >= iota((LEN, LEN), 1)).astype(F32)
    cumul = dot_full(earlier, rate)
    state_in = active[:, INNER : INNER + 128].astype(BF16)
    state_out = active[:, INNER + 128 :].astype(BF16)
    return mixed, total, active, step, rate, cumul, state_in, state_out


def stepped(step, pair, left):
    return jnp.where(left, step[:, 2 * pair : 2 * pair + 1], step[:, 2 * pair + 1 : 2 * pair + 2])


def mamba_forward(proj, rows, kernel, bias, step_bias, decay_log, skip, gain, ssm, mamba):
    left = left_half()
    parts = mamba_parts(proj, rows, kernel, bias, step_bias, decay_log)
    mixed, total, active, step, rate, cumul, state_in, state_out = parts
    across = cumul.T
    hidden = jnp.where(iota((LEN, LEN), 0) >= iota((LEN, LEN), 1), 0.0, HIDE)
    meeting = dot_nt(state_out, state_in)
    for pair in range(HEADS // 2):
        at = 128 * pair
        inputs = active[:, at : at + 128]
        scaled = (inputs * stepped(step, pair, left)).astype(BF16)
        mixing = []
        for head in (2 * pair, 2 * pair + 1):
            spread = cumul[:, head : head + 1] - across[head : head + 1, :] + hidden
            mixing.append((meeting * jnp.exp(spread)).astype(BF16))
        both = dot(jnp.concatenate(mixing, axis=0), scaled)
        out = unstacked(both, 0, left) + skip[:, at : at + 128] * inputs
        ssm[rows, at : at + 128] = out
    z = proj[rows, Z0:X0]
    gated = ssm[rows, :] * (z * sigmoid(z))
    mamba[rows, :] = (gated * rms(gated) * gain[...]).astype(BF16)


def head_sums(v, pick):
    high = v.astype(BF16)
    low = (v - high.astype(F32)).astype(BF16)
    return dot(high, pick) + dot(low, pick)


def mamba_backward(
    proj, rows, kernel, bias, step_bias, decay_log, skip, gain, pick, ssm, grad_mamba, grad_cat,
    across_scratch, balance_scratch, touch_scratch, grad_active, add_small,
):
    left = left_half()
    parts = mamba_parts(proj, rows, kernel, bias, step_bias, decay_log)
    mixed, total, active, step, rate, cumul, state_in, state_out = parts
    across = cumul.T
    hidden = jnp.where(iota((LEN, LEN), 1) >= iota((LEN, LEN), 0), 0.0, HIDE)
    meeting = dot_nt(state_out, state_in).T
    z = proj[rows, Z0:X0]
    out = ssm[rows, :]
    gate = sigmoid(z)
    gated = out * (z * gate)
    grad_gated, grad_gain = rms_backward(gated, gain[...], grad_mamba)
    add_small(6, grad_gain)
    grad_cat[rows, Z0:X0] = (grad_gated * out * (gate * (1.0 + z * (1.0 - gate)))).astype(BF16)
    grad_out = grad_gated * (z * gate)
    add_small(5, jnp.sum(grad_out * active[:, :INNER], axis=0, keepdims=True))
    grad_meeting = jnp.zeros((LEN, LEN), F32)
    for pair in range(HEADS // 2):
        at = 128 * pair
        inputs = active[:, at : at + 128]
        steps = stepped(step, pair, left)
        scaled = (inputs * steps).astype(BF16)
        grad_pair = grad_out[:, at : at + 128]
        grad_low = grad_pair.astype(BF16)
        halves = jnp.concatenate(
            [jnp.where(left, scaled, jnp.zeros_like(scaled)), jnp.where(left, jnp.zeros_like(scaled), scaled)],
            axis=0,
        )
        grad_mixing = dot_nt(halves, grad_low)
        mixing = []
        for place, head in enumerate((2 * pair, 2 * pair + 1)):
            spread = across[head : head + 1, :] - cumul[:, head : head + 1] + hidden
            decay = jnp.exp(spread)
            mixing.append((meeting * decay).astype(BF16))
            grad_meeting = grad_meeting + grad_mixing[LEN * place : LEN * place + LEN] * decay
        both = dot(jnp.concatenate(mixing, axis=0), grad_low)
        grad_scaled = unstacked(both, 0, left)
        skips = skip[:, at : at + 128]
        grad_active[:, at : at + 128] = grad_scaled * steps + skips * grad_pair
        touch_scratch[:, at : at + 128] = grad_scaled * inputs
        balance_scratch[:, at : at + 128] = grad_low.astype(F32) * (
            out[:, at : at + 128] - skips * inputs
        ) - scaled.astype(F32) * grad_scaled
    grad_low = grad_meeting.astype(BF16)
    grad_active[:, INNER : INNER + 128] = dot(grad_low, state_out)
    grad_active[:, INNER + 128 :] = dot_tn(grad_low, state_in)
    later = (iota((LEN, LEN), 1) >= iota((LEN, LEN), 0)).astype(F32)
    grad_rate = dot_full(later, head_sums(balance_scratch[...], pick[...]))
    add_small(4, jnp.sum(grad_rate * rate, axis=0, keepdims=True))
    grad_step = head_sums(touch_scratch[...], pick[...]) - grad_rate * jnp.exp(decay_log[...])
    grad_dt = grad_step * sigmoid(proj[rows, T0:CAT] + step_bias[...])
    add_small(3, jnp.sum(grad_dt, axis=0, keepdims=True))
    grad_cat[rows, T0:CAT] = grad_dt.astype(BF16)
    slope = sigmoid(total)
    grad_total = grad_active[...] * (slope * (1.0 + total * (1.0 - slope)))
    add_small(2, jnp.sum(grad_total, axis=0, keepdims=True))
    grad_mixed = grad_total * kernel[3:4, :]
    taps = []
    for tap in range(4):
        taps.append(jnp.sum(grad_total * shifted_down(mixed, 3 - tap), axis=0, keepdims=True))
        if tap < 3:
            grad_mixed = grad_mixed + shifted_up(grad_total, 3 - tap) * kernel[tap : tap + 1, :]
    add_small(1, jnp.concatenate(taps, axis=0))
    grad_cat[rows, X0:T0] = grad_mixed.astype(BF16)


def flat(block):
    return block.reshape(block.shape[0] * block.shape[1], block.shape[2])


def start_all(copies):
    for copy in copies:
        copy.start()


def forward_kernel(
    x, packed, dt_weight, out_weight, heads_weight, input_gain, kernel, bias, step_bias, decay_log, skip,
    mixer_gain, feed_gain, cosine, sine,
    result_out, normed_out, proj_out, ssm_out, mamba_out, attended_out, middle_out, ffin_out, gate_out,
    upper_out, hidden_out,
    result, normed, proj, ssm, mamba, attended, middle, ffin, gate, upper, hidden,
    cat, gate_up, down, out_mat, heads_mat, sems, out_sems,
):
    leaving = []

    def leave(*pairs):
        for source, target in pairs:
            copy = pltpu.make_async_copy(source, target, out_sems.at[len(leaving)])
            copy.start()
            leaving.append(copy)

    copies = [
        pltpu.make_async_copy(packed.at[:, pl.ds(16 * j, 16), :], cat.at[j], sems.at[j])
        for j in range(4)
    ]
    copies.append(pltpu.make_async_copy(out_weight, out_mat, sems.at[4]))
    copies.append(pltpu.make_async_copy(heads_weight, heads_mat, sems.at[5]))
    for j in range(4):
        copies.append(
            pltpu.make_async_copy(
                packed.at[:, pl.ds(GATE0 + 16 * j, 16), :], gate_up.at[j], sems.at[6 + j]
            )
        )
    copies.append(pltpu.make_async_copy(packed.at[:, pl.ds(DOWN0, 32), :], down, sems.at[10]))
    start_all(copies)
    state = x[...].astype(F32)
    normed[...] = (state * rms(state) * input_gain[...]).astype(BF16)
    proj[:, T0:CAT] = dot(normed[...], dt_weight[...])
    for j in range(4):
        copies[j].wait()

        def columns(tile, carry, j=j):
            at = pl.multiple_of(tile * 256, 256)
            block = flat(cat[j, :, :, pl.ds(at, 256)])
            proj[:, pl.ds(pl.multiple_of(j * 1024 + at, 256), 256)] = dot(normed[...], block)
            return carry

        lax.fori_loop(0, 4, columns, 0)
    leave((normed, normed_out), (proj, proj_out))

    def sequence(index, carry):
        rows = pl.ds(pl.multiple_of(index * LEN, LEN), LEN)
        attention_forward(proj, rows, cosine, sine, attended)
        mamba_forward(proj, rows, kernel, bias, step_bias, decay_log, skip, mixer_gain, ssm, mamba)
        return carry

    lax.fori_loop(0, 2, sequence, 0)
    leave((ssm, ssm_out), (mamba, mamba_out), (attended, attended_out))
    copies[4].wait()
    copies[5].wait()

    def joined(tile, carry):
        at = pl.ds(pl.multiple_of(tile * 256, 256), 256)
        part = dot(mamba[...], out_mat[:, at]) + dot(attended[...], heads_mat[:, at])
        middle[:, at] = x[:, at].astype(F32) + part
        return carry

    lax.fori_loop(0, 4, joined, 0)
    value = middle[...]
    ffin[...] = (value * rms(value) * feed_gain[...]).astype(BF16)
    leave((middle, middle_out), (ffin, ffin_out))
    for j in range(2):
        copies[6 + j].wait()
        copies[8 + j].wait()

        def feed(tile, carry, j=j):
            at = pl.multiple_of(tile * 256, 256)
            to = pl.ds(pl.multiple_of(j * 1024 + at, 256), 256)
            low = dot(ffin[...], flat(gate_up[j, :, :, pl.ds(at, 256)]))
            high = dot(ffin[...], flat(gate_up[2 + j, :, :, pl.ds(at, 256)]))
            gate[:, to] = low
            upper[:, to] = high
            hidden[:, to] = (low * sigmoid(low) * high).astype(BF16)
            return carry

        lax.fori_loop(0, 4, feed, 0)
    leave((gate, gate_out), (upper, upper_out), (hidden, hidden_out))
    copies[10].wait()

    def last(tile, carry):
        at = pl.ds(pl.multiple_of(tile * 256, 256), 256)
        result[:, at] = (middle[:, at] + dot(hidden[...], flat(down[:, :, at]))).astype(BF16)
        return carry

    lax.fori_loop(0, 4, last, 0)
    leave((result, result_out))
    for copy in leaving:
        copy.wait()


def leave_all(pairs, sems):
    copies = [
        pltpu.make_async_copy(source, target, sems.at[k]) for k, (source, target) in enumerate(pairs)
    ]
    start_all(copies)
    return copies


def feed_backward_kernel(earlier, active, *refs):
    @pl.when(active[0] == 1)
    def run():
        feed_backward_body(*refs[:6], *refs[6 + earlier :])


def feed_backward_body(
    grad_top, packed, gate_in, upper_in, middle_in, feed_gain,
    grad_gate_out, grad_upper_out, grad_middle_out, feed_grad_out,
    grad_gate, grad_upper, grad_middle, feed_grad,
    gate, upper, middle, gate_up, down, grad_ffin, sems, out_sems,
):
    inputs = [
        pltpu.make_async_copy(gate_in, gate, sems.at[5]),
        pltpu.make_async_copy(upper_in, upper, sems.at[6]),
        pltpu.make_async_copy(middle_in, middle, sems.at[7]),
    ]
    copies = [
        pltpu.make_async_copy(packed.at[:, pl.ds(DOWN0, 32), :], down, sems.at[4]),
    ]
    for j in range(4):
        copies.append(
            pltpu.make_async_copy(
                packed.at[:, pl.ds(GATE0 + 16 * j, 16), :], gate_up.at[j], sems.at[j]
            )
        )
    start_all(copies[:1] + inputs + copies[1:])
    copies[0].wait()
    for copy in inputs:
        copy.wait()

    def through(tile, carry):
        at = pl.ds(pl.multiple_of(tile * 256, 256), 256)
        block = flat(down[pl.ds(tile * 8, 8)])
        grad_hidden = dot_nt(grad_top[...], block)
        low, high = gate[:, at], upper[:, at]
        slope = sigmoid(low)
        grad_upper[:, at] = (grad_hidden * (low * slope)).astype(BF16)
        part = grad_hidden * high * (slope * (1.0 + low * (1.0 - slope)))
        grad_gate[:, at] = part.astype(BF16)
        return carry

    lax.fori_loop(0, 8, through, 0)
    leaving = leave_all(((grad_gate, grad_gate_out), (grad_upper, grad_upper_out)), out_sems)
    for copy in copies[1:]:
        copy.wait()

    def back(tile, carry):
        at = pl.ds(pl.multiple_of(tile * 256, 256), 256)
        total = jnp.zeros((ROWS, 256), F32)
        for j in range(2):
            block = flat(gate_up[j, pl.ds(tile * 16, 16)])
            total = total + dot_nt(grad_gate[:, 1024 * j : 1024 * j + 1024], block)
            block = flat(gate_up[2 + j, pl.ds(tile * 16, 16)])
            total = total + dot_nt(grad_upper[:, 1024 * j : 1024 * j + 1024], block)
        grad_ffin[:, at] = total
        return carry

    lax.fori_loop(0, 4, back, 0)
    grad_part, grad_gain = rms_backward(middle[...], feed_gain[...], grad_ffin[...])
    feed_grad[...] = grad_gain
    grad_middle[...] = grad_top[...].astype(F32) + grad_part
    leaving += leave_all(
        ((grad_middle, grad_middle_out), (feed_grad, feed_grad_out)), out_sems.at[pl.ds(2, 2)]
    )
    for copy in leaving:
        copy.wait()


def mix_backward_kernel(earlier, active, *refs):
    @pl.when(active[0] == 1)
    def run():
        mix_backward_body(*refs[:14], *refs[14 + earlier :])


def mix_backward_body(
    grad_middle, out_weight, heads_weight, proj_in, ssm_in, kernel, bias,
    step_bias, decay_log, skip, mixer_gain, cosine, sine, pick,
    grad_branch_out, grad_cat_out, kernel_grad_out, bias_grad_out,
    step_grad_out, decay_grad_out, skip_grad_out, mixer_grad_out,
    grad_branch, grad_cat, kernel_grad, bias_grad, step_grad, decay_grad,
    skip_grad, mixer_grad,
    proj, ssm,
    out_mat, heads_mat, grad_mamba, grad_attended, balance, touch, grad_active, sems,
    out_sems,
):
    copies = [
        pltpu.make_async_copy(out_weight, out_mat, sems.at[0]),
        pltpu.make_async_copy(heads_weight, heads_mat, sems.at[1]),
        pltpu.make_async_copy(proj_in, proj, sems.at[2]),
        pltpu.make_async_copy(ssm_in, ssm, sems.at[3]),
    ]
    start_all(copies)
    grad_branch[...] = grad_middle[...].astype(BF16)
    copies[0].wait()
    copies[1].wait()

    def through(tile, carry):
        at = pl.ds(pl.multiple_of(tile * 256, 256), 256)
        grad_mamba[:, at] = dot_nt(grad_branch[...], out_mat[at, :])
        return carry

    lax.fori_loop(0, 6, through, 0)

    def through_heads(tile, carry):
        at = pl.ds(pl.multiple_of(tile * 256, 256), 256)
        grad_attended[:, at] = dot_nt(grad_branch[...], heads_mat[at, :])
        return carry

    lax.fori_loop(0, 2, through_heads, 0)
    small = {
        1: kernel_grad,
        2: bias_grad,
        3: step_grad,
        4: decay_grad,
        5: skip_grad,
        6: mixer_grad,
    }
    for ref in small.values():
        ref[...] = jnp.zeros_like(ref)

    def add_small(slot, value):
        small[slot][...] += value

    copies[2].wait()
    copies[3].wait()

    def sequence(index, carry):
        rows = pl.ds(pl.multiple_of(index * LEN, LEN), LEN)
        grads = grad_attended[rows, :]
        attention_backward(proj, rows, cosine, sine, grads, grad_cat)
        mamba_backward(
            proj, rows, kernel, bias, step_bias, decay_log, skip, mixer_gain, pick, ssm,
            grad_mamba[rows, :], grad_cat, None, balance, touch, grad_active, add_small,
        )
        return carry

    lax.fori_loop(0, 2, sequence, 0)
    leaving = leave_all(
        (
            (grad_branch, grad_branch_out),
            (grad_cat, grad_cat_out),
            (kernel_grad, kernel_grad_out),
            (bias_grad, bias_grad_out),
            (step_grad, step_grad_out),
            (decay_grad, decay_grad_out),
            (skip_grad, skip_grad_out),
            (mixer_grad, mixer_grad_out),
        ),
        out_sems,
    )
    for copy in leaving:
        copy.wait()


def input_backward_kernel(earlier, active, *refs):
    @pl.when(active[0] == 1)
    def run():
        input_backward_body(*refs[:6], *refs[6 + earlier :])


def input_backward_body(
    grad_cat, grad_middle, x, packed, dt_weight, input_gain,
    grad_start_out, start_low_out, input_grad_out,
    grad_start, start_low, input_grad,
    cat, grad_normed, sems, out_sems,
):
    copies = [
        pltpu.make_async_copy(packed.at[:, pl.ds(16 * j, 16), :], cat.at[j], sems.at[j])
        for j in range(4)
    ]
    start_all(copies)
    for copy in copies:
        copy.wait()

    def back(tile, carry):
        at = pl.ds(pl.multiple_of(tile * 256, 256), 256)
        total = dot_nt(grad_cat[:, T0:CAT], dt_weight[at, :])
        for j in range(4):
            block = flat(cat[j, pl.ds(tile * 16, 16)])
            total = total + dot_nt(grad_cat[:, 1024 * j : 1024 * j + 1024], block)
        grad_normed[:, at] = total
        return carry

    lax.fori_loop(0, 4, back, 0)
    state = x[...].astype(F32)
    grad_state, grad_gain = rms_backward(state, input_gain[...], grad_normed[...])
    input_grad[...] = grad_gain
    total = grad_middle[...] + grad_state
    grad_start[...] = total
    start_low[...] = total.astype(BF16)
    leaving = leave_all(
        ((grad_start, grad_start_out), (start_low, start_low_out), (input_grad, input_grad_out)),
        out_sems,
    )
    for copy in leaving:
        copy.wait()


VMEM = pl.BlockSpec(memory_space=pltpu.VMEM)
SMEM = pl.BlockSpec(memory_space=pltpu.SMEM)
ANY = pl.BlockSpec(memory_space=pl.ANY)
LIMIT = 60 * 1024 * 1024


def shape(rows, columns, dtype):
    return jax.ShapeDtypeStruct((rows, columns), dtype)


def scratch(*dims, dtype=BF16):
    return pltpu.VMEM(dims, dtype)


def mirrored(shapes):
    return [pltpu.VMEM(s.shape, s.dtype) for s in shapes]


def run_forward(start, mats, small, rope):
    packed, dt_weight, out_weight, heads_weight = mats
    shapes = (
        shape(ROWS, WIDTH, BF16),
        shape(ROWS, WIDTH, BF16),
        shape(ROWS, CAT, F32),
        shape(ROWS, INNER, F32),
        shape(ROWS, INNER, BF16),
        shape(ROWS, 512, BF16),
        shape(ROWS, WIDTH, F32),
        shape(ROWS, WIDTH, BF16),
        shape(ROWS, FEED, F32),
        shape(ROWS, FEED, F32),
        shape(ROWS, FEED, BF16),
    )
    return pl.pallas_call(
        forward_kernel,
        out_shape=shapes,
        in_specs=[VMEM, ANY, VMEM, ANY, ANY] + [VMEM] * 10,
        out_specs=(ANY,) * len(shapes),
        scratch_shapes=[
            *mirrored(shapes),
            scratch(4, 64, 16, 1024),
            scratch(4, 64, 16, 1024),
            scratch(64, 32, 1024),
            scratch(INNER, WIDTH),
            scratch(512, WIDTH),
            pltpu.SemaphoreType.DMA((11,)),
            pltpu.SemaphoreType.DMA((len(shapes),)),
        ],
        compiler_params=pltpu.CompilerParams(vmem_limit_bytes=LIMIT),
        cost_estimate=pl.CostEstimate(
            flops=2 * ROWS * 12_600_000, bytes_accessed=40_000_000, transcendentals=2_000_000
        ),
        name="forward",
    )(start, packed, dt_weight, out_weight, heads_weight, *small, *rope)


def run_feed_backward(active, grad_top, mats, gate, upper, middle, feed_gain, earlier=()):
    shapes = (
        shape(ROWS, FEED, BF16),
        shape(ROWS, FEED, BF16),
        shape(ROWS, WIDTH, F32),
        shape(1, WIDTH, F32),
    )
    return pl.pallas_call(
        functools.partial(feed_backward_kernel, len(earlier)),
        out_shape=shapes,
        in_specs=[SMEM, VMEM, ANY, ANY, ANY, ANY, VMEM] + [ANY] * len(earlier),
        out_specs=(ANY,) * len(shapes),
        scratch_shapes=[
            *mirrored(shapes),
            scratch(ROWS, FEED, dtype=F32),
            scratch(ROWS, FEED, dtype=F32),
            scratch(ROWS, WIDTH, dtype=F32),
            scratch(4, 64, 16, 1024),
            scratch(64, 32, 1024),
            scratch(ROWS, WIDTH, dtype=F32),
            pltpu.SemaphoreType.DMA((8,)),
            pltpu.SemaphoreType.DMA((4,)),
        ],
        input_output_aliases={7 + k: k for k in range(len(earlier))},
        compiler_params=pltpu.CompilerParams(vmem_limit_bytes=LIMIT),
        cost_estimate=pl.CostEstimate(
            flops=2 * ROWS * 6_300_000, bytes_accessed=22_000_000, transcendentals=1_000_000
        ),
        name="feed_backward",
    )(active, grad_top, mats[0], gate, upper, middle, feed_gain, *earlier)


def run_mix_backward(active, grad_middle, mats, proj, ssm, small, rope, pick, earlier=()):
    packed, dt_weight, out_weight, heads_weight = mats
    shapes = (
        shape(ROWS, WIDTH, BF16),
        shape(ROWS, CAT, BF16),
        shape(4, MIXED, F32),
        shape(1, MIXED, F32),
        shape(1, 128, F32),
        shape(1, 128, F32),
        shape(1, INNER, F32),
        shape(1, INNER, F32),
    )
    return pl.pallas_call(
        functools.partial(mix_backward_kernel, len(earlier)),
        out_shape=shapes,
        in_specs=[SMEM, VMEM] + [ANY] * 4 + [VMEM] * 9 + [ANY] * len(earlier),
        out_specs=(ANY,) * len(shapes),
        scratch_shapes=[
            *mirrored(shapes),
            scratch(ROWS, CAT, dtype=F32),
            scratch(ROWS, INNER, dtype=F32),
            scratch(INNER, WIDTH),
            scratch(512, WIDTH),
            scratch(ROWS, INNER, dtype=F32),
            scratch(ROWS, 512, dtype=F32),
            scratch(LEN, INNER, dtype=F32),
            scratch(LEN, INNER, dtype=F32),
            scratch(LEN, MIXED, dtype=F32),
            pltpu.SemaphoreType.DMA((4,)),
            pltpu.SemaphoreType.DMA((8,)),
        ],
        input_output_aliases={15 + k: k for k in range(len(earlier))},
        compiler_params=pltpu.CompilerParams(vmem_limit_bytes=LIMIT),
        cost_estimate=pl.CostEstimate(
            flops=2 * ROWS * 2_100_000, bytes_accessed=14_000_000, transcendentals=4_000_000
        ),
        name="mix_backward",
    )(
        active, grad_middle, out_weight, heads_weight, proj, ssm, *small[1:7], *rope, pick, *earlier
    )


def run_input_backward(active, grad_cat, grad_middle, start, mats, input_gain, earlier=()):
    shapes = (shape(ROWS, WIDTH, F32), shape(ROWS, WIDTH, BF16), shape(1, WIDTH, F32))
    return pl.pallas_call(
        functools.partial(input_backward_kernel, len(earlier)),
        out_shape=shapes,
        in_specs=[SMEM, VMEM, VMEM, VMEM, ANY, VMEM, VMEM] + [ANY] * len(earlier),
        out_specs=(ANY,) * len(shapes),
        scratch_shapes=[
            *mirrored(shapes),
            scratch(4, 64, 16, 1024),
            scratch(ROWS, WIDTH, dtype=F32),
            pltpu.SemaphoreType.DMA((4,)),
            pltpu.SemaphoreType.DMA((3,)),
        ],
        input_output_aliases={7 + k: k for k in range(len(earlier))},
        compiler_params=pltpu.CompilerParams(vmem_limit_bytes=LIMIT),
        cost_estimate=pl.CostEstimate(
            flops=2 * ROWS * 4_200_000, bytes_accessed=13_000_000, transcendentals=1000
        ),
        name="input_backward",
    )(active, grad_cat, grad_middle, start, *mats[:2], input_gain, *earlier)


def rope_tables():
    position = jnp.arange(LEN).astype(F32)
    inverse = 10000.0 ** (-(jnp.arange(32).astype(F32) * 2.0) / 64)
    angle = position[:, None] * inverse[None, :]
    cosine = jnp.tile(jnp.cos(angle), (1, 16))
    sine = jnp.sin(angle)
    return cosine, jnp.tile(jnp.concatenate([-sine, sine], axis=1), (1, 8))


def head_pick():
    lanes = lax.broadcasted_iota(jnp.int32, (INNER, 128), 0) // 64
    return (lanes == lax.broadcasted_iota(jnp.int32, (INNER, 128), 1)).astype(BF16)


def prepared_small(pieces):
    input_gain, kernel, bias, step_bias, decay_log, skip, mixer_gain, feed_gain = pieces

    def padded(v):
        return jnp.pad(v, (0, 128 - HEADS))[None]

    return (
        input_gain[None],
        kernel,
        bias[None],
        padded(step_bias),
        padded(decay_log),
        jnp.repeat(skip, 64)[None],
        mixer_gain[None],
        feed_gain[None],
    )


FIRST = (1, 0, 3, 2)
SECOND = (3, 2, 1, 0)


def partners(axis, turn):
    me = lax.axis_index(axis)
    near, far = me + 1 - 2 * lax.rem(me, 2), 3 - me
    flipped = lax.rem(lax.axis_index("section") + turn, 2) == 1
    found = (jnp.where(flipped, far, near), jnp.where(flipped, near, far))
    swaps = []
    for step in range(2):
        tables = [(FIRST, SECOND)[(core + turn + step) % 2] for core in range(2)]
        swaps.append([(4 * c + i, 4 * c + tables[c][i]) for c in range(2) for i in range(4)])
    return me, found, swaps


def exchange(array, axis, pairs):
    return lax.ppermute(array, ("section", axis), pairs)


def first_sent(part, axis, turn):
    me, (one, two), swaps = partners(axis, turn)
    return part([one, lax.rem(me + 2, 4)]).astype(BF16)


def first_got(sent, axis, turn):
    return exchange(sent, axis, partners(axis, turn)[2][0])


def exchanged(part, got, axis, turn):
    me, (one, two), (swap_one, swap_two) = partners(axis, turn)
    half = got.shape[0] // 2
    handed = part([two]) + got[half:].astype(F32)
    last = exchange(handed.astype(BF16), axis, swap_two)
    return part([me]) + got[:half].astype(F32) + last.astype(F32)


def product_of(left, right, place):
    blocks = left.reshape(4, 4, 4, left.shape[0] // 64, left.shape[1])

    def part(places):
        picked = [lax.dynamic_index_in_dim(blocks, p, place, keepdims=False) for p in places]
        return dot(jnp.concatenate(picked, axis=0).reshape(-1, left.shape[1]), right)

    return part


def quarters_of(array, dim):
    def part(places):
        picked = [lax.dynamic_index_in_dim(array, p, dim, keepdims=False) for p in places]
        return jnp.concatenate(picked, axis=0).reshape(-1, array.shape[-1]).astype(F32)

    return part


def summed_on(array, axis, dim, turn):
    part = quarters_of(array, dim)
    got = first_got(first_sent(part, axis, turn), axis, turn)
    return exchanged(part, got, axis, turn)


def second_summed(parts, order, depth):
    array = jnp.concatenate([p.astype(BF16) for p in parts], axis=1)
    width = array.shape[1]
    rest = [0, 1, 2]
    rest.remove(order[0])
    array = array.reshape(4, 4, depth, width)
    array = summed_on(array, DP[order[1]], rest.index(order[1]), 0).astype(BF16)
    return array.reshape(4, depth, width)


def column_blocks(matrix):
    return [matrix[:, at : at + 1024] for at in range(0, matrix.shape[1], 1024)]


def on_device(
    layer_input,
    out_grad,
    in_weight,
    query_weight,
    key_weight,
    value_weight,
    out_weight,
    heads_weight,
    gate_weight,
    up_weight,
    down_weight,
    *pieces,
):
    micro, part, width = layer_input.shape
    rows = micro * part
    cat = jnp.concatenate(
        [query_weight[0], key_weight[0], value_weight[0], in_weight[0, :, :3328]], axis=1
    )
    steps = jnp.pad(in_weight[0, :, 3328:].reshape(1, -1), ((0, 7), (0, 1024 - 16 * HEADS)))
    own = jnp.concatenate(
        [
            *column_blocks(cat),
            *column_blocks(gate_weight[0]),
            *column_blocks(up_weight[0]),
            down_weight[0],
            out_weight[0],
            heads_weight[0],
            steps,
        ],
        axis=0,
    )
    packed = lax.all_gather(own, DP, axis=0, tiled=False)
    dt_weight = packed[:, DT0, : 16 * HEADS].reshape(WIDTH, HEADS)
    mats = (
        packed,
        jnp.pad(dt_weight, ((0, 0), (0, 128 - HEADS))),
        packed[:, OUT0:HEADS0].reshape(INNER, WIDTH),
        packed[:, HEADS0:DT0].reshape(512, WIDTH),
    )
    small = prepared_small([piece[0] for piece in pieces])
    rope = rope_tables()
    pick = head_pick()
    first = lax.axis_index("section") == 0

    start_low = layer_input.reshape(rows, width)
    kept_low = run_forward(start_low, mats, small, rope)
    start_high = lax.ppermute(kept_low[0], "section", [(0, 1)])
    kept_high = run_forward(start_high, mats, small, rope)
    layer_outputs = jnp.where(first, kept_low[0], kept_high[0]).reshape(1, micro, part, width)

    on_high = jnp.where(first, 0, 1).astype(jnp.int32).reshape(1)
    on_low = 1 - on_high
    top_high = out_grad.reshape(rows, width)
    feed_high = run_feed_backward(
        on_high, top_high, mats, kept_high[8], kept_high[9], kept_high[6], small[7]
    )
    mix_high = run_mix_backward(
        on_high, feed_high[2], mats, kept_high[2], kept_high[3], small, rope, pick
    )
    input_high = run_input_backward(
        on_high, mix_high[1], feed_high[2], start_high, mats, small[0]
    )
    top_low = lax.ppermute(input_high[1], "section", [(1, 0)])

    def chosen(slot):
        return jnp.where(first, kept_low[slot], kept_high[slot])

    normed_t, ffin_t, hidden_t = (chosen(slot).T for slot in (1, 7, 10))
    joined_t = jnp.concatenate(
        [chosen(4).T.reshape(64, 24, rows), chosen(5).T.reshape(64, 8, rows)], axis=1
    ).reshape(2048, rows)

    feed = run_feed_backward(
        on_low, top_low, mats, kept_low[8], kept_low[9], kept_low[6], small[7], feed_high
    )
    grad_gate, grad_upper, grad_middle, feed_grad = feed
    grad_low = jnp.where(first, top_low, top_high)
    grad_low, grad_gate, grad_upper = lax.optimization_barrier((grad_low, grad_gate, grad_upper))
    orders = ((2, 0, 1), (0, 1, 2), (1, 2, 0))
    products = [
        product_of(left, right, order[0])
        for left, right, order in zip(
            (hidden_t, ffin_t, ffin_t), (grad_low, grad_gate, grad_upper), orders
        )
    ]
    sents = [first_sent(p, DP[order[0]], 0) for p, order in zip(products, orders)]
    grad_middle, *sents = lax.optimization_barrier((grad_middle, *sents))
    gots = [first_got(sent, DP[order[0]], 0) for sent, order in zip(sents, orders)]
    mix = run_mix_backward(
        on_low, grad_middle, mats, kept_low[2], kept_low[3], small, rope, pick, mix_high
    )
    grad_branch, grad_cat, *small_grads = mix
    grad_branch, grad_cat, *gots = lax.optimization_barrier((grad_branch, grad_cat, *gots))
    feed_parts = [
        exchanged(p, got, DP[order[0]], 0) for p, got, order in zip(products, gots, orders)
    ]
    products = [
        product_of(left, right, order[0])
        for left, right, order in zip(
            (joined_t, normed_t, normed_t),
            (grad_branch, grad_cat[:, :2048], grad_cat[:, 2048:]),
            orders,
        )
    ]
    sents = [first_sent(p, DP[order[0]], 1) for p, order in zip(products, orders)]
    grad_middle, *sents = lax.optimization_barrier((grad_middle, *sents))
    mix_parts = []
    for p, sent, order in zip(products, sents, orders):
        got = first_got(sent, DP[order[0]], 1)
        mix_parts.append(exchanged(p, got, DP[order[0]], 1))
    grad_start, unused, input_grad = run_input_backward(
        on_low, grad_cat, grad_middle, start_low, mats, small[0], input_high
    )
    small_grads = [input_grad, *small_grads]
    input_g, kernel_g, bias_g, step_g, decay_g, skip_g, mixer_g = small_grads
    small_grads = (
        input_g[0],
        kernel_g,
        bias_g[0],
        step_g[0, :HEADS],
        decay_g[0, :HEADS],
        skip_g.reshape(HEADS, 64).sum(axis=1),
        mixer_g[0],
        feed_grad[0],
    )
    vector = jnp.concatenate([piece.reshape(-1) for piece in small_grads])
    vector = jnp.pad(vector, (0, -vector.shape[0] % 1024)).reshape(-1, 128)
    total = jnp.sum(lax.all_gather(vector, DP, axis=0, tiled=False), axis=0).reshape(-1)
    seconds = [
        second_summed(pair, order, depth)
        for pair, order, depth in zip(zip(feed_parts, mix_parts), orders, (32, 16, 16))
    ]
    total, *seconds = lax.optimization_barrier((total, *seconds))
    rows_grad, gate_cat, up_cat = (
        summed_on(array, DP[order[2]], 0, 0) for array, order in zip(seconds, orders)
    )
    down_grad, joined_grad = rows_grad[:, :WIDTH], rows_grad[:, WIDTH:]
    gate_grad, up_grad = gate_cat[:, :FEED], up_cat[:, :FEED]
    cat_grad = jnp.concatenate([gate_cat[:, FEED:], up_cat[:, FEED:]], axis=1)

    summed, at = ([], 0)
    for piece in small_grads:
        summed.append(total[at : at + piece.size].reshape(1, *piece.shape))
        at += piece.size
    return (
        layer_outputs,
        grad_start.reshape(1, micro, part, width),
        cat_grad[None, :, Z0 : T0 + HEADS],
        cat_grad[None, :, :K0],
        cat_grad[None, :, K0:V0],
        cat_grad[None, :, V0:Z0],
        joined_grad[None, :24],
        joined_grad[None, 24:],
        gate_grad[None],
        up_grad[None],
        down_grad[None],
        *summed,
    )


def solution(mesh):
    torus = Mesh(
        mesh.devices.reshape(mesh.shape["section"], 4, 4, 4), ("section", "dp_0", "dp_1", "dp_2")
    )
    in_specs = (
        P(None, DP, None),
        P(None, DP, None),
        P("section", DP, None),
        P("section", DP, None),
        P("section", DP, None),
        P("section", DP, None),
        P("section", DP, None),
        P("section", DP, None),
        P("section", DP, None),
        P("section", DP, None),
        P("section", DP, None),
        P("section", None),
        P("section", None, None),
        P("section", None),
        P("section", None),
        P("section", None),
        P("section", None),
        P("section", None),
        P("section", None),
    )
    out_specs = (
        P("section", None, DP, None),
        P("section", None, DP, None),
        P("section", DP, None),
        P("section", DP, None),
        P("section", DP, None),
        P("section", DP, None),
        P("section", DP, None),
        P("section", DP, None),
        P("section", DP, None),
        P("section", DP, None),
        P("section", DP, None),
        P("section", None),
        P("section", None, None),
        P("section", None),
        P("section", None),
        P("section", None),
        P("section", None),
        P("section", None),
        P("section", None),
    )
    return jax.shard_map(
        on_device, mesh=torus, in_specs=in_specs, out_specs=out_specs, check_vma=False
    )
```

```python
import functools

import jax
import jax.numpy as jnp
from jax import lax
from jax.experimental import pallas as pl
from jax.experimental.pallas import tpu as pltpu
from jax.sharding import Mesh
from jax.sharding import PartitionSpec as P

LEN = 128
ROWS = 256
WIDTH = 1024
FEED = 2048
INNER = 1536
MIXED = 1792
CAT = 4224
HEADS = 24
DP = ("dp_0", "dp_1", "dp_2")
F32 = jnp.float32
BF16 = jnp.bfloat16
HIDE = -1e30
Q0, K0, V0, Z0, X0, T0 = 0, 512, 640, 768, 2304, 4096
OUT0, HEADS0, DT0, PACKED = 64, 88, 96, 104


def dot(left, right):
    return jnp.dot(left, right, preferred_element_type=F32)


def dot_nt(left, right):
    return lax.dot_general(left, right, (((1,), (1,)), ((), ())), preferred_element_type=F32)


def dot_tn(left, right):
    return lax.dot_general(left, right, (((0,), (0,)), ((), ())), preferred_element_type=F32)


def dot_full(left, right):
    return jnp.dot(left, right, precision=lax.Precision.HIGHEST, preferred_element_type=F32)


def iota(shape, dim):
    return lax.broadcasted_iota(jnp.int32, shape, dim)


def sigmoid(v):
    return 1.0 / (1.0 + jnp.exp(-v))


def softplus(v):
    return jnp.maximum(v, 0.0) + jnp.log(1.0 + jnp.exp(-jnp.abs(v)))


def swap_halves(v):
    width = v.shape[1]
    near = lax.rem(iota(v.shape, 1), 64) < 32
    return jnp.where(near, pltpu.roll(v, width - 32, 1), pltpu.roll(v, 32, 1))


def shifted_down(v, by):
    if by == 0:
        return v
    return jnp.where(iota(v.shape, 0) >= by, pltpu.roll(v, by, 0), 0.0)


def shifted_up(v, by):
    if by == 0:
        return v
    rows = v.shape[0]
    return jnp.where(iota(v.shape, 0) < rows - by, pltpu.roll(v, rows - by, 0), 0.0)


def rms(v):
    return lax.rsqrt(jnp.mean(v * v, axis=-1, keepdims=True) + 1e-05)


def rms_backward(v, gain, grad):
    scale = rms(v)
    gained = grad * gain
    inner = jnp.mean(gained * v, axis=-1, keepdims=True)
    grad_v = scale * gained - v * (scale * scale * scale * inner)
    return grad_v, jnp.sum(grad * v * scale, axis=0, keepdims=True)


def left_half():
    return iota((LEN, 128), 1) < 64


def both_halves(v, group, left):
    turned = pltpu.roll(v, 64, 1)
    return jnp.where(left, v, turned) if group == 0 else jnp.where(left, turned, v)


def stacked(pairs, left):
    parts = []
    for pair in pairs:
        parts.append(jnp.where(left, pair, 0.0))
        parts.append(jnp.where(left, 0.0, pair))
    return jnp.concatenate(parts, axis=0).astype(BF16)


def unstacked(rows, index, left):
    low = rows[2 * index * LEN : (2 * index + 1) * LEN]
    high = rows[(2 * index + 1) * LEN : (2 * index + 2) * LEN]
    return jnp.where(left, low, high)


def attention_parts(proj, rows, cosine, sine):
    left = left_half()
    query = proj[rows, Q0:K0]
    query = query * cosine[...] + swap_halves(query) * sine[...]
    key = proj[rows, K0:V0]
    key = key * cosine[:, :128] + swap_halves(key) * sine[:, :128]
    value = proj[rows, V0:Z0]
    groups = []
    for group in range(2):
        pairs = [query[:, 128 * p : 128 * p + 128] for p in (2 * group, 2 * group + 1)]
        queries = stacked(pairs, left)
        keys = both_halves(key, group, left).astype(BF16)
        values = both_halves(value, group, left).astype(BF16)
        scores = dot_nt(queries, keys) * 0.125
        time = lax.rem(iota(scores.shape, 0), LEN)
        scores = jnp.where(iota(scores.shape, 1) <= time, scores, HIDE)
        top = jnp.max(scores, axis=-1, keepdims=True)
        expo = jnp.exp(scores - top)
        probs = expo / jnp.sum(expo, axis=-1, keepdims=True)
        groups.append((queries, keys, values, probs))
    return left, groups


def attention_forward(proj, rows, cosine, sine, attended):
    left, groups = attention_parts(proj, rows, cosine, sine)
    for group, (queries, keys, values, probs) in enumerate(groups):
        mixed = dot(probs.astype(BF16), values)
        for index in range(2):
            at = 256 * group + 128 * index
            attended[rows, at : at + 128] = unstacked(mixed, index, left).astype(BF16)


def attention_backward(proj, rows, cosine, sine, grad_attended, grad_cat):
    left, groups = attention_parts(proj, rows, cosine, sine)
    key_parts, value_parts = [], []
    for group, (queries, keys, values, probs) in enumerate(groups):
        pairs = [grad_attended[:, 128 * p : 128 * p + 128] for p in (2 * group, 2 * group + 1)]
        grads = stacked(pairs, left)
        grad_values = dot_tn(probs.astype(BF16), grads)
        grad_probs = dot_nt(grads, values)
        inner = jnp.sum(probs * grad_probs, axis=-1, keepdims=True)
        grad_scores = (probs * (grad_probs - inner)).astype(BF16)
        grad_queries = dot(grad_scores, keys) * 0.125
        grad_keys = dot_tn(grad_scores, queries) * 0.125
        for index in range(2):
            at = 256 * group + 128 * index
            grad = unstacked(grad_queries, index, left)
            grad = grad * cosine[:, :128] - swap_halves(grad) * sine[:, :128]
            grad_cat[rows, at : at + 128] = grad.astype(BF16)
        key_parts.append(grad_keys + pltpu.roll(grad_keys, 64, 1))
        value_parts.append(grad_values + pltpu.roll(grad_values, 64, 1))
    grad = jnp.where(left, key_parts[0], key_parts[1])
    grad = grad * cosine[:, :128] - swap_halves(grad) * sine[:, :128]
    grad_cat[rows, K0:V0] = grad.astype(BF16)
    grad_cat[rows, V0:Z0] = jnp.where(left, value_parts[0], value_parts[1]).astype(BF16)


def mamba_parts(proj, rows, kernel, bias, step_bias, decay_log):
    mixed = proj[rows, X0:T0]
    total = bias[...] + mixed * kernel[3:4, :]
    for tap in range(3):
        total = total + shifted_down(mixed, 3 - tap) * kernel[tap : tap + 1, :]
    active = total * sigmoid(total)
    step = softplus(proj[rows, T0:CAT] + step_bias[...])
    rate = -step * jnp.exp(decay_log[...])
    earlier = (iota((LEN, LEN), 0) >= iota((LEN, LEN), 1)).astype(F32)
    cumul = dot_full(earlier, rate)
    state_in = active[:, INNER : INNER + 128].astype(BF16)
    state_out = active[:, INNER + 128 :].astype(BF16)
    return mixed, total, active, step, rate, cumul, state_in, state_out


def stepped(step, pair, left):
    return jnp.where(left, step[:, 2 * pair : 2 * pair + 1], step[:, 2 * pair + 1 : 2 * pair + 2])


def mamba_forward(proj, rows, kernel, bias, step_bias, decay_log, skip, gain, ssm, mamba):
    left = left_half()
    parts = mamba_parts(proj, rows, kernel, bias, step_bias, decay_log)
    mixed, total, active, step, rate, cumul, state_in, state_out = parts
    across = cumul.T
    hidden = jnp.where(iota((LEN, LEN), 0) >= iota((LEN, LEN), 1), 0.0, HIDE)
    meeting = dot_nt(state_out, state_in)
    for pair in range(HEADS // 2):
        at = 128 * pair
        inputs = active[:, at : at + 128]
        scaled = (inputs * stepped(step, pair, left)).astype(BF16)
        mixing = []
        for head in (2 * pair, 2 * pair + 1):
            spread = cumul[:, head : head + 1] - across[head : head + 1, :] + hidden
            mixing.append((meeting * jnp.exp(spread)).astype(BF16))
        both = dot(jnp.concatenate(mixing, axis=0), scaled)
        out = unstacked(both, 0, left) + skip[:, at : at + 128] * inputs
        ssm[rows, at : at + 128] = out
    z = proj[rows, Z0:X0]
    gated = ssm[rows, :] * (z * sigmoid(z))
    mamba[rows, :] = (gated * rms(gated) * gain[...]).astype(BF16)


def head_sums(v, pick):
    high = v.astype(BF16)
    low = (v - high.astype(F32)).astype(BF16)
    return dot(high, pick) + dot(low, pick)


def mamba_backward(
    proj, rows, kernel, bias, step_bias, decay_log, skip, gain, pick, ssm, grad_mamba, grad_cat,
    across_scratch, balance_scratch, touch_scratch, grad_active, add_small,
):
    left = left_half()
    parts = mamba_parts(proj, rows, kernel, bias, step_bias, decay_log)
    mixed, total, active, step, rate, cumul, state_in, state_out = parts
    across = cumul.T
    hidden = jnp.where(iota((LEN, LEN), 1) >= iota((LEN, LEN), 0), 0.0, HIDE)
    meeting = dot_nt(state_out, state_in).T
    z = proj[rows, Z0:X0]
    out = ssm[rows, :]
    gate = sigmoid(z)
    gated = out * (z * gate)
    grad_gated, grad_gain = rms_backward(gated, gain[...], grad_mamba)
    add_small(6, grad_gain)
    grad_cat[rows, Z0:X0] = (grad_gated * out * (gate * (1.0 + z * (1.0 - gate)))).astype(BF16)
    grad_out = grad_gated * (z * gate)
    add_small(5, jnp.sum(grad_out * active[:, :INNER], axis=0, keepdims=True))
    grad_meeting = jnp.zeros((LEN, LEN), F32)
    for pair in range(HEADS // 2):
        at = 128 * pair
        inputs = active[:, at : at + 128]
        steps = stepped(step, pair, left)
        scaled = (inputs * steps).astype(BF16)
        grad_pair = grad_out[:, at : at + 128]
        grad_low = grad_pair.astype(BF16)
        halves = jnp.concatenate(
            [jnp.where(left, scaled, jnp.zeros_like(scaled)), jnp.where(left, jnp.zeros_like(scaled), scaled)],
            axis=0,
        )
        grad_mixing = dot_nt(halves, grad_low)
        mixing = []
        for place, head in enumerate((2 * pair, 2 * pair + 1)):
            spread = across[head : head + 1, :] - cumul[:, head : head + 1] + hidden
            decay = jnp.exp(spread)
            mixing.append((meeting * decay).astype(BF16))
            grad_meeting = grad_meeting + grad_mixing[LEN * place : LEN * place + LEN] * decay
        both = dot(jnp.concatenate(mixing, axis=0), grad_low)
        grad_scaled = unstacked(both, 0, left)
        skips = skip[:, at : at + 128]
        grad_active[:, at : at + 128] = grad_scaled * steps + skips * grad_pair
        touch_scratch[:, at : at + 128] = grad_scaled * inputs
        balance_scratch[:, at : at + 128] = grad_low.astype(F32) * (
            out[:, at : at + 128] - skips * inputs
        ) - scaled.astype(F32) * grad_scaled
    grad_low = grad_meeting.astype(BF16)
    grad_active[:, INNER : INNER + 128] = dot(grad_low, state_out)
    grad_active[:, INNER + 128 :] = dot_tn(grad_low, state_in)
    later = (iota((LEN, LEN), 1) >= iota((LEN, LEN), 0)).astype(F32)
    grad_rate = dot_full(later, head_sums(balance_scratch[...], pick[...]))
    add_small(4, jnp.sum(grad_rate * rate, axis=0, keepdims=True))
    grad_step = head_sums(touch_scratch[...], pick[...]) - grad_rate * jnp.exp(decay_log[...])
    grad_dt = grad_step * sigmoid(proj[rows, T0:CAT] + step_bias[...])
    add_small(3, jnp.sum(grad_dt, axis=0, keepdims=True))
    grad_cat[rows, T0:CAT] = grad_dt.astype(BF16)
    slope = sigmoid(total)
    grad_total = grad_active[...] * (slope * (1.0 + total * (1.0 - slope)))
    add_small(2, jnp.sum(grad_total, axis=0, keepdims=True))
    grad_mixed = grad_total * kernel[3:4, :]
    taps = []
    for tap in range(4):
        taps.append(jnp.sum(grad_total * shifted_down(mixed, 3 - tap), axis=0, keepdims=True))
        if tap < 3:
            grad_mixed = grad_mixed + shifted_up(grad_total, 3 - tap) * kernel[tap : tap + 1, :]
    add_small(1, jnp.concatenate(taps, axis=0))
    grad_cat[rows, X0:T0] = grad_mixed.astype(BF16)


def flat(block):
    return block.reshape(block.shape[0] * block.shape[1], block.shape[2])


def start_all(copies):
    for copy in copies:
        copy.start()


def feed_copies(places, pieces, buffers, sems):
    copies = []
    for k, buffer in enumerate(buffers):
        own, got, far = pieces[3 * k : 3 * k + 3]
        for q, source in enumerate((own, got, far.at[0], far.at[1])):
            target = buffer.at[(slice(None),) * k + (places[4 * k + q],)]
            copies.append(pltpu.make_async_copy(source, target, sems.at[4 * k + q]))
    return copies


def rows_of(block):
    return block.reshape(-1, block.shape[-1])


def forward_kernel(
    x, packed, dt_weight, out_weight, heads_weight,
    places, gate_own, gate_got, gate_far, up_own, up_got, up_far, down_own, down_got, down_far,
    input_gain, kernel, bias, step_bias, decay_log, skip,
    mixer_gain, feed_gain, cosine, sine,
    result_out, normed_out, proj_out, ssm_out, mamba_out, attended_out, middle_out, ffin_out, gate_out,
    upper_out, hidden_out,
    result, normed, proj, ssm, mamba, attended, middle, ffin, gate, upper, hidden,
    cat, gate_mat, up_mat, down_mat, out_mat, heads_mat, sems, out_sems, feed_sems,
):
    leaving = []

    def leave(*pairs):
        for source, target in pairs:
            copy = pltpu.make_async_copy(source, target, out_sems.at[len(leaving)])
            copy.start()
            leaving.append(copy)

    copies = [
        pltpu.make_async_copy(packed.at[:, pl.ds(16 * j, 16), :], cat.at[j], sems.at[j])
        for j in range(4)
    ]
    copies.append(pltpu.make_async_copy(out_weight, out_mat, sems.at[4]))
    copies.append(pltpu.make_async_copy(heads_weight, heads_mat, sems.at[5]))
    pieces = (gate_own, gate_got, gate_far, up_own, up_got, up_far, down_own, down_got, down_far)
    feeds = feed_copies(places, pieces, (gate_mat, up_mat, down_mat), feed_sems)
    start_all(copies + feeds)
    state = x[...].astype(F32)
    normed[...] = (state * rms(state) * input_gain[...]).astype(BF16)
    proj[:, T0:CAT] = dot(normed[...], dt_weight[...])
    for j in range(4):
        copies[j].wait()

        def columns(tile, carry, j=j):
            at = pl.multiple_of(tile * 256, 256)
            block = flat(cat[j, :, :, pl.ds(at, 256)])
            proj[:, pl.ds(pl.multiple_of(j * 1024 + at, 256), 256)] = dot(normed[...], block)
            return carry

        lax.fori_loop(0, 4, columns, 0)
    leave((normed, normed_out), (proj, proj_out))

    def sequence(index, carry):
        rows = pl.ds(pl.multiple_of(index * LEN, LEN), LEN)
        attention_forward(proj, rows, cosine, sine, attended)
        mamba_forward(proj, rows, kernel, bias, step_bias, decay_log, skip, mixer_gain, ssm, mamba)
        return carry

    lax.fori_loop(0, 2, sequence, 0)
    leave((ssm, ssm_out), (mamba, mamba_out), (attended, attended_out))
    copies[4].wait()
    copies[5].wait()

    def joined(tile, carry):
        at = pl.ds(pl.multiple_of(tile * 256, 256), 256)
        part = dot(mamba[...], out_mat[:, at]) + dot(attended[...], heads_mat[:, at])
        middle[:, at] = x[:, at].astype(F32) + part
        return carry

    lax.fori_loop(0, 4, joined, 0)
    value = middle[...]
    ffin[...] = (value * rms(value) * feed_gain[...]).astype(BF16)
    leave((middle, middle_out), (ffin, ffin_out))
    for copy in feeds[:8]:
        copy.wait()

    def feed(tile, carry):
        at = pl.ds(pl.multiple_of(tile * 256, 256), 256)
        low = dot(ffin[...], rows_of(gate_mat[:, :, :, :, at]))
        high = dot(ffin[...], rows_of(up_mat[:, :, :, :, at]))
        gate[:, at] = low
        upper[:, at] = high
        hidden[:, at] = (low * sigmoid(low) * high).astype(BF16)
        return carry

    lax.fori_loop(0, 8, feed, 0)
    leave((gate, gate_out), (upper, upper_out), (hidden, hidden_out))
    for copy in feeds[8:]:
        copy.wait()

    def last(tile, carry):
        at = pl.ds(pl.multiple_of(tile * 256, 256), 256)
        part = dot(hidden[...], rows_of(down_mat[:, :, :, :, at]))
        result[:, at] = (middle[:, at] + part).astype(BF16)
        return carry

    lax.fori_loop(0, 4, last, 0)
    leave((result, result_out))
    for copy in leaving:
        copy.wait()


def leave_all(pairs, sems):
    copies = [
        pltpu.make_async_copy(source, target, sems.at[k]) for k, (source, target) in enumerate(pairs)
    ]
    start_all(copies)
    return copies


def feed_backward_kernel(earlier, active, *refs):
    @pl.when(active[0] == 1)
    def run():
        feed_backward_body(*refs[:15], *refs[15 + earlier :])


def feed_backward_body(
    grad_top, places, gate_own, gate_got, gate_far, up_own, up_got, up_far, down_own, down_got, down_far,
    gate_in, upper_in, middle_in, feed_gain,
    grad_gate_out, grad_upper_out, grad_middle_out, feed_grad_out,
    grad_gate, grad_upper, grad_middle, feed_grad,
    gate, upper, middle, gate_mat, up_mat, down_mat, grad_ffin, sems, out_sems, feed_sems,
):
    inputs = [
        pltpu.make_async_copy(gate_in, gate, sems.at[0]),
        pltpu.make_async_copy(upper_in, upper, sems.at[1]),
        pltpu.make_async_copy(middle_in, middle, sems.at[2]),
    ]
    pieces = (gate_own, gate_got, gate_far, up_own, up_got, up_far, down_own, down_got, down_far)
    feeds = feed_copies(places, pieces, (gate_mat, up_mat, down_mat), feed_sems)
    start_all(feeds[8:] + inputs + feeds[:8])
    for copy in feeds[8:] + inputs:
        copy.wait()

    def through(tile, carry):
        at = pl.ds(pl.multiple_of(tile * 256, 256), 256)
        block = down_mat[tile // 2, pl.ds(lax.rem(tile, 2) * 2, 2)]
        grad_hidden = dot_nt(grad_top[...], rows_of(block))
        low, high = gate[:, at], upper[:, at]
        slope = sigmoid(low)
        grad_upper[:, at] = (grad_hidden * (low * slope)).astype(BF16)
        part = grad_hidden * high * (slope * (1.0 + low * (1.0 - slope)))
        grad_gate[:, at] = part.astype(BF16)
        return carry

    lax.fori_loop(0, 8, through, 0)
    leaving = leave_all(((grad_gate, grad_gate_out), (grad_upper, grad_upper_out)), out_sems)
    for copy in feeds[:8]:
        copy.wait()

    def back(tile, carry):
        at = pl.ds(pl.multiple_of(tile * 256, 256), 256)
        total = dot_nt(grad_gate[...], rows_of(gate_mat[tile]))
        grad_ffin[:, at] = total + dot_nt(grad_upper[...], rows_of(up_mat[tile]))
        return carry

    lax.fori_loop(0, 4, back, 0)
    grad_part, grad_gain = rms_backward(middle[...], feed_gain[...], grad_ffin[...])
    feed_grad[...] = grad_gain
    grad_middle[...] = grad_top[...].astype(F32) + grad_part
    leaving += leave_all(
        ((grad_middle, grad_middle_out), (feed_grad, feed_grad_out)), out_sems.at[pl.ds(2, 2)]
    )
    for copy in leaving:
        copy.wait()


def mix_backward_kernel(earlier, active, *refs):
    @pl.when(active[0] == 1)
    def run():
        mix_backward_body(*refs[:14], *refs[14 + earlier :])


def mix_backward_body(
    grad_middle, out_weight, heads_weight, proj_in, ssm_in, kernel, bias,
    step_bias, decay_log, skip, mixer_gain, cosine, sine, pick,
    grad_branch_out, grad_cat_out, kernel_grad_out, bias_grad_out,
    step_grad_out, decay_grad_out, skip_grad_out, mixer_grad_out,
    grad_branch, grad_cat, kernel_grad, bias_grad, step_grad, decay_grad,
    skip_grad, mixer_grad,
    proj, ssm,
    out_mat, heads_mat, grad_mamba, grad_attended, balance, touch, grad_active, sems,
    out_sems,
):
    copies = [
        pltpu.make_async_copy(out_weight, out_mat, sems.at[0]),
        pltpu.make_async_copy(heads_weight, heads_mat, sems.at[1]),
        pltpu.make_async_copy(proj_in, proj, sems.at[2]),
        pltpu.make_async_copy(ssm_in, ssm, sems.at[3]),
    ]
    start_all(copies)
    grad_branch[...] = grad_middle[...].astype(BF16)
    copies[0].wait()
    copies[1].wait()

    def through(tile, carry):
        at = pl.ds(pl.multiple_of(tile * 256, 256), 256)
        grad_mamba[:, at] = dot_nt(grad_branch[...], out_mat[at, :])
        return carry

    lax.fori_loop(0, 6, through, 0)

    def through_heads(tile, carry):
        at = pl.ds(pl.multiple_of(tile * 256, 256), 256)
        grad_attended[:, at] = dot_nt(grad_branch[...], heads_mat[at, :])
        return carry

    lax.fori_loop(0, 2, through_heads, 0)
    small = {
        1: kernel_grad,
        2: bias_grad,
        3: step_grad,
        4: decay_grad,
        5: skip_grad,
        6: mixer_grad,
    }
    for ref in small.values():
        ref[...] = jnp.zeros_like(ref)

    def add_small(slot, value):
        small[slot][...] += value

    copies[2].wait()
    copies[3].wait()

    def sequence(index, carry):
        rows = pl.ds(pl.multiple_of(index * LEN, LEN), LEN)
        grads = grad_attended[rows, :]
        attention_backward(proj, rows, cosine, sine, grads, grad_cat)
        mamba_backward(
            proj, rows, kernel, bias, step_bias, decay_log, skip, mixer_gain, pick, ssm,
            grad_mamba[rows, :], grad_cat, None, balance, touch, grad_active, add_small,
        )
        return carry

    lax.fori_loop(0, 2, sequence, 0)
    leaving = leave_all(
        (
            (grad_branch, grad_branch_out),
            (grad_cat, grad_cat_out),
            (kernel_grad, kernel_grad_out),
            (bias_grad, bias_grad_out),
            (step_grad, step_grad_out),
            (decay_grad, decay_grad_out),
            (skip_grad, skip_grad_out),
            (mixer_grad, mixer_grad_out),
        ),
        out_sems,
    )
    for copy in leaving:
        copy.wait()


def input_backward_kernel(earlier, active, *refs):
    @pl.when(active[0] == 1)
    def run():
        input_backward_body(*refs[:6], *refs[6 + earlier :])


def input_backward_body(
    grad_cat, grad_middle, x, packed, dt_weight, input_gain,
    grad_start_out, start_low_out, input_grad_out,
    grad_start, start_low, input_grad,
    cat, grad_normed, sems, out_sems,
):
    copies = [
        pltpu.make_async_copy(packed.at[:, pl.ds(16 * j, 16), :], cat.at[j], sems.at[j])
        for j in range(4)
    ]
    start_all(copies)
    for copy in copies:
        copy.wait()

    def back(tile, carry):
        at = pl.ds(pl.multiple_of(tile * 256, 256), 256)
        total = dot_nt(grad_cat[:, T0:CAT], dt_weight[at, :])
        for j in range(4):
            block = flat(cat[j, pl.ds(tile * 16, 16)])
            total = total + dot_nt(grad_cat[:, 1024 * j : 1024 * j + 1024], block)
        grad_normed[:, at] = total
        return carry

    lax.fori_loop(0, 4, back, 0)
    state = x[...].astype(F32)
    grad_state, grad_gain = rms_backward(state, input_gain[...], grad_normed[...])
    input_grad[...] = grad_gain
    total = grad_middle[...] + grad_state
    grad_start[...] = total
    start_low[...] = total.astype(BF16)
    leaving = leave_all(
        ((grad_start, grad_start_out), (start_low, start_low_out), (input_grad, input_grad_out)),
        out_sems,
    )
    for copy in leaving:
        copy.wait()


VMEM = pl.BlockSpec(memory_space=pltpu.VMEM)
SMEM = pl.BlockSpec(memory_space=pltpu.SMEM)
ANY = pl.BlockSpec(memory_space=pl.ANY)
LIMIT = 60 * 1024 * 1024


def shape(rows, columns, dtype):
    return jax.ShapeDtypeStruct((rows, columns), dtype)


def scratch(*dims, dtype=BF16):
    return pltpu.VMEM(dims, dtype)


FEED_MATS = (
    scratch(4, 4, 4, 16, FEED),
    scratch(4, 4, 4, 16, FEED),
    scratch(4, 4, 4, 32, WIDTH),
)


def mirrored(shapes):
    return [pltpu.VMEM(s.shape, s.dtype) for s in shapes]


def run_forward(start, mats, small, rope):
    packed, dt_weight, out_weight, heads_weight, feeds = mats
    shapes = (
        shape(ROWS, WIDTH, BF16),
        shape(ROWS, WIDTH, BF16),
        shape(ROWS, CAT, F32),
        shape(ROWS, INNER, F32),
        shape(ROWS, INNER, BF16),
        shape(ROWS, 512, BF16),
        shape(ROWS, WIDTH, F32),
        shape(ROWS, WIDTH, BF16),
        shape(ROWS, FEED, F32),
        shape(ROWS, FEED, F32),
        shape(ROWS, FEED, BF16),
    )
    return pl.pallas_call(
        forward_kernel,
        out_shape=shapes,
        in_specs=[VMEM, ANY, VMEM, ANY, ANY, SMEM] + [ANY] * 9 + [VMEM] * 10,
        out_specs=(ANY,) * len(shapes),
        scratch_shapes=[
            *mirrored(shapes),
            scratch(4, 64, 16, 1024),
            *FEED_MATS,
            scratch(INNER, WIDTH),
            scratch(512, WIDTH),
            pltpu.SemaphoreType.DMA((6,)),
            pltpu.SemaphoreType.DMA((len(shapes),)),
            pltpu.SemaphoreType.DMA((12,)),
        ],
        compiler_params=pltpu.CompilerParams(vmem_limit_bytes=LIMIT),
        cost_estimate=pl.CostEstimate(
            flops=2 * ROWS * 12_600_000, bytes_accessed=40_000_000, transcendentals=2_000_000
        ),
        name="forward",
    )(start, packed, dt_weight, out_weight, heads_weight, *feeds, *small, *rope)


def run_feed_backward(active, grad_top, mats, gate, upper, middle, feed_gain, earlier=()):
    shapes = (
        shape(ROWS, FEED, BF16),
        shape(ROWS, FEED, BF16),
        shape(ROWS, WIDTH, F32),
        shape(1, WIDTH, F32),
    )
    return pl.pallas_call(
        functools.partial(feed_backward_kernel, len(earlier)),
        out_shape=shapes,
        in_specs=[SMEM, VMEM, SMEM] + [ANY] * 12 + [VMEM] + [ANY] * len(earlier),
        out_specs=(ANY,) * len(shapes),
        scratch_shapes=[
            *mirrored(shapes),
            scratch(ROWS, FEED, dtype=F32),
            scratch(ROWS, FEED, dtype=F32),
            scratch(ROWS, WIDTH, dtype=F32),
            *FEED_MATS,
            scratch(ROWS, WIDTH, dtype=F32),
            pltpu.SemaphoreType.DMA((3,)),
            pltpu.SemaphoreType.DMA((4,)),
            pltpu.SemaphoreType.DMA((12,)),
        ],
        input_output_aliases={16 + k: k for k in range(len(earlier))},
        compiler_params=pltpu.CompilerParams(vmem_limit_bytes=LIMIT),
        cost_estimate=pl.CostEstimate(
            flops=2 * ROWS * 6_300_000, bytes_accessed=22_000_000, transcendentals=1_000_000
        ),
        name="feed_backward",
    )(active, grad_top, *mats[4], gate, upper, middle, feed_gain, *earlier)


def run_mix_backward(active, grad_middle, mats, proj, ssm, small, rope, pick, earlier=()):
    packed, dt_weight, out_weight, heads_weight, feeds = mats
    shapes = (
        shape(ROWS, WIDTH, BF16),
        shape(ROWS, CAT, BF16),
        shape(4, MIXED, F32),
        shape(1, MIXED, F32),
        shape(1, 128, F32),
        shape(1, 128, F32),
        shape(1, INNER, F32),
        shape(1, INNER, F32),
    )
    return pl.pallas_call(
        functools.partial(mix_backward_kernel, len(earlier)),
        out_shape=shapes,
        in_specs=[SMEM, VMEM] + [ANY] * 4 + [VMEM] * 9 + [ANY] * len(earlier),
        out_specs=(ANY,) * len(shapes),
        scratch_shapes=[
            *mirrored(shapes),
            scratch(ROWS, CAT, dtype=F32),
            scratch(ROWS, INNER, dtype=F32),
            scratch(INNER, WIDTH),
            scratch(512, WIDTH),
            scratch(ROWS, INNER, dtype=F32),
            scratch(ROWS, 512, dtype=F32),
            scratch(LEN, INNER, dtype=F32),
            scratch(LEN, INNER, dtype=F32),
            scratch(LEN, MIXED, dtype=F32),
            pltpu.SemaphoreType.DMA((4,)),
            pltpu.SemaphoreType.DMA((8,)),
        ],
        input_output_aliases={15 + k: k for k in range(len(earlier))},
        compiler_params=pltpu.CompilerParams(vmem_limit_bytes=LIMIT),
        cost_estimate=pl.CostEstimate(
            flops=2 * ROWS * 2_100_000, bytes_accessed=14_000_000, transcendentals=4_000_000
        ),
        name="mix_backward",
    )(
        active, grad_middle, out_weight, heads_weight, proj, ssm, *small[1:7], *rope, pick, *earlier
    )


def run_input_backward(active, grad_cat, grad_middle, start, mats, input_gain, earlier=()):
    shapes = (shape(ROWS, WIDTH, F32), shape(ROWS, WIDTH, BF16), shape(1, WIDTH, F32))
    return pl.pallas_call(
        functools.partial(input_backward_kernel, len(earlier)),
        out_shape=shapes,
        in_specs=[SMEM, VMEM, VMEM, VMEM, ANY, VMEM, VMEM] + [ANY] * len(earlier),
        out_specs=(ANY,) * len(shapes),
        scratch_shapes=[
            *mirrored(shapes),
            scratch(4, 64, 16, 1024),
            scratch(ROWS, WIDTH, dtype=F32),
            pltpu.SemaphoreType.DMA((4,)),
            pltpu.SemaphoreType.DMA((3,)),
        ],
        input_output_aliases={7 + k: k for k in range(len(earlier))},
        compiler_params=pltpu.CompilerParams(vmem_limit_bytes=LIMIT),
        cost_estimate=pl.CostEstimate(
            flops=2 * ROWS * 4_200_000, bytes_accessed=13_000_000, transcendentals=1000
        ),
        name="input_backward",
    )(active, grad_cat, grad_middle, start, *mats[:2], input_gain, *earlier)


def rope_tables():
    position = jnp.arange(LEN).astype(F32)
    inverse = 10000.0 ** (-(jnp.arange(32).astype(F32) * 2.0) / 64)
    angle = position[:, None] * inverse[None, :]
    cosine = jnp.tile(jnp.cos(angle), (1, 16))
    sine = jnp.sin(angle)
    return cosine, jnp.tile(jnp.concatenate([-sine, sine], axis=1), (1, 8))


def head_pick():
    lanes = lax.broadcasted_iota(jnp.int32, (INNER, 128), 0) // 64
    return (lanes == lax.broadcasted_iota(jnp.int32, (INNER, 128), 1)).astype(BF16)


def prepared_small(pieces):
    input_gain, kernel, bias, step_bias, decay_log, skip, mixer_gain, feed_gain = pieces

    def padded(v):
        return jnp.pad(v, (0, 128 - HEADS))[None]

    return (
        input_gain[None],
        kernel,
        bias[None],
        padded(step_bias),
        padded(decay_log),
        jnp.repeat(skip, 64)[None],
        mixer_gain[None],
        feed_gain[None],
    )


FIRST = (1, 0, 3, 2)
SECOND = (3, 2, 1, 0)


def partners(axis, turn):
    me = lax.axis_index(axis)
    near, far = me + 1 - 2 * lax.rem(me, 2), 3 - me
    flipped = lax.rem(lax.axis_index("section") + turn, 2) == 1
    found = (jnp.where(flipped, far, near), jnp.where(flipped, near, far))
    swaps = []
    for step in range(2):
        tables = [(FIRST, SECOND)[(core + turn + step) % 2] for core in range(2)]
        swaps.append([(4 * c + i, 4 * c + tables[c][i]) for c in range(2) for i in range(4)])
    return me, found, swaps


def exchange(array, axis, pairs):
    return lax.ppermute(array, ("section", axis), pairs)


def first_sent(part, axis, turn):
    me, (one, two), swaps = partners(axis, turn)
    return part([one, lax.rem(me + 2, 4)]).astype(BF16)


def first_got(sent, axis, turn):
    return exchange(sent, axis, partners(axis, turn)[2][0])


def exchanged(part, got, axis, turn):
    me, (one, two), (swap_one, swap_two) = partners(axis, turn)
    half = got.shape[0] // 2
    handed = part([two]) + got[half:].astype(F32)
    last = exchange(handed.astype(BF16), axis, swap_two)
    return part([me]) + got[:half].astype(F32) + last.astype(F32)


def product_of(left, right, place):
    blocks = left.reshape(4, 4, 4, left.shape[0] // 64, left.shape[1])

    def part(places):
        picked = [lax.dynamic_index_in_dim(blocks, p, place, keepdims=False) for p in places]
        return dot(jnp.concatenate(picked, axis=0).reshape(-1, left.shape[1]), right)

    return part


def quarters_of(array, dim):
    def part(places):
        picked = [lax.dynamic_index_in_dim(array, p, dim, keepdims=False) for p in places]
        return jnp.concatenate(picked, axis=0).reshape(-1, array.shape[-1]).astype(F32)

    return part


def summed_on(array, axis, dim, turn):
    part = quarters_of(array, dim)
    got = first_got(first_sent(part, axis, turn), axis, turn)
    return exchanged(part, got, axis, turn)


def second_summed(parts, order, depth):
    array = jnp.concatenate([p.astype(BF16) for p in parts], axis=1)
    width = array.shape[1]
    rest = [0, 1, 2]
    rest.remove(order[0])
    array = array.reshape(4, 4, depth, width)
    array = summed_on(array, DP[order[1]], rest.index(order[1]), 0).astype(BF16)
    return array.reshape(4, depth, width)


def gathered_on(array, axis):
    me, (one, two), (swap_one, swap_two) = partners(axis, 0)
    got = exchange(array, axis, swap_one)
    far = exchange(jnp.stack([array, got]), axis, swap_two)
    return (array, got, far), (me, one, two, lax.rem(me + 2, 4))


def placed(blocks, places, dim):
    own, got, far = blocks
    whole = jnp.zeros((*own.shape[:dim], 4, *own.shape[dim:]), own.dtype)
    for block, place in zip((own, got, far[0], far[1]), places):
        whole = lax.dynamic_update_index_in_dim(whole, block, place, dim)
    return whole


def gathered(block, order):
    block = placed(*gathered_on(block, DP[order[2]]), 0)
    block = placed(*gathered_on(block, DP[order[1]]), 0 if order[1] < order[2] else 1)
    return gathered_on(block, DP[order[0]])


def column_blocks(matrix):
    return [matrix[:, at : at + 1024] for at in range(0, matrix.shape[1], 1024)]


def on_device(
    layer_input,
    out_grad,
    in_weight,
    query_weight,
    key_weight,
    value_weight,
    out_weight,
    heads_weight,
    gate_weight,
    up_weight,
    down_weight,
    *pieces,
):
    micro, part, width = layer_input.shape
    rows = micro * part
    cat = jnp.concatenate(
        [query_weight[0], key_weight[0], value_weight[0], in_weight[0, :, :3328]], axis=1
    )
    steps = jnp.pad(in_weight[0, :, 3328:].reshape(1, -1), ((0, 7), (0, 1024 - 16 * HEADS)))
    own = jnp.concatenate(
        [
            *column_blocks(cat),
            out_weight[0],
            heads_weight[0],
            steps,
        ],
        axis=0,
    )
    packed = lax.all_gather(own, DP, axis=0, tiled=False)
    dt_weight = packed[:, DT0, : 16 * HEADS].reshape(WIDTH, HEADS)
    feeds = [
        gathered(weight[0], order)
        for weight, order in (
            (gate_weight, (0, 1, 2)),
            (up_weight, (1, 2, 0)),
            (down_weight, (2, 0, 1)),
        )
    ]
    places = jnp.stack([place for blocks, found in feeds for place in found]).astype(jnp.int32)
    mats = (
        packed,
        jnp.pad(dt_weight, ((0, 0), (0, 128 - HEADS))),
        packed[:, OUT0:HEADS0].reshape(INNER, WIDTH),
        packed[:, HEADS0:DT0].reshape(512, WIDTH),
        (places, *(piece for blocks, found in feeds for piece in blocks)),
    )
    small = prepared_small([piece[0] for piece in pieces])
    rope = rope_tables()
    pick = head_pick()
    first = lax.axis_index("section") == 0

    start_low = layer_input.reshape(rows, width)
    kept_low = run_forward(start_low, mats, small, rope)
    start_high = lax.ppermute(kept_low[0], "section", [(0, 1)])
    kept_high = run_forward(start_high, mats, small, rope)
    layer_outputs = jnp.where(first, kept_low[0], kept_high[0]).reshape(1, micro, part, width)

    on_high = jnp.where(first, 0, 1).astype(jnp.int32).reshape(1)
    on_low = 1 - on_high
    top_high = out_grad.reshape(rows, width)
    feed_high = run_feed_backward(
        on_high, top_high, mats, kept_high[8], kept_high[9], kept_high[6], small[7]
    )
    mix_high = run_mix_backward(
        on_high, feed_high[2], mats, kept_high[2], kept_high[3], small, rope, pick
    )
    input_high = run_input_backward(
        on_high, mix_high[1], feed_high[2], start_high, mats, small[0]
    )
    top_low = lax.ppermute(input_high[1], "section", [(1, 0)])

    def chosen(slot):
        return jnp.where(first, kept_low[slot], kept_high[slot])

    normed_t, ffin_t, hidden_t = (chosen(slot).T for slot in (1, 7, 10))
    joined_t = jnp.concatenate(
        [chosen(4).T.reshape(64, 24, rows), chosen(5).T.reshape(64, 8, rows)], axis=1
    ).reshape(2048, rows)

    feed = run_feed_backward(
        on_low, top_low, mats, kept_low[8], kept_low[9], kept_low[6], small[7], feed_high
    )
    grad_gate, grad_upper, grad_middle, feed_grad = feed
    grad_low = jnp.where(first, top_low, top_high)
    grad_low, grad_gate, grad_upper = lax.optimization_barrier((grad_low, grad_gate, grad_upper))
    orders = ((2, 0, 1), (0, 1, 2), (1, 2, 0))
    products = [
        product_of(left, right, order[0])
        for left, right, order in zip(
            (hidden_t, ffin_t, ffin_t), (grad_low, grad_gate, grad_upper), orders
        )
    ]
    sents = [first_sent(p, DP[order[0]], 0) for p, order in zip(products, orders)]
    grad_middle, *sents = lax.optimization_barrier((grad_middle, *sents))
    gots = [first_got(sent, DP[order[0]], 0) for sent, order in zip(sents, orders)]
    mix = run_mix_backward(
        on_low, grad_middle, mats, kept_low[2], kept_low[3], small, rope, pick, mix_high
    )
    grad_branch, grad_cat, *small_grads = mix
    grad_branch, grad_cat, *gots = lax.optimization_barrier((grad_branch, grad_cat, *gots))
    feed_parts = [
        exchanged(p, got, DP[order[0]], 0) for p, got, order in zip(products, gots, orders)
    ]
    products = [
        product_of(left, right, order[0])
        for left, right, order in zip(
            (joined_t, normed_t, normed_t),
            (grad_branch, grad_cat[:, :2048], grad_cat[:, 2048:]),
            orders,
        )
    ]
    sents = [first_sent(p, DP[order[0]], 1) for p, order in zip(products, orders)]
    grad_middle, *sents = lax.optimization_barrier((grad_middle, *sents))
    mix_parts = []
    for p, sent, order in zip(products, sents, orders):
        got = first_got(sent, DP[order[0]], 1)
        mix_parts.append(exchanged(p, got, DP[order[0]], 1))
    grad_start, unused, input_grad = run_input_backward(
        on_low, grad_cat, grad_middle, start_low, mats, small[0], input_high
    )
    small_grads = [input_grad, *small_grads]
    input_g, kernel_g, bias_g, step_g, decay_g, skip_g, mixer_g = small_grads
    small_grads = (
        input_g[0],
        kernel_g,
        bias_g[0],
        step_g[0, :HEADS],
        decay_g[0, :HEADS],
        skip_g.reshape(HEADS, 64).sum(axis=1),
        mixer_g[0],
        feed_grad[0],
    )
    vector = jnp.concatenate([piece.reshape(-1) for piece in small_grads])
    vector = jnp.pad(vector, (0, -vector.shape[0] % 1024)).reshape(-1, 128)
    total = jnp.sum(lax.all_gather(vector, DP, axis=0, tiled=False), axis=0).reshape(-1)
    seconds = [
        second_summed(pair, order, depth)
        for pair, order, depth in zip(zip(feed_parts, mix_parts), orders, (32, 16, 16))
    ]
    total, *seconds = lax.optimization_barrier((total, *seconds))
    rows_grad, gate_cat, up_cat = (
        summed_on(array, DP[order[2]], 0, 0) for array, order in zip(seconds, orders)
    )
    down_grad, joined_grad = rows_grad[:, :WIDTH], rows_grad[:, WIDTH:]
    gate_grad, up_grad = gate_cat[:, :FEED], up_cat[:, :FEED]
    cat_grad = jnp.concatenate([gate_cat[:, FEED:], up_cat[:, FEED:]], axis=1)

    summed, at = ([], 0)
    for piece in small_grads:
        summed.append(total[at : at + piece.size].reshape(1, *piece.shape))
        at += piece.size
    return (
        layer_outputs,
        grad_start.reshape(1, micro, part, width),
        cat_grad[None, :, Z0 : T0 + HEADS],
        cat_grad[None, :, :K0],
        cat_grad[None, :, K0:V0],
        cat_grad[None, :, V0:Z0],
        joined_grad[None, :24],
        joined_grad[None, 24:],
        gate_grad[None],
        up_grad[None],
        down_grad[None],
        *summed,
    )


def solution(mesh):
    torus = Mesh(
        mesh.devices.reshape(mesh.shape["section"], 4, 4, 4), ("section", "dp_0", "dp_1", "dp_2")
    )
    in_specs = (
        P(None, DP, None),
        P(None, DP, None),
        P("section", DP, None),
        P("section", DP, None),
        P("section", DP, None),
        P("section", DP, None),
        P("section", DP, None),
        P("section", DP, None),
        P("section", DP, None),
        P("section", DP, None),
        P("section", DP, None),
        P("section", None),
        P("section", None, None),
        P("section", None),
        P("section", None),
        P("section", None),
        P("section", None),
        P("section", None),
        P("section", None),
    )
    out_specs = (
        P("section", None, DP, None),
        P("section", None, DP, None),
        P("section", DP, None),
        P("section", DP, None),
        P("section", DP, None),
        P("section", DP, None),
        P("section", DP, None),
        P("section", DP, None),
        P("section", DP, None),
        P("section", DP, None),
        P("section", DP, None),
        P("section", None),
        P("section", None, None),
        P("section", None),
        P("section", None),
        P("section", None),
        P("section", None),
        P("section", None),
        P("section", None),
    )
    return jax.shard_map(
        on_device, mesh=torus, in_specs=in_specs, out_specs=out_specs, check_vma=False
    )
```

```python
import functools

import jax
import jax.numpy as jnp
from jax import lax
from jax.experimental import pallas as pl
from jax.experimental.pallas import tpu as pltpu
from jax.sharding import Mesh
from jax.sharding import PartitionSpec as P

LEN = 128
ROWS = 256
WIDTH = 1024
FEED = 2048
INNER = 1536
MIXED = 1792
CAT = 4224
HEADS = 24
DP = ("dp_0", "dp_1", "dp_2")
F32 = jnp.float32
BF16 = jnp.bfloat16
HIDE = -1e30
Q0, K0, V0, Z0, X0, T0 = 0, 512, 640, 768, 2304, 4096
OUT0, HEADS0, DT0, PACKED = 64, 88, 96, 104


def dot(left, right):
    return jnp.dot(left, right, preferred_element_type=F32)


def dot_nt(left, right):
    return lax.dot_general(left, right, (((1,), (1,)), ((), ())), preferred_element_type=F32)


def dot_tn(left, right):
    return lax.dot_general(left, right, (((0,), (0,)), ((), ())), preferred_element_type=F32)


def dot_full(left, right):
    return jnp.dot(left, right, precision=lax.Precision.HIGHEST, preferred_element_type=F32)


def iota(shape, dim):
    return lax.broadcasted_iota(jnp.int32, shape, dim)


def sigmoid(v):
    return 1.0 / (1.0 + jnp.exp(-v))


def softplus(v):
    return jnp.maximum(v, 0.0) + jnp.log(1.0 + jnp.exp(-jnp.abs(v)))


def swap_halves(v):
    width = v.shape[1]
    near = lax.rem(iota(v.shape, 1), 64) < 32
    return jnp.where(near, pltpu.roll(v, width - 32, 1), pltpu.roll(v, 32, 1))


def shifted_down(v, by):
    if by == 0:
        return v
    return jnp.where(iota(v.shape, 0) >= by, pltpu.roll(v, by, 0), 0.0)


def shifted_up(v, by):
    if by == 0:
        return v
    rows = v.shape[0]
    return jnp.where(iota(v.shape, 0) < rows - by, pltpu.roll(v, rows - by, 0), 0.0)


def rms(v):
    return lax.rsqrt(jnp.mean(v * v, axis=-1, keepdims=True) + 1e-05)


def rms_backward(v, gain, grad):
    scale = rms(v)
    gained = grad * gain
    inner = jnp.mean(gained * v, axis=-1, keepdims=True)
    grad_v = scale * gained - v * (scale * scale * scale * inner)
    return grad_v, jnp.sum(grad * v * scale, axis=0, keepdims=True)


def left_half():
    return iota((LEN, 128), 1) < 64


def both_halves(v, group, left):
    turned = pltpu.roll(v, 64, 1)
    return jnp.where(left, v, turned) if group == 0 else jnp.where(left, turned, v)


def stacked(pairs, left):
    parts = []
    for pair in pairs:
        parts.append(jnp.where(left, pair, 0.0))
        parts.append(jnp.where(left, 0.0, pair))
    return jnp.concatenate(parts, axis=0).astype(BF16)


def unstacked(rows, index, left):
    low = rows[2 * index * LEN : (2 * index + 1) * LEN]
    high = rows[(2 * index + 1) * LEN : (2 * index + 2) * LEN]
    return jnp.where(left, low, high)


def attention_parts(proj, rows, cosine, sine):
    left = left_half()
    query = proj[rows, Q0:K0]
    query = query * cosine[...] + swap_halves(query) * sine[...]
    key = proj[rows, K0:V0]
    key = key * cosine[:, :128] + swap_halves(key) * sine[:, :128]
    value = proj[rows, V0:Z0]
    groups = []
    for group in range(2):
        pairs = [query[:, 128 * p : 128 * p + 128] for p in (2 * group, 2 * group + 1)]
        queries = stacked(pairs, left)
        keys = both_halves(key, group, left).astype(BF16)
        values = both_halves(value, group, left).astype(BF16)
        scores = dot_nt(queries, keys) * 0.125
        time = lax.rem(iota(scores.shape, 0), LEN)
        scores = jnp.where(iota(scores.shape, 1) <= time, scores, HIDE)
        top = jnp.max(scores, axis=-1, keepdims=True)
        expo = jnp.exp(scores - top)
        probs = expo / jnp.sum(expo, axis=-1, keepdims=True)
        groups.append((queries, keys, values, probs))
    return left, groups


def attention_forward(proj, rows, cosine, sine, attended):
    left, groups = attention_parts(proj, rows, cosine, sine)
    for group, (queries, keys, values, probs) in enumerate(groups):
        mixed = dot(probs.astype(BF16), values)
        for index in range(2):
            at = 256 * group + 128 * index
            attended[rows, at : at + 128] = unstacked(mixed, index, left).astype(BF16)


def attention_backward(proj, rows, cosine, sine, grad_attended, grad_cat):
    left, groups = attention_parts(proj, rows, cosine, sine)
    key_parts, value_parts = [], []
    for group, (queries, keys, values, probs) in enumerate(groups):
        pairs = [grad_attended[:, 128 * p : 128 * p + 128] for p in (2 * group, 2 * group + 1)]
        grads = stacked(pairs, left)
        grad_values = dot_tn(probs.astype(BF16), grads)
        grad_probs = dot_nt(grads, values)
        inner = jnp.sum(probs * grad_probs, axis=-1, keepdims=True)
        grad_scores = (probs * (grad_probs - inner)).astype(BF16)
        grad_queries = dot(grad_scores, keys) * 0.125
        grad_keys = dot_tn(grad_scores, queries) * 0.125
        for index in range(2):
            at = 256 * group + 128 * index
            grad = unstacked(grad_queries, index, left)
            grad = grad * cosine[:, :128] - swap_halves(grad) * sine[:, :128]
            grad_cat[rows, at : at + 128] = grad.astype(BF16)
        key_parts.append(grad_keys + pltpu.roll(grad_keys, 64, 1))
        value_parts.append(grad_values + pltpu.roll(grad_values, 64, 1))
    grad = jnp.where(left, key_parts[0], key_parts[1])
    grad = grad * cosine[:, :128] - swap_halves(grad) * sine[:, :128]
    grad_cat[rows, K0:V0] = grad.astype(BF16)
    grad_cat[rows, V0:Z0] = jnp.where(left, value_parts[0], value_parts[1]).astype(BF16)


def mamba_parts(proj, rows, kernel, bias, step_bias, decay_log):
    mixed = proj[rows, X0:T0]
    total = bias[...] + mixed * kernel[3:4, :]
    for tap in range(3):
        total = total + shifted_down(mixed, 3 - tap) * kernel[tap : tap + 1, :]
    active = total * sigmoid(total)
    step = softplus(proj[rows, T0:CAT] + step_bias[...])
    rate = -step * jnp.exp(decay_log[...])
    earlier = (iota((LEN, LEN), 0) >= iota((LEN, LEN), 1)).astype(F32)
    cumul = dot_full(earlier, rate)
    state_in = active[:, INNER : INNER + 128].astype(BF16)
    state_out = active[:, INNER + 128 :].astype(BF16)
    return mixed, total, active, step, rate, cumul, state_in, state_out


def stepped(step, pair, left):
    return jnp.where(left, step[:, 2 * pair : 2 * pair + 1], step[:, 2 * pair + 1 : 2 * pair + 2])


def mamba_forward(proj, rows, kernel, bias, step_bias, decay_log, skip, gain, ssm, mamba):
    left = left_half()
    parts = mamba_parts(proj, rows, kernel, bias, step_bias, decay_log)
    mixed, total, active, step, rate, cumul, state_in, state_out = parts
    across = cumul.T
    hidden = jnp.where(iota((LEN, LEN), 0) >= iota((LEN, LEN), 1), 0.0, HIDE)
    meeting = dot_nt(state_out, state_in)
    for pair in range(HEADS // 2):
        at = 128 * pair
        inputs = active[:, at : at + 128]
        scaled = (inputs * stepped(step, pair, left)).astype(BF16)
        mixing = []
        for head in (2 * pair, 2 * pair + 1):
            spread = cumul[:, head : head + 1] - across[head : head + 1, :] + hidden
            mixing.append((meeting * jnp.exp(spread)).astype(BF16))
        both = dot(jnp.concatenate(mixing, axis=0), scaled)
        out = unstacked(both, 0, left) + skip[:, at : at + 128] * inputs
        ssm[rows, at : at + 128] = out
    z = proj[rows, Z0:X0]
    gated = ssm[rows, :] * (z * sigmoid(z))
    mamba[rows, :] = (gated * rms(gated) * gain[...]).astype(BF16)


def head_sums(v, pick):
    high = v.astype(BF16)
    low = (v - high.astype(F32)).astype(BF16)
    return dot(high, pick) + dot(low, pick)


def mamba_backward(
    proj, rows, kernel, bias, step_bias, decay_log, skip, gain, pick, ssm, grad_mamba, grad_cat,
    across_scratch, balance_scratch, touch_scratch, grad_active, add_small,
):
    left = left_half()
    parts = mamba_parts(proj, rows, kernel, bias, step_bias, decay_log)
    mixed, total, active, step, rate, cumul, state_in, state_out = parts
    across = cumul.T
    hidden = jnp.where(iota((LEN, LEN), 1) >= iota((LEN, LEN), 0), 0.0, HIDE)
    meeting = dot_nt(state_out, state_in).T
    z = proj[rows, Z0:X0]
    out = ssm[rows, :]
    gate = sigmoid(z)
    gated = out * (z * gate)
    grad_gated, grad_gain = rms_backward(gated, gain[...], grad_mamba)
    add_small(6, grad_gain)
    grad_cat[rows, Z0:X0] = (grad_gated * out * (gate * (1.0 + z * (1.0 - gate)))).astype(BF16)
    grad_out = grad_gated * (z * gate)
    add_small(5, jnp.sum(grad_out * active[:, :INNER], axis=0, keepdims=True))
    grad_meeting = jnp.zeros((LEN, LEN), F32)
    for pair in range(HEADS // 2):
        at = 128 * pair
        inputs = active[:, at : at + 128]
        steps = stepped(step, pair, left)
        scaled = (inputs * steps).astype(BF16)
        grad_pair = grad_out[:, at : at + 128]
        grad_low = grad_pair.astype(BF16)
        halves = jnp.concatenate(
            [jnp.where(left, scaled, jnp.zeros_like(scaled)), jnp.where(left, jnp.zeros_like(scaled), scaled)],
            axis=0,
        )
        grad_mixing = dot_nt(halves, grad_low)
        mixing = []
        for place, head in enumerate((2 * pair, 2 * pair + 1)):
            spread = across[head : head + 1, :] - cumul[:, head : head + 1] + hidden
            decay = jnp.exp(spread)
            mixing.append((meeting * decay).astype(BF16))
            grad_meeting = grad_meeting + grad_mixing[LEN * place : LEN * place + LEN] * decay
        both = dot(jnp.concatenate(mixing, axis=0), grad_low)
        grad_scaled = unstacked(both, 0, left)
        skips = skip[:, at : at + 128]
        grad_active[:, at : at + 128] = grad_scaled * steps + skips * grad_pair
        touch_scratch[:, at : at + 128] = grad_scaled * inputs
        balance_scratch[:, at : at + 128] = grad_low.astype(F32) * (
            out[:, at : at + 128] - skips * inputs
        ) - scaled.astype(F32) * grad_scaled
    grad_low = grad_meeting.astype(BF16)
    grad_active[:, INNER : INNER + 128] = dot(grad_low, state_out)
    grad_active[:, INNER + 128 :] = dot_tn(grad_low, state_in)
    later = (iota((LEN, LEN), 1) >= iota((LEN, LEN), 0)).astype(F32)
    grad_rate = dot_full(later, head_sums(balance_scratch[...], pick[...]))
    add_small(4, jnp.sum(grad_rate * rate, axis=0, keepdims=True))
    grad_step = head_sums(touch_scratch[...], pick[...]) - grad_rate * jnp.exp(decay_log[...])
    grad_dt = grad_step * sigmoid(proj[rows, T0:CAT] + step_bias[...])
    add_small(3, jnp.sum(grad_dt, axis=0, keepdims=True))
    grad_cat[rows, T0:CAT] = grad_dt.astype(BF16)
    slope = sigmoid(total)
    grad_total = grad_active[...] * (slope * (1.0 + total * (1.0 - slope)))
    add_small(2, jnp.sum(grad_total, axis=0, keepdims=True))
    grad_mixed = grad_total * kernel[3:4, :]
    taps = []
    for tap in range(4):
        taps.append(jnp.sum(grad_total * shifted_down(mixed, 3 - tap), axis=0, keepdims=True))
        if tap < 3:
            grad_mixed = grad_mixed + shifted_up(grad_total, 3 - tap) * kernel[tap : tap + 1, :]
    add_small(1, jnp.concatenate(taps, axis=0))
    grad_cat[rows, X0:T0] = grad_mixed.astype(BF16)


def flat(block):
    return block.reshape(block.shape[0] * block.shape[1], block.shape[2])


def start_all(copies):
    for copy in copies:
        copy.start()


def feed_copies(places, pieces, buffers, sems):
    copies = []
    for k, buffer in enumerate(buffers):
        own, got, far = pieces[3 * k : 3 * k + 3]
        for q, source in enumerate((own, got, far.at[0], far.at[1])):
            target = buffer.at[(slice(None),) * k + (places[4 * k + q],)]
            copies.append(pltpu.make_async_copy(source, target, sems.at[4 * k + q]))
    return copies


def rows_of(block):
    return block.reshape(-1, block.shape[-1])


def forward_kernel(unpack, x, packed, dt_weight, *refs):
    if unpack:
        given, results = (None, None), refs[20:22]
        rest = refs[:20] + refs[22:]
    else:
        given, results = refs[:2], (None, None)
        rest = refs[2:]
    forward_body(unpack, x, packed, dt_weight, *given, *results, *rest)


def forward_body(
    unpack, x, packed, dt_weight, out_weight, heads_weight, out_result, heads_result,
    places, gate_own, gate_got, gate_far, up_own, up_got, up_far, down_own, down_got, down_far,
    input_gain, kernel, bias, step_bias, decay_log, skip,
    mixer_gain, feed_gain, cosine, sine,
    result_out, normed_out, proj_out, ssm_out, mamba_out, attended_out, middle_out, ffin_out, gate_out,
    upper_out, hidden_out,
    result, normed, proj, ssm, mamba, attended, middle, ffin, gate, upper, hidden,
    cat, gate_mat, up_mat, down_mat, out_mat, heads_mat, mixed, sems, out_sems, feed_sems,
):
    leaving = []

    def leave(*pairs):
        for source, target in pairs:
            copy = pltpu.make_async_copy(source, target, out_sems.at[len(leaving)])
            copy.start()
            leaving.append(copy)

    copies = [
        pltpu.make_async_copy(packed.at[:, pl.ds(16 * j, 16), :], cat.at[j], sems.at[j])
        for j in range(4)
    ]
    if unpack:
        copies.append(pltpu.make_async_copy(packed.at[:, pl.ds(OUT0, 32), :], mixed, sems.at[4]))
    else:
        copies.append(pltpu.make_async_copy(out_weight, out_mat, sems.at[4]))
        copies.append(pltpu.make_async_copy(heads_weight, heads_mat, sems.at[5]))
    pieces = (gate_own, gate_got, gate_far, up_own, up_got, up_far, down_own, down_got, down_far)
    feeds = feed_copies(places, pieces, (gate_mat, up_mat, down_mat), feed_sems)
    start_all(copies + feeds)
    state = x[...].astype(F32)
    normed[...] = (state * rms(state) * input_gain[...]).astype(BF16)
    proj[:, T0:CAT] = dot(normed[...], dt_weight[...])
    for j in range(4):
        copies[j].wait()
        proj[:, 1024 * j : 1024 * j + 1024] = dot(normed[...], flat(cat[j]))
    leave((normed, normed_out), (proj, proj_out))

    def sequence(index, carry):
        rows = pl.ds(pl.multiple_of(index * LEN, LEN), LEN)
        attention_forward(proj, rows, cosine, sine, attended)
        mamba_forward(proj, rows, kernel, bias, step_bias, decay_log, skip, mixer_gain, ssm, mamba)
        return carry

    lax.fori_loop(0, 2, sequence, 0)
    leave((ssm, ssm_out), (mamba, mamba_out), (attended, attended_out))
    for copy in copies[4:]:
        copy.wait()
    if unpack:
        wide = mixed[...].astype(F32)
        out_mat[...] = wide[:, :24].reshape(INNER, WIDTH).astype(BF16)
        heads_mat[...] = wide[:, 24:].reshape(512, WIDTH).astype(BF16)
        leave((out_mat, out_result), (heads_mat, heads_result))

    part = dot(mamba[...], out_mat[...]) + dot(attended[...], heads_mat[...])
    middle[...] = x[...].astype(F32) + part
    value = middle[...]
    ffin[...] = (value * rms(value) * feed_gain[...]).astype(BF16)
    leave((middle, middle_out), (ffin, ffin_out))
    for copy in feeds[:8]:
        copy.wait()

    for half in range(2):
        at = slice(1024 * half, 1024 * half + 1024)
        low = dot(ffin[...], rows_of(gate_mat[:, :, :, :, at]))
        high = dot(ffin[...], rows_of(up_mat[:, :, :, :, at]))
        gate[:, at] = low
        upper[:, at] = high
        hidden[:, at] = (low * sigmoid(low) * high).astype(BF16)
    leave((gate, gate_out), (upper, upper_out), (hidden, hidden_out))
    for copy in feeds[8:]:
        copy.wait()

    result[...] = (middle[...] + dot(hidden[...], rows_of(down_mat[...]))).astype(BF16)
    leave((result, result_out))
    for copy in leaving:
        copy.wait()


def leave_all(pairs, sems):
    copies = [
        pltpu.make_async_copy(source, target, sems.at[k]) for k, (source, target) in enumerate(pairs)
    ]
    start_all(copies)
    return copies


def feed_backward_kernel(earlier, active, *refs):
    @pl.when(active[0] == 1)
    def run():
        feed_backward_body(*refs[:15], *refs[15 + earlier :])


def feed_backward_body(
    grad_top, places, gate_own, gate_got, gate_far, up_own, up_got, up_far, down_own, down_got, down_far,
    gate_in, upper_in, middle_in, feed_gain,
    grad_gate_out, grad_upper_out, grad_middle_out, feed_grad_out,
    grad_gate, grad_upper, grad_middle, feed_grad,
    gate, upper, middle, gate_mat, up_mat, down_mat, sems, out_sems, feed_sems,
):
    inputs = [
        pltpu.make_async_copy(gate_in, gate, sems.at[0]),
        pltpu.make_async_copy(upper_in, upper, sems.at[1]),
        pltpu.make_async_copy(middle_in, middle, sems.at[2]),
    ]
    pieces = (gate_own, gate_got, gate_far, up_own, up_got, up_far, down_own, down_got, down_far)
    feeds = feed_copies(places, pieces, (gate_mat, up_mat, down_mat), feed_sems)
    start_all(feeds[8:] + inputs + feeds[:8])
    for copy in feeds[8:]:
        copy.wait()

    for half in range(2):
        at = slice(1024 * half, 1024 * half + 1024)
        grad_hidden = dot_nt(grad_top[...], rows_of(down_mat[2 * half : 2 * half + 2]))
        if half == 0:
            inputs[0].wait()
            inputs[1].wait()
        low, high = gate[:, at], upper[:, at]
        slope = sigmoid(low)
        grad_upper[:, at] = (grad_hidden * (low * slope)).astype(BF16)
        part = grad_hidden * high * (slope * (1.0 + low * (1.0 - slope)))
        grad_gate[:, at] = part.astype(BF16)
    leaving = leave_all(((grad_gate, grad_gate_out), (grad_upper, grad_upper_out)), out_sems)
    for copy in feeds[:8]:
        copy.wait()

    grad_ffin = dot_nt(grad_gate[...], rows_of(gate_mat[...]))
    grad_ffin = grad_ffin + dot_nt(grad_upper[...], rows_of(up_mat[...]))
    inputs[2].wait()
    grad_part, grad_gain = rms_backward(middle[...], feed_gain[...], grad_ffin)
    feed_grad[...] = grad_gain
    grad_middle[...] = grad_top[...].astype(F32) + grad_part
    leaving += leave_all(
        ((grad_middle, grad_middle_out), (feed_grad, feed_grad_out)), out_sems.at[pl.ds(2, 2)]
    )
    for copy in leaving:
        copy.wait()


def mix_backward_kernel(earlier, active, *refs):
    @pl.when(active[0] == 1)
    def run():
        mix_backward_body(*refs[:14], *refs[14 + earlier :])


def mix_backward_body(
    grad_middle, out_weight, heads_weight, proj_in, ssm_in, kernel, bias,
    step_bias, decay_log, skip, mixer_gain, cosine, sine, pick,
    grad_branch_out, grad_cat_out, kernel_grad_out, bias_grad_out,
    step_grad_out, decay_grad_out, skip_grad_out, mixer_grad_out,
    grad_branch, grad_cat, kernel_grad, bias_grad, step_grad, decay_grad,
    skip_grad, mixer_grad,
    proj, ssm,
    out_mat, heads_mat, grad_mamba, grad_attended, balance, touch, grad_active, sems,
    out_sems,
):
    copies = [
        pltpu.make_async_copy(out_weight, out_mat, sems.at[0]),
        pltpu.make_async_copy(heads_weight, heads_mat, sems.at[1]),
        pltpu.make_async_copy(proj_in, proj, sems.at[2]),
        pltpu.make_async_copy(ssm_in, ssm, sems.at[3]),
    ]
    start_all(copies)
    grad_branch[...] = grad_middle[...].astype(BF16)
    copies[0].wait()
    copies[1].wait()

    grad_mamba[...] = dot_nt(grad_branch[...], out_mat[...])
    grad_attended[...] = dot_nt(grad_branch[...], heads_mat[...])
    small = {
        1: kernel_grad,
        2: bias_grad,
        3: step_grad,
        4: decay_grad,
        5: skip_grad,
        6: mixer_grad,
    }
    for ref in small.values():
        ref[...] = jnp.zeros_like(ref)

    def add_small(slot, value):
        small[slot][...] += value

    copies[2].wait()
    copies[3].wait()

    def sequence(index, carry):
        rows = pl.ds(pl.multiple_of(index * LEN, LEN), LEN)
        grads = grad_attended[rows, :]
        attention_backward(proj, rows, cosine, sine, grads, grad_cat)
        mamba_backward(
            proj, rows, kernel, bias, step_bias, decay_log, skip, mixer_gain, pick, ssm,
            grad_mamba[rows, :], grad_cat, None, balance, touch, grad_active, add_small,
        )
        return carry

    lax.fori_loop(0, 2, sequence, 0)
    leaving = leave_all(
        (
            (grad_branch, grad_branch_out),
            (grad_cat, grad_cat_out),
            (kernel_grad, kernel_grad_out),
            (bias_grad, bias_grad_out),
            (step_grad, step_grad_out),
            (decay_grad, decay_grad_out),
            (skip_grad, skip_grad_out),
            (mixer_grad, mixer_grad_out),
        ),
        out_sems,
    )
    for copy in leaving:
        copy.wait()


def input_backward_kernel(earlier, active, *refs):
    @pl.when(active[0] == 1)
    def run():
        input_backward_body(*refs[:6], *refs[6 + earlier :])


def input_backward_body(
    grad_cat, grad_middle, x, packed, dt_weight, input_gain,
    grad_start_out, start_low_out, input_grad_out,
    grad_start, start_low, input_grad,
    cat, sems, out_sems,
):
    copies = [
        pltpu.make_async_copy(packed.at[:, pl.ds(16 * j, 16), :], cat.at[j], sems.at[j])
        for j in range(4)
    ]
    start_all(copies)
    grad_normed = dot_nt(grad_cat[:, T0:CAT], dt_weight[...])
    for j in range(4):
        copies[j].wait()
        part = dot_nt(grad_cat[:, 1024 * j : 1024 * j + 1024], flat(cat[j]))
        grad_normed = grad_normed + part
    state = x[...].astype(F32)
    grad_state, grad_gain = rms_backward(state, input_gain[...], grad_normed)
    input_grad[...] = grad_gain
    total = grad_middle[...] + grad_state
    grad_start[...] = total
    start_low[...] = total.astype(BF16)
    leaving = leave_all(
        ((grad_start, grad_start_out), (start_low, start_low_out), (input_grad, input_grad_out)),
        out_sems,
    )
    for copy in leaving:
        copy.wait()


VMEM = pl.BlockSpec(memory_space=pltpu.VMEM)
SMEM = pl.BlockSpec(memory_space=pltpu.SMEM)
ANY = pl.BlockSpec(memory_space=pl.ANY)
LIMIT = 60 * 1024 * 1024


def shape(rows, columns, dtype):
    return jax.ShapeDtypeStruct((rows, columns), dtype)


def scratch(*dims, dtype=BF16):
    return pltpu.VMEM(dims, dtype)


FEED_MATS = (
    scratch(4, 4, 4, 16, FEED),
    scratch(4, 4, 4, 16, FEED),
    scratch(4, 4, 4, 32, WIDTH),
)


def mirrored(shapes):
    return [pltpu.VMEM(s.shape, s.dtype) for s in shapes]


def run_forward(start, mats, small, rope):
    packed, dt_weight, *given, feeds = mats
    unpack = not given
    extra = (shape(INNER, WIDTH, BF16), shape(512, WIDTH, BF16))
    shapes = (
        shape(ROWS, WIDTH, BF16),
        shape(ROWS, WIDTH, BF16),
        shape(ROWS, CAT, F32),
        shape(ROWS, INNER, F32),
        shape(ROWS, INNER, BF16),
        shape(ROWS, 512, BF16),
        shape(ROWS, WIDTH, F32),
        shape(ROWS, WIDTH, BF16),
        shape(ROWS, FEED, F32),
        shape(ROWS, FEED, F32),
        shape(ROWS, FEED, BF16),
    )
    return pl.pallas_call(
        functools.partial(forward_kernel, unpack),
        out_shape=extra + shapes if unpack else shapes,
        in_specs=[VMEM, ANY, VMEM] + [ANY] * len(given) + [SMEM] + [ANY] * 9 + [VMEM] * 10,
        out_specs=(ANY,) * (len(shapes) + 2 * unpack),
        scratch_shapes=[
            *mirrored(shapes),
            scratch(4, 64, 16, 1024),
            *FEED_MATS,
            scratch(INNER, WIDTH),
            scratch(512, WIDTH),
            scratch(64, 32, WIDTH) if unpack else scratch(16, 128),
            pltpu.SemaphoreType.DMA((6,)),
            pltpu.SemaphoreType.DMA((len(shapes) + 2,)),
            pltpu.SemaphoreType.DMA((12,)),
        ],
        compiler_params=pltpu.CompilerParams(vmem_limit_bytes=LIMIT),
        cost_estimate=pl.CostEstimate(
            flops=2 * ROWS * 12_600_000, bytes_accessed=40_000_000, transcendentals=2_000_000
        ),
        name="forward",
    )(start, packed, dt_weight, *given, *feeds, *small, *rope)


def run_feed_backward(active, grad_top, mats, gate, upper, middle, feed_gain, earlier=()):
    shapes = (
        shape(ROWS, FEED, BF16),
        shape(ROWS, FEED, BF16),
        shape(ROWS, WIDTH, F32),
        shape(1, WIDTH, F32),
    )
    return pl.pallas_call(
        functools.partial(feed_backward_kernel, len(earlier)),
        out_shape=shapes,
        in_specs=[SMEM, VMEM, SMEM] + [ANY] * 12 + [VMEM] + [ANY] * len(earlier),
        out_specs=(ANY,) * len(shapes),
        scratch_shapes=[
            *mirrored(shapes),
            scratch(ROWS, FEED, dtype=F32),
            scratch(ROWS, FEED, dtype=F32),
            scratch(ROWS, WIDTH, dtype=F32),
            *FEED_MATS,
            pltpu.SemaphoreType.DMA((3,)),
            pltpu.SemaphoreType.DMA((4,)),
            pltpu.SemaphoreType.DMA((12,)),
        ],
        input_output_aliases={16 + k: k for k in range(len(earlier))},
        compiler_params=pltpu.CompilerParams(vmem_limit_bytes=LIMIT),
        cost_estimate=pl.CostEstimate(
            flops=2 * ROWS * 6_300_000, bytes_accessed=22_000_000, transcendentals=1_000_000
        ),
        name="feed_backward",
    )(active, grad_top, *mats[4], gate, upper, middle, feed_gain, *earlier)


def run_mix_backward(active, grad_middle, mats, proj, ssm, small, rope, pick, earlier=()):
    packed, dt_weight, out_weight, heads_weight, feeds = mats
    shapes = (
        shape(ROWS, WIDTH, BF16),
        shape(ROWS, CAT, BF16),
        shape(4, MIXED, F32),
        shape(1, MIXED, F32),
        shape(1, 128, F32),
        shape(1, 128, F32),
        shape(1, INNER, F32),
        shape(1, INNER, F32),
    )
    return pl.pallas_call(
        functools.partial(mix_backward_kernel, len(earlier)),
        out_shape=shapes,
        in_specs=[SMEM, VMEM] + [ANY] * 4 + [VMEM] * 9 + [ANY] * len(earlier),
        out_specs=(ANY,) * len(shapes),
        scratch_shapes=[
            *mirrored(shapes),
            scratch(ROWS, CAT, dtype=F32),
            scratch(ROWS, INNER, dtype=F32),
            scratch(INNER, WIDTH),
            scratch(512, WIDTH),
            scratch(ROWS, INNER, dtype=F32),
            scratch(ROWS, 512, dtype=F32),
            scratch(LEN, INNER, dtype=F32),
            scratch(LEN, INNER, dtype=F32),
            scratch(LEN, MIXED, dtype=F32),
            pltpu.SemaphoreType.DMA((4,)),
            pltpu.SemaphoreType.DMA((8,)),
        ],
        input_output_aliases={15 + k: k for k in range(len(earlier))},
        compiler_params=pltpu.CompilerParams(vmem_limit_bytes=LIMIT),
        cost_estimate=pl.CostEstimate(
            flops=2 * ROWS * 2_100_000, bytes_accessed=14_000_000, transcendentals=4_000_000
        ),
        name="mix_backward",
    )(
        active, grad_middle, out_weight, heads_weight, proj, ssm, *small[1:7], *rope, pick, *earlier
    )


def run_input_backward(active, grad_cat, grad_middle, start, mats, input_gain, earlier=()):
    shapes = (shape(ROWS, WIDTH, F32), shape(ROWS, WIDTH, BF16), shape(1, WIDTH, F32))
    return pl.pallas_call(
        functools.partial(input_backward_kernel, len(earlier)),
        out_shape=shapes,
        in_specs=[SMEM, VMEM, VMEM, VMEM, ANY, VMEM, VMEM] + [ANY] * len(earlier),
        out_specs=(ANY,) * len(shapes),
        scratch_shapes=[
            *mirrored(shapes),
            scratch(4, 64, 16, 1024),
            pltpu.SemaphoreType.DMA((4,)),
            pltpu.SemaphoreType.DMA((3,)),
        ],
        input_output_aliases={7 + k: k for k in range(len(earlier))},
        compiler_params=pltpu.CompilerParams(vmem_limit_bytes=LIMIT),
        cost_estimate=pl.CostEstimate(
            flops=2 * ROWS * 4_200_000, bytes_accessed=13_000_000, transcendentals=1000
        ),
        name="input_backward",
    )(active, grad_cat, grad_middle, start, *mats[:2], input_gain, *earlier)


def rope_tables():
    position = jnp.arange(LEN).astype(F32)
    inverse = 10000.0 ** (-(jnp.arange(32).astype(F32) * 2.0) / 64)
    angle = position[:, None] * inverse[None, :]
    cosine = jnp.tile(jnp.cos(angle), (1, 16))
    sine = jnp.sin(angle)
    return cosine, jnp.tile(jnp.concatenate([-sine, sine], axis=1), (1, 8))


def head_pick():
    lanes = lax.broadcasted_iota(jnp.int32, (INNER, 128), 0) // 64
    return (lanes == lax.broadcasted_iota(jnp.int32, (INNER, 128), 1)).astype(BF16)


def prepared_small(pieces):
    input_gain, kernel, bias, step_bias, decay_log, skip, mixer_gain, feed_gain = pieces

    def padded(v):
        return jnp.pad(v, (0, 128 - HEADS))[None]

    return (
        input_gain[None],
        kernel,
        bias[None],
        padded(step_bias),
        padded(decay_log),
        jnp.repeat(skip, 64)[None],
        mixer_gain[None],
        feed_gain[None],
    )


FIRST = (1, 0, 3, 2)
SECOND = (3, 2, 1, 0)


def partners(axis, turn):
    me = lax.axis_index(axis)
    near, far = me + 1 - 2 * lax.rem(me, 2), 3 - me
    flipped = lax.rem(lax.axis_index("section") + turn, 2) == 1
    found = (jnp.where(flipped, far, near), jnp.where(flipped, near, far))
    swaps = []
    for step in range(2):
        tables = [(FIRST, SECOND)[(core + turn + step) % 2] for core in range(2)]
        swaps.append([(4 * c + i, 4 * c + tables[c][i]) for c in range(2) for i in range(4)])
    return me, found, swaps


def exchange(array, axis, pairs):
    return lax.ppermute(array, ("section", axis), pairs)


def first_sent(part, axis, turn):
    me, (one, two), swaps = partners(axis, turn)
    return part([one, lax.rem(me + 2, 4)]).astype(BF16)


def first_got(sent, axis, turn):
    return exchange(sent, axis, partners(axis, turn)[2][0])


def handed_on(part, got, axis, turn):
    me, (one, two), swaps = partners(axis, turn)
    return (part([two]) + got[got.shape[0] // 2 :].astype(F32)).astype(BF16)


def totalled(part, got, handed, axis, turn):
    me, found, (swap_one, swap_two) = partners(axis, turn)
    last = exchange(handed, axis, swap_two)
    return part([me]) + got[: got.shape[0] // 2].astype(F32) + last.astype(F32)


def product_of(left, right, place):
    blocks = left.reshape(4, 4, 4, left.shape[0] // 64, left.shape[1])

    def part(places):
        picked = [lax.dynamic_index_in_dim(blocks, p, place, keepdims=False) for p in places]
        return dot(jnp.concatenate(picked, axis=0).reshape(-1, left.shape[1]), right)

    return part


def quarters_of(array, dim):
    def part(places):
        picked = [lax.dynamic_index_in_dim(array, p, dim, keepdims=False) for p in places]
        return jnp.concatenate(picked, axis=0).reshape(-1, array.shape[-1]).astype(F32)

    return part


def summed_on(array, axis, dim, turn):
    part = quarters_of(array, dim)
    got = first_got(first_sent(part, axis, turn), axis, turn)
    return totalled(part, got, handed_on(part, got, axis, turn), axis, turn)


def second_summed(parts, order, depth):
    array = jnp.concatenate([p.astype(BF16) for p in parts], axis=1)
    width = array.shape[1]
    rest = [0, 1, 2]
    rest.remove(order[0])
    array = array.reshape(4, 4, depth, width)
    array = summed_on(array, DP[order[1]], rest.index(order[1]), 0).astype(BF16)
    return array.reshape(4, depth, width)


def gathered_on(array, axis):
    me, (one, two), (swap_one, swap_two) = partners(axis, 0)
    got = exchange(array, axis, swap_one)
    far = exchange(jnp.stack([array, got]), axis, swap_two)
    return (array, got, far), (me, one, two, lax.rem(me + 2, 4))


def placed(blocks, places, dim):
    own, got, far = blocks
    whole = jnp.zeros((*own.shape[:dim], 4, *own.shape[dim:]), own.dtype)
    for block, place in zip((own, got, far[0], far[1]), places):
        whole = lax.dynamic_update_index_in_dim(whole, block, place, dim)
    return whole


def gathered(block, order):
    block = placed(*gathered_on(block, DP[order[2]]), 0)
    block = placed(*gathered_on(block, DP[order[1]]), 0 if order[1] < order[2] else 1)
    return gathered_on(block, DP[order[0]])


def column_blocks(matrix):
    return [matrix[:, at : at + 1024] for at in range(0, matrix.shape[1], 1024)]


def on_device(
    layer_input,
    out_grad,
    in_weight,
    query_weight,
    key_weight,
    value_weight,
    out_weight,
    heads_weight,
    gate_weight,
    up_weight,
    down_weight,
    *pieces,
):
    micro, part, width = layer_input.shape
    rows = micro * part
    cat = jnp.concatenate(
        [query_weight[0], key_weight[0], value_weight[0], in_weight[0, :, :3328]], axis=1
    )
    steps = jnp.pad(in_weight[0, :, 3328:].reshape(1, -1), ((0, 7), (0, 1024 - 16 * HEADS)))
    own = jnp.concatenate(
        [
            *column_blocks(cat),
            out_weight[0],
            heads_weight[0],
            steps,
        ],
        axis=0,
    )
    packed = lax.all_gather(own, DP, axis=0, tiled=False)
    dt_weight = packed[:, DT0, : 16 * HEADS].reshape(WIDTH, HEADS)
    feeds = [
        gathered(weight[0], order)
        for weight, order in (
            (gate_weight, (0, 1, 2)),
            (up_weight, (1, 2, 0)),
            (down_weight, (2, 0, 1)),
        )
    ]
    places = jnp.stack([place for blocks, found in feeds for place in found]).astype(jnp.int32)
    mats = (
        packed,
        jnp.pad(dt_weight, ((0, 0), (0, 128 - HEADS))),
        (places, *(piece for blocks, found in feeds for piece in blocks)),
    )
    small = prepared_small([piece[0] for piece in pieces])
    rope = rope_tables()
    pick = head_pick()
    first = lax.axis_index("section") == 0

    start_low = layer_input.reshape(rows, width)
    out_mat, heads_mat, *kept_low = run_forward(start_low, mats, small, rope)
    mats = (*mats[:2], out_mat, heads_mat, mats[2])
    start_high = lax.ppermute(kept_low[0], "section", [(0, 1)])
    kept_high = run_forward(start_high, mats, small, rope)
    layer_outputs = jnp.where(first, kept_low[0], kept_high[0]).reshape(1, micro, part, width)

    on_high = jnp.where(first, 0, 1).astype(jnp.int32).reshape(1)
    on_low = 1 - on_high
    top_high = out_grad.reshape(rows, width)
    feed_high = run_feed_backward(
        on_high, top_high, mats, kept_high[8], kept_high[9], kept_high[6], small[7]
    )
    mix_high = run_mix_backward(
        on_high, feed_high[2], mats, kept_high[2], kept_high[3], small, rope, pick
    )
    input_high = run_input_backward(
        on_high, mix_high[1], feed_high[2], start_high, mats, small[0]
    )
    top_low = lax.ppermute(input_high[1], "section", [(1, 0)])

    def chosen(slot):
        return jnp.where(first, kept_low[slot], kept_high[slot])

    normed_t, ffin_t, hidden_t = (chosen(slot).T for slot in (1, 7, 10))
    joined_t = jnp.concatenate(
        [chosen(4).T.reshape(64, 24, rows), chosen(5).T.reshape(64, 8, rows)], axis=1
    ).reshape(2048, rows)

    feed = run_feed_backward(
        on_low, top_low, mats, kept_low[8], kept_low[9], kept_low[6], small[7], feed_high
    )
    grad_gate, grad_upper, grad_middle, feed_grad = feed
    grad_low = jnp.where(first, top_low, top_high)
    grad_low, grad_gate, grad_upper = lax.optimization_barrier((grad_low, grad_gate, grad_upper))
    orders = ((2, 0, 1), (0, 1, 2), (1, 2, 0))
    axes = [DP[order[0]] for order in orders]
    products = [
        product_of(left, right, order[0])
        for left, right, order in zip(
            (hidden_t, ffin_t, ffin_t), (grad_low, grad_gate, grad_upper), orders
        )
    ]
    sents = [first_sent(p, axis, 0) for p, axis in zip(products, axes)]
    grad_middle, *sents = lax.optimization_barrier((grad_middle, *sents))
    gots = [first_got(sent, axis, 0) for sent, axis in zip(sents, axes)]
    mix = run_mix_backward(
        on_low, grad_middle, mats, kept_low[2], kept_low[3], small, rope, pick, mix_high
    )
    grad_branch, grad_cat, *small_grads = mix
    mix_products = [
        product_of(left, right, order[0])
        for left, right, order in zip(
            (joined_t, normed_t, normed_t),
            (grad_branch, grad_cat[:, :2048], grad_cat[:, 2048:]),
            orders,
        )
    ]
    mix_sents = [first_sent(p, axis, 1) for p, axis in zip(mix_products, axes)]
    pending = lax.optimization_barrier((*gots, *mix_sents))
    gots, mix_sents = pending[:3], pending[3:]
    mix_gots = [first_got(sent, axis, 1) for sent, axis in zip(mix_sents, axes)]
    handed = [handed_on(p, got, axis, 0) for p, got, axis in zip(products, gots, axes)]
    last_middle, *unused = lax.optimization_barrier((grad_middle, *handed))
    feed_parts = [
        totalled(p, got, hand, axis, 0)
        for p, got, hand, axis in zip(products, gots, handed, axes)
    ]
    mix_parts = [
        totalled(p, got, handed_on(p, got, axis, 1), axis, 1)
        for p, got, axis in zip(mix_products, mix_gots, axes)
    ]
    grad_start, unused, input_grad = run_input_backward(
        on_low, grad_cat, last_middle, start_low, mats, small[0], input_high
    )
    small_grads = [input_grad, *small_grads]
    input_g, kernel_g, bias_g, step_g, decay_g, skip_g, mixer_g = small_grads
    small_grads = (
        input_g[0],
        kernel_g,
        bias_g[0],
        step_g[0, :HEADS],
        decay_g[0, :HEADS],
        skip_g.reshape(HEADS, 64).sum(axis=1),
        mixer_g[0],
        feed_grad[0],
    )
    vector = jnp.concatenate([piece.reshape(-1) for piece in small_grads])
    vector = jnp.pad(vector, (0, -vector.shape[0] % 1024)).reshape(-1, 128)
    vectors = lax.all_gather(vector.astype(BF16), DP, axis=0, tiled=False)
    total = jnp.sum(vectors.astype(F32), axis=0).reshape(-1)
    seconds = [
        second_summed(pair, order, depth)
        for pair, order, depth in zip(zip(feed_parts, mix_parts), orders, (32, 16, 16))
    ]
    total, *seconds = lax.optimization_barrier((total, *seconds))
    rows_grad, gate_cat, up_cat = (
        summed_on(array, DP[order[2]], 0, 0) for array, order in zip(seconds, orders)
    )
    down_grad, joined_grad = rows_grad[:, :WIDTH], rows_grad[:, WIDTH:]
    gate_grad, up_grad = gate_cat[:, :FEED], up_cat[:, :FEED]
    cat_grad = jnp.concatenate([gate_cat[:, FEED:], up_cat[:, FEED:]], axis=1)

    summed, at = ([], 0)
    for piece in small_grads:
        summed.append(total[at : at + piece.size].reshape(1, *piece.shape))
        at += piece.size
    return (
        layer_outputs,
        grad_start.reshape(1, micro, part, width),
        cat_grad[None, :, Z0 : T0 + HEADS],
        cat_grad[None, :, :K0],
        cat_grad[None, :, K0:V0],
        cat_grad[None, :, V0:Z0],
        joined_grad[None, :24],
        joined_grad[None, 24:],
        gate_grad[None],
        up_grad[None],
        down_grad[None],
        *summed,
    )


def solution(mesh):
    torus = Mesh(
        mesh.devices.reshape(mesh.shape["section"], 4, 4, 4), ("section", "dp_0", "dp_1", "dp_2")
    )
    in_specs = (
        P(None, DP, None),
        P(None, DP, None),
        P("section", DP, None),
        P("section", DP, None),
        P("section", DP, None),
        P("section", DP, None),
        P("section", DP, None),
        P("section", DP, None),
        P("section", DP, None),
        P("section", DP, None),
        P("section", DP, None),
        P("section", None),
        P("section", None, None),
        P("section", None),
        P("section", None),
        P("section", None),
        P("section", None),
        P("section", None),
        P("section", None),
    )
    out_specs = (
        P("section", None, DP, None),
        P("section", None, DP, None),
        P("section", DP, None),
        P("section", DP, None),
        P("section", DP, None),
        P("section", DP, None),
        P("section", DP, None),
        P("section", DP, None),
        P("section", DP, None),
        P("section", DP, None),
        P("section", DP, None),
        P("section", None),
        P("section", None, None),
        P("section", None),
        P("section", None),
        P("section", None),
        P("section", None),
        P("section", None),
        P("section", None),
    )
    return jax.shard_map(
        on_device, mesh=torus, in_specs=in_specs, out_specs=out_specs, check_vma=False
    )
```

```python
import functools

import jax
import jax.numpy as jnp
from jax import lax
from jax.experimental import pallas as pl
from jax.experimental.pallas import tpu as pltpu
from jax.sharding import Mesh
from jax.sharding import PartitionSpec as P

LEN = 128
ROWS = 256
WIDTH = 1024
FEED = 2048
INNER = 1536
MIXED = 1792
CAT = 4224
HEADS = 24
DP = ("dp_0", "dp_1", "dp_2")
F32 = jnp.float32
BF16 = jnp.bfloat16
HIDE = -1e30
Q0, K0, V0, Z0, X0, T0 = 0, 512, 640, 768, 2304, 4096
OUT0, HEADS0, DT0, PACKED = 64, 88, 96, 104


def dot(left, right):
    return jnp.dot(left, right, preferred_element_type=F32)


def dot_nt(left, right):
    return lax.dot_general(left, right, (((1,), (1,)), ((), ())), preferred_element_type=F32)


def dot_tn(left, right):
    return lax.dot_general(left, right, (((0,), (0,)), ((), ())), preferred_element_type=F32)


def dot_full(left, right):
    return jnp.dot(left, right, precision=lax.Precision.HIGHEST, preferred_element_type=F32)


def iota(shape, dim):
    return lax.broadcasted_iota(jnp.int32, shape, dim)


def sigmoid(v):
    return 1.0 / (1.0 + jnp.exp(-v))


def softplus(v):
    return jnp.maximum(v, 0.0) + jnp.log(1.0 + jnp.exp(-jnp.abs(v)))


def swap_halves(v):
    width = v.shape[1]
    near = lax.rem(iota(v.shape, 1), 64) < 32
    return jnp.where(near, pltpu.roll(v, width - 32, 1), pltpu.roll(v, 32, 1))


def shifted_down(v, by):
    if by == 0:
        return v
    return jnp.where(iota(v.shape, 0) >= by, pltpu.roll(v, by, 0), 0.0)


def shifted_up(v, by):
    if by == 0:
        return v
    rows = v.shape[0]
    return jnp.where(iota(v.shape, 0) < rows - by, pltpu.roll(v, rows - by, 0), 0.0)


def rms(v):
    return lax.rsqrt(jnp.mean(v * v, axis=-1, keepdims=True) + 1e-05)


def rms_backward(v, gain, grad):
    scale = rms(v)
    gained = grad * gain
    inner = jnp.mean(gained * v, axis=-1, keepdims=True)
    grad_v = scale * gained - v * (scale * scale * scale * inner)
    return grad_v, jnp.sum(grad * v * scale, axis=0, keepdims=True)


def left_half():
    return iota((LEN, 128), 1) < 64


def both_halves(v, group, left):
    turned = pltpu.roll(v, 64, 1)
    return jnp.where(left, v, turned) if group == 0 else jnp.where(left, turned, v)


def stacked(pairs, left):
    parts = []
    for pair in pairs:
        parts.append(jnp.where(left, pair, 0.0))
        parts.append(jnp.where(left, 0.0, pair))
    return jnp.concatenate(parts, axis=0).astype(BF16)


def unstacked(rows, index, left):
    low = rows[2 * index * LEN : (2 * index + 1) * LEN]
    high = rows[(2 * index + 1) * LEN : (2 * index + 2) * LEN]
    return jnp.where(left, low, high)


def attention_parts(proj, rows, cosine, sine):
    left = left_half()
    query = proj[rows, Q0:K0]
    query = query * cosine[...] + swap_halves(query) * sine[...]
    key = proj[rows, K0:V0]
    key = key * cosine[:, :128] + swap_halves(key) * sine[:, :128]
    value = proj[rows, V0:Z0]
    groups = []
    for group in range(2):
        pairs = [query[:, 128 * p : 128 * p + 128] for p in (2 * group, 2 * group + 1)]
        queries = stacked(pairs, left)
        keys = both_halves(key, group, left).astype(BF16)
        values = both_halves(value, group, left).astype(BF16)
        scores = dot_nt(queries, keys) * 0.125
        time = lax.rem(iota(scores.shape, 0), LEN)
        scores = jnp.where(iota(scores.shape, 1) <= time, scores, HIDE)
        top = jnp.max(scores, axis=-1, keepdims=True)
        expo = jnp.exp(scores - top)
        probs = expo / jnp.sum(expo, axis=-1, keepdims=True)
        groups.append((queries, keys, values, probs))
    return left, groups


def attention_forward(proj, rows, cosine, sine, attended):
    left, groups = attention_parts(proj, rows, cosine, sine)
    for group, (queries, keys, values, probs) in enumerate(groups):
        mixed = dot(probs.astype(BF16), values)
        for index in range(2):
            at = 256 * group + 128 * index
            attended[rows, at : at + 128] = unstacked(mixed, index, left).astype(BF16)


def attention_backward(proj, rows, cosine, sine, grad_attended, grad_cat):
    left, groups = attention_parts(proj, rows, cosine, sine)
    key_parts, value_parts = [], []
    for group, (queries, keys, values, probs) in enumerate(groups):
        pairs = [grad_attended[:, 128 * p : 128 * p + 128] for p in (2 * group, 2 * group + 1)]
        grads = stacked(pairs, left)
        grad_values = dot_tn(probs.astype(BF16), grads)
        grad_probs = dot_nt(grads, values)
        inner = jnp.sum(probs * grad_probs, axis=-1, keepdims=True)
        grad_scores = (probs * (grad_probs - inner)).astype(BF16)
        grad_queries = dot(grad_scores, keys) * 0.125
        grad_keys = dot_tn(grad_scores, queries) * 0.125
        for index in range(2):
            at = 256 * group + 128 * index
            grad = unstacked(grad_queries, index, left)
            grad = grad * cosine[:, :128] - swap_halves(grad) * sine[:, :128]
            grad_cat[rows, at : at + 128] = grad.astype(BF16)
        key_parts.append(grad_keys + pltpu.roll(grad_keys, 64, 1))
        value_parts.append(grad_values + pltpu.roll(grad_values, 64, 1))
    grad = jnp.where(left, key_parts[0], key_parts[1])
    grad = grad * cosine[:, :128] - swap_halves(grad) * sine[:, :128]
    grad_cat[rows, K0:V0] = grad.astype(BF16)
    grad_cat[rows, V0:Z0] = jnp.where(left, value_parts[0], value_parts[1]).astype(BF16)


def mamba_parts(proj, rows, kernel, bias, step_bias, decay_log):
    mixed = proj[rows, X0:T0]
    total = bias[...] + mixed * kernel[3:4, :]
    for tap in range(3):
        total = total + shifted_down(mixed, 3 - tap) * kernel[tap : tap + 1, :]
    active = total * sigmoid(total)
    step = softplus(proj[rows, T0:CAT] + step_bias[...])
    rate = -step * jnp.exp(decay_log[...])
    earlier = (iota((LEN, LEN), 0) >= iota((LEN, LEN), 1)).astype(F32)
    cumul = dot_full(earlier, rate)
    state_in = active[:, INNER : INNER + 128].astype(BF16)
    state_out = active[:, INNER + 128 :].astype(BF16)
    return mixed, total, active, step, rate, cumul, state_in, state_out


def stepped(step, pair, left):
    return jnp.where(left, step[:, 2 * pair : 2 * pair + 1], step[:, 2 * pair + 1 : 2 * pair + 2])


def mamba_forward(proj, rows, kernel, bias, step_bias, decay_log, skip, gain, ssm, mamba):
    left = left_half()
    parts = mamba_parts(proj, rows, kernel, bias, step_bias, decay_log)
    mixed, total, active, step, rate, cumul, state_in, state_out = parts
    across = cumul.T
    hidden = jnp.where(iota((LEN, LEN), 0) >= iota((LEN, LEN), 1), 0.0, HIDE)
    meeting = dot_nt(state_out, state_in)
    for pair in range(HEADS // 2):
        at = 128 * pair
        inputs = active[:, at : at + 128]
        scaled = (inputs * stepped(step, pair, left)).astype(BF16)
        mixing = []
        for head in (2 * pair, 2 * pair + 1):
            spread = cumul[:, head : head + 1] - across[head : head + 1, :] + hidden
            mixing.append((meeting * jnp.exp(spread)).astype(BF16))
        both = dot(jnp.concatenate(mixing, axis=0), scaled)
        out = unstacked(both, 0, left) + skip[:, at : at + 128] * inputs
        ssm[rows, at : at + 128] = out
    z = proj[rows, Z0:X0]
    gated = ssm[rows, :] * (z * sigmoid(z))
    mamba[rows, :] = (gated * rms(gated) * gain[...]).astype(BF16)


def head_sums(v, pick):
    high = v.astype(BF16)
    low = (v - high.astype(F32)).astype(BF16)
    return dot(high, pick) + dot(low, pick)


def mamba_backward(
    proj, rows, kernel, bias, step_bias, decay_log, skip, gain, pick, ssm, grad_mamba, grad_cat,
    across_scratch, balance_scratch, touch_scratch, grad_active, add_small,
):
    left = left_half()
    parts = mamba_parts(proj, rows, kernel, bias, step_bias, decay_log)
    mixed, total, active, step, rate, cumul, state_in, state_out = parts
    across = cumul.T
    hidden = jnp.where(iota((LEN, LEN), 1) >= iota((LEN, LEN), 0), 0.0, HIDE)
    meeting = dot_nt(state_out, state_in).T
    z = proj[rows, Z0:X0]
    out = ssm[rows, :]
    gate = sigmoid(z)
    gated = out * (z * gate)
    grad_gated, grad_gain = rms_backward(gated, gain[...], grad_mamba)
    add_small(6, grad_gain)
    grad_cat[rows, Z0:X0] = (grad_gated * out * (gate * (1.0 + z * (1.0 - gate)))).astype(BF16)
    grad_out = grad_gated * (z * gate)
    add_small(5, jnp.sum(grad_out * active[:, :INNER], axis=0, keepdims=True))
    grad_meeting = jnp.zeros((LEN, LEN), F32)
    for pair in range(HEADS // 2):
        at = 128 * pair
        inputs = active[:, at : at + 128]
        steps = stepped(step, pair, left)
        scaled = (inputs * steps).astype(BF16)
        grad_pair = grad_out[:, at : at + 128]
        grad_low = grad_pair.astype(BF16)
        halves = jnp.concatenate(
            [jnp.where(left, scaled, jnp.zeros_like(scaled)), jnp.where(left, jnp.zeros_like(scaled), scaled)],
            axis=0,
        )
        grad_mixing = dot_nt(halves, grad_low)
        mixing = []
        for place, head in enumerate((2 * pair, 2 * pair + 1)):
            spread = across[head : head + 1, :] - cumul[:, head : head + 1] + hidden
            decay = jnp.exp(spread)
            mixing.append((meeting * decay).astype(BF16))
            grad_meeting = grad_meeting + grad_mixing[LEN * place : LEN * place + LEN] * decay
        both = dot(jnp.concatenate(mixing, axis=0), grad_low)
        grad_scaled = unstacked(both, 0, left)
        skips = skip[:, at : at + 128]
        grad_active[:, at : at + 128] = grad_scaled * steps + skips * grad_pair
        touch_scratch[:, at : at + 128] = grad_scaled * inputs
        balance_scratch[:, at : at + 128] = grad_low.astype(F32) * (
            out[:, at : at + 128] - skips * inputs
        ) - scaled.astype(F32) * grad_scaled
    grad_low = grad_meeting.astype(BF16)
    grad_active[:, INNER : INNER + 128] = dot(grad_low, state_out)
    grad_active[:, INNER + 128 :] = dot_tn(grad_low, state_in)
    later = (iota((LEN, LEN), 1) >= iota((LEN, LEN), 0)).astype(F32)
    grad_rate = dot_full(later, head_sums(balance_scratch[...], pick[...]))
    add_small(4, jnp.sum(grad_rate * rate, axis=0, keepdims=True))
    grad_step = head_sums(touch_scratch[...], pick[...]) - grad_rate * jnp.exp(decay_log[...])
    grad_dt = grad_step * sigmoid(proj[rows, T0:CAT] + step_bias[...])
    add_small(3, jnp.sum(grad_dt, axis=0, keepdims=True))
    grad_cat[rows, T0:CAT] = grad_dt.astype(BF16)
    slope = sigmoid(total)
    grad_total = grad_active[...] * (slope * (1.0 + total * (1.0 - slope)))
    add_small(2, jnp.sum(grad_total, axis=0, keepdims=True))
    grad_mixed = grad_total * kernel[3:4, :]
    taps = []
    for tap in range(4):
        taps.append(jnp.sum(grad_total * shifted_down(mixed, 3 - tap), axis=0, keepdims=True))
        if tap < 3:
            grad_mixed = grad_mixed + shifted_up(grad_total, 3 - tap) * kernel[tap : tap + 1, :]
    add_small(1, jnp.concatenate(taps, axis=0))
    grad_cat[rows, X0:T0] = grad_mixed.astype(BF16)


def flat(block):
    return block.reshape(block.shape[0] * block.shape[1], block.shape[2])


def start_all(copies):
    for copy in copies:
        copy.start()


def feed_copies(places, pieces, buffers, sems):
    copies = []
    for k, buffer in enumerate(buffers):
        own, got, far = pieces[3 * k : 3 * k + 3]
        for q, source in enumerate((own, got, far.at[0], far.at[1])):
            target = buffer.at[(slice(None),) * k + (places[4 * k + q],)]
            copies.append(pltpu.make_async_copy(source, target, sems.at[4 * k + q]))
    return copies


def rows_of(block):
    return block.reshape(-1, block.shape[-1])


def forward_kernel(unpack, x, packed, dt_weight, *refs):
    if unpack:
        given, results = (None, None), refs[20:22]
        rest = refs[:20] + refs[22:]
    else:
        given, results = refs[:2], (None, None)
        rest = refs[2:]
    forward_body(unpack, x, packed, dt_weight, *given, *results, *rest)


def forward_body(
    unpack, x, packed, dt_weight, out_weight, heads_weight, out_result, heads_result,
    places, gate_own, gate_got, gate_far, up_own, up_got, up_far, down_own, down_got, down_far,
    input_gain, kernel, bias, step_bias, decay_log, skip,
    mixer_gain, feed_gain, cosine, sine,
    result_out, normed_out, proj_out, ssm_out, mamba_out, attended_out, middle_out, ffin_out, gate_out,
    upper_out, hidden_out,
    result, normed, proj, ssm, mamba, attended, middle, ffin, gate, upper, hidden,
    cat, gate_mat, up_mat, down_mat, out_mat, heads_mat, mixed, sems, out_sems, feed_sems,
):
    leaving = []

    def leave(*pairs):
        for source, target in pairs:
            copy = pltpu.make_async_copy(source, target, out_sems.at[len(leaving)])
            copy.start()
            leaving.append(copy)

    copies = [
        pltpu.make_async_copy(packed.at[:, pl.ds(16 * j, 16), :], cat.at[j], sems.at[j])
        for j in range(4)
    ]
    if unpack:
        copies.append(pltpu.make_async_copy(packed.at[:, pl.ds(OUT0, 32), :], mixed, sems.at[4]))
    else:
        copies.append(pltpu.make_async_copy(out_weight, out_mat, sems.at[4]))
        copies.append(pltpu.make_async_copy(heads_weight, heads_mat, sems.at[5]))
    pieces = (gate_own, gate_got, gate_far, up_own, up_got, up_far, down_own, down_got, down_far)
    feeds = feed_copies(places, pieces, (gate_mat, up_mat, down_mat), feed_sems)
    start_all(copies + feeds)
    state = x[...].astype(F32)
    normed[...] = (state * rms(state) * input_gain[...]).astype(BF16)
    proj[:, T0:CAT] = dot(normed[...], dt_weight[...])
    for j in range(4):
        copies[j].wait()
        proj[:, 1024 * j : 1024 * j + 1024] = dot(normed[...], flat(cat[j]))
    leave((normed, normed_out), (proj, proj_out))

    def sequence(index, carry):
        rows = pl.ds(pl.multiple_of(index * LEN, LEN), LEN)
        attention_forward(proj, rows, cosine, sine, attended)
        mamba_forward(proj, rows, kernel, bias, step_bias, decay_log, skip, mixer_gain, ssm, mamba)
        return carry

    lax.fori_loop(0, 2, sequence, 0)
    leave((ssm, ssm_out), (mamba, mamba_out), (attended, attended_out))
    for copy in copies[4:]:
        copy.wait()
    if unpack:
        wide = mixed[...].astype(F32)
        out_mat[...] = wide[:, :24].reshape(INNER, WIDTH).astype(BF16)
        heads_mat[...] = wide[:, 24:].reshape(512, WIDTH).astype(BF16)
        leave((out_mat, out_result), (heads_mat, heads_result))

    part = dot(mamba[...], out_mat[...]) + dot(attended[...], heads_mat[...])
    middle[...] = x[...].astype(F32) + part
    value = middle[...]
    ffin[...] = (value * rms(value) * feed_gain[...]).astype(BF16)
    leave((middle, middle_out), (ffin, ffin_out))
    for copy in feeds[:8]:
        copy.wait()

    for half in range(2):
        at = slice(1024 * half, 1024 * half + 1024)
        low = dot(ffin[...], rows_of(gate_mat[:, :, :, :, at]))
        high = dot(ffin[...], rows_of(up_mat[:, :, :, :, at]))
        gate[:, at] = low
        upper[:, at] = high
        hidden[:, at] = (low * sigmoid(low) * high).astype(BF16)
    leave((gate, gate_out), (upper, upper_out), (hidden, hidden_out))
    for copy in feeds[8:]:
        copy.wait()

    result[...] = (middle[...] + dot(hidden[...], rows_of(down_mat[...]))).astype(BF16)
    leave((result, result_out))
    for copy in leaving:
        copy.wait()


def leave_all(pairs, sems):
    copies = [
        pltpu.make_async_copy(source, target, sems.at[k]) for k, (source, target) in enumerate(pairs)
    ]
    start_all(copies)
    return copies


def feed_backward_kernel(earlier, active, *refs):
    @pl.when(active[0] == 1)
    def run():
        feed_backward_body(*refs[:15], *refs[15 + earlier :])


def feed_backward_body(
    grad_top, places, gate_own, gate_got, gate_far, up_own, up_got, up_far, down_own, down_got, down_far,
    gate_in, upper_in, middle_in, feed_gain,
    grad_gate_out, grad_upper_out, grad_middle_out, feed_grad_out,
    grad_gate, grad_upper, grad_middle, feed_grad,
    gate, upper, middle, gate_mat, up_mat, down_mat, sems, out_sems, feed_sems,
):
    inputs = [
        pltpu.make_async_copy(gate_in, gate, sems.at[0]),
        pltpu.make_async_copy(upper_in, upper, sems.at[1]),
        pltpu.make_async_copy(middle_in, middle, sems.at[2]),
    ]
    pieces = (gate_own, gate_got, gate_far, up_own, up_got, up_far, down_own, down_got, down_far)
    feeds = feed_copies(places, pieces, (gate_mat, up_mat, down_mat), feed_sems)
    start_all(feeds[8:] + inputs + feeds[:8])
    for copy in feeds[8:]:
        copy.wait()

    for half in range(2):
        at = slice(1024 * half, 1024 * half + 1024)
        grad_hidden = dot_nt(grad_top[...], rows_of(down_mat[2 * half : 2 * half + 2]))
        if half == 0:
            inputs[0].wait()
            inputs[1].wait()
        low, high = gate[:, at], upper[:, at]
        slope = sigmoid(low)
        grad_upper[:, at] = (grad_hidden * (low * slope)).astype(BF16)
        part = grad_hidden * high * (slope * (1.0 + low * (1.0 - slope)))
        grad_gate[:, at] = part.astype(BF16)
    leaving = leave_all(((grad_gate, grad_gate_out), (grad_upper, grad_upper_out)), out_sems)
    for copy in feeds[:8]:
        copy.wait()

    grad_ffin = dot_nt(grad_gate[...], rows_of(gate_mat[...]))
    grad_ffin = grad_ffin + dot_nt(grad_upper[...], rows_of(up_mat[...]))
    inputs[2].wait()
    grad_part, grad_gain = rms_backward(middle[...], feed_gain[...], grad_ffin)
    feed_grad[...] = grad_gain
    grad_middle[...] = grad_top[...].astype(F32) + grad_part
    leaving += leave_all(
        ((grad_middle, grad_middle_out), (feed_grad, feed_grad_out)), out_sems.at[pl.ds(2, 2)]
    )
    for copy in leaving:
        copy.wait()


def mix_backward_kernel(earlier, active, *refs):
    @pl.when(active[0] == 1)
    def run():
        mix_backward_body(*refs[:14], *refs[14 + earlier :])


def mix_backward_body(
    grad_middle, out_weight, heads_weight, proj_in, ssm_in, kernel, bias,
    step_bias, decay_log, skip, mixer_gain, cosine, sine, pick,
    grad_branch_out, grad_cat_out, kernel_grad_out, bias_grad_out,
    step_grad_out, decay_grad_out, skip_grad_out, mixer_grad_out,
    grad_branch, grad_cat, kernel_grad, bias_grad, step_grad, decay_grad,
    skip_grad, mixer_grad,
    proj, ssm,
    out_mat, heads_mat, grad_mamba, grad_attended, balance, touch, grad_active, sems,
    out_sems,
):
    copies = [
        pltpu.make_async_copy(out_weight, out_mat, sems.at[0]),
        pltpu.make_async_copy(heads_weight, heads_mat, sems.at[1]),
        pltpu.make_async_copy(proj_in, proj, sems.at[2]),
        pltpu.make_async_copy(ssm_in, ssm, sems.at[3]),
    ]
    start_all(copies)
    grad_branch[...] = grad_middle[...].astype(BF16)
    copies[0].wait()
    copies[1].wait()

    grad_mamba[...] = dot_nt(grad_branch[...], out_mat[...])
    grad_attended[...] = dot_nt(grad_branch[...], heads_mat[...])
    small = {
        1: kernel_grad,
        2: bias_grad,
        3: step_grad,
        4: decay_grad,
        5: skip_grad,
        6: mixer_grad,
    }
    for ref in small.values():
        ref[...] = jnp.zeros_like(ref)

    def add_small(slot, value):
        small[slot][...] += value

    copies[2].wait()
    copies[3].wait()

    def sequence(index, carry):
        rows = pl.ds(pl.multiple_of(index * LEN, LEN), LEN)
        grads = grad_attended[rows, :]
        attention_backward(proj, rows, cosine, sine, grads, grad_cat)
        mamba_backward(
            proj, rows, kernel, bias, step_bias, decay_log, skip, mixer_gain, pick, ssm,
            grad_mamba[rows, :], grad_cat, None, balance, touch, grad_active, add_small,
        )
        return carry

    lax.fori_loop(0, 2, sequence, 0)
    leaving = leave_all(
        (
            (grad_branch, grad_branch_out),
            (grad_cat, grad_cat_out),
            (kernel_grad, kernel_grad_out),
            (bias_grad, bias_grad_out),
            (step_grad, step_grad_out),
            (decay_grad, decay_grad_out),
            (skip_grad, skip_grad_out),
            (mixer_grad, mixer_grad_out),
        ),
        out_sems,
    )
    for copy in leaving:
        copy.wait()


def input_backward_kernel(earlier, active, *refs):
    @pl.when(active[0] == 1)
    def run():
        input_backward_body(*refs[:6], *refs[6 + earlier :])


def input_backward_body(
    grad_cat, grad_middle, x, packed, dt_weight, input_gain,
    grad_start_out, start_low_out, input_grad_out,
    grad_start, start_low, input_grad,
    cat, sems, out_sems,
):
    copies = [
        pltpu.make_async_copy(packed.at[:, pl.ds(16 * j, 16), :], cat.at[j], sems.at[j])
        for j in range(4)
    ]
    start_all(copies)
    grad_normed = dot_nt(grad_cat[:, T0:CAT], dt_weight[...])
    for j in range(4):
        copies[j].wait()
        part = dot_nt(grad_cat[:, 1024 * j : 1024 * j + 1024], flat(cat[j]))
        grad_normed = grad_normed + part
    state = x[...].astype(F32)
    grad_state, grad_gain = rms_backward(state, input_gain[...], grad_normed)
    input_grad[...] = grad_gain
    total = grad_middle[...] + grad_state
    grad_start[...] = total
    start_low[...] = total.astype(BF16)
    leaving = leave_all(
        ((grad_start, grad_start_out), (start_low, start_low_out), (input_grad, input_grad_out)),
        out_sems,
    )
    for copy in leaving:
        copy.wait()


VMEM = pl.BlockSpec(memory_space=pltpu.VMEM)
SMEM = pl.BlockSpec(memory_space=pltpu.SMEM)
ANY = pl.BlockSpec(memory_space=pl.ANY)
LIMIT = 60 * 1024 * 1024


def shape(rows, columns, dtype):
    return jax.ShapeDtypeStruct((rows, columns), dtype)


def scratch(*dims, dtype=BF16):
    return pltpu.VMEM(dims, dtype)


FEED_MATS = (
    scratch(4, 4, 4, 16, FEED),
    scratch(4, 4, 4, 16, FEED),
    scratch(4, 4, 4, 32, WIDTH),
)


def mirrored(shapes):
    return [pltpu.VMEM(s.shape, s.dtype) for s in shapes]


def run_forward(start, mats, small, rope):
    packed, dt_weight, *given, feeds = mats
    unpack = not given
    extra = (shape(INNER, WIDTH, BF16), shape(512, WIDTH, BF16))
    shapes = (
        shape(ROWS, WIDTH, BF16),
        shape(ROWS, WIDTH, BF16),
        shape(ROWS, CAT, F32),
        shape(ROWS, INNER, F32),
        shape(ROWS, INNER, BF16),
        shape(ROWS, 512, BF16),
        shape(ROWS, WIDTH, F32),
        shape(ROWS, WIDTH, BF16),
        shape(ROWS, FEED, F32),
        shape(ROWS, FEED, F32),
        shape(ROWS, FEED, BF16),
    )
    return pl.pallas_call(
        functools.partial(forward_kernel, unpack),
        out_shape=extra + shapes if unpack else shapes,
        in_specs=[VMEM, ANY, VMEM] + [ANY] * len(given) + [SMEM] + [ANY] * 9 + [VMEM] * 10,
        out_specs=(ANY,) * (len(shapes) + 2 * unpack),
        scratch_shapes=[
            *mirrored(shapes),
            scratch(4, 64, 16, 1024),
            *FEED_MATS,
            scratch(INNER, WIDTH),
            scratch(512, WIDTH),
            scratch(64, 32, WIDTH) if unpack else scratch(16, 128),
            pltpu.SemaphoreType.DMA((6,)),
            pltpu.SemaphoreType.DMA((len(shapes) + 2,)),
            pltpu.SemaphoreType.DMA((12,)),
        ],
        compiler_params=pltpu.CompilerParams(vmem_limit_bytes=LIMIT),
        cost_estimate=pl.CostEstimate(
            flops=2 * ROWS * 12_600_000, bytes_accessed=40_000_000, transcendentals=2_000_000
        ),
        name="forward",
    )(start, packed, dt_weight, *given, *feeds, *small, *rope)


def run_feed_backward(active, grad_top, mats, gate, upper, middle, feed_gain, earlier=()):
    shapes = (
        shape(ROWS, FEED, BF16),
        shape(ROWS, FEED, BF16),
        shape(ROWS, WIDTH, F32),
        shape(1, WIDTH, F32),
    )
    return pl.pallas_call(
        functools.partial(feed_backward_kernel, len(earlier)),
        out_shape=shapes,
        in_specs=[SMEM, VMEM, SMEM] + [ANY] * 12 + [VMEM] + [ANY] * len(earlier),
        out_specs=(ANY,) * len(shapes),
        scratch_shapes=[
            *mirrored(shapes),
            scratch(ROWS, FEED, dtype=F32),
            scratch(ROWS, FEED, dtype=F32),
            scratch(ROWS, WIDTH, dtype=F32),
            *FEED_MATS,
            pltpu.SemaphoreType.DMA((3,)),
            pltpu.SemaphoreType.DMA((4,)),
            pltpu.SemaphoreType.DMA((12,)),
        ],
        input_output_aliases={16 + k: k for k in range(len(earlier))},
        compiler_params=pltpu.CompilerParams(vmem_limit_bytes=LIMIT),
        cost_estimate=pl.CostEstimate(
            flops=2 * ROWS * 6_300_000, bytes_accessed=22_000_000, transcendentals=1_000_000
        ),
        name="feed_backward",
    )(active, grad_top, *mats[4], gate, upper, middle, feed_gain, *earlier)


def run_mix_backward(active, grad_middle, mats, proj, ssm, small, rope, pick, earlier=()):
    packed, dt_weight, out_weight, heads_weight, feeds = mats
    shapes = (
        shape(ROWS, WIDTH, BF16),
        shape(ROWS, CAT, BF16),
        shape(4, MIXED, F32),
        shape(1, MIXED, F32),
        shape(1, 128, F32),
        shape(1, 128, F32),
        shape(1, INNER, F32),
        shape(1, INNER, F32),
    )
    return pl.pallas_call(
        functools.partial(mix_backward_kernel, len(earlier)),
        out_shape=shapes,
        in_specs=[SMEM, VMEM] + [ANY] * 4 + [VMEM] * 9 + [ANY] * len(earlier),
        out_specs=(ANY,) * len(shapes),
        scratch_shapes=[
            *mirrored(shapes),
            scratch(ROWS, CAT, dtype=F32),
            scratch(ROWS, INNER, dtype=F32),
            scratch(INNER, WIDTH),
            scratch(512, WIDTH),
            scratch(ROWS, INNER, dtype=F32),
            scratch(ROWS, 512, dtype=F32),
            scratch(LEN, INNER, dtype=F32),
            scratch(LEN, INNER, dtype=F32),
            scratch(LEN, MIXED, dtype=F32),
            pltpu.SemaphoreType.DMA((4,)),
            pltpu.SemaphoreType.DMA((8,)),
        ],
        input_output_aliases={15 + k: k for k in range(len(earlier))},
        compiler_params=pltpu.CompilerParams(vmem_limit_bytes=LIMIT),
        cost_estimate=pl.CostEstimate(
            flops=2 * ROWS * 2_100_000, bytes_accessed=14_000_000, transcendentals=4_000_000
        ),
        name="mix_backward",
    )(
        active, grad_middle, out_weight, heads_weight, proj, ssm, *small[1:7], *rope, pick, *earlier
    )


def run_input_backward(active, grad_cat, grad_middle, start, mats, input_gain, earlier=()):
    shapes = (shape(ROWS, WIDTH, F32), shape(ROWS, WIDTH, BF16), shape(1, WIDTH, F32))
    return pl.pallas_call(
        functools.partial(input_backward_kernel, len(earlier)),
        out_shape=shapes,
        in_specs=[SMEM, VMEM, VMEM, VMEM, ANY, VMEM, VMEM] + [ANY] * len(earlier),
        out_specs=(ANY,) * len(shapes),
        scratch_shapes=[
            *mirrored(shapes),
            scratch(4, 64, 16, 1024),
            pltpu.SemaphoreType.DMA((4,)),
            pltpu.SemaphoreType.DMA((3,)),
        ],
        input_output_aliases={7 + k: k for k in range(len(earlier))},
        compiler_params=pltpu.CompilerParams(vmem_limit_bytes=LIMIT),
        cost_estimate=pl.CostEstimate(
            flops=2 * ROWS * 4_200_000, bytes_accessed=13_000_000, transcendentals=1000
        ),
        name="input_backward",
    )(active, grad_cat, grad_middle, start, *mats[:2], input_gain, *earlier)


def rope_tables():
    position = jnp.arange(LEN).astype(F32)
    inverse = 10000.0 ** (-(jnp.arange(32).astype(F32) * 2.0) / 64)
    angle = position[:, None] * inverse[None, :]
    cosine = jnp.tile(jnp.cos(angle), (1, 16))
    sine = jnp.sin(angle)
    return cosine, jnp.tile(jnp.concatenate([-sine, sine], axis=1), (1, 8))


def head_pick():
    lanes = lax.broadcasted_iota(jnp.int32, (INNER, 128), 0) // 64
    return (lanes == lax.broadcasted_iota(jnp.int32, (INNER, 128), 1)).astype(BF16)


def prepared_small(pieces):
    input_gain, kernel, bias, step_bias, decay_log, skip, mixer_gain, feed_gain = pieces

    def padded(v):
        return jnp.pad(v, (0, 128 - HEADS))[None]

    return (
        input_gain[None],
        kernel,
        bias[None],
        padded(step_bias),
        padded(decay_log),
        jnp.repeat(skip, 64)[None],
        mixer_gain[None],
        feed_gain[None],
    )


FIRST = (1, 0, 3, 2)
SECOND = (3, 2, 1, 0)


def partners(axis, turn):
    me = lax.axis_index(axis)
    near, far = me + 1 - 2 * lax.rem(me, 2), 3 - me
    flipped = lax.rem(lax.axis_index("section") + turn, 2) == 1
    found = (jnp.where(flipped, far, near), jnp.where(flipped, near, far))
    swaps = []
    for step in range(2):
        tables = [(FIRST, SECOND)[(core + turn + step) % 2] for core in range(2)]
        swaps.append([(4 * c + i, 4 * c + tables[c][i]) for c in range(2) for i in range(4)])
    return me, found, swaps


def exchange(array, axis, pairs):
    return lax.ppermute(array, ("section", axis), pairs)


def first_sent(part, axis, turn):
    me, (one, two), swaps = partners(axis, turn)
    return part([one, lax.rem(me + 2, 4)]).astype(BF16)


def first_got(sent, axis, turn):
    return exchange(sent, axis, partners(axis, turn)[2][0])


def handed_on(part, got, axis, turn):
    me, (one, two), swaps = partners(axis, turn)
    return (part([two]) + got[got.shape[0] // 2 :].astype(F32)).astype(BF16)


def totalled(part, got, handed, axis, turn):
    me, found, (swap_one, swap_two) = partners(axis, turn)
    last = exchange(handed, axis, swap_two)
    return part([me]) + got[: got.shape[0] // 2].astype(F32) + last.astype(F32)


def product_of(left, right, place):
    blocks = left.reshape(4, 4, 4, left.shape[0] // 64, left.shape[1])

    def part(places):
        picked = [lax.dynamic_index_in_dim(blocks, p, place, keepdims=False) for p in places]
        return dot(jnp.concatenate(picked, axis=0).reshape(-1, left.shape[1]), right)

    return part


def quarters_of(array, dim):
    def part(places):
        picked = [lax.dynamic_index_in_dim(array, p, dim, keepdims=False) for p in places]
        return jnp.concatenate(picked, axis=0).reshape(-1, array.shape[-1]).astype(F32)

    return part


def summed_on(array, axis, dim, turn):
    part = quarters_of(array, dim)
    got = first_got(first_sent(part, axis, turn), axis, turn)
    return totalled(part, got, handed_on(part, got, axis, turn), axis, turn)


def second_summed(parts, order, depth):
    array = jnp.concatenate([p.astype(BF16) for p in parts], axis=1)
    width = array.shape[1]
    rest = [0, 1, 2]
    rest.remove(order[0])
    array = array.reshape(4, 4, depth, width)
    array = summed_on(array, DP[order[1]], rest.index(order[1]), 0).astype(BF16)
    return array.reshape(4, depth, width)


def gathered_on(array, axis):
    me, (one, two), (swap_one, swap_two) = partners(axis, 0)
    got = exchange(array, axis, swap_one)
    far = exchange(jnp.stack([array, got]), axis, swap_two)
    return (array, got, far), (me, one, two, lax.rem(me + 2, 4))


def placed(blocks, places, dim):
    own, got, far = blocks
    whole = jnp.zeros((*own.shape[:dim], 4, *own.shape[dim:]), own.dtype)
    for block, place in zip((own, got, far[0], far[1]), places):
        whole = lax.dynamic_update_index_in_dim(whole, block, place, dim)
    return whole


def gathered(block, order):
    block = placed(*gathered_on(block, DP[order[2]]), 0)
    block = placed(*gathered_on(block, DP[order[1]]), 0 if order[1] < order[2] else 1)
    return gathered_on(block, DP[order[0]])


def column_blocks(matrix):
    return [matrix[:, at : at + 1024] for at in range(0, matrix.shape[1], 1024)]


def on_device(
    layer_input,
    out_grad,
    in_weight,
    query_weight,
    key_weight,
    value_weight,
    out_weight,
    heads_weight,
    gate_weight,
    up_weight,
    down_weight,
    *pieces,
):
    micro, part, width = layer_input.shape
    rows = micro * part
    cat = jnp.concatenate(
        [query_weight[0], key_weight[0], value_weight[0], in_weight[0, :, :3328]], axis=1
    )
    steps = jnp.pad(in_weight[0, :, 3328:].reshape(1, -1), ((0, 7), (0, 1024 - 16 * HEADS)))
    own = jnp.concatenate(
        [
            *column_blocks(cat),
            out_weight[0],
            heads_weight[0],
            steps,
        ],
        axis=0,
    )
    packed = lax.all_gather(own, DP, axis=0, tiled=False)
    dt_weight = packed[:, DT0, : 16 * HEADS].reshape(WIDTH, HEADS)
    feeds = [
        gathered(weight[0], order)
        for weight, order in (
            (gate_weight, (0, 1, 2)),
            (up_weight, (1, 2, 0)),
            (down_weight, (2, 0, 1)),
        )
    ]
    places = jnp.stack([place for blocks, found in feeds for place in found]).astype(jnp.int32)
    mats = (
        packed,
        jnp.pad(dt_weight, ((0, 0), (0, 128 - HEADS))),
        (places, *(piece for blocks, found in feeds for piece in blocks)),
    )
    small = prepared_small([piece[0] for piece in pieces])
    rope = rope_tables()
    pick = head_pick()
    first = lax.axis_index("section") == 0

    start_low = layer_input.reshape(rows, width)
    out_mat, heads_mat, *kept_low = run_forward(start_low, mats, small, rope)
    mats = (*mats[:2], out_mat, heads_mat, mats[2])
    start_high = lax.ppermute(kept_low[0], "section", [(0, 1)])
    kept_high = run_forward(start_high, mats, small, rope)
    layer_outputs = jnp.where(first, kept_low[0], kept_high[0]).reshape(1, micro, part, width)

    on_high = jnp.where(first, 0, 1).astype(jnp.int32).reshape(1)
    on_low = 1 - on_high
    top_high = out_grad.reshape(rows, width)
    feed_high = run_feed_backward(
        on_high, top_high, mats, kept_high[8], kept_high[9], kept_high[6], small[7]
    )
    mix_high = run_mix_backward(
        on_high, feed_high[2], mats, kept_high[2], kept_high[3], small, rope, pick
    )
    input_high = run_input_backward(
        on_high, mix_high[1], feed_high[2], start_high, mats, small[0]
    )
    slots = (1, 4, 5, 7, 10)
    low_top, *tied = lax.optimization_barrier((input_high[1], *(kept_high[s] for s in slots)))
    tied = dict(zip(slots, tied))
    top_low = lax.ppermute(low_top, "section", [(1, 0)])

    def chosen(slot):
        return jnp.where(first, kept_low[slot], tied[slot])

    normed_t, ffin_t, hidden_t = (chosen(slot).T for slot in (1, 7, 10))
    joined_t = jnp.concatenate(
        [chosen(4).T.reshape(64, 24, rows), chosen(5).T.reshape(64, 8, rows)], axis=1
    ).reshape(2048, rows)

    feed = run_feed_backward(
        on_low, top_low, mats, kept_low[8], kept_low[9], kept_low[6], small[7], feed_high
    )
    grad_gate, grad_upper, grad_middle, feed_grad = feed
    grad_low = jnp.where(first, top_low, top_high)
    grad_low, grad_gate, grad_upper = lax.optimization_barrier((grad_low, grad_gate, grad_upper))
    orders = ((2, 0, 1), (0, 1, 2), (1, 2, 0))
    axes = [DP[order[0]] for order in orders]
    products = [
        product_of(left, right, order[0])
        for left, right, order in zip(
            (hidden_t, ffin_t, ffin_t), (grad_low, grad_gate, grad_upper), orders
        )
    ]
    sents = [first_sent(p, axis, 0) for p, axis in zip(products, axes)]
    grad_middle, *sents = lax.optimization_barrier((grad_middle, *sents))
    gots = [first_got(sent, axis, 0) for sent, axis in zip(sents, axes)]
    mix = run_mix_backward(
        on_low, grad_middle, mats, kept_low[2], kept_low[3], small, rope, pick, mix_high
    )
    grad_branch, grad_cat, *small_grads = mix
    mix_products = [
        product_of(left, right, order[0])
        for left, right, order in zip(
            (joined_t, normed_t, normed_t),
            (grad_branch, grad_cat[:, :2048], grad_cat[:, 2048:]),
            orders,
        )
    ]
    mix_sents = [first_sent(p, axis, 1) for p, axis in zip(mix_products, axes)]
    pending = lax.optimization_barrier((*gots, *mix_sents))
    gots, mix_sents = pending[:3], pending[3:]
    mix_gots = [first_got(sent, axis, 1) for sent, axis in zip(mix_sents, axes)]
    handed = [handed_on(p, got, axis, 0) for p, got, axis in zip(products, gots, axes)]
    last_middle, *pending = lax.optimization_barrier(
        (grad_middle, grad_low, grad_gate, grad_upper, grad_branch, grad_cat, *handed)
    )
    rights, (late_branch, late_cat), handed = pending[:3], pending[3:5], pending[5:]
    products = [
        product_of(left, right, order[0])
        for left, right, order in zip((hidden_t, ffin_t, ffin_t), rights, orders)
    ]
    mix_products = [
        product_of(left, right, order[0])
        for left, right, order in zip(
            (joined_t, normed_t, normed_t),
            (late_branch, late_cat[:, :2048], late_cat[:, 2048:]),
            orders,
        )
    ]
    feed_parts = [
        totalled(p, got, hand, axis, 0)
        for p, got, hand, axis in zip(products, gots, handed, axes)
    ]
    mix_parts = [
        totalled(p, got, handed_on(p, got, axis, 1), axis, 1)
        for p, got, axis in zip(mix_products, mix_gots, axes)
    ]
    grad_start, unused, input_grad = run_input_backward(
        on_low, grad_cat, last_middle, start_low, mats, small[0], input_high
    )
    small_grads = [input_grad, *small_grads]
    input_g, kernel_g, bias_g, step_g, decay_g, skip_g, mixer_g = small_grads
    small_grads = (
        input_g[0],
        kernel_g,
        bias_g[0],
        step_g[0, :HEADS],
        decay_g[0, :HEADS],
        skip_g.reshape(HEADS, 64).sum(axis=1),
        mixer_g[0],
        feed_grad[0],
    )
    vector = jnp.concatenate([piece.reshape(-1) for piece in small_grads])
    vector = jnp.pad(vector, (0, -vector.shape[0] % 1024)).reshape(-1, 128)
    vectors = lax.all_gather(vector.astype(BF16), DP, axis=0, tiled=False)
    seconds = [
        second_summed(pair, order, depth)
        for pair, order, depth in zip(zip(feed_parts, mix_parts), orders, (32, 16, 16))
    ]
    axes = [DP[order[2]] for order in orders]
    quarters = [quarters_of(array, 0) for array in seconds]
    gots = [first_got(first_sent(p, axis, 0), axis, 0) for p, axis in zip(quarters, axes)]
    handed = [handed_on(p, got, axis, 0) for p, got, axis in zip(quarters, gots, axes)]
    vectors, *unused = lax.optimization_barrier((vectors, *handed))
    total = jnp.sum(vectors.astype(F32), axis=0).reshape(-1)
    rows_grad, gate_cat, up_cat = (
        totalled(p, got, hand, axis, 0)
        for p, got, hand, axis in zip(quarters, gots, handed, axes)
    )
    down_grad, joined_grad = rows_grad[:, :WIDTH], rows_grad[:, WIDTH:]
    gate_grad, up_grad = gate_cat[:, :FEED], up_cat[:, :FEED]
    cat_grad = jnp.concatenate([gate_cat[:, FEED:], up_cat[:, FEED:]], axis=1)

    summed, at = ([], 0)
    for piece in small_grads:
        summed.append(total[at : at + piece.size].reshape(1, *piece.shape))
        at += piece.size
    return (
        layer_outputs,
        grad_start.reshape(1, micro, part, width),
        cat_grad[None, :, Z0 : T0 + HEADS],
        cat_grad[None, :, :K0],
        cat_grad[None, :, K0:V0],
        cat_grad[None, :, V0:Z0],
        joined_grad[None, :24],
        joined_grad[None, 24:],
        gate_grad[None],
        up_grad[None],
        down_grad[None],
        *summed,
    )


def solution(mesh):
    torus = Mesh(
        mesh.devices.reshape(mesh.shape["section"], 4, 4, 4), ("section", "dp_0", "dp_1", "dp_2")
    )
    in_specs = (
        P(None, DP, None),
        P(None, DP, None),
        P("section", DP, None),
        P("section", DP, None),
        P("section", DP, None),
        P("section", DP, None),
        P("section", DP, None),
        P("section", DP, None),
        P("section", DP, None),
        P("section", DP, None),
        P("section", DP, None),
        P("section", None),
        P("section", None, None),
        P("section", None),
        P("section", None),
        P("section", None),
        P("section", None),
        P("section", None),
        P("section", None),
    )
    out_specs = (
        P("section", None, DP, None),
        P("section", None, DP, None),
        P("section", DP, None),
        P("section", DP, None),
        P("section", DP, None),
        P("section", DP, None),
        P("section", DP, None),
        P("section", DP, None),
        P("section", DP, None),
        P("section", DP, None),
        P("section", DP, None),
        P("section", None),
        P("section", None, None),
        P("section", None),
        P("section", None),
        P("section", None),
        P("section", None),
        P("section", None),
        P("section", None),
    )
    return jax.shard_map(
        on_device, mesh=torus, in_specs=in_specs, out_specs=out_specs, check_vma=False
    )
```

```python
import functools

import jax
import jax.numpy as jnp
from jax import lax
from jax.experimental import pallas as pl
from jax.experimental.pallas import tpu as pltpu
from jax.sharding import Mesh
from jax.sharding import PartitionSpec as P

LEN = 128
ROWS = 256
WIDTH = 1024
FEED = 2048
INNER = 1536
MIXED = 1792
CAT = 4224
HEADS = 24
DP = ("dp_0", "dp_1", "dp_2")
F32 = jnp.float32
BF16 = jnp.bfloat16
HIDE = -1e30
Q0, K0, V0, Z0, X0, T0 = 0, 512, 640, 768, 2304, 4096
OUT0, PACKED = 64, 96


def dot(left, right):
    return jnp.dot(left, right, preferred_element_type=F32)


def dot_nt(left, right):
    return lax.dot_general(left, right, (((1,), (1,)), ((), ())), preferred_element_type=F32)


def dot_tn(left, right):
    return lax.dot_general(left, right, (((0,), (0,)), ((), ())), preferred_element_type=F32)


def dot_full(left, right):
    return jnp.dot(left, right, precision=lax.Precision.HIGHEST, preferred_element_type=F32)


def iota(shape, dim):
    return lax.broadcasted_iota(jnp.int32, shape, dim)


def sigmoid(v):
    return 1.0 / (1.0 + jnp.exp(-v))


def softplus(v):
    return jnp.maximum(v, 0.0) + jnp.log(1.0 + jnp.exp(-jnp.abs(v)))


def swap_halves(v):
    width = v.shape[1]
    near = lax.rem(iota(v.shape, 1), 64) < 32
    return jnp.where(near, pltpu.roll(v, width - 32, 1), pltpu.roll(v, 32, 1))


def shifted_down(v, by):
    if by == 0:
        return v
    return jnp.where(iota(v.shape, 0) >= by, pltpu.roll(v, by, 0), 0.0)


def shifted_up(v, by):
    if by == 0:
        return v
    rows = v.shape[0]
    return jnp.where(iota(v.shape, 0) < rows - by, pltpu.roll(v, rows - by, 0), 0.0)


def rms(v):
    return lax.rsqrt(jnp.mean(v * v, axis=-1, keepdims=True) + 1e-05)


def rms_backward(v, gain, grad):
    scale = rms(v)
    gained = grad * gain
    inner = jnp.mean(gained * v, axis=-1, keepdims=True)
    grad_v = scale * gained - v * (scale * scale * scale * inner)
    return grad_v, jnp.sum(grad * v * scale, axis=0, keepdims=True)


def left_half():
    return iota((LEN, 128), 1) < 64


def both_halves(v, group, left):
    turned = pltpu.roll(v, 64, 1)
    return jnp.where(left, v, turned) if group == 0 else jnp.where(left, turned, v)


def stacked(pairs, left):
    parts = []
    for pair in pairs:
        parts.append(jnp.where(left, pair, 0.0))
        parts.append(jnp.where(left, 0.0, pair))
    return jnp.concatenate(parts, axis=0).astype(BF16)


def unstacked(rows, index, left):
    low = rows[2 * index * LEN : (2 * index + 1) * LEN]
    high = rows[(2 * index + 1) * LEN : (2 * index + 2) * LEN]
    return jnp.where(left, low, high)


def attention_parts(proj, rows, cosine, sine):
    left = left_half()
    query = proj[rows, Q0:K0]
    query = query * cosine[...] + swap_halves(query) * sine[...]
    key = proj[rows, K0:V0]
    key = key * cosine[:, :128] + swap_halves(key) * sine[:, :128]
    value = proj[rows, V0:Z0]
    groups = []
    for group in range(2):
        pairs = [query[:, 128 * p : 128 * p + 128] for p in (2 * group, 2 * group + 1)]
        queries = stacked(pairs, left)
        keys = both_halves(key, group, left).astype(BF16)
        values = both_halves(value, group, left).astype(BF16)
        scores = dot_nt(queries, keys) * 0.125
        time = lax.rem(iota(scores.shape, 0), LEN)
        scores = jnp.where(iota(scores.shape, 1) <= time, scores, HIDE)
        top = jnp.max(scores, axis=-1, keepdims=True)
        expo = jnp.exp(scores - top)
        probs = expo / jnp.sum(expo, axis=-1, keepdims=True)
        groups.append((queries, keys, values, probs))
    return left, groups


def attention_forward(proj, rows, cosine, sine, attended):
    left, groups = attention_parts(proj, rows, cosine, sine)
    for group, (queries, keys, values, probs) in enumerate(groups):
        mixed = dot(probs.astype(BF16), values)
        for index in range(2):
            at = 256 * group + 128 * index
            attended[rows, at : at + 128] = unstacked(mixed, index, left).astype(BF16)


def attention_backward(proj, rows, cosine, sine, grad_attended, grad_cat):
    left, groups = attention_parts(proj, rows, cosine, sine)
    key_parts, value_parts = [], []
    for group, (queries, keys, values, probs) in enumerate(groups):
        pairs = [grad_attended[:, 128 * p : 128 * p + 128] for p in (2 * group, 2 * group + 1)]
        grads = stacked(pairs, left)
        grad_values = dot_tn(probs.astype(BF16), grads)
        grad_probs = dot_nt(grads, values)
        inner = jnp.sum(probs * grad_probs, axis=-1, keepdims=True)
        grad_scores = (probs * (grad_probs - inner)).astype(BF16)
        grad_queries = dot(grad_scores, keys) * 0.125
        grad_keys = dot_tn(grad_scores, queries) * 0.125
        for index in range(2):
            at = 256 * group + 128 * index
            grad = unstacked(grad_queries, index, left)
            grad = grad * cosine[:, :128] - swap_halves(grad) * sine[:, :128]
            grad_cat[rows, at : at + 128] = grad.astype(BF16)
        key_parts.append(grad_keys + pltpu.roll(grad_keys, 64, 1))
        value_parts.append(grad_values + pltpu.roll(grad_values, 64, 1))
    grad = jnp.where(left, key_parts[0], key_parts[1])
    grad = grad * cosine[:, :128] - swap_halves(grad) * sine[:, :128]
    grad_cat[rows, K0:V0] = grad.astype(BF16)
    grad_cat[rows, V0:Z0] = jnp.where(left, value_parts[0], value_parts[1]).astype(BF16)


def mamba_parts(proj, rows, kernel, bias, step_bias, decay_log):
    mixed = proj[rows, X0:T0]
    total = bias[...] + mixed * kernel[3:4, :]
    for tap in range(3):
        total = total + shifted_down(mixed, 3 - tap) * kernel[tap : tap + 1, :]
    active = total * sigmoid(total)
    step = softplus(proj[rows, T0:CAT] + step_bias[...])
    rate = -step * jnp.exp(decay_log[...])
    earlier = (iota((LEN, LEN), 0) >= iota((LEN, LEN), 1)).astype(F32)
    cumul = dot_full(earlier, rate)
    state_in = active[:, INNER : INNER + 128].astype(BF16)
    state_out = active[:, INNER + 128 :].astype(BF16)
    return mixed, total, active, step, rate, cumul, state_in, state_out


def stepped(step, pair, left):
    return jnp.where(left, step[:, 2 * pair : 2 * pair + 1], step[:, 2 * pair + 1 : 2 * pair + 2])


def mamba_forward(proj, rows, kernel, bias, step_bias, decay_log, skip, gain, ssm, mamba):
    left = left_half()
    parts = mamba_parts(proj, rows, kernel, bias, step_bias, decay_log)
    mixed, total, active, step, rate, cumul, state_in, state_out = parts
    across = cumul.T
    hidden = jnp.where(iota((LEN, LEN), 0) >= iota((LEN, LEN), 1), 0.0, HIDE)
    meeting = dot_nt(state_out, state_in)
    for pair in range(HEADS // 2):
        at = 128 * pair
        inputs = active[:, at : at + 128]
        scaled = (inputs * stepped(step, pair, left)).astype(BF16)
        mixing = []
        for head in (2 * pair, 2 * pair + 1):
            spread = cumul[:, head : head + 1] - across[head : head + 1, :] + hidden
            mixing.append((meeting * jnp.exp(spread)).astype(BF16))
        both = dot(jnp.concatenate(mixing, axis=0), scaled)
        out = unstacked(both, 0, left) + skip[:, at : at + 128] * inputs
        ssm[rows, at : at + 128] = out
    z = proj[rows, Z0:X0]
    gated = ssm[rows, :] * (z * sigmoid(z))
    mamba[rows, :] = (gated * rms(gated) * gain[...]).astype(BF16)


def head_sums(v, pick):
    high = v.astype(BF16)
    low = (v - high.astype(F32)).astype(BF16)
    return dot(high, pick) + dot(low, pick)


def mamba_backward(
    proj, rows, kernel, bias, step_bias, decay_log, skip, gain, pick, ssm, grad_mamba, grad_cat,
    across_scratch, balance_scratch, touch_scratch, grad_active, add_small,
):
    left = left_half()
    parts = mamba_parts(proj, rows, kernel, bias, step_bias, decay_log)
    mixed, total, active, step, rate, cumul, state_in, state_out = parts
    across = cumul.T
    hidden = jnp.where(iota((LEN, LEN), 1) >= iota((LEN, LEN), 0), 0.0, HIDE)
    meeting = dot_nt(state_out, state_in).T
    z = proj[rows, Z0:X0]
    out = ssm[rows, :]
    gate = sigmoid(z)
    gated = out * (z * gate)
    grad_gated, grad_gain = rms_backward(gated, gain[...], grad_mamba)
    add_small(6, grad_gain)
    grad_cat[rows, Z0:X0] = (grad_gated * out * (gate * (1.0 + z * (1.0 - gate)))).astype(BF16)
    grad_out = grad_gated * (z * gate)
    add_small(5, jnp.sum(grad_out * active[:, :INNER], axis=0, keepdims=True))
    grad_meeting = jnp.zeros((LEN, LEN), F32)
    for pair in range(HEADS // 2):
        at = 128 * pair
        inputs = active[:, at : at + 128]
        steps = stepped(step, pair, left)
        scaled = (inputs * steps).astype(BF16)
        grad_pair = grad_out[:, at : at + 128]
        grad_low = grad_pair.astype(BF16)
        halves = jnp.concatenate(
            [jnp.where(left, scaled, jnp.zeros_like(scaled)), jnp.where(left, jnp.zeros_like(scaled), scaled)],
            axis=0,
        )
        grad_mixing = dot_nt(halves, grad_low)
        mixing = []
        for place, head in enumerate((2 * pair, 2 * pair + 1)):
            spread = across[head : head + 1, :] - cumul[:, head : head + 1] + hidden
            decay = jnp.exp(spread)
            mixing.append((meeting * decay).astype(BF16))
            grad_meeting = grad_meeting + grad_mixing[LEN * place : LEN * place + LEN] * decay
        both = dot(jnp.concatenate(mixing, axis=0), grad_low)
        grad_scaled = unstacked(both, 0, left)
        skips = skip[:, at : at + 128]
        grad_active[:, at : at + 128] = grad_scaled * steps + skips * grad_pair
        touch_scratch[:, at : at + 128] = grad_scaled * inputs
        balance_scratch[:, at : at + 128] = grad_low.astype(F32) * (
            out[:, at : at + 128] - skips * inputs
        ) - scaled.astype(F32) * grad_scaled
    grad_low = grad_meeting.astype(BF16)
    grad_active[:, INNER : INNER + 128] = dot(grad_low, state_out)
    grad_active[:, INNER + 128 :] = dot_tn(grad_low, state_in)
    later = (iota((LEN, LEN), 1) >= iota((LEN, LEN), 0)).astype(F32)
    grad_rate = dot_full(later, head_sums(balance_scratch[...], pick[...]))
    add_small(4, jnp.sum(grad_rate * rate, axis=0, keepdims=True))
    grad_step = head_sums(touch_scratch[...], pick[...]) - grad_rate * jnp.exp(decay_log[...])
    grad_dt = grad_step * sigmoid(proj[rows, T0:CAT] + step_bias[...])
    add_small(3, jnp.sum(grad_dt, axis=0, keepdims=True))
    grad_cat[rows, T0:CAT] = grad_dt.astype(BF16)
    slope = sigmoid(total)
    grad_total = grad_active[...] * (slope * (1.0 + total * (1.0 - slope)))
    add_small(2, jnp.sum(grad_total, axis=0, keepdims=True))
    grad_mixed = grad_total * kernel[3:4, :]
    taps = []
    for tap in range(4):
        taps.append(jnp.sum(grad_total * shifted_down(mixed, 3 - tap), axis=0, keepdims=True))
        if tap < 3:
            grad_mixed = grad_mixed + shifted_up(grad_total, 3 - tap) * kernel[tap : tap + 1, :]
    add_small(1, jnp.concatenate(taps, axis=0))
    grad_cat[rows, X0:T0] = grad_mixed.astype(BF16)


def flat(block):
    return block.reshape(block.shape[0] * block.shape[1], block.shape[2])


def start_all(copies):
    for copy in copies:
        copy.start()


def feed_copies(places, pieces, buffers, sems):
    copies = []
    for k, buffer in enumerate(buffers):
        own, got, far = pieces[3 * k : 3 * k + 3]
        for q, source in enumerate((own, got, far.at[0], far.at[1])):
            target = buffer.at[(slice(None),) * k + (places[4 * k + q],)]
            copies.append(pltpu.make_async_copy(source, target, sems.at[4 * k + q]))
    return copies


def rows_of(block):
    return block.reshape(-1, block.shape[-1])


def forward_kernel(unpack, x, packed, *refs):
    if unpack:
        given, results = (None, None), refs[20:23]
        rest = refs[:20] + refs[23:]
    else:
        given, results = refs[:2], (None, None, None)
        rest = refs[2:]
    forward_body(unpack, x, packed, *given, *results, *rest)


def forward_body(
    unpack, x, packed, out_weight, heads_weight, dt_result, out_result, heads_result,
    places, gate_own, gate_got, gate_far, up_own, up_got, up_far, down_own, down_got, down_far,
    input_gain, kernel, bias, step_bias, decay_log, skip,
    mixer_gain, feed_gain, cosine, sine,
    result_out, normed_out, proj_out, ssm_out, mamba_out, attended_out, middle_out, ffin_out, gate_out,
    upper_out, hidden_out,
    result, normed, proj, ssm, mamba, attended, middle, ffin, gate, upper, hidden,
    cat, gate_mat, up_mat, down_mat, out_mat, heads_mat, mixed, dt_mat, sems, out_sems, feed_sems,
):
    leaving = []

    def leave(*pairs):
        for source, target in pairs:
            copy = pltpu.make_async_copy(source, target, out_sems.at[len(leaving)])
            copy.start()
            leaving.append(copy)

    copies = [
        pltpu.make_async_copy(packed.at[:, pl.ds(16 * j, 16), :], cat.at[j], sems.at[j])
        for j in range(4)
    ]
    if unpack:
        copies.append(pltpu.make_async_copy(packed.at[:, pl.ds(OUT0, 32), :], mixed, sems.at[4]))
    else:
        copies.append(pltpu.make_async_copy(out_weight, out_mat, sems.at[4]))
        copies.append(pltpu.make_async_copy(heads_weight, heads_mat, sems.at[5]))
    pieces = (gate_own, gate_got, gate_far, up_own, up_got, up_far, down_own, down_got, down_far)
    feeds = feed_copies(places, pieces, (gate_mat, up_mat, down_mat), feed_sems)
    start_all(copies + feeds)
    state = x[...].astype(F32)
    normed[...] = (state * rms(state) * input_gain[...]).astype(BF16)
    for j in range(4):
        copies[j].wait()
        proj[:, 1024 * j : 1024 * j + 1024] = dot(normed[...], flat(cat[j]))
    for copy in feeds[4:8]:
        copy.wait()
    dt_mat[...] = rows_of(up_mat[:, :, :, :, FEED:])
    proj[:, T0:CAT] = dot(normed[...], dt_mat[...])
    leave((normed, normed_out), (proj, proj_out))

    def sequence(index, carry):
        rows = pl.ds(pl.multiple_of(index * LEN, LEN), LEN)
        attention_forward(proj, rows, cosine, sine, attended)
        mamba_forward(proj, rows, kernel, bias, step_bias, decay_log, skip, mixer_gain, ssm, mamba)
        return carry

    lax.fori_loop(0, 2, sequence, 0)
    leave((ssm, ssm_out), (mamba, mamba_out), (attended, attended_out))
    for copy in copies[4:]:
        copy.wait()
    if unpack:
        wide = mixed[...].astype(F32)
        out_mat[...] = wide[:, :24].reshape(INNER, WIDTH).astype(BF16)
        heads_mat[...] = wide[:, 24:].reshape(512, WIDTH).astype(BF16)
        leave((dt_mat, dt_result), (out_mat, out_result), (heads_mat, heads_result))

    part = dot(mamba[...], out_mat[...]) + dot(attended[...], heads_mat[...])
    middle[...] = x[...].astype(F32) + part
    value = middle[...]
    ffin[...] = (value * rms(value) * feed_gain[...]).astype(BF16)
    leave((middle, middle_out), (ffin, ffin_out))
    for copy in feeds[:4]:
        copy.wait()

    for half in range(2):
        at = slice(1024 * half, 1024 * half + 1024)
        low = dot(ffin[...], rows_of(gate_mat[:, :, :, :, at]))
        high = dot(ffin[...], rows_of(up_mat[:, :, :, :, at]))
        gate[:, at] = low
        upper[:, at] = high
        hidden[:, at] = (low * sigmoid(low) * high).astype(BF16)
    leave((gate, gate_out), (upper, upper_out), (hidden, hidden_out))
    for copy in feeds[8:]:
        copy.wait()

    result[...] = (middle[...] + dot(hidden[...], rows_of(down_mat[...]))).astype(BF16)
    leave((result, result_out))
    for copy in leaving:
        copy.wait()


def leave_all(pairs, sems):
    copies = [
        pltpu.make_async_copy(source, target, sems.at[k]) for k, (source, target) in enumerate(pairs)
    ]
    start_all(copies)
    return copies


def feed_backward_kernel(earlier, active, *refs):
    @pl.when(active[0] == 1)
    def run():
        feed_backward_body(*refs[:15], *refs[15 + earlier :])


def feed_backward_body(
    grad_top, places, gate_own, gate_got, gate_far, up_own, up_got, up_far, down_own, down_got, down_far,
    gate_in, upper_in, middle_in, feed_gain,
    grad_gate_out, grad_upper_out, grad_middle_out, feed_grad_out,
    grad_gate, grad_upper, grad_middle, feed_grad,
    gate, upper, middle, gate_mat, up_mat, down_mat, sems, out_sems, feed_sems,
):
    inputs = [
        pltpu.make_async_copy(gate_in, gate, sems.at[0]),
        pltpu.make_async_copy(upper_in, upper, sems.at[1]),
        pltpu.make_async_copy(middle_in, middle, sems.at[2]),
    ]
    pieces = (gate_own, gate_got, gate_far, up_own, up_got, up_far, down_own, down_got, down_far)
    feeds = feed_copies(places, pieces, (gate_mat, up_mat, down_mat), feed_sems)
    start_all(feeds[8:] + inputs + feeds[:8])
    for copy in feeds[8:]:
        copy.wait()

    for half in range(2):
        at = slice(1024 * half, 1024 * half + 1024)
        grad_hidden = dot_nt(grad_top[...], rows_of(down_mat[2 * half : 2 * half + 2]))
        if half == 0:
            inputs[0].wait()
            inputs[1].wait()
        low, high = gate[:, at], upper[:, at]
        slope = sigmoid(low)
        grad_upper[:, at] = (grad_hidden * (low * slope)).astype(BF16)
        part = grad_hidden * high * (slope * (1.0 + low * (1.0 - slope)))
        grad_gate[:, at] = part.astype(BF16)
    leaving = leave_all(((grad_gate, grad_gate_out), (grad_upper, grad_upper_out)), out_sems)
    for copy in feeds[:8]:
        copy.wait()

    grad_ffin = dot_nt(grad_gate[...], rows_of(gate_mat[...]))
    grad_ffin = grad_ffin + dot_nt(grad_upper[...], rows_of(up_mat[:, :, :, :, :FEED]))
    inputs[2].wait()
    grad_part, grad_gain = rms_backward(middle[...], feed_gain[...], grad_ffin)
    feed_grad[...] = grad_gain
    grad_middle[...] = grad_top[...].astype(F32) + grad_part
    leaving += leave_all(
        ((grad_middle, grad_middle_out), (feed_grad, feed_grad_out)), out_sems.at[pl.ds(2, 2)]
    )
    for copy in leaving:
        copy.wait()


def mix_backward_kernel(earlier, active, *refs):
    @pl.when(active[0] == 1)
    def run():
        mix_backward_body(*refs[:14], *refs[14 + earlier :])


def mix_backward_body(
    grad_middle, out_weight, heads_weight, proj_in, ssm_in, kernel, bias,
    step_bias, decay_log, skip, mixer_gain, cosine, sine, pick,
    grad_branch_out, grad_cat_out, kernel_grad_out, bias_grad_out,
    step_grad_out, decay_grad_out, skip_grad_out, mixer_grad_out,
    grad_branch, grad_cat, kernel_grad, bias_grad, step_grad, decay_grad,
    skip_grad, mixer_grad,
    proj, ssm,
    out_mat, heads_mat, grad_mamba, grad_attended, balance, touch, grad_active, sems,
    out_sems,
):
    copies = [
        pltpu.make_async_copy(out_weight, out_mat, sems.at[0]),
        pltpu.make_async_copy(heads_weight, heads_mat, sems.at[1]),
        pltpu.make_async_copy(proj_in, proj, sems.at[2]),
        pltpu.make_async_copy(ssm_in, ssm, sems.at[3]),
    ]
    start_all(copies)
    grad_branch[...] = grad_middle[...].astype(BF16)
    copies[0].wait()
    copies[1].wait()

    grad_mamba[...] = dot_nt(grad_branch[...], out_mat[...])
    grad_attended[...] = dot_nt(grad_branch[...], heads_mat[...])
    small = {
        1: kernel_grad,
        2: bias_grad,
        3: step_grad,
        4: decay_grad,
        5: skip_grad,
        6: mixer_grad,
    }
    for ref in small.values():
        ref[...] = jnp.zeros_like(ref)

    def add_small(slot, value):
        small[slot][...] += value

    copies[2].wait()
    copies[3].wait()

    def sequence(index, carry):
        rows = pl.ds(pl.multiple_of(index * LEN, LEN), LEN)
        grads = grad_attended[rows, :]
        attention_backward(proj, rows, cosine, sine, grads, grad_cat)
        mamba_backward(
            proj, rows, kernel, bias, step_bias, decay_log, skip, mixer_gain, pick, ssm,
            grad_mamba[rows, :], grad_cat, None, balance, touch, grad_active, add_small,
        )
        return carry

    lax.fori_loop(0, 2, sequence, 0)
    leaving = leave_all(
        (
            (grad_branch, grad_branch_out),
            (grad_cat, grad_cat_out),
            (kernel_grad, kernel_grad_out),
            (bias_grad, bias_grad_out),
            (step_grad, step_grad_out),
            (decay_grad, decay_grad_out),
            (skip_grad, skip_grad_out),
            (mixer_grad, mixer_grad_out),
        ),
        out_sems,
    )
    for copy in leaving:
        copy.wait()


def input_backward_kernel(earlier, active, *refs):
    @pl.when(active[0] == 1)
    def run():
        input_backward_body(*refs[:6], *refs[6 + earlier :])


def input_backward_body(
    grad_cat, grad_middle, x, packed, dt_weight, input_gain,
    grad_start_out, start_low_out, input_grad_out,
    grad_start, start_low, input_grad,
    cat, sems, out_sems,
):
    copies = [
        pltpu.make_async_copy(packed.at[:, pl.ds(16 * j, 16), :], cat.at[j], sems.at[j])
        for j in range(4)
    ]
    start_all(copies)
    grad_normed = dot_nt(grad_cat[:, T0:CAT], dt_weight[...])
    for j in range(4):
        copies[j].wait()
        part = dot_nt(grad_cat[:, 1024 * j : 1024 * j + 1024], flat(cat[j]))
        grad_normed = grad_normed + part
    state = x[...].astype(F32)
    grad_state, grad_gain = rms_backward(state, input_gain[...], grad_normed)
    input_grad[...] = grad_gain
    total = grad_middle[...] + grad_state
    grad_start[...] = total
    start_low[...] = total.astype(BF16)
    leaving = leave_all(
        ((grad_start, grad_start_out), (start_low, start_low_out), (input_grad, input_grad_out)),
        out_sems,
    )
    for copy in leaving:
        copy.wait()


VMEM = pl.BlockSpec(memory_space=pltpu.VMEM)
SMEM = pl.BlockSpec(memory_space=pltpu.SMEM)
ANY = pl.BlockSpec(memory_space=pl.ANY)
LIMIT = 60 * 1024 * 1024


def shape(rows, columns, dtype):
    return jax.ShapeDtypeStruct((rows, columns), dtype)


def scratch(*dims, dtype=BF16):
    return pltpu.VMEM(dims, dtype)


FEED_MATS = (
    scratch(4, 4, 4, 16, FEED),
    scratch(4, 4, 4, 16, FEED + 128),
    scratch(4, 4, 4, 32, WIDTH),
)


def mirrored(shapes):
    return [pltpu.VMEM(s.shape, s.dtype) for s in shapes]


def run_forward(start, mats, small, rope):
    packed, *given, feeds = mats
    unpack = not given
    given = given[1:]
    extra = (shape(WIDTH, 128, BF16), shape(INNER, WIDTH, BF16), shape(512, WIDTH, BF16))
    shapes = (
        shape(ROWS, WIDTH, BF16),
        shape(ROWS, WIDTH, BF16),
        shape(ROWS, CAT, F32),
        shape(ROWS, INNER, F32),
        shape(ROWS, INNER, BF16),
        shape(ROWS, 512, BF16),
        shape(ROWS, WIDTH, F32),
        shape(ROWS, WIDTH, BF16),
        shape(ROWS, FEED, F32),
        shape(ROWS, FEED, F32),
        shape(ROWS, FEED, BF16),
    )
    return pl.pallas_call(
        functools.partial(forward_kernel, unpack),
        out_shape=extra + shapes if unpack else shapes,
        in_specs=[VMEM, ANY] + [ANY] * len(given) + [SMEM] + [ANY] * 9 + [VMEM] * 10,
        out_specs=(ANY,) * (len(shapes) + 3 * unpack),
        scratch_shapes=[
            *mirrored(shapes),
            scratch(4, 64, 16, 1024),
            *FEED_MATS,
            scratch(INNER, WIDTH),
            scratch(512, WIDTH),
            scratch(64, 32, WIDTH) if unpack else scratch(16, 128),
            scratch(WIDTH, 128),
            pltpu.SemaphoreType.DMA((6,)),
            pltpu.SemaphoreType.DMA((len(shapes) + 3,)),
            pltpu.SemaphoreType.DMA((12,)),
        ],
        compiler_params=pltpu.CompilerParams(vmem_limit_bytes=LIMIT),
        cost_estimate=pl.CostEstimate(
            flops=2 * ROWS * 12_600_000, bytes_accessed=40_000_000, transcendentals=2_000_000
        ),
        name="forward",
    )(start, packed, *given, *feeds, *small, *rope)


def run_feed_backward(active, grad_top, mats, gate, upper, middle, feed_gain, earlier=()):
    shapes = (
        shape(ROWS, FEED, BF16),
        shape(ROWS, FEED, BF16),
        shape(ROWS, WIDTH, F32),
        shape(1, WIDTH, F32),
    )
    return pl.pallas_call(
        functools.partial(feed_backward_kernel, len(earlier)),
        out_shape=shapes,
        in_specs=[SMEM, VMEM, SMEM] + [ANY] * 12 + [VMEM] + [ANY] * len(earlier),
        out_specs=(ANY,) * len(shapes),
        scratch_shapes=[
            *mirrored(shapes),
            scratch(ROWS, FEED, dtype=F32),
            scratch(ROWS, FEED, dtype=F32),
            scratch(ROWS, WIDTH, dtype=F32),
            *FEED_MATS,
            pltpu.SemaphoreType.DMA((3,)),
            pltpu.SemaphoreType.DMA((4,)),
            pltpu.SemaphoreType.DMA((12,)),
        ],
        input_output_aliases={16 + k: k for k in range(len(earlier))},
        compiler_params=pltpu.CompilerParams(vmem_limit_bytes=LIMIT),
        cost_estimate=pl.CostEstimate(
            flops=2 * ROWS * 6_300_000, bytes_accessed=22_000_000, transcendentals=1_000_000
        ),
        name="feed_backward",
    )(active, grad_top, *mats[4], gate, upper, middle, feed_gain, *earlier)


def run_mix_backward(active, grad_middle, mats, proj, ssm, small, rope, pick, earlier=()):
    packed, dt_weight, out_weight, heads_weight, feeds = mats
    shapes = (
        shape(ROWS, WIDTH, BF16),
        shape(ROWS, CAT, BF16),
        shape(4, MIXED, F32),
        shape(1, MIXED, F32),
        shape(1, 128, F32),
        shape(1, 128, F32),
        shape(1, INNER, F32),
        shape(1, INNER, F32),
    )
    return pl.pallas_call(
        functools.partial(mix_backward_kernel, len(earlier)),
        out_shape=shapes,
        in_specs=[SMEM, VMEM] + [ANY] * 4 + [VMEM] * 9 + [ANY] * len(earlier),
        out_specs=(ANY,) * len(shapes),
        scratch_shapes=[
            *mirrored(shapes),
            scratch(ROWS, CAT, dtype=F32),
            scratch(ROWS, INNER, dtype=F32),
            scratch(INNER, WIDTH),
            scratch(512, WIDTH),
            scratch(ROWS, INNER, dtype=F32),
            scratch(ROWS, 512, dtype=F32),
            scratch(LEN, INNER, dtype=F32),
            scratch(LEN, INNER, dtype=F32),
            scratch(LEN, MIXED, dtype=F32),
            pltpu.SemaphoreType.DMA((4,)),
            pltpu.SemaphoreType.DMA((8,)),
        ],
        input_output_aliases={15 + k: k for k in range(len(earlier))},
        compiler_params=pltpu.CompilerParams(vmem_limit_bytes=LIMIT),
        cost_estimate=pl.CostEstimate(
            flops=2 * ROWS * 2_100_000, bytes_accessed=14_000_000, transcendentals=4_000_000
        ),
        name="mix_backward",
    )(
        active, grad_middle, out_weight, heads_weight, proj, ssm, *small[1:7], *rope, pick, *earlier
    )


def run_input_backward(active, grad_cat, grad_middle, start, mats, input_gain, earlier=()):
    shapes = (shape(ROWS, WIDTH, F32), shape(ROWS, WIDTH, BF16), shape(1, WIDTH, F32))
    return pl.pallas_call(
        functools.partial(input_backward_kernel, len(earlier)),
        out_shape=shapes,
        in_specs=[SMEM, VMEM, VMEM, VMEM, ANY, VMEM, VMEM] + [ANY] * len(earlier),
        out_specs=(ANY,) * len(shapes),
        scratch_shapes=[
            *mirrored(shapes),
            scratch(4, 64, 16, 1024),
            pltpu.SemaphoreType.DMA((4,)),
            pltpu.SemaphoreType.DMA((3,)),
        ],
        input_output_aliases={7 + k: k for k in range(len(earlier))},
        compiler_params=pltpu.CompilerParams(vmem_limit_bytes=LIMIT),
        cost_estimate=pl.CostEstimate(
            flops=2 * ROWS * 4_200_000, bytes_accessed=13_000_000, transcendentals=1000
        ),
        name="input_backward",
    )(active, grad_cat, grad_middle, start, *mats[:2], input_gain, *earlier)


def finish_kernel(
    mine, rows_own, gate_own, up_own, rows_got, gate_got, up_got, rows_last, gate_last, up_last,
    in_grad, query_grad, key_grad, value_grad, out_grad, heads_grad, gate_grad, up_grad, down_grad,
):
    def total(k, own, got, last):
        depth = own.shape[1]
        part = own[mine[k]].astype(F32) + got[:depth].astype(F32)
        return part + last[...].astype(F32)

    value = total(0, rows_own, rows_got, rows_last)
    down_grad[0] = value[:, :WIDTH]
    out_grad[0] = value[:24, WIDTH:]
    heads_grad[0] = value[24:, WIDTH:]
    value = total(1, gate_own, gate_got, gate_last)
    gate_grad[0] = value[:, :FEED]
    query_grad[0] = value[:, FEED : FEED + K0]
    key_grad[0] = value[:, FEED + K0 : FEED + V0]
    value_grad[0] = value[:, FEED + V0 : FEED + Z0]
    in_grad[0, :, : 2048 - Z0] = value[:, FEED + Z0 :]
    value = total(2, up_own, up_got, up_last)
    up_grad[0] = value[:, :FEED]
    in_grad[0, :, 2048 - Z0 :] = value[:, FEED : FEED + T0 + HEADS - 2048]


def run_finish(mine, owns, gots, lasts):
    shapes = tuple(
        jax.ShapeDtypeStruct((1, *dims), F32)
        for dims in (
            (16, T0 + HEADS - Z0),
            (16, 512),
            (16, 128),
            (16, 128),
            (24, WIDTH),
            (8, WIDTH),
            (16, FEED),
            (16, FEED),
            (32, WIDTH),
        )
    )
    return pl.pallas_call(
        finish_kernel,
        out_shape=shapes,
        in_specs=[SMEM] + [VMEM] * 9,
        out_specs=(VMEM,) * 9,
        compiler_params=pltpu.CompilerParams(vmem_limit_bytes=LIMIT // 2),
        name="finish",
    )(mine, *owns, *gots, *lasts)


def rope_tables():
    position = jnp.arange(LEN).astype(F32)
    inverse = 10000.0 ** (-(jnp.arange(32).astype(F32) * 2.0) / 64)
    angle = position[:, None] * inverse[None, :]
    cosine = jnp.tile(jnp.cos(angle), (1, 16))
    sine = jnp.sin(angle)
    return cosine, jnp.tile(jnp.concatenate([-sine, sine], axis=1), (1, 8))


def head_pick():
    lanes = lax.broadcasted_iota(jnp.int32, (INNER, 128), 0) // 64
    return (lanes == lax.broadcasted_iota(jnp.int32, (INNER, 128), 1)).astype(BF16)


def prepared_small(pieces):
    input_gain, kernel, bias, step_bias, decay_log, skip, mixer_gain, feed_gain = pieces

    def padded(v):
        return jnp.pad(v, (0, 128 - HEADS))[None]

    return (
        input_gain[None],
        kernel,
        bias[None],
        padded(step_bias),
        padded(decay_log),
        jnp.repeat(skip, 64)[None],
        mixer_gain[None],
        feed_gain[None],
    )


FIRST = (1, 0, 3, 2)
SECOND = (3, 2, 1, 0)


def partners(axis, turn):
    me = lax.axis_index(axis)
    near, far = me + 1 - 2 * lax.rem(me, 2), 3 - me
    flipped = lax.rem(lax.axis_index("section") + turn, 2) == 1
    found = (jnp.where(flipped, far, near), jnp.where(flipped, near, far))
    swaps = []
    for step in range(2):
        tables = [(FIRST, SECOND)[(core + turn + step) % 2] for core in range(2)]
        swaps.append([(4 * c + i, 4 * c + tables[c][i]) for c in range(2) for i in range(4)])
    return me, found, swaps


def exchange(array, axis, pairs):
    return lax.ppermute(array, ("section", axis), pairs)


def first_sent(part, axis, turn):
    me, (one, two), swaps = partners(axis, turn)
    return part([one, lax.rem(me + 2, 4)]).astype(BF16)


def first_got(sent, axis, turn):
    return exchange(sent, axis, partners(axis, turn)[2][0])


def handed_on(part, got, axis, turn):
    me, (one, two), swaps = partners(axis, turn)
    return (part([two]) + got[got.shape[0] // 2 :].astype(F32)).astype(BF16)


def totalled(part, got, handed, axis, turn):
    me, found, (swap_one, swap_two) = partners(axis, turn)
    last = exchange(handed, axis, swap_two)
    return part([me]) + got[: got.shape[0] // 2].astype(F32) + last.astype(F32)


def product_of(left, right, place):
    blocks = left.reshape(4, 4, 4, left.shape[0] // 64, left.shape[1])

    def part(places):
        picked = [lax.dynamic_index_in_dim(blocks, p, place, keepdims=False) for p in places]
        return dot(jnp.concatenate(picked, axis=0).reshape(-1, left.shape[1]), right)

    return part


def quarters_of(array, dim):
    def part(places):
        picked = [lax.dynamic_index_in_dim(array, p, dim, keepdims=False) for p in places]
        return jnp.concatenate(picked, axis=0).reshape(-1, array.shape[-1]).astype(F32)

    return part


def summed_on(array, axis, dim, turn):
    part = quarters_of(array, dim)
    got = first_got(first_sent(part, axis, turn), axis, turn)
    return totalled(part, got, handed_on(part, got, axis, turn), axis, turn)


def second_summed(parts, order, depth):
    array = jnp.concatenate([p.astype(BF16) for p in parts], axis=1)
    width = array.shape[1]
    rest = [0, 1, 2]
    rest.remove(order[0])
    array = array.reshape(4, 4, depth, width)
    array = summed_on(array, DP[order[1]], rest.index(order[1]), 1).astype(BF16)
    return array.reshape(4, depth, width)


def gathered_on(array, axis):
    me, (one, two), (swap_one, swap_two) = partners(axis, 0)
    got = exchange(array, axis, swap_one)
    far = exchange(jnp.stack([array, got]), axis, swap_two)
    return (array, got, far), (me, one, two, lax.rem(me + 2, 4))


def placed(blocks, places, dim):
    own, got, far = blocks
    whole = jnp.zeros((*own.shape[:dim], 4, *own.shape[dim:]), own.dtype)
    for block, place in zip((own, got, far[0], far[1]), places):
        whole = lax.dynamic_update_index_in_dim(whole, block, place, dim)
    return whole


def gathered(block, order):
    block = placed(*gathered_on(block, DP[order[2]]), 0)
    block = placed(*gathered_on(block, DP[order[1]]), 0 if order[1] < order[2] else 1)
    return gathered_on(block, DP[order[0]])


def column_blocks(matrix):
    return [matrix[:, at : at + 1024] for at in range(0, matrix.shape[1], 1024)]


def on_device(
    layer_input,
    out_grad,
    in_weight,
    query_weight,
    key_weight,
    value_weight,
    out_weight,
    heads_weight,
    gate_weight,
    up_weight,
    down_weight,
    *pieces,
):
    micro, part, width = layer_input.shape
    rows = micro * part
    cat = jnp.concatenate(
        [query_weight[0], key_weight[0], value_weight[0], in_weight[0, :, :3328]], axis=1
    )
    steps = jnp.pad(in_weight[0, :, 3328:], ((0, 0), (0, 128 - HEADS)))
    own = jnp.concatenate(
        [
            *column_blocks(cat),
            out_weight[0],
            heads_weight[0],
        ],
        axis=0,
    )
    packed = lax.all_gather(own, DP, axis=0, tiled=False)
    feeds = [
        gathered(block, order)
        for block, order in (
            (gate_weight[0], (0, 1, 2)),
            (jnp.concatenate([up_weight[0], steps], axis=1), (1, 2, 0)),
            (down_weight[0], (2, 0, 1)),
        )
    ]
    places = jnp.stack([place for blocks, found in feeds for place in found]).astype(jnp.int32)
    mats = (
        packed,
        (places, *(piece for blocks, found in feeds for piece in blocks)),
    )
    small = prepared_small([piece[0] for piece in pieces])
    rope = rope_tables()
    pick = head_pick()
    first = lax.axis_index("section") == 0

    start_low = layer_input.reshape(rows, width)
    dt_weight, out_mat, heads_mat, *kept_low = run_forward(start_low, mats, small, rope)
    mats = (packed, dt_weight, out_mat, heads_mat, mats[1])
    start_high = lax.ppermute(kept_low[0], "section", [(0, 1)])
    kept_high = run_forward(start_high, mats, small, rope)
    layer_outputs = jnp.where(first, kept_low[0], kept_high[0]).reshape(1, micro, part, width)

    on_high = jnp.where(first, 0, 1).astype(jnp.int32).reshape(1)
    on_low = 1 - on_high
    top_high = out_grad.reshape(rows, width)
    feed_high = run_feed_backward(
        on_high, top_high, mats, kept_high[8], kept_high[9], kept_high[6], small[7]
    )
    mix_high = run_mix_backward(
        on_high, feed_high[2], mats, kept_high[2], kept_high[3], small, rope, pick
    )
    input_high = run_input_backward(
        on_high, mix_high[1], feed_high[2], start_high, mats, small[0]
    )
    slots = (1, 4, 5, 7, 10)
    low_top, *tied = lax.optimization_barrier((input_high[1], *(kept_high[s] for s in slots)))
    tied = dict(zip(slots, tied))
    top_low = lax.ppermute(low_top, "section", [(1, 0)])

    def chosen(slot):
        return jnp.where(first, kept_low[slot], tied[slot])

    normed_t, ffin_t, hidden_t = (chosen(slot).T for slot in (1, 7, 10))
    joined_t = jnp.concatenate(
        [chosen(4).T.reshape(64, 24, rows), chosen(5).T.reshape(64, 8, rows)], axis=1
    ).reshape(2048, rows)

    feed = run_feed_backward(
        on_low, top_low, mats, kept_low[8], kept_low[9], kept_low[6], small[7], feed_high
    )
    grad_gate, grad_upper, grad_middle, feed_grad = feed
    grad_low = jnp.where(first, top_low, top_high)
    grad_low, grad_gate, grad_upper = lax.optimization_barrier((grad_low, grad_gate, grad_upper))
    orders = ((2, 0, 1), (0, 1, 2), (1, 2, 0))
    axes = [DP[order[0]] for order in orders]
    products = [
        product_of(left, right, order[0])
        for left, right, order in zip(
            (hidden_t, ffin_t, ffin_t), (grad_low, grad_gate, grad_upper), orders
        )
    ]
    sents = [first_sent(p, axis, 0) for p, axis in zip(products, axes)]
    grad_middle, *sents = lax.optimization_barrier((grad_middle, *sents))
    gots = [first_got(sent, axis, 0) for sent, axis in zip(sents, axes)]
    mix = run_mix_backward(
        on_low, grad_middle, mats, kept_low[2], kept_low[3], small, rope, pick, mix_high
    )
    grad_branch, grad_cat, *small_grads = mix
    mix_products = [
        product_of(left, right, order[0])
        for left, right, order in zip(
            (joined_t, normed_t, normed_t),
            (grad_branch, grad_cat[:, :2048], grad_cat[:, 2048:]),
            orders,
        )
    ]
    mix_sents = [first_sent(p, axis, 1) for p, axis in zip(mix_products, axes)]
    pending = lax.optimization_barrier((*gots, *mix_sents))
    gots, mix_sents = pending[:3], pending[3:]
    mix_gots = [first_got(sent, axis, 1) for sent, axis in zip(mix_sents, axes)]
    handed = [handed_on(p, got, axis, 0) for p, got, axis in zip(products, gots, axes)]
    last_middle, *pending = lax.optimization_barrier(
        (grad_middle, grad_low, grad_gate, grad_upper, grad_branch, grad_cat, *handed)
    )
    rights, (late_branch, late_cat), handed = pending[:3], pending[3:5], pending[5:]
    products = [
        product_of(left, right, order[0])
        for left, right, order in zip((hidden_t, ffin_t, ffin_t), rights, orders)
    ]
    mix_products = [
        product_of(left, right, order[0])
        for left, right, order in zip(
            (joined_t, normed_t, normed_t),
            (late_branch, late_cat[:, :2048], late_cat[:, 2048:]),
            orders,
        )
    ]
    feed_parts = [
        totalled(p, got, hand, axis, 0)
        for p, got, hand, axis in zip(products, gots, handed, axes)
    ]
    mix_parts = [
        totalled(p, got, handed_on(p, got, axis, 1), axis, 1)
        for p, got, axis in zip(mix_products, mix_gots, axes)
    ]
    grad_start, unused, input_grad = run_input_backward(
        on_low, grad_cat, last_middle, start_low, mats, small[0], input_high
    )
    small_grads = [input_grad, *small_grads]
    input_g, kernel_g, bias_g, step_g, decay_g, skip_g, mixer_g = small_grads
    small_grads = (
        input_g[0],
        kernel_g,
        bias_g[0],
        step_g[0, :HEADS],
        decay_g[0, :HEADS],
        skip_g.reshape(HEADS, 64).sum(axis=1),
        mixer_g[0],
        feed_grad[0],
    )
    vector = jnp.concatenate([piece.reshape(-1) for piece in small_grads])
    vector = jnp.pad(vector, (0, -vector.shape[0] % 1024)).reshape(-1, 128)
    vectors = lax.all_gather(vector.astype(BF16), DP, axis=0, tiled=False)
    seconds = [
        second_summed(pair, order, depth)
        for pair, order, depth in zip(zip(feed_parts, mix_parts), orders, (32, 16, 16))
    ]
    axes = [DP[order[2]] for order in orders]
    quarters = [quarters_of(array, 0) for array in seconds]
    sents = [first_sent(p, axis, 0) for p, axis in zip(quarters, axes)]
    gots = [first_got(sent, axis, 0) for sent, axis in zip(sents, axes)]
    vectors, *unused = lax.optimization_barrier((vectors, *sents))
    total = jnp.sum(vectors.astype(F32), axis=0).reshape(-1)
    handed = [handed_on(p, got, axis, 0) for p, got, axis in zip(quarters, gots, axes)]
    lasts = [
        exchange(hand, axis, partners(axis, 0)[2][1]) for hand, axis in zip(handed, axes)
    ]
    mine = jnp.stack([lax.axis_index(axis) for axis in axes]).astype(jnp.int32)
    mat_grads = run_finish(mine, seconds, gots, lasts)

    summed, at = ([], 0)
    for piece in small_grads:
        summed.append(total[at : at + piece.size].reshape(1, *piece.shape))
        at += piece.size
    return (
        layer_outputs,
        grad_start.reshape(1, micro, part, width),
        *mat_grads,
        *summed,
    )


def solution(mesh):
    torus = Mesh(
        mesh.devices.reshape(mesh.shape["section"], 4, 4, 4), ("section", "dp_0", "dp_1", "dp_2")
    )
    in_specs = (
        P(None, DP, None),
        P(None, DP, None),
        P("section", DP, None),
        P("section", DP, None),
        P("section", DP, None),
        P("section", DP, None),
        P("section", DP, None),
        P("section", DP, None),
        P("section", DP, None),
        P("section", DP, None),
        P("section", DP, None),
        P("section", None),
        P("section", None, None),
        P("section", None),
        P("section", None),
        P("section", None),
        P("section", None),
        P("section", None),
        P("section", None),
    )
    out_specs = (
        P("section", None, DP, None),
        P("section", None, DP, None),
        P("section", DP, None),
        P("section", DP, None),
        P("section", DP, None),
        P("section", DP, None),
        P("section", DP, None),
        P("section", DP, None),
        P("section", DP, None),
        P("section", DP, None),
        P("section", DP, None),
        P("section", None),
        P("section", None, None),
        P("section", None),
        P("section", None),
        P("section", None),
        P("section", None),
        P("section", None),
        P("section", None),
    )
    return jax.shard_map(
        on_device, mesh=torus, in_specs=in_specs, out_specs=out_specs, check_vma=False
    )
```

```python
import functools

import jax
import jax.numpy as jnp
from jax import lax
from jax.experimental import pallas as pl
from jax.experimental.pallas import tpu as pltpu
from jax.sharding import Mesh
from jax.sharding import PartitionSpec as P

LEN = 128
ROWS = 256
WIDTH = 1024
FEED = 2048
INNER = 1536
MIXED = 1792
CAT = 4224
HEADS = 24
DP = ("dp_0", "dp_1", "dp_2")
F32 = jnp.float32
BF16 = jnp.bfloat16
HIDE = -1e30
Q0, K0, V0, Z0, X0, T0 = 0, 512, 640, 768, 2304, 4096
OUT0, HEADS0, DT0, PACKED = 64, 88, 96, 104


def dot(left, right):
    return jnp.dot(left, right, preferred_element_type=F32)


def dot_nt(left, right):
    return lax.dot_general(left, right, (((1,), (1,)), ((), ())), preferred_element_type=F32)


def dot_tn(left, right):
    return lax.dot_general(left, right, (((0,), (0,)), ((), ())), preferred_element_type=F32)


def dot_full(left, right):
    return jnp.dot(left, right, precision=lax.Precision.HIGHEST, preferred_element_type=F32)


def iota(shape, dim):
    return lax.broadcasted_iota(jnp.int32, shape, dim)


def sigmoid(v):
    return 1.0 / (1.0 + jnp.exp(-v))


def softplus(v):
    return jnp.maximum(v, 0.0) + jnp.log(1.0 + jnp.exp(-jnp.abs(v)))


def swap_halves(v):
    width = v.shape[1]
    near = lax.rem(iota(v.shape, 1), 64) < 32
    return jnp.where(near, pltpu.roll(v, width - 32, 1), pltpu.roll(v, 32, 1))


def shifted_down(v, by):
    if by == 0:
        return v
    return jnp.where(iota(v.shape, 0) >= by, pltpu.roll(v, by, 0), 0.0)


def shifted_up(v, by):
    if by == 0:
        return v
    rows = v.shape[0]
    return jnp.where(iota(v.shape, 0) < rows - by, pltpu.roll(v, rows - by, 0), 0.0)


def rms(v):
    return lax.rsqrt(jnp.mean(v * v, axis=-1, keepdims=True) + 1e-05)


def rms_backward(v, gain, grad):
    scale = rms(v)
    gained = grad * gain
    inner = jnp.mean(gained * v, axis=-1, keepdims=True)
    grad_v = scale * gained - v * (scale * scale * scale * inner)
    return grad_v, jnp.sum(grad * v * scale, axis=0, keepdims=True)


def left_half():
    return iota((LEN, 128), 1) < 64


def both_halves(v, group, left):
    turned = pltpu.roll(v, 64, 1)
    return jnp.where(left, v, turned) if group == 0 else jnp.where(left, turned, v)


def stacked(pairs, left):
    parts = []
    for pair in pairs:
        parts.append(jnp.where(left, pair, 0.0))
        parts.append(jnp.where(left, 0.0, pair))
    return jnp.concatenate(parts, axis=0).astype(BF16)


def unstacked(rows, index, left):
    low = rows[2 * index * LEN : (2 * index + 1) * LEN]
    high = rows[(2 * index + 1) * LEN : (2 * index + 2) * LEN]
    return jnp.where(left, low, high)


def attention_parts(proj, rows, cosine, sine):
    left = left_half()
    query = proj[rows, Q0:K0]
    query = query * cosine[...] + swap_halves(query) * sine[...]
    key = proj[rows, K0:V0]
    key = key * cosine[:, :128] + swap_halves(key) * sine[:, :128]
    value = proj[rows, V0:Z0]
    groups = []
    for group in range(2):
        pairs = [query[:, 128 * p : 128 * p + 128] for p in (2 * group, 2 * group + 1)]
        queries = stacked(pairs, left)
        keys = both_halves(key, group, left).astype(BF16)
        values = both_halves(value, group, left).astype(BF16)
        scores = dot_nt(queries, keys) * 0.125
        time = lax.rem(iota(scores.shape, 0), LEN)
        scores = jnp.where(iota(scores.shape, 1) <= time, scores, HIDE)
        top = jnp.max(scores, axis=-1, keepdims=True)
        expo = jnp.exp(scores - top)
        probs = expo / jnp.sum(expo, axis=-1, keepdims=True)
        groups.append((queries, keys, values, probs))
    return left, groups


def attention_forward(proj, rows, cosine, sine, attended):
    left, groups = attention_parts(proj, rows, cosine, sine)
    for group, (queries, keys, values, probs) in enumerate(groups):
        mixed = dot(probs.astype(BF16), values)
        for index in range(2):
            at = 256 * group + 128 * index
            attended[rows, at : at + 128] = unstacked(mixed, index, left).astype(BF16)


def attention_backward(proj, rows, cosine, sine, grad_attended, grad_cat):
    left, groups = attention_parts(proj, rows, cosine, sine)
    key_parts, value_parts = [], []
    for group, (queries, keys, values, probs) in enumerate(groups):
        pairs = [grad_attended[:, 128 * p : 128 * p + 128] for p in (2 * group, 2 * group + 1)]
        grads = stacked(pairs, left)
        grad_values = dot_tn(probs.astype(BF16), grads)
        grad_probs = dot_nt(grads, values)
        inner = jnp.sum(probs * grad_probs, axis=-1, keepdims=True)
        grad_scores = (probs * (grad_probs - inner)).astype(BF16)
        grad_queries = dot(grad_scores, keys) * 0.125
        grad_keys = dot_tn(grad_scores, queries) * 0.125
        for index in range(2):
            at = 256 * group + 128 * index
            grad = unstacked(grad_queries, index, left)
            grad = grad * cosine[:, :128] - swap_halves(grad) * sine[:, :128]
            grad_cat[rows, at : at + 128] = grad.astype(BF16)
        key_parts.append(grad_keys + pltpu.roll(grad_keys, 64, 1))
        value_parts.append(grad_values + pltpu.roll(grad_values, 64, 1))
    grad = jnp.where(left, key_parts[0], key_parts[1])
    grad = grad * cosine[:, :128] - swap_halves(grad) * sine[:, :128]
    grad_cat[rows, K0:V0] = grad.astype(BF16)
    grad_cat[rows, V0:Z0] = jnp.where(left, value_parts[0], value_parts[1]).astype(BF16)


def mamba_parts(proj, rows, kernel, bias, step_bias, decay_log):
    mixed = proj[rows, X0:T0]
    total = bias[...] + mixed * kernel[3:4, :]
    for tap in range(3):
        total = total + shifted_down(mixed, 3 - tap) * kernel[tap : tap + 1, :]
    active = total * sigmoid(total)
    step = softplus(proj[rows, T0:CAT] + step_bias[...])
    rate = -step * jnp.exp(decay_log[...])
    earlier = (iota((LEN, LEN), 0) >= iota((LEN, LEN), 1)).astype(F32)
    cumul = dot_full(earlier, rate)
    state_in = active[:, INNER : INNER + 128].astype(BF16)
    state_out = active[:, INNER + 128 :].astype(BF16)
    return mixed, total, active, step, rate, cumul, state_in, state_out


def stepped(step, pair, left):
    return jnp.where(left, step[:, 2 * pair : 2 * pair + 1], step[:, 2 * pair + 1 : 2 * pair + 2])


def mamba_forward(proj, rows, kernel, bias, step_bias, decay_log, skip, gain, ssm, mamba):
    left = left_half()
    parts = mamba_parts(proj, rows, kernel, bias, step_bias, decay_log)
    mixed, total, active, step, rate, cumul, state_in, state_out = parts
    across = cumul.T
    hidden = jnp.where(iota((LEN, LEN), 0) >= iota((LEN, LEN), 1), 0.0, HIDE)
    meeting = dot_nt(state_out, state_in)
    for pair in range(HEADS // 2):
        at = 128 * pair
        inputs = active[:, at : at + 128]
        scaled = (inputs * stepped(step, pair, left)).astype(BF16)
        mixing = []
        for head in (2 * pair, 2 * pair + 1):
            spread = cumul[:, head : head + 1] - across[head : head + 1, :] + hidden
            mixing.append((meeting * jnp.exp(spread)).astype(BF16))
        both = dot(jnp.concatenate(mixing, axis=0), scaled)
        out = unstacked(both, 0, left) + skip[:, at : at + 128] * inputs
        ssm[rows, at : at + 128] = out
    z = proj[rows, Z0:X0]
    gated = ssm[rows, :] * (z * sigmoid(z))
    mamba[rows, :] = (gated * rms(gated) * gain[...]).astype(BF16)


def head_sums(v, pick):
    high = v.astype(BF16)
    low = (v - high.astype(F32)).astype(BF16)
    return dot(high, pick) + dot(low, pick)


def mamba_backward(
    proj, rows, kernel, bias, step_bias, decay_log, skip, gain, pick, ssm, grad_mamba, grad_cat,
    across_scratch, balance_scratch, touch_scratch, grad_active, add_small,
):
    left = left_half()
    parts = mamba_parts(proj, rows, kernel, bias, step_bias, decay_log)
    mixed, total, active, step, rate, cumul, state_in, state_out = parts
    across = cumul.T
    hidden = jnp.where(iota((LEN, LEN), 1) >= iota((LEN, LEN), 0), 0.0, HIDE)
    meeting = dot_nt(state_out, state_in).T
    z = proj[rows, Z0:X0]
    out = ssm[rows, :]
    gate = sigmoid(z)
    gated = out * (z * gate)
    grad_gated, grad_gain = rms_backward(gated, gain[...], grad_mamba)
    add_small(6, grad_gain)
    grad_cat[rows, Z0:X0] = (grad_gated * out * (gate * (1.0 + z * (1.0 - gate)))).astype(BF16)
    grad_out = grad_gated * (z * gate)
    add_small(5, jnp.sum(grad_out * active[:, :INNER], axis=0, keepdims=True))
    grad_meeting = jnp.zeros((LEN, LEN), F32)
    for pair in range(HEADS // 2):
        at = 128 * pair
        inputs = active[:, at : at + 128]
        steps = stepped(step, pair, left)
        scaled = (inputs * steps).astype(BF16)
        grad_pair = grad_out[:, at : at + 128]
        grad_low = grad_pair.astype(BF16)
        halves = jnp.concatenate(
            [jnp.where(left, scaled, jnp.zeros_like(scaled)), jnp.where(left, jnp.zeros_like(scaled), scaled)],
            axis=0,
        )
        grad_mixing = dot_nt(halves, grad_low)
        mixing = []
        for place, head in enumerate((2 * pair, 2 * pair + 1)):
            spread = across[head : head + 1, :] - cumul[:, head : head + 1] + hidden
            decay = jnp.exp(spread)
            mixing.append((meeting * decay).astype(BF16))
            grad_meeting = grad_meeting + grad_mixing[LEN * place : LEN * place + LEN] * decay
        both = dot(jnp.concatenate(mixing, axis=0), grad_low)
        grad_scaled = unstacked(both, 0, left)
        skips = skip[:, at : at + 128]
        grad_active[:, at : at + 128] = grad_scaled * steps + skips * grad_pair
        touch_scratch[:, at : at + 128] = grad_scaled * inputs
        balance_scratch[:, at : at + 128] = grad_low.astype(F32) * (
            out[:, at : at + 128] - skips * inputs
        ) - scaled.astype(F32) * grad_scaled
    grad_low = grad_meeting.astype(BF16)
    grad_active[:, INNER : INNER + 128] = dot(grad_low, state_out)
    grad_active[:, INNER + 128 :] = dot_tn(grad_low, state_in)
    later = (iota((LEN, LEN), 1) >= iota((LEN, LEN), 0)).astype(F32)
    grad_rate = dot_full(later, head_sums(balance_scratch[...], pick[...]))
    add_small(4, jnp.sum(grad_rate * rate, axis=0, keepdims=True))
    grad_step = head_sums(touch_scratch[...], pick[...]) - grad_rate * jnp.exp(decay_log[...])
    grad_dt = grad_step * sigmoid(proj[rows, T0:CAT] + step_bias[...])
    add_small(3, jnp.sum(grad_dt, axis=0, keepdims=True))
    grad_cat[rows, T0:CAT] = grad_dt.astype(BF16)
    slope = sigmoid(total)
    grad_total = grad_active[...] * (slope * (1.0 + total * (1.0 - slope)))
    add_small(2, jnp.sum(grad_total, axis=0, keepdims=True))
    grad_mixed = grad_total * kernel[3:4, :]
    taps = []
    for tap in range(4):
        taps.append(jnp.sum(grad_total * shifted_down(mixed, 3 - tap), axis=0, keepdims=True))
        if tap < 3:
            grad_mixed = grad_mixed + shifted_up(grad_total, 3 - tap) * kernel[tap : tap + 1, :]
    add_small(1, jnp.concatenate(taps, axis=0))
    grad_cat[rows, X0:T0] = grad_mixed.astype(BF16)


def flat(block):
    return block.reshape(block.shape[0] * block.shape[1], block.shape[2])


def start_all(copies):
    for copy in copies:
        copy.start()


def feed_copies(places, pieces, buffers, sems):
    copies = []
    for k, buffer in enumerate(buffers):
        own, got, far = pieces[3 * k : 3 * k + 3]
        for q, source in enumerate((own, got, far.at[0], far.at[1])):
            target = buffer.at[(slice(None),) * k + (places[4 * k + q],)]
            copies.append(pltpu.make_async_copy(source, target, sems.at[4 * k + q]))
    return copies


def rows_of(block):
    return block.reshape(-1, block.shape[-1])


def forward_kernel(unpack, x, packed, dt_weight, *refs):
    if unpack:
        given, results = (None, None), refs[20:22]
        rest = refs[:20] + refs[22:]
    else:
        given, results = refs[:2], (None, None)
        rest = refs[2:]
    forward_body(unpack, x, packed, dt_weight, *given, *results, *rest)


def forward_body(
    unpack, x, packed, dt_weight, out_weight, heads_weight, out_result, heads_result,
    places, gate_own, gate_got, gate_far, up_own, up_got, up_far, down_own, down_got, down_far,
    input_gain, kernel, bias, step_bias, decay_log, skip,
    mixer_gain, feed_gain, cosine, sine,
    result_out, normed_out, proj_out, ssm_out, mamba_out, attended_out, middle_out, ffin_out, gate_out,
    upper_out, hidden_out,
    result, normed, proj, ssm, mamba, attended, middle, ffin, gate, upper, hidden,
    cat, gate_mat, up_mat, down_mat, out_mat, heads_mat, mixed, sems, out_sems, feed_sems,
):
    leaving = []

    def leave(*pairs):
        for source, target in pairs:
            copy = pltpu.make_async_copy(source, target, out_sems.at[len(leaving)])
            copy.start()
            leaving.append(copy)

    copies = [
        pltpu.make_async_copy(packed.at[:, pl.ds(16 * j, 16), :], cat.at[j], sems.at[j])
        for j in range(4)
    ]
    if unpack:
        copies.append(pltpu.make_async_copy(packed.at[:, pl.ds(OUT0, 32), :], mixed, sems.at[4]))
    else:
        copies.append(pltpu.make_async_copy(out_weight, out_mat, sems.at[4]))
        copies.append(pltpu.make_async_copy(heads_weight, heads_mat, sems.at[5]))
    pieces = (gate_own, gate_got, gate_far, up_own, up_got, up_far, down_own, down_got, down_far)
    feeds = feed_copies(places, pieces, (gate_mat, up_mat, down_mat), feed_sems)
    start_all(copies + feeds)
    state = x[...].astype(F32)
    normed[...] = (state * rms(state) * input_gain[...]).astype(BF16)
    proj[:, T0:CAT] = dot(normed[...], dt_weight[...])
    for j in range(4):
        copies[j].wait()
        proj[:, 1024 * j : 1024 * j + 1024] = dot(normed[...], flat(cat[j]))
    leave((normed, normed_out), (proj, proj_out))

    def sequence(index, carry):
        rows = pl.ds(pl.multiple_of(index * LEN, LEN), LEN)
        attention_forward(proj, rows, cosine, sine, attended)
        mamba_forward(proj, rows, kernel, bias, step_bias, decay_log, skip, mixer_gain, ssm, mamba)
        return carry

    lax.fori_loop(0, 2, sequence, 0)
    leave((ssm, ssm_out), (mamba, mamba_out), (attended, attended_out))
    for copy in copies[4:]:
        copy.wait()
    if unpack:
        wide = mixed[...].astype(F32)
        out_mat[...] = wide[:, :24].reshape(INNER, WIDTH).astype(BF16)
        heads_mat[...] = wide[:, 24:].reshape(512, WIDTH).astype(BF16)
        leave((out_mat, out_result), (heads_mat, heads_result))

    part = dot(mamba[...], out_mat[...]) + dot(attended[...], heads_mat[...])
    middle[...] = x[...].astype(F32) + part
    value = middle[...]
    ffin[...] = (value * rms(value) * feed_gain[...]).astype(BF16)
    leave((middle, middle_out), (ffin, ffin_out))
    for copy in feeds[:8]:
        copy.wait()

    for half in range(2):
        at = slice(1024 * half, 1024 * half + 1024)
        low = dot(ffin[...], rows_of(gate_mat[:, :, :, :, at]))
        high = dot(ffin[...], rows_of(up_mat[:, :, :, :, at]))
        gate[:, at] = low
        upper[:, at] = high
        hidden[:, at] = (low * sigmoid(low) * high).astype(BF16)
    leave((gate, gate_out), (upper, upper_out), (hidden, hidden_out))
    for copy in feeds[8:]:
        copy.wait()

    result[...] = (middle[...] + dot(hidden[...], rows_of(down_mat[...]))).astype(BF16)
    leave((result, result_out))
    for copy in leaving:
        copy.wait()


def leave_all(pairs, sems):
    copies = [
        pltpu.make_async_copy(source, target, sems.at[k]) for k, (source, target) in enumerate(pairs)
    ]
    start_all(copies)
    return copies


def feed_backward_kernel(earlier, active, *refs):
    @pl.when(active[0] == 1)
    def run():
        feed_backward_body(*refs[:15], *refs[15 + earlier :])


def feed_backward_body(
    grad_top, places, gate_own, gate_got, gate_far, up_own, up_got, up_far, down_own, down_got, down_far,
    gate_in, upper_in, middle_in, feed_gain,
    grad_gate_out, grad_upper_out, grad_middle_out, feed_grad_out,
    grad_gate, grad_upper, grad_middle, feed_grad,
    gate, upper, middle, gate_mat, up_mat, down_mat, sems, out_sems, feed_sems,
):
    inputs = [
        pltpu.make_async_copy(gate_in, gate, sems.at[0]),
        pltpu.make_async_copy(upper_in, upper, sems.at[1]),
        pltpu.make_async_copy(middle_in, middle, sems.at[2]),
    ]
    pieces = (gate_own, gate_got, gate_far, up_own, up_got, up_far, down_own, down_got, down_far)
    feeds = feed_copies(places, pieces, (gate_mat, up_mat, down_mat), feed_sems)
    start_all(feeds[8:] + inputs + feeds[:8])
    for copy in feeds[8:]:
        copy.wait()

    for half in range(2):
        at = slice(1024 * half, 1024 * half + 1024)
        grad_hidden = dot_nt(grad_top[...], rows_of(down_mat[2 * half : 2 * half + 2]))
        if half == 0:
            inputs[0].wait()
            inputs[1].wait()
        low, high = gate[:, at], upper[:, at]
        slope = sigmoid(low)
        grad_upper[:, at] = (grad_hidden * (low * slope)).astype(BF16)
        part = grad_hidden * high * (slope * (1.0 + low * (1.0 - slope)))
        grad_gate[:, at] = part.astype(BF16)
    leaving = leave_all(((grad_gate, grad_gate_out), (grad_upper, grad_upper_out)), out_sems)
    for copy in feeds[:8]:
        copy.wait()

    grad_ffin = dot_nt(grad_gate[...], rows_of(gate_mat[...]))
    grad_ffin = grad_ffin + dot_nt(grad_upper[...], rows_of(up_mat[...]))
    inputs[2].wait()
    grad_part, grad_gain = rms_backward(middle[...], feed_gain[...], grad_ffin)
    feed_grad[...] = grad_gain
    grad_middle[...] = grad_top[...].astype(F32) + grad_part
    leaving += leave_all(
        ((grad_middle, grad_middle_out), (feed_grad, feed_grad_out)), out_sems.at[pl.ds(2, 2)]
    )
    for copy in leaving:
        copy.wait()


def mix_backward_kernel(earlier, active, *refs):
    @pl.when(active[0] == 1)
    def run():
        mix_backward_body(*refs[:14], *refs[14 + earlier :])


def mix_backward_body(
    grad_middle, out_weight, heads_weight, proj_in, ssm_in, kernel, bias,
    step_bias, decay_log, skip, mixer_gain, cosine, sine, pick,
    grad_branch_out, grad_cat_out, kernel_grad_out, bias_grad_out,
    step_grad_out, decay_grad_out, skip_grad_out, mixer_grad_out,
    grad_branch, grad_cat, kernel_grad, bias_grad, step_grad, decay_grad,
    skip_grad, mixer_grad,
    proj, ssm,
    out_mat, heads_mat, grad_mamba, grad_attended, balance, touch, grad_active, sems,
    out_sems,
):
    copies = [
        pltpu.make_async_copy(out_weight, out_mat, sems.at[0]),
        pltpu.make_async_copy(heads_weight, heads_mat, sems.at[1]),
        pltpu.make_async_copy(proj_in, proj, sems.at[2]),
        pltpu.make_async_copy(ssm_in, ssm, sems.at[3]),
    ]
    start_all(copies)
    grad_branch[...] = grad_middle[...].astype(BF16)
    copies[0].wait()
    copies[1].wait()

    grad_mamba[...] = dot_nt(grad_branch[...], out_mat[...])
    grad_attended[...] = dot_nt(grad_branch[...], heads_mat[...])
    small = {
        1: kernel_grad,
        2: bias_grad,
        3: step_grad,
        4: decay_grad,
        5: skip_grad,
        6: mixer_grad,
    }
    for ref in small.values():
        ref[...] = jnp.zeros_like(ref)

    def add_small(slot, value):
        small[slot][...] += value

    copies[2].wait()
    copies[3].wait()

    def sequence(index, carry):
        rows = pl.ds(pl.multiple_of(index * LEN, LEN), LEN)
        grads = grad_attended[rows, :]
        attention_backward(proj, rows, cosine, sine, grads, grad_cat)
        mamba_backward(
            proj, rows, kernel, bias, step_bias, decay_log, skip, mixer_gain, pick, ssm,
            grad_mamba[rows, :], grad_cat, None, balance, touch, grad_active, add_small,
        )
        return carry

    lax.fori_loop(0, 2, sequence, 0)
    leaving = leave_all(
        (
            (grad_branch, grad_branch_out),
            (grad_cat, grad_cat_out),
            (kernel_grad, kernel_grad_out),
            (bias_grad, bias_grad_out),
            (step_grad, step_grad_out),
            (decay_grad, decay_grad_out),
            (skip_grad, skip_grad_out),
            (mixer_grad, mixer_grad_out),
        ),
        out_sems,
    )
    for copy in leaving:
        copy.wait()


def input_backward_kernel(earlier, active, *refs):
    @pl.when(active[0] == 1)
    def run():
        input_backward_body(*refs[:6], *refs[6 + earlier :])


def input_backward_body(
    grad_cat, grad_middle, x, packed, dt_weight, input_gain,
    grad_start_out, start_low_out, input_grad_out,
    grad_start, start_low, input_grad,
    cat, sems, out_sems,
):
    copies = [
        pltpu.make_async_copy(packed.at[:, pl.ds(16 * j, 16), :], cat.at[j], sems.at[j])
        for j in range(4)
    ]
    start_all(copies)
    grad_normed = dot_nt(grad_cat[:, T0:CAT], dt_weight[...])
    for j in range(4):
        copies[j].wait()
        part = dot_nt(grad_cat[:, 1024 * j : 1024 * j + 1024], flat(cat[j]))
        grad_normed = grad_normed + part
    state = x[...].astype(F32)
    grad_state, grad_gain = rms_backward(state, input_gain[...], grad_normed)
    input_grad[...] = grad_gain
    total = grad_middle[...] + grad_state
    grad_start[...] = total
    start_low[...] = total.astype(BF16)
    leaving = leave_all(
        ((grad_start, grad_start_out), (start_low, start_low_out), (input_grad, input_grad_out)),
        out_sems,
    )
    for copy in leaving:
        copy.wait()


VMEM = pl.BlockSpec(memory_space=pltpu.VMEM)
SMEM = pl.BlockSpec(memory_space=pltpu.SMEM)
ANY = pl.BlockSpec(memory_space=pl.ANY)
LIMIT = 60 * 1024 * 1024


def shape(rows, columns, dtype):
    return jax.ShapeDtypeStruct((rows, columns), dtype)


def scratch(*dims, dtype=BF16):
    return pltpu.VMEM(dims, dtype)


FEED_MATS = (
    scratch(4, 4, 4, 16, FEED),
    scratch(4, 4, 4, 16, FEED),
    scratch(4, 4, 4, 32, WIDTH),
)


def mirrored(shapes):
    return [pltpu.VMEM(s.shape, s.dtype) for s in shapes]


def run_forward(start, mats, small, rope):
    packed, dt_weight, *given, feeds = mats
    unpack = not given
    extra = (shape(INNER, WIDTH, BF16), shape(512, WIDTH, BF16))
    shapes = (
        shape(ROWS, WIDTH, BF16),
        shape(ROWS, WIDTH, BF16),
        shape(ROWS, CAT, F32),
        shape(ROWS, INNER, F32),
        shape(ROWS, INNER, BF16),
        shape(ROWS, 512, BF16),
        shape(ROWS, WIDTH, F32),
        shape(ROWS, WIDTH, BF16),
        shape(ROWS, FEED, F32),
        shape(ROWS, FEED, F32),
        shape(ROWS, FEED, BF16),
    )
    return pl.pallas_call(
        functools.partial(forward_kernel, unpack),
        out_shape=extra + shapes if unpack else shapes,
        in_specs=[VMEM, ANY, VMEM] + [ANY] * len(given) + [SMEM] + [ANY] * 9 + [VMEM] * 10,
        out_specs=(ANY,) * (len(shapes) + 2 * unpack),
        scratch_shapes=[
            *mirrored(shapes),
            scratch(4, 64, 16, 1024),
            *FEED_MATS,
            scratch(INNER, WIDTH),
            scratch(512, WIDTH),
            scratch(64, 32, WIDTH) if unpack else scratch(16, 128),
            pltpu.SemaphoreType.DMA((6,)),
            pltpu.SemaphoreType.DMA((len(shapes) + 2,)),
            pltpu.SemaphoreType.DMA((12,)),
        ],
        compiler_params=pltpu.CompilerParams(vmem_limit_bytes=LIMIT),
        cost_estimate=pl.CostEstimate(
            flops=2 * ROWS * 12_600_000, bytes_accessed=40_000_000, transcendentals=2_000_000
        ),
        name="forward",
    )(start, packed, dt_weight, *given, *feeds, *small, *rope)


def run_feed_backward(active, grad_top, mats, gate, upper, middle, feed_gain, earlier=()):
    shapes = (
        shape(ROWS, FEED, BF16),
        shape(ROWS, FEED, BF16),
        shape(ROWS, WIDTH, F32),
        shape(1, WIDTH, F32),
    )
    return pl.pallas_call(
        functools.partial(feed_backward_kernel, len(earlier)),
        out_shape=shapes,
        in_specs=[SMEM, VMEM, SMEM] + [ANY] * 12 + [VMEM] + [ANY] * len(earlier),
        out_specs=(ANY,) * len(shapes),
        scratch_shapes=[
            *mirrored(shapes),
            scratch(ROWS, FEED, dtype=F32),
            scratch(ROWS, FEED, dtype=F32),
            scratch(ROWS, WIDTH, dtype=F32),
            *FEED_MATS,
            pltpu.SemaphoreType.DMA((3,)),
            pltpu.SemaphoreType.DMA((4,)),
            pltpu.SemaphoreType.DMA((12,)),
        ],
        input_output_aliases={16 + k: k for k in range(len(earlier))},
        compiler_params=pltpu.CompilerParams(vmem_limit_bytes=LIMIT),
        cost_estimate=pl.CostEstimate(
            flops=2 * ROWS * 6_300_000, bytes_accessed=22_000_000, transcendentals=1_000_000
        ),
        name="feed_backward",
    )(active, grad_top, *mats[4], gate, upper, middle, feed_gain, *earlier)


def run_mix_backward(active, grad_middle, mats, proj, ssm, small, rope, pick, earlier=()):
    packed, dt_weight, out_weight, heads_weight, feeds = mats
    shapes = (
        shape(ROWS, WIDTH, BF16),
        shape(ROWS, CAT, BF16),
        shape(4, MIXED, F32),
        shape(1, MIXED, F32),
        shape(1, 128, F32),
        shape(1, 128, F32),
        shape(1, INNER, F32),
        shape(1, INNER, F32),
    )
    return pl.pallas_call(
        functools.partial(mix_backward_kernel, len(earlier)),
        out_shape=shapes,
        in_specs=[SMEM, VMEM] + [ANY] * 4 + [VMEM] * 9 + [ANY] * len(earlier),
        out_specs=(ANY,) * len(shapes),
        scratch_shapes=[
            *mirrored(shapes),
            scratch(ROWS, CAT, dtype=F32),
            scratch(ROWS, INNER, dtype=F32),
            scratch(INNER, WIDTH),
            scratch(512, WIDTH),
            scratch(ROWS, INNER, dtype=F32),
            scratch(ROWS, 512, dtype=F32),
            scratch(LEN, INNER, dtype=F32),
            scratch(LEN, INNER, dtype=F32),
            scratch(LEN, MIXED, dtype=F32),
            pltpu.SemaphoreType.DMA((4,)),
            pltpu.SemaphoreType.DMA((8,)),
        ],
        input_output_aliases={15 + k: k for k in range(len(earlier))},
        compiler_params=pltpu.CompilerParams(vmem_limit_bytes=LIMIT),
        cost_estimate=pl.CostEstimate(
            flops=2 * ROWS * 2_100_000, bytes_accessed=14_000_000, transcendentals=4_000_000
        ),
        name="mix_backward",
    )(
        active, grad_middle, out_weight, heads_weight, proj, ssm, *small[1:7], *rope, pick, *earlier
    )


def run_input_backward(active, grad_cat, grad_middle, start, mats, input_gain, earlier=()):
    shapes = (shape(ROWS, WIDTH, F32), shape(ROWS, WIDTH, BF16), shape(1, WIDTH, F32))
    return pl.pallas_call(
        functools.partial(input_backward_kernel, len(earlier)),
        out_shape=shapes,
        in_specs=[SMEM, VMEM, VMEM, VMEM, ANY, VMEM, VMEM] + [ANY] * len(earlier),
        out_specs=(ANY,) * len(shapes),
        scratch_shapes=[
            *mirrored(shapes),
            scratch(4, 64, 16, 1024),
            pltpu.SemaphoreType.DMA((4,)),
            pltpu.SemaphoreType.DMA((3,)),
        ],
        input_output_aliases={7 + k: k for k in range(len(earlier))},
        compiler_params=pltpu.CompilerParams(vmem_limit_bytes=LIMIT),
        cost_estimate=pl.CostEstimate(
            flops=2 * ROWS * 4_200_000, bytes_accessed=13_000_000, transcendentals=1000
        ),
        name="input_backward",
    )(active, grad_cat, grad_middle, start, *mats[:2], input_gain, *earlier)


def finish_kernel(
    mine, rows_own, gate_own, up_own, rows_got, gate_got, up_got, rows_last, gate_last, up_last,
    in_grad, query_grad, key_grad, value_grad, out_grad, heads_grad, gate_grad, up_grad, down_grad,
):
    def total(k, own, got, last):
        depth = own.shape[1]
        part = own[mine[k]].astype(F32) + got[:depth].astype(F32)
        return part + last[...].astype(F32)

    value = total(0, rows_own, rows_got, rows_last)
    down_grad[0] = value[:, :WIDTH]
    out_grad[0] = value[:24, WIDTH:]
    heads_grad[0] = value[24:, WIDTH:]
    value = total(1, gate_own, gate_got, gate_last)
    gate_grad[0] = value[:, :FEED]
    query_grad[0] = value[:, FEED : FEED + K0]
    key_grad[0] = value[:, FEED + K0 : FEED + V0]
    value_grad[0] = value[:, FEED + V0 : FEED + Z0]
    in_grad[0, :, : 2048 - Z0] = value[:, FEED + Z0 :]
    value = total(2, up_own, up_got, up_last)
    up_grad[0] = value[:, :FEED]
    in_grad[0, :, 2048 - Z0 :] = value[:, FEED : FEED + T0 + HEADS - 2048]


def run_finish(mine, owns, gots, lasts):
    shapes = tuple(
        jax.ShapeDtypeStruct((1, *dims), F32)
        for dims in (
            (16, T0 + HEADS - Z0),
            (16, 512),
            (16, 128),
            (16, 128),
            (24, WIDTH),
            (8, WIDTH),
            (16, FEED),
            (16, FEED),
            (32, WIDTH),
        )
    )
    return pl.pallas_call(
        finish_kernel,
        out_shape=shapes,
        in_specs=[SMEM] + [VMEM] * 9,
        out_specs=(VMEM,) * 9,
        compiler_params=pltpu.CompilerParams(vmem_limit_bytes=LIMIT // 2),
        name="finish",
    )(mine, *owns, *gots, *lasts)


def rope_tables():
    position = jnp.arange(LEN).astype(F32)
    inverse = 10000.0 ** (-(jnp.arange(32).astype(F32) * 2.0) / 64)
    angle = position[:, None] * inverse[None, :]
    cosine = jnp.tile(jnp.cos(angle), (1, 16))
    sine = jnp.sin(angle)
    return cosine, jnp.tile(jnp.concatenate([-sine, sine], axis=1), (1, 8))


def head_pick():
    lanes = lax.broadcasted_iota(jnp.int32, (INNER, 128), 0) // 64
    return (lanes == lax.broadcasted_iota(jnp.int32, (INNER, 128), 1)).astype(BF16)


def prepared_small(pieces):
    input_gain, kernel, bias, step_bias, decay_log, skip, mixer_gain, feed_gain = pieces

    def padded(v):
        return jnp.pad(v, (0, 128 - HEADS))[None]

    return (
        input_gain[None],
        kernel,
        bias[None],
        padded(step_bias),
        padded(decay_log),
        jnp.repeat(skip, 64)[None],
        mixer_gain[None],
        feed_gain[None],
    )


FIRST = (1, 0, 3, 2)
SECOND = (3, 2, 1, 0)


def partners(axis, turn):
    me = lax.axis_index(axis)
    near, far = me + 1 - 2 * lax.rem(me, 2), 3 - me
    flipped = lax.rem(lax.axis_index("section") + turn, 2) == 1
    found = (jnp.where(flipped, far, near), jnp.where(flipped, near, far))
    swaps = []
    for step in range(2):
        tables = [(FIRST, SECOND)[(core + turn + step) % 2] for core in range(2)]
        swaps.append([(4 * c + i, 4 * c + tables[c][i]) for c in range(2) for i in range(4)])
    return me, found, swaps


def exchange(array, axis, pairs):
    return lax.ppermute(array, ("section", axis), pairs)


def first_sent(part, axis, turn):
    me, (one, two), swaps = partners(axis, turn)
    return part([one, lax.rem(me + 2, 4)]).astype(BF16)


def first_got(sent, axis, turn):
    return exchange(sent, axis, partners(axis, turn)[2][0])


def handed_on(part, got, axis, turn):
    me, (one, two), swaps = partners(axis, turn)
    return (part([two]) + got[got.shape[0] // 2 :].astype(F32)).astype(BF16)


def totalled(part, got, handed, axis, turn):
    me, found, (swap_one, swap_two) = partners(axis, turn)
    last = exchange(handed, axis, swap_two)
    return part([me]) + got[: got.shape[0] // 2].astype(F32) + last.astype(F32)


def product_of(left, right, place):
    blocks = left.reshape(4, 4, 4, left.shape[0] // 64, left.shape[1])

    def part(places):
        picked = [lax.dynamic_index_in_dim(blocks, p, place, keepdims=False) for p in places]
        return dot(jnp.concatenate(picked, axis=0).reshape(-1, left.shape[1]), right)

    return part


def quarters_of(array, dim):
    def part(places):
        picked = [lax.dynamic_index_in_dim(array, p, dim, keepdims=False) for p in places]
        return jnp.concatenate(picked, axis=0).reshape(-1, array.shape[-1]).astype(F32)

    return part


def summed_on(array, axis, dim, turn):
    part = quarters_of(array, dim)
    got = first_got(first_sent(part, axis, turn), axis, turn)
    return totalled(part, got, handed_on(part, got, axis, turn), axis, turn)


def second_summed(parts, order, depth):
    array = jnp.concatenate([p.astype(BF16) for p in parts], axis=1)
    width = array.shape[1]
    rest = [0, 1, 2]
    rest.remove(order[0])
    array = array.reshape(4, 4, depth, width)
    array = summed_on(array, DP[order[1]], rest.index(order[1]), 0).astype(BF16)
    return array.reshape(4, depth, width)


def gathered_on(array, axis):
    me, (one, two), (swap_one, swap_two) = partners(axis, 0)
    got = exchange(array, axis, swap_one)
    far = exchange(jnp.stack([array, got]), axis, swap_two)
    return (array, got, far), (me, one, two, lax.rem(me + 2, 4))


def placed(blocks, places, dim):
    own, got, far = blocks
    whole = jnp.zeros((*own.shape[:dim], 4, *own.shape[dim:]), own.dtype)
    for block, place in zip((own, got, far[0], far[1]), places):
        whole = lax.dynamic_update_index_in_dim(whole, block, place, dim)
    return whole


def gathered(block, order):
    block = placed(*gathered_on(block, DP[order[2]]), 0)
    block = placed(*gathered_on(block, DP[order[1]]), 0 if order[1] < order[2] else 1)
    return gathered_on(block, DP[order[0]])


def column_blocks(matrix):
    return [matrix[:, at : at + 1024] for at in range(0, matrix.shape[1], 1024)]


def on_device(
    layer_input,
    out_grad,
    in_weight,
    query_weight,
    key_weight,
    value_weight,
    out_weight,
    heads_weight,
    gate_weight,
    up_weight,
    down_weight,
    *pieces,
):
    micro, part, width = layer_input.shape
    rows = micro * part
    cat = jnp.concatenate(
        [query_weight[0], key_weight[0], value_weight[0], in_weight[0, :, :3328]], axis=1
    )
    steps = jnp.pad(in_weight[0, :, 3328:].reshape(1, -1), ((0, 7), (0, 1024 - 16 * HEADS)))
    own = jnp.concatenate(
        [
            *column_blocks(cat),
            out_weight[0],
            heads_weight[0],
            steps,
        ],
        axis=0,
    )
    packed = lax.all_gather(own, DP, axis=0, tiled=False)
    dt_weight = packed[:, DT0, : 16 * HEADS].reshape(WIDTH, HEADS)
    feeds = [
        gathered(weight[0], order)
        for weight, order in (
            (gate_weight, (0, 1, 2)),
            (up_weight, (1, 2, 0)),
            (down_weight, (2, 0, 1)),
        )
    ]
    places = jnp.stack([place for blocks, found in feeds for place in found]).astype(jnp.int32)
    mats = (
        packed,
        jnp.pad(dt_weight, ((0, 0), (0, 128 - HEADS))),
        (places, *(piece for blocks, found in feeds for piece in blocks)),
    )
    small = prepared_small([piece[0] for piece in pieces])
    rope = rope_tables()
    pick = head_pick()
    first = lax.axis_index("section") == 0

    start_low = layer_input.reshape(rows, width)
    out_mat, heads_mat, *kept_low = run_forward(start_low, mats, small, rope)
    mats = (*mats[:2], out_mat, heads_mat, mats[2])
    start_high = lax.ppermute(kept_low[0], "section", [(0, 1)])
    kept_high = run_forward(start_high, mats, small, rope)
    layer_outputs = jnp.where(first, kept_low[0], kept_high[0]).reshape(1, micro, part, width)

    on_high = jnp.where(first, 0, 1).astype(jnp.int32).reshape(1)
    on_low = 1 - on_high
    top_high = out_grad.reshape(rows, width)
    feed_high = run_feed_backward(
        on_high, top_high, mats, kept_high[8], kept_high[9], kept_high[6], small[7]
    )
    mix_high = run_mix_backward(
        on_high, feed_high[2], mats, kept_high[2], kept_high[3], small, rope, pick
    )
    input_high = run_input_backward(
        on_high, mix_high[1], feed_high[2], start_high, mats, small[0]
    )
    slots = (1, 4, 5, 7, 10)
    low_top, *tied = lax.optimization_barrier((input_high[1], *(kept_high[s] for s in slots)))
    tied = dict(zip(slots, tied))
    top_low = lax.ppermute(low_top, "section", [(1, 0)])

    def chosen(slot):
        return jnp.where(first, kept_low[slot], tied[slot])

    normed_t, ffin_t, hidden_t = (chosen(slot).T for slot in (1, 7, 10))
    joined_t = jnp.concatenate(
        [chosen(4).T.reshape(64, 24, rows), chosen(5).T.reshape(64, 8, rows)], axis=1
    ).reshape(2048, rows)

    feed = run_feed_backward(
        on_low, top_low, mats, kept_low[8], kept_low[9], kept_low[6], small[7], feed_high
    )
    grad_gate, grad_upper, grad_middle, feed_grad = feed
    grad_low = jnp.where(first, top_low, top_high)
    grad_low, grad_gate, grad_upper = lax.optimization_barrier((grad_low, grad_gate, grad_upper))
    orders = ((2, 0, 1), (0, 1, 2), (1, 2, 0))
    axes = [DP[order[0]] for order in orders]
    products = [
        product_of(left, right, order[0])
        for left, right, order in zip(
            (hidden_t, ffin_t, ffin_t), (grad_low, grad_gate, grad_upper), orders
        )
    ]
    sents = [first_sent(p, axis, 0) for p, axis in zip(products, axes)]
    grad_middle, *sents = lax.optimization_barrier((grad_middle, *sents))
    gots = [first_got(sent, axis, 0) for sent, axis in zip(sents, axes)]
    mix = run_mix_backward(
        on_low, grad_middle, mats, kept_low[2], kept_low[3], small, rope, pick, mix_high
    )
    grad_branch, grad_cat, *small_grads = mix
    mix_products = [
        product_of(left, right, order[0])
        for left, right, order in zip(
            (joined_t, normed_t, normed_t),
            (grad_branch, grad_cat[:, :2048], grad_cat[:, 2048:]),
            orders,
        )
    ]
    mix_sents = [first_sent(p, axis, 1) for p, axis in zip(mix_products, axes)]
    pending = lax.optimization_barrier((*gots, *mix_sents))
    gots, mix_sents = pending[:3], pending[3:]
    mix_gots = [first_got(sent, axis, 1) for sent, axis in zip(mix_sents, axes)]
    handed = [handed_on(p, got, axis, 0) for p, got, axis in zip(products, gots, axes)]
    last_middle, *pending = lax.optimization_barrier(
        (grad_middle, grad_low, grad_gate, grad_upper, grad_branch, grad_cat, *handed)
    )
    rights, (late_branch, late_cat), handed = pending[:3], pending[3:5], pending[5:]
    products = [
        product_of(left, right, order[0])
        for left, right, order in zip((hidden_t, ffin_t, ffin_t), rights, orders)
    ]
    mix_products = [
        product_of(left, right, order[0])
        for left, right, order in zip(
            (joined_t, normed_t, normed_t),
            (late_branch, late_cat[:, :2048], late_cat[:, 2048:]),
            orders,
        )
    ]
    feed_parts = [
        totalled(p, got, hand, axis, 0)
        for p, got, hand, axis in zip(products, gots, handed, axes)
    ]
    mix_parts = [
        totalled(p, got, handed_on(p, got, axis, 1), axis, 1)
        for p, got, axis in zip(mix_products, mix_gots, axes)
    ]
    grad_start, unused, input_grad = run_input_backward(
        on_low, grad_cat, last_middle, start_low, mats, small[0], input_high
    )
    small_grads = [input_grad, *small_grads]
    input_g, kernel_g, bias_g, step_g, decay_g, skip_g, mixer_g = small_grads
    small_grads = (
        input_g[0],
        kernel_g,
        bias_g[0],
        step_g[0, :HEADS],
        decay_g[0, :HEADS],
        skip_g.reshape(HEADS, 64).sum(axis=1),
        mixer_g[0],
        feed_grad[0],
    )
    vector = jnp.concatenate([piece.reshape(-1) for piece in small_grads])
    vector = jnp.pad(vector, (0, -vector.shape[0] % 1024)).reshape(-1, 128)
    vectors = lax.all_gather(vector.astype(BF16), DP, axis=0, tiled=False)
    seconds = [
        second_summed(pair, order, depth)
        for pair, order, depth in zip(zip(feed_parts, mix_parts), orders, (32, 16, 16))
    ]
    axes = [DP[order[2]] for order in orders]
    quarters = [quarters_of(array, 0) for array in seconds]
    sents = [first_sent(p, axis, 0) for p, axis in zip(quarters, axes)]
    gots = [first_got(sent, axis, 0) for sent, axis in zip(sents, axes)]
    vectors, *unused = lax.optimization_barrier((vectors, *sents))
    total = jnp.sum(vectors.astype(F32), axis=0).reshape(-1)
    handed = [handed_on(p, got, axis, 0) for p, got, axis in zip(quarters, gots, axes)]
    lasts = [
        exchange(hand, axis, partners(axis, 0)[2][1]) for hand, axis in zip(handed, axes)
    ]
    mine = jnp.stack([lax.axis_index(axis) for axis in axes]).astype(jnp.int32)
    mat_grads = run_finish(mine, seconds, gots, lasts)

    summed, at = ([], 0)
    for piece in small_grads:
        summed.append(total[at : at + piece.size].reshape(1, *piece.shape))
        at += piece.size
    return (
        layer_outputs,
        grad_start.reshape(1, micro, part, width),
        *mat_grads,
        *summed,
    )


def solution(mesh):
    torus = Mesh(
        mesh.devices.reshape(mesh.shape["section"], 4, 4, 4), ("section", "dp_0", "dp_1", "dp_2")
    )
    in_specs = (
        P(None, DP, None),
        P(None, DP, None),
        P("section", DP, None),
        P("section", DP, None),
        P("section", DP, None),
        P("section", DP, None),
        P("section", DP, None),
        P("section", DP, None),
        P("section", DP, None),
        P("section", DP, None),
        P("section", DP, None),
        P("section", None),
        P("section", None, None),
        P("section", None),
        P("section", None),
        P("section", None),
        P("section", None),
        P("section", None),
        P("section", None),
    )
    out_specs = (
        P("section", None, DP, None),
        P("section", None, DP, None),
        P("section", DP, None),
        P("section", DP, None),
        P("section", DP, None),
        P("section", DP, None),
        P("section", DP, None),
        P("section", DP, None),
        P("section", DP, None),
        P("section", DP, None),
        P("section", DP, None),
        P("section", None),
        P("section", None, None),
        P("section", None),
        P("section", None),
        P("section", None),
        P("section", None),
        P("section", None),
        P("section", None),
    )
    return jax.shard_map(
        on_device, mesh=torus, in_specs=in_specs, out_specs=out_specs, check_vma=False
    )
```

```python
import functools

import jax
import jax.numpy as jnp
from jax import lax
from jax.experimental import pallas as pl
from jax.experimental.pallas import tpu as pltpu
from jax.sharding import Mesh
from jax.sharding import PartitionSpec as P

LEN = 128
ROWS = 256
WIDTH = 1024
FEED = 2048
INNER = 1536
MIXED = 1792
CAT = 4224
HEADS = 24
DP = ("dp_0", "dp_1", "dp_2")
F32 = jnp.float32
BF16 = jnp.bfloat16
HIDE = -1e30
Q0, K0, V0, Z0, X0, T0 = 0, 512, 640, 768, 2304, 4096
OUT0, HEADS0, DT0, PACKED = 64, 88, 96, 104


def dot(left, right):
    return jnp.dot(left, right, preferred_element_type=F32)


def dot_nt(left, right):
    return lax.dot_general(left, right, (((1,), (1,)), ((), ())), preferred_element_type=F32)


def dot_tn(left, right):
    return lax.dot_general(left, right, (((0,), (0,)), ((), ())), preferred_element_type=F32)


def dot_full(left, right):
    return jnp.dot(left, right, precision=lax.Precision.HIGHEST, preferred_element_type=F32)


def iota(shape, dim):
    return lax.broadcasted_iota(jnp.int32, shape, dim)


def sigmoid(v):
    return 1.0 / (1.0 + jnp.exp(-v))


def softplus(v):
    return jnp.maximum(v, 0.0) + jnp.log(1.0 + jnp.exp(-jnp.abs(v)))


def swap_halves(v):
    width = v.shape[1]
    near = lax.rem(iota(v.shape, 1), 64) < 32
    return jnp.where(near, pltpu.roll(v, width - 32, 1), pltpu.roll(v, 32, 1))


def shifted_down(v, by):
    if by == 0:
        return v
    return jnp.where(iota(v.shape, 0) >= by, pltpu.roll(v, by, 0), 0.0)


def shifted_up(v, by):
    if by == 0:
        return v
    rows = v.shape[0]
    return jnp.where(iota(v.shape, 0) < rows - by, pltpu.roll(v, rows - by, 0), 0.0)


def rms(v):
    return lax.rsqrt(jnp.mean(v * v, axis=-1, keepdims=True) + 1e-05)


def rms_backward(v, gain, grad):
    scale = rms(v)
    gained = grad * gain
    inner = jnp.mean(gained * v, axis=-1, keepdims=True)
    grad_v = scale * gained - v * (scale * scale * scale * inner)
    return grad_v, jnp.sum(grad * v * scale, axis=0, keepdims=True)


def left_half():
    return iota((LEN, 128), 1) < 64


def both_halves(v, group, left):
    turned = pltpu.roll(v, 64, 1)
    return jnp.where(left, v, turned) if group == 0 else jnp.where(left, turned, v)


def stacked(pairs, left):
    parts = []
    for pair in pairs:
        parts.append(jnp.where(left, pair, 0.0))
        parts.append(jnp.where(left, 0.0, pair))
    return jnp.concatenate(parts, axis=0).astype(BF16)


def unstacked(rows, index, left):
    low = rows[2 * index * LEN : (2 * index + 1) * LEN]
    high = rows[(2 * index + 1) * LEN : (2 * index + 2) * LEN]
    return jnp.where(left, low, high)


def attention_parts(proj, rows, cosine, sine):
    left = left_half()
    query = proj[rows, Q0:K0]
    query = query * cosine[...] + swap_halves(query) * sine[...]
    key = proj[rows, K0:V0]
    key = key * cosine[:, :128] + swap_halves(key) * sine[:, :128]
    value = proj[rows, V0:Z0]
    groups = []
    for group in range(2):
        pairs = [query[:, 128 * p : 128 * p + 128] for p in (2 * group, 2 * group + 1)]
        queries = stacked(pairs, left)
        keys = both_halves(key, group, left).astype(BF16)
        values = both_halves(value, group, left).astype(BF16)
        scores = dot_nt(queries, keys) * 0.125
        time = lax.rem(iota(scores.shape, 0), LEN)
        scores = jnp.where(iota(scores.shape, 1) <= time, scores, HIDE)
        top = jnp.max(scores, axis=-1, keepdims=True)
        expo = jnp.exp(scores - top)
        probs = expo / jnp.sum(expo, axis=-1, keepdims=True)
        groups.append((queries, keys, values, probs))
    return left, groups


def attention_forward(proj, rows, cosine, sine, attended):
    left, groups = attention_parts(proj, rows, cosine, sine)
    for group, (queries, keys, values, probs) in enumerate(groups):
        mixed = dot(probs.astype(BF16), values)
        for index in range(2):
            at = 256 * group + 128 * index
            attended[rows, at : at + 128] = unstacked(mixed, index, left).astype(BF16)


def attention_backward(proj, rows, cosine, sine, grad_attended, grad_cat):
    left, groups = attention_parts(proj, rows, cosine, sine)
    key_parts, value_parts = [], []
    for group, (queries, keys, values, probs) in enumerate(groups):
        pairs = [grad_attended[:, 128 * p : 128 * p + 128] for p in (2 * group, 2 * group + 1)]
        grads = stacked(pairs, left)
        grad_values = dot_tn(probs.astype(BF16), grads)
        grad_probs = dot_nt(grads, values)
        inner = jnp.sum(probs * grad_probs, axis=-1, keepdims=True)
        grad_scores = (probs * (grad_probs - inner)).astype(BF16)
        grad_queries = dot(grad_scores, keys) * 0.125
        grad_keys = dot_tn(grad_scores, queries) * 0.125
        for index in range(2):
            at = 256 * group + 128 * index
            grad = unstacked(grad_queries, index, left)
            grad = grad * cosine[:, :128] - swap_halves(grad) * sine[:, :128]
            grad_cat[rows, at : at + 128] = grad.astype(BF16)
        key_parts.append(grad_keys + pltpu.roll(grad_keys, 64, 1))
        value_parts.append(grad_values + pltpu.roll(grad_values, 64, 1))
    grad = jnp.where(left, key_parts[0], key_parts[1])
    grad = grad * cosine[:, :128] - swap_halves(grad) * sine[:, :128]
    grad_cat[rows, K0:V0] = grad.astype(BF16)
    grad_cat[rows, V0:Z0] = jnp.where(left, value_parts[0], value_parts[1]).astype(BF16)


def mamba_parts(proj, rows, kernel, bias, step_bias, decay_log):
    mixed = proj[rows, X0:T0]
    total = bias[...] + mixed * kernel[3:4, :]
    for tap in range(3):
        total = total + shifted_down(mixed, 3 - tap) * kernel[tap : tap + 1, :]
    active = total * sigmoid(total)
    step = softplus(proj[rows, T0:CAT] + step_bias[...])
    rate = -step * jnp.exp(decay_log[...])
    earlier = (iota((LEN, LEN), 0) >= iota((LEN, LEN), 1)).astype(F32)
    cumul = dot_full(earlier, rate)
    state_in = active[:, INNER : INNER + 128].astype(BF16)
    state_out = active[:, INNER + 128 :].astype(BF16)
    return mixed, total, active, step, rate, cumul, state_in, state_out


def stepped(step, pair, left):
    return jnp.where(left, step[:, 2 * pair : 2 * pair + 1], step[:, 2 * pair + 1 : 2 * pair + 2])


def mamba_forward(proj, rows, kernel, bias, step_bias, decay_log, skip, gain, ssm, mamba):
    left = left_half()
    parts = mamba_parts(proj, rows, kernel, bias, step_bias, decay_log)
    mixed, total, active, step, rate, cumul, state_in, state_out = parts
    across = cumul.T
    hidden = jnp.where(iota((LEN, LEN), 0) >= iota((LEN, LEN), 1), 0.0, HIDE)
    meeting = dot_nt(state_out, state_in)
    for pair in range(HEADS // 2):
        at = 128 * pair
        inputs = active[:, at : at + 128]
        scaled = (inputs * stepped(step, pair, left)).astype(BF16)
        mixing = []
        for head in (2 * pair, 2 * pair + 1):
            spread = cumul[:, head : head + 1] - across[head : head + 1, :] + hidden
            mixing.append((meeting * jnp.exp(spread)).astype(BF16))
        both = dot(jnp.concatenate(mixing, axis=0), scaled)
        out = unstacked(both, 0, left) + skip[:, at : at + 128] * inputs
        ssm[rows, at : at + 128] = out
    z = proj[rows, Z0:X0]
    gated = ssm[rows, :] * (z * sigmoid(z))
    mamba[rows, :] = (gated * rms(gated) * gain[...]).astype(BF16)


def head_sums(v, pick):
    high = v.astype(BF16)
    low = (v - high.astype(F32)).astype(BF16)
    return dot(high, pick) + dot(low, pick)


def mamba_backward(
    proj, rows, kernel, bias, step_bias, decay_log, skip, gain, pick, ssm, grad_mamba, grad_cat,
    across_scratch, balance_scratch, touch_scratch, grad_active, add_small,
):
    left = left_half()
    parts = mamba_parts(proj, rows, kernel, bias, step_bias, decay_log)
    mixed, total, active, step, rate, cumul, state_in, state_out = parts
    across = cumul.T
    hidden = jnp.where(iota((LEN, LEN), 1) >= iota((LEN, LEN), 0), 0.0, HIDE)
    meeting = dot_nt(state_out, state_in).T
    z = proj[rows, Z0:X0]
    out = ssm[rows, :]
    gate = sigmoid(z)
    gated = out * (z * gate)
    grad_gated, grad_gain = rms_backward(gated, gain[...], grad_mamba)
    add_small(6, grad_gain)
    grad_cat[rows, Z0:X0] = (grad_gated * out * (gate * (1.0 + z * (1.0 - gate)))).astype(BF16)
    grad_out = grad_gated * (z * gate)
    add_small(5, jnp.sum(grad_out * active[:, :INNER], axis=0, keepdims=True))
    grad_meeting = jnp.zeros((LEN, LEN), F32)
    for pair in range(HEADS // 2):
        at = 128 * pair
        inputs = active[:, at : at + 128]
        steps = stepped(step, pair, left)
        scaled = (inputs * steps).astype(BF16)
        grad_pair = grad_out[:, at : at + 128]
        grad_low = grad_pair.astype(BF16)
        halves = jnp.concatenate(
            [jnp.where(left, scaled, jnp.zeros_like(scaled)), jnp.where(left, jnp.zeros_like(scaled), scaled)],
            axis=0,
        )
        grad_mixing = dot_nt(halves, grad_low)
        mixing = []
        for place, head in enumerate((2 * pair, 2 * pair + 1)):
            spread = across[head : head + 1, :] - cumul[:, head : head + 1] + hidden
            decay = jnp.exp(spread)
            mixing.append((meeting * decay).astype(BF16))
            grad_meeting = grad_meeting + grad_mixing[LEN * place : LEN * place + LEN] * decay
        both = dot(jnp.concatenate(mixing, axis=0), grad_low)
        grad_scaled = unstacked(both, 0, left)
        skips = skip[:, at : at + 128]
        grad_active[:, at : at + 128] = grad_scaled * steps + skips * grad_pair
        touch_scratch[:, at : at + 128] = grad_scaled * inputs
        balance_scratch[:, at : at + 128] = grad_low.astype(F32) * (
            out[:, at : at + 128] - skips * inputs
        ) - scaled.astype(F32) * grad_scaled
    grad_low = grad_meeting.astype(BF16)
    grad_active[:, INNER : INNER + 128] = dot(grad_low, state_out)
    grad_active[:, INNER + 128 :] = dot_tn(grad_low, state_in)
    later = (iota((LEN, LEN), 1) >= iota((LEN, LEN), 0)).astype(F32)
    grad_rate = dot_full(later, head_sums(balance_scratch[...], pick[...]))
    add_small(4, jnp.sum(grad_rate * rate, axis=0, keepdims=True))
    grad_step = head_sums(touch_scratch[...], pick[...]) - grad_rate * jnp.exp(decay_log[...])
    grad_dt = grad_step * sigmoid(proj[rows, T0:CAT] + step_bias[...])
    add_small(3, jnp.sum(grad_dt, axis=0, keepdims=True))
    grad_cat[rows, T0:CAT] = grad_dt.astype(BF16)
    slope = sigmoid(total)
    grad_total = grad_active[...] * (slope * (1.0 + total * (1.0 - slope)))
    add_small(2, jnp.sum(grad_total, axis=0, keepdims=True))
    grad_mixed = grad_total * kernel[3:4, :]
    taps = []
    for tap in range(4):
        taps.append(jnp.sum(grad_total * shifted_down(mixed, 3 - tap), axis=0, keepdims=True))
        if tap < 3:
            grad_mixed = grad_mixed + shifted_up(grad_total, 3 - tap) * kernel[tap : tap + 1, :]
    add_small(1, jnp.concatenate(taps, axis=0))
    grad_cat[rows, X0:T0] = grad_mixed.astype(BF16)


def flat(block):
    return block.reshape(block.shape[0] * block.shape[1], block.shape[2])


def start_all(copies):
    for copy in copies:
        copy.start()


def feed_copies(places, pieces, buffers, sems):
    copies = []
    for k, buffer in enumerate(buffers):
        own, got, far = pieces[3 * k : 3 * k + 3]
        for q, source in enumerate((own, got, far.at[0], far.at[1])):
            target = buffer.at[(slice(None),) * k + (places[4 * k + q],)]
            copies.append(pltpu.make_async_copy(source, target, sems.at[4 * k + q]))
    return copies


def rows_of(block):
    return block.reshape(-1, block.shape[-1])


def forward_kernel(unpack, x, packed, dt_weight, *refs):
    if unpack:
        given, results = (None, None), refs[20:22]
        rest = refs[:20] + refs[22:]
    else:
        given, results = refs[:2], (None, None)
        rest = refs[2:]
    forward_body(unpack, x, packed, dt_weight, *given, *results, *rest)


def forward_body(
    unpack, x, packed, dt_weight, out_weight, heads_weight, out_result, heads_result,
    places, gate_own, gate_got, gate_far, up_own, up_got, up_far, down_own, down_got, down_far,
    input_gain, kernel, bias, step_bias, decay_log, skip,
    mixer_gain, feed_gain, cosine, sine,
    result_out, normed_out, proj_out, ssm_out, mamba_out, attended_out, middle_out, ffin_out, gate_out,
    upper_out, hidden_out,
    result, normed, proj, ssm, mamba, attended, middle, ffin, gate, upper, hidden,
    cat, gate_mat, up_mat, down_mat, out_mat, heads_mat, mixed, sems, out_sems, feed_sems,
):
    leaving = []

    def leave(*pairs):
        for source, target in pairs:
            copy = pltpu.make_async_copy(source, target, out_sems.at[len(leaving)])
            copy.start()
            leaving.append(copy)

    copies = [
        pltpu.make_async_copy(packed.at[:, pl.ds(16 * j, 16), :], cat.at[j], sems.at[j])
        for j in range(4)
    ]
    if unpack:
        copies.append(pltpu.make_async_copy(packed.at[:, pl.ds(OUT0, 32), :], mixed, sems.at[4]))
    else:
        copies.append(pltpu.make_async_copy(out_weight, out_mat, sems.at[4]))
        copies.append(pltpu.make_async_copy(heads_weight, heads_mat, sems.at[5]))
    pieces = (gate_own, gate_got, gate_far, up_own, up_got, up_far, down_own, down_got, down_far)
    feeds = feed_copies(places, pieces, (gate_mat, up_mat, down_mat), feed_sems)
    start_all(copies + feeds)
    state = x[...].astype(F32)
    normed[...] = (state * rms(state) * input_gain[...]).astype(BF16)
    proj[:, T0:CAT] = dot(normed[...], dt_weight[...])
    for j in range(4):
        copies[j].wait()
        proj[:, 1024 * j : 1024 * j + 1024] = dot(normed[...], flat(cat[j]))
    leave((normed, normed_out), (proj, proj_out))

    def sequence(index, carry):
        rows = pl.ds(pl.multiple_of(index * LEN, LEN), LEN)
        attention_forward(proj, rows, cosine, sine, attended)
        mamba_forward(proj, rows, kernel, bias, step_bias, decay_log, skip, mixer_gain, ssm, mamba)
        return carry

    lax.fori_loop(0, 2, sequence, 0)
    leave((ssm, ssm_out), (mamba, mamba_out), (attended, attended_out))
    for copy in copies[4:]:
        copy.wait()
    if unpack:
        wide = mixed[...].astype(F32)
        out_mat[...] = wide[:, :24].reshape(INNER, WIDTH).astype(BF16)
        heads_mat[...] = wide[:, 24:].reshape(512, WIDTH).astype(BF16)
        leave((out_mat, out_result), (heads_mat, heads_result))

    part = dot(mamba[...], out_mat[...]) + dot(attended[...], heads_mat[...])
    middle[...] = x[...].astype(F32) + part
    value = middle[...]
    ffin[...] = (value * rms(value) * feed_gain[...]).astype(BF16)
    leave((middle, middle_out), (ffin, ffin_out))
    for copy in feeds[:8]:
        copy.wait()

    for half in range(2):
        at = slice(1024 * half, 1024 * half + 1024)
        low = dot(ffin[...], rows_of(gate_mat[:, :, :, :, at]))
        high = dot(ffin[...], rows_of(up_mat[:, :, :, :, at]))
        gate[:, at] = low
        upper[:, at] = high
        hidden[:, at] = (low * sigmoid(low) * high).astype(BF16)
    leave((gate, gate_out), (upper, upper_out), (hidden, hidden_out))
    for copy in feeds[8:]:
        copy.wait()

    result[...] = (middle[...] + dot(hidden[...], rows_of(down_mat[...]))).astype(BF16)
    leave((result, result_out))
    for copy in leaving:
        copy.wait()


def leave_all(pairs, sems):
    copies = [
        pltpu.make_async_copy(source, target, sems.at[k]) for k, (source, target) in enumerate(pairs)
    ]
    start_all(copies)
    return copies


def feed_backward_kernel(earlier, active, *refs):
    @pl.when(active[0] == 1)
    def run():
        feed_backward_body(*refs[:15], *refs[15 + earlier :])


def feed_backward_body(
    grad_top, places, gate_own, gate_got, gate_far, up_own, up_got, up_far, down_own, down_got, down_far,
    gate_in, upper_in, middle_in, feed_gain,
    grad_gate_out, grad_upper_out, grad_middle_out, feed_grad_out,
    grad_gate, grad_upper, grad_middle, feed_grad,
    gate, upper, middle, gate_mat, up_mat, down_mat, sems, out_sems, feed_sems,
):
    inputs = [
        pltpu.make_async_copy(gate_in, gate, sems.at[0]),
        pltpu.make_async_copy(upper_in, upper, sems.at[1]),
        pltpu.make_async_copy(middle_in, middle, sems.at[2]),
    ]
    pieces = (gate_own, gate_got, gate_far, up_own, up_got, up_far, down_own, down_got, down_far)
    feeds = feed_copies(places, pieces, (gate_mat, up_mat, down_mat), feed_sems)
    start_all(feeds[8:] + inputs + feeds[:8])
    for copy in feeds[8:]:
        copy.wait()

    for half in range(2):
        at = slice(1024 * half, 1024 * half + 1024)
        grad_hidden = dot_nt(grad_top[...], rows_of(down_mat[2 * half : 2 * half + 2]))
        if half == 0:
            inputs[0].wait()
            inputs[1].wait()
        low, high = gate[:, at], upper[:, at]
        slope = sigmoid(low)
        grad_upper[:, at] = (grad_hidden * (low * slope)).astype(BF16)
        part = grad_hidden * high * (slope * (1.0 + low * (1.0 - slope)))
        grad_gate[:, at] = part.astype(BF16)
    leaving = leave_all(((grad_gate, grad_gate_out), (grad_upper, grad_upper_out)), out_sems)
    for copy in feeds[:8]:
        copy.wait()

    grad_ffin = dot_nt(grad_gate[...], rows_of(gate_mat[...]))
    grad_ffin = grad_ffin + dot_nt(grad_upper[...], rows_of(up_mat[...]))
    inputs[2].wait()
    grad_part, grad_gain = rms_backward(middle[...], feed_gain[...], grad_ffin)
    feed_grad[...] = grad_gain
    grad_middle[...] = grad_top[...].astype(F32) + grad_part
    leaving += leave_all(
        ((grad_middle, grad_middle_out), (feed_grad, feed_grad_out)), out_sems.at[pl.ds(2, 2)]
    )
    for copy in leaving:
        copy.wait()


def mix_backward_kernel(earlier, active, *refs):
    @pl.when(active[0] == 1)
    def run():
        mix_backward_body(*refs[:14], *refs[14 + earlier :])


def mix_backward_body(
    grad_middle, out_weight, heads_weight, proj_in, ssm_in, kernel, bias,
    step_bias, decay_log, skip, mixer_gain, cosine, sine, pick,
    grad_branch_out, grad_cat_out, kernel_grad_out, bias_grad_out,
    step_grad_out, decay_grad_out, skip_grad_out, mixer_grad_out,
    grad_branch, grad_cat, kernel_grad, bias_grad, step_grad, decay_grad,
    skip_grad, mixer_grad,
    proj, ssm,
    out_mat, heads_mat, grad_mamba, grad_attended, balance, touch, grad_active, sems,
    out_sems,
):
    copies = [
        pltpu.make_async_copy(out_weight, out_mat, sems.at[0]),
        pltpu.make_async_copy(heads_weight, heads_mat, sems.at[1]),
        pltpu.make_async_copy(proj_in, proj, sems.at[2]),
        pltpu.make_async_copy(ssm_in, ssm, sems.at[3]),
    ]
    start_all(copies)
    grad_branch[...] = grad_middle[...].astype(BF16)
    copies[0].wait()
    copies[1].wait()

    grad_mamba[...] = dot_nt(grad_branch[...], out_mat[...])
    grad_attended[...] = dot_nt(grad_branch[...], heads_mat[...])
    small = {
        1: kernel_grad,
        2: bias_grad,
        3: step_grad,
        4: decay_grad,
        5: skip_grad,
        6: mixer_grad,
    }
    for ref in small.values():
        ref[...] = jnp.zeros_like(ref)

    def add_small(slot, value):
        small[slot][...] += value

    copies[2].wait()
    copies[3].wait()

    def sequence(index, carry):
        rows = pl.ds(pl.multiple_of(index * LEN, LEN), LEN)
        grads = grad_attended[rows, :]
        attention_backward(proj, rows, cosine, sine, grads, grad_cat)
        mamba_backward(
            proj, rows, kernel, bias, step_bias, decay_log, skip, mixer_gain, pick, ssm,
            grad_mamba[rows, :], grad_cat, None, balance, touch, grad_active, add_small,
        )
        return carry

    lax.fori_loop(0, 2, sequence, 0)
    leaving = leave_all(
        (
            (grad_branch, grad_branch_out),
            (grad_cat, grad_cat_out),
            (kernel_grad, kernel_grad_out),
            (bias_grad, bias_grad_out),
            (step_grad, step_grad_out),
            (decay_grad, decay_grad_out),
            (skip_grad, skip_grad_out),
            (mixer_grad, mixer_grad_out),
        ),
        out_sems,
    )
    for copy in leaving:
        copy.wait()


def input_backward_kernel(earlier, active, *refs):
    @pl.when(active[0] == 1)
    def run():
        input_backward_body(*refs[:6], *refs[6 + earlier :])


def input_backward_body(
    grad_cat, grad_middle, x, packed, dt_weight, input_gain,
    grad_start_out, start_low_out, input_grad_out,
    grad_start, start_low, input_grad,
    cat, sems, out_sems,
):
    copies = [
        pltpu.make_async_copy(packed.at[:, pl.ds(16 * j, 16), :], cat.at[j], sems.at[j])
        for j in range(4)
    ]
    start_all(copies)
    grad_normed = dot_nt(grad_cat[:, T0:CAT], dt_weight[...])
    for j in range(4):
        copies[j].wait()
        part = dot_nt(grad_cat[:, 1024 * j : 1024 * j + 1024], flat(cat[j]))
        grad_normed = grad_normed + part
    state = x[...].astype(F32)
    grad_state, grad_gain = rms_backward(state, input_gain[...], grad_normed)
    input_grad[...] = grad_gain
    total = grad_middle[...] + grad_state
    grad_start[...] = total
    start_low[...] = total.astype(BF16)
    leaving = leave_all(
        ((grad_start, grad_start_out), (start_low, start_low_out), (input_grad, input_grad_out)),
        out_sems,
    )
    for copy in leaving:
        copy.wait()


VMEM = pl.BlockSpec(memory_space=pltpu.VMEM)
SMEM = pl.BlockSpec(memory_space=pltpu.SMEM)
ANY = pl.BlockSpec(memory_space=pl.ANY)
LIMIT = 60 * 1024 * 1024


def shape(rows, columns, dtype):
    return jax.ShapeDtypeStruct((rows, columns), dtype)


def scratch(*dims, dtype=BF16):
    return pltpu.VMEM(dims, dtype)


FEED_MATS = (
    scratch(4, 4, 4, 16, FEED),
    scratch(4, 4, 4, 16, FEED),
    scratch(4, 4, 4, 32, WIDTH),
)


def mirrored(shapes):
    return [pltpu.VMEM(s.shape, s.dtype) for s in shapes]


def run_forward(start, mats, small, rope):
    packed, dt_weight, *given, feeds = mats
    unpack = not given
    extra = (shape(INNER, WIDTH, BF16), shape(512, WIDTH, BF16))
    shapes = (
        shape(ROWS, WIDTH, BF16),
        shape(ROWS, WIDTH, BF16),
        shape(ROWS, CAT, F32),
        shape(ROWS, INNER, F32),
        shape(ROWS, INNER, BF16),
        shape(ROWS, 512, BF16),
        shape(ROWS, WIDTH, F32),
        shape(ROWS, WIDTH, BF16),
        shape(ROWS, FEED, F32),
        shape(ROWS, FEED, F32),
        shape(ROWS, FEED, BF16),
    )
    return pl.pallas_call(
        functools.partial(forward_kernel, unpack),
        out_shape=extra + shapes if unpack else shapes,
        in_specs=[VMEM, ANY, VMEM] + [ANY] * len(given) + [SMEM] + [ANY] * 9 + [VMEM] * 10,
        out_specs=(ANY,) * (len(shapes) + 2 * unpack),
        scratch_shapes=[
            *mirrored(shapes),
            scratch(4, 64, 16, 1024),
            *FEED_MATS,
            scratch(INNER, WIDTH),
            scratch(512, WIDTH),
            scratch(64, 32, WIDTH) if unpack else scratch(16, 128),
            pltpu.SemaphoreType.DMA((6,)),
            pltpu.SemaphoreType.DMA((len(shapes) + 2,)),
            pltpu.SemaphoreType.DMA((12,)),
        ],
        compiler_params=pltpu.CompilerParams(vmem_limit_bytes=LIMIT),
        cost_estimate=pl.CostEstimate(
            flops=2 * ROWS * 12_600_000, bytes_accessed=40_000_000, transcendentals=2_000_000
        ),
        name="forward",
    )(start, packed, dt_weight, *given, *feeds, *small, *rope)


def run_feed_backward(active, grad_top, mats, gate, upper, middle, feed_gain, earlier=()):
    shapes = (
        shape(ROWS, FEED, BF16),
        shape(ROWS, FEED, BF16),
        shape(ROWS, WIDTH, F32),
        shape(1, WIDTH, F32),
    )
    return pl.pallas_call(
        functools.partial(feed_backward_kernel, len(earlier)),
        out_shape=shapes,
        in_specs=[SMEM, VMEM, SMEM] + [ANY] * 12 + [VMEM] + [ANY] * len(earlier),
        out_specs=(ANY,) * len(shapes),
        scratch_shapes=[
            *mirrored(shapes),
            scratch(ROWS, FEED, dtype=F32),
            scratch(ROWS, FEED, dtype=F32),
            scratch(ROWS, WIDTH, dtype=F32),
            *FEED_MATS,
            pltpu.SemaphoreType.DMA((3,)),
            pltpu.SemaphoreType.DMA((4,)),
            pltpu.SemaphoreType.DMA((12,)),
        ],
        input_output_aliases={16 + k: k for k in range(len(earlier))},
        compiler_params=pltpu.CompilerParams(vmem_limit_bytes=LIMIT),
        cost_estimate=pl.CostEstimate(
            flops=2 * ROWS * 6_300_000, bytes_accessed=22_000_000, transcendentals=1_000_000
        ),
        name="feed_backward",
    )(active, grad_top, *mats[4], gate, upper, middle, feed_gain, *earlier)


def run_mix_backward(active, grad_middle, mats, proj, ssm, small, rope, pick, earlier=()):
    packed, dt_weight, out_weight, heads_weight, feeds = mats
    shapes = (
        shape(ROWS, WIDTH, BF16),
        shape(ROWS, CAT, BF16),
        shape(4, MIXED, F32),
        shape(1, MIXED, F32),
        shape(1, 128, F32),
        shape(1, 128, F32),
        shape(1, INNER, F32),
        shape(1, INNER, F32),
    )
    return pl.pallas_call(
        functools.partial(mix_backward_kernel, len(earlier)),
        out_shape=shapes,
        in_specs=[SMEM, VMEM] + [ANY] * 4 + [VMEM] * 9 + [ANY] * len(earlier),
        out_specs=(ANY,) * len(shapes),
        scratch_shapes=[
            *mirrored(shapes),
            scratch(ROWS, CAT, dtype=F32),
            scratch(ROWS, INNER, dtype=F32),
            scratch(INNER, WIDTH),
            scratch(512, WIDTH),
            scratch(ROWS, INNER, dtype=F32),
            scratch(ROWS, 512, dtype=F32),
            scratch(LEN, INNER, dtype=F32),
            scratch(LEN, INNER, dtype=F32),
            scratch(LEN, MIXED, dtype=F32),
            pltpu.SemaphoreType.DMA((4,)),
            pltpu.SemaphoreType.DMA((8,)),
        ],
        input_output_aliases={15 + k: k for k in range(len(earlier))},
        compiler_params=pltpu.CompilerParams(vmem_limit_bytes=LIMIT),
        cost_estimate=pl.CostEstimate(
            flops=2 * ROWS * 2_100_000, bytes_accessed=14_000_000, transcendentals=4_000_000
        ),
        name="mix_backward",
    )(
        active, grad_middle, out_weight, heads_weight, proj, ssm, *small[1:7], *rope, pick, *earlier
    )


def run_input_backward(active, grad_cat, grad_middle, start, mats, input_gain, earlier=()):
    shapes = (shape(ROWS, WIDTH, F32), shape(ROWS, WIDTH, BF16), shape(1, WIDTH, F32))
    return pl.pallas_call(
        functools.partial(input_backward_kernel, len(earlier)),
        out_shape=shapes,
        in_specs=[SMEM, VMEM, VMEM, VMEM, ANY, VMEM, VMEM] + [ANY] * len(earlier),
        out_specs=(ANY,) * len(shapes),
        scratch_shapes=[
            *mirrored(shapes),
            scratch(4, 64, 16, 1024),
            pltpu.SemaphoreType.DMA((4,)),
            pltpu.SemaphoreType.DMA((3,)),
        ],
        input_output_aliases={7 + k: k for k in range(len(earlier))},
        compiler_params=pltpu.CompilerParams(vmem_limit_bytes=LIMIT),
        cost_estimate=pl.CostEstimate(
            flops=2 * ROWS * 4_200_000, bytes_accessed=13_000_000, transcendentals=1000
        ),
        name="input_backward",
    )(active, grad_cat, grad_middle, start, *mats[:2], input_gain, *earlier)


def finish_kernel(
    mine, rows_own, gate_own, up_own, rows_got, gate_got, up_got, rows_last, gate_last, up_last,
    in_grad, query_grad, key_grad, value_grad, out_grad, heads_grad, gate_grad, up_grad, down_grad,
):
    def total(k, own, got, last):
        depth = own.shape[1]
        part = own[mine[k]].astype(F32) + got[:depth].astype(F32)
        return part + last[...].astype(F32)

    value = total(0, rows_own, rows_got, rows_last)
    down_grad[0] = value[:, :WIDTH]
    out_grad[0] = value[:24, WIDTH:]
    heads_grad[0] = value[24:, WIDTH:]
    value = total(1, gate_own, gate_got, gate_last)
    gate_grad[0] = value[:, :FEED]
    query_grad[0] = value[:, FEED : FEED + K0]
    key_grad[0] = value[:, FEED + K0 : FEED + V0]
    value_grad[0] = value[:, FEED + V0 : FEED + Z0]
    in_grad[0, :, : 2048 - Z0] = value[:, FEED + Z0 :]
    value = total(2, up_own, up_got, up_last)
    up_grad[0] = value[:, :FEED]
    in_grad[0, :, 2048 - Z0 :] = value[:, FEED : FEED + T0 + HEADS - 2048]


def run_finish(mine, owns, gots, lasts):
    shapes = tuple(
        jax.ShapeDtypeStruct((1, *dims), F32)
        for dims in (
            (16, T0 + HEADS - Z0),
            (16, 512),
            (16, 128),
            (16, 128),
            (24, WIDTH),
            (8, WIDTH),
            (16, FEED),
            (16, FEED),
            (32, WIDTH),
        )
    )
    return pl.pallas_call(
        finish_kernel,
        out_shape=shapes,
        in_specs=[SMEM] + [VMEM] * 9,
        out_specs=(VMEM,) * 9,
        compiler_params=pltpu.CompilerParams(vmem_limit_bytes=LIMIT // 2),
        name="finish",
    )(mine, *owns, *gots, *lasts)


def rope_tables():
    position = jnp.arange(LEN).astype(F32)
    inverse = 10000.0 ** (-(jnp.arange(32).astype(F32) * 2.0) / 64)
    angle = position[:, None] * inverse[None, :]
    cosine = jnp.tile(jnp.cos(angle), (1, 16))
    sine = jnp.sin(angle)
    return cosine, jnp.tile(jnp.concatenate([-sine, sine], axis=1), (1, 8))


def head_pick():
    lanes = lax.broadcasted_iota(jnp.int32, (INNER, 128), 0) // 64
    return (lanes == lax.broadcasted_iota(jnp.int32, (INNER, 128), 1)).astype(BF16)


def prepared_small(pieces):
    input_gain, kernel, bias, step_bias, decay_log, skip, mixer_gain, feed_gain = pieces

    def padded(v):
        return jnp.pad(v, (0, 128 - HEADS))[None]

    return (
        input_gain[None],
        kernel,
        bias[None],
        padded(step_bias),
        padded(decay_log),
        jnp.repeat(skip, 64)[None],
        mixer_gain[None],
        feed_gain[None],
    )


FIRST = (1, 0, 3, 2)
SECOND = (3, 2, 1, 0)


def partners(axis, turn):
    me = lax.axis_index(axis)
    near, far = me + 1 - 2 * lax.rem(me, 2), 3 - me
    flipped = lax.rem(lax.axis_index("section") + turn, 2) == 1
    found = (jnp.where(flipped, far, near), jnp.where(flipped, near, far))
    swaps = []
    for step in range(2):
        tables = [(FIRST, SECOND)[(core + turn + step) % 2] for core in range(2)]
        swaps.append([(4 * c + i, 4 * c + tables[c][i]) for c in range(2) for i in range(4)])
    return me, found, swaps


def exchange(array, axis, pairs):
    return lax.ppermute(array, ("section", axis), pairs)


def first_sent(part, axis, turn):
    me, (one, two), swaps = partners(axis, turn)
    return part([one, lax.rem(me + 2, 4)]).astype(BF16)


def first_got(sent, axis, turn):
    return exchange(sent, axis, partners(axis, turn)[2][0])


def handed_on(part, got, axis, turn):
    me, (one, two), swaps = partners(axis, turn)
    return (part([two]) + got[got.shape[0] // 2 :].astype(F32)).astype(BF16)


def totalled(part, got, handed, axis, turn):
    me, found, (swap_one, swap_two) = partners(axis, turn)
    last = exchange(handed, axis, swap_two)
    return part([me]) + got[: got.shape[0] // 2].astype(F32) + last.astype(F32)


def product_of(left, right, place):
    blocks = left.reshape(4, 4, 4, left.shape[0] // 64, left.shape[1])

    def part(places):
        picked = [lax.dynamic_index_in_dim(blocks, p, place, keepdims=False) for p in places]
        return dot(jnp.concatenate(picked, axis=0).reshape(-1, left.shape[1]), right)

    return part


def quarters_of(array, dim):
    def part(places):
        picked = [lax.dynamic_index_in_dim(array, p, dim, keepdims=False) for p in places]
        return jnp.concatenate(picked, axis=0).reshape(-1, array.shape[-1]).astype(F32)

    return part


def summed_on(array, axis, dim, turn):
    part = quarters_of(array, dim)
    got = first_got(first_sent(part, axis, turn), axis, turn)
    return totalled(part, got, handed_on(part, got, axis, turn), axis, turn)


def second_summed(parts, order, depth):
    array = jnp.concatenate([p.astype(BF16) for p in parts], axis=1)
    width = array.shape[1]
    rest = [0, 1, 2]
    rest.remove(order[0])
    array = array.reshape(4, 4, depth, width)
    array = summed_on(array, DP[order[1]], rest.index(order[1]), 0).astype(BF16)
    return array.reshape(4, depth, width)


def gathered_on(array, axis):
    me, (one, two), (swap_one, swap_two) = partners(axis, 0)
    got = exchange(array, axis, swap_one)
    far = exchange(jnp.stack([array, got]), axis, swap_two)
    return (array, got, far), (me, one, two, lax.rem(me + 2, 4))


def placed(blocks, places, dim):
    own, got, far = blocks
    whole = jnp.zeros((*own.shape[:dim], 4, *own.shape[dim:]), own.dtype)
    for block, place in zip((own, got, far[0], far[1]), places):
        whole = lax.dynamic_update_index_in_dim(whole, block, place, dim)
    return whole


def gathered(block, order):
    block = placed(*gathered_on(block, DP[order[2]]), 0)
    block = placed(*gathered_on(block, DP[order[1]]), 0 if order[1] < order[2] else 1)
    return gathered_on(block, DP[order[0]])


def column_blocks(matrix):
    return [matrix[:, at : at + 1024] for at in range(0, matrix.shape[1], 1024)]


def on_device(
    layer_input,
    out_grad,
    in_weight,
    query_weight,
    key_weight,
    value_weight,
    out_weight,
    heads_weight,
    gate_weight,
    up_weight,
    down_weight,
    *pieces,
):
    micro, part, width = layer_input.shape
    rows = micro * part
    cat = jnp.concatenate(
        [query_weight[0], key_weight[0], value_weight[0], in_weight[0, :, :3328]], axis=1
    )
    steps = jnp.pad(in_weight[0, :, 3328:].reshape(1, -1), ((0, 7), (0, 1024 - 16 * HEADS)))
    own = jnp.concatenate(
        [
            *column_blocks(cat),
            out_weight[0],
            heads_weight[0],
            steps,
        ],
        axis=0,
    )
    packed = lax.all_gather(own, DP, axis=0, tiled=False)
    dt_weight = packed[:, DT0, : 16 * HEADS].reshape(WIDTH, HEADS)
    feeds = [
        gathered(weight[0], order)
        for weight, order in (
            (gate_weight, (0, 1, 2)),
            (up_weight, (1, 2, 0)),
            (down_weight, (2, 0, 1)),
        )
    ]
    places = jnp.stack([place for blocks, found in feeds for place in found]).astype(jnp.int32)
    mats = (
        packed,
        jnp.pad(dt_weight, ((0, 0), (0, 128 - HEADS))),
        (places, *(piece for blocks, found in feeds for piece in blocks)),
    )
    small = prepared_small([piece[0] for piece in pieces])
    rope = rope_tables()
    pick = head_pick()
    first = lax.axis_index("section") == 0

    start_low = layer_input.reshape(rows, width)
    out_mat, heads_mat, *kept_low = run_forward(start_low, mats, small, rope)
    mats = (*mats[:2], out_mat, heads_mat, mats[2])
    start_high = lax.ppermute(kept_low[0], "section", [(0, 1)])
    kept_high = run_forward(start_high, mats, small, rope)
    layer_outputs = jnp.where(first, kept_low[0], kept_high[0]).reshape(1, micro, part, width)

    on_high = jnp.where(first, 0, 1).astype(jnp.int32).reshape(1)
    on_low = 1 - on_high
    top_high = out_grad.reshape(rows, width)
    feed_high = run_feed_backward(
        on_high, top_high, mats, kept_high[8], kept_high[9], kept_high[6], small[7]
    )
    mix_high = run_mix_backward(
        on_high, feed_high[2], mats, kept_high[2], kept_high[3], small, rope, pick
    )
    input_high = run_input_backward(
        on_high, mix_high[1], feed_high[2], start_high, mats, small[0]
    )
    slots = (1, 4, 5, 7, 10)
    low_top, *tied = lax.optimization_barrier((input_high[1], *(kept_high[s] for s in slots)))
    tied = dict(zip(slots, tied))
    top_low = lax.ppermute(low_top, "section", [(1, 0)])

    def chosen(slot):
        return jnp.where(first, kept_low[slot], tied[slot])

    normed_t, ffin_t, hidden_t = (chosen(slot).T for slot in (1, 7, 10))
    joined_t = jnp.concatenate(
        [chosen(4).T.reshape(64, 24, rows), chosen(5).T.reshape(64, 8, rows)], axis=1
    ).reshape(2048, rows)

    feed = run_feed_backward(
        on_low, top_low, mats, kept_low[8], kept_low[9], kept_low[6], small[7], feed_high
    )
    grad_gate, grad_upper, grad_middle, feed_grad = feed
    grad_low = jnp.where(first, top_low, top_high)
    grad_low, grad_gate, grad_upper = lax.optimization_barrier((grad_low, grad_gate, grad_upper))
    orders = ((2, 0, 1), (0, 1, 2), (1, 2, 0))
    axes = [DP[order[0]] for order in orders]
    products = [
        product_of(left, right, order[0])
        for left, right, order in zip(
            (hidden_t, ffin_t, ffin_t), (grad_low, grad_gate, grad_upper), orders
        )
    ]
    sents = [first_sent(p, axis, 0) for p, axis in zip(products, axes)]
    grad_middle, *sents = lax.optimization_barrier((grad_middle, *sents))
    gots = [first_got(sent, axis, 0) for sent, axis in zip(sents, axes)]
    mix = run_mix_backward(
        on_low, grad_middle, mats, kept_low[2], kept_low[3], small, rope, pick, mix_high
    )
    grad_branch, grad_cat, *small_grads = mix
    mix_products = [
        product_of(left, right, order[0])
        for left, right, order in zip(
            (joined_t, normed_t, normed_t),
            (grad_branch, grad_cat[:, :2048], grad_cat[:, 2048:]),
            orders,
        )
    ]
    mix_sents = [first_sent(p, axis, 0) for p, axis in zip(mix_products, axes)]
    pending = lax.optimization_barrier((*gots, *mix_sents))
    gots, mix_sents = pending[:3], pending[3:]
    mix_gots = [first_got(sent, axis, 0) for sent, axis in zip(mix_sents, axes)]
    handed = [handed_on(p, got, axis, 0) for p, got, axis in zip(products, gots, axes)]
    last_middle, *pending = lax.optimization_barrier(
        (grad_middle, grad_low, grad_gate, grad_upper, grad_branch, grad_cat, *handed)
    )
    rights, (late_branch, late_cat), handed = pending[:3], pending[3:5], pending[5:]
    products = [
        product_of(left, right, order[0])
        for left, right, order in zip((hidden_t, ffin_t, ffin_t), rights, orders)
    ]
    mix_products = [
        product_of(left, right, order[0])
        for left, right, order in zip(
            (joined_t, normed_t, normed_t),
            (late_branch, late_cat[:, :2048], late_cat[:, 2048:]),
            orders,
        )
    ]
    feed_parts = [
        totalled(p, got, hand, axis, 0)
        for p, got, hand, axis in zip(products, gots, handed, axes)
    ]
    mix_parts = [
        totalled(p, got, handed_on(p, got, axis, 0), axis, 0)
        for p, got, axis in zip(mix_products, mix_gots, axes)
    ]
    grad_start, unused, input_grad = run_input_backward(
        on_low, grad_cat, last_middle, start_low, mats, small[0], input_high
    )
    small_grads = [input_grad, *small_grads]
    input_g, kernel_g, bias_g, step_g, decay_g, skip_g, mixer_g = small_grads
    small_grads = (
        input_g[0],
        kernel_g,
        bias_g[0],
        step_g[0, :HEADS],
        decay_g[0, :HEADS],
        skip_g.reshape(HEADS, 64).sum(axis=1),
        mixer_g[0],
        feed_grad[0],
    )
    vector = jnp.concatenate([piece.reshape(-1) for piece in small_grads])
    vector = jnp.pad(vector, (0, -vector.shape[0] % 1024)).reshape(-1, 128)
    vectors = lax.all_gather(vector.astype(BF16), DP, axis=0, tiled=False)
    seconds = [
        second_summed(pair, order, depth)
        for pair, order, depth in zip(zip(feed_parts, mix_parts), orders, (32, 16, 16))
    ]
    axes = [DP[order[2]] for order in orders]
    quarters = [quarters_of(array, 0) for array in seconds]
    sents = [first_sent(p, axis, 0) for p, axis in zip(quarters, axes)]
    gots = [first_got(sent, axis, 0) for sent, axis in zip(sents, axes)]
    vectors, *unused = lax.optimization_barrier((vectors, *sents))
    total = jnp.sum(vectors.astype(F32), axis=0).reshape(-1)
    handed = [handed_on(p, got, axis, 0) for p, got, axis in zip(quarters, gots, axes)]
    lasts = [
        exchange(hand, axis, partners(axis, 0)[2][1]) for hand, axis in zip(handed, axes)
    ]
    mine = jnp.stack([lax.axis_index(axis) for axis in axes]).astype(jnp.int32)
    mat_grads = run_finish(mine, seconds, gots, lasts)

    summed, at = ([], 0)
    for piece in small_grads:
        summed.append(total[at : at + piece.size].reshape(1, *piece.shape))
        at += piece.size
    return (
        layer_outputs,
        grad_start.reshape(1, micro, part, width),
        *mat_grads,
        *summed,
    )


def solution(mesh):
    torus = Mesh(
        mesh.devices.reshape(mesh.shape["section"], 4, 4, 4), ("section", "dp_0", "dp_1", "dp_2")
    )
    in_specs = (
        P(None, DP, None),
        P(None, DP, None),
        P("section", DP, None),
        P("section", DP, None),
        P("section", DP, None),
        P("section", DP, None),
        P("section", DP, None),
        P("section", DP, None),
        P("section", DP, None),
        P("section", DP, None),
        P("section", DP, None),
        P("section", None),
        P("section", None, None),
        P("section", None),
        P("section", None),
        P("section", None),
        P("section", None),
        P("section", None),
        P("section", None),
    )
    out_specs = (
        P("section", None, DP, None),
        P("section", None, DP, None),
        P("section", DP, None),
        P("section", DP, None),
        P("section", DP, None),
        P("section", DP, None),
        P("section", DP, None),
        P("section", DP, None),
        P("section", DP, None),
        P("section", DP, None),
        P("section", DP, None),
        P("section", None),
        P("section", None, None),
        P("section", None),
        P("section", None),
        P("section", None),
        P("section", None),
        P("section", None),
        P("section", None),
    )
    return jax.shard_map(
        on_device, mesh=torus, in_specs=in_specs, out_specs=out_specs, check_vma=False
    )
```
